32 devices in a mesh: grp: 2 (over y), gx: 4 (over z), gy: 2 (over core), shot: 2 (over x).
Axes of the slice: x: 2, y: 2, z: 4, core: 2. Of those that a mesh axis runs over, the one named last changes fastest.
Arguments:
- conductivity: float32 [64, 128, 128], P(('grp', 'gx'), 'gy'), parts along dimension 0, may hold values from 0.2 to 5
- stations: int32 [512], P('grp'), parts along dimension 0, may hold values from 0 to 524287
- currents: float32 [4, 256], P(('grp', 'shot')), parts along dimension 0, may hold values from 0.5 to 2
- receivers: int32 [1024, 2], P('grp'), parts along dimension 0, may hold values from 0 to 255
- observed: float32 [4, 512], P(('grp', 'shot')), parts along dimension 0, may hold values from -4 to 4
Outputs:
- potentials: float32 [4, 32, 128, 128], P(('grp', 'shot'), 'gx', 'gy'), parts along dimension 0
- gradient: float32 [64, 128, 128], P(('grp', 'gx'), ('gy', 'shot')), parts along dimension 0
The draws below stay inside these ranges and needn't reach their ends.
There are 2 independent parts, one for each index of `grp`. The reference program is written for one: setup_inputs(seed, part) draws one part's arguments, and reference() takes and returns one part's arrays. A program takes and returns all parts, laid end to end along the dimension named above; each array names one. Nothing has to cross between parts.
All inputs are finite; a program needn't handle non-finite values.
Results may differ from the reference program's by a relative error of at most 0.00014.
Values sent between devices are 32-bit elements; how exact they have to be, the bound alone decides.
No kernel may reach another device: no remote copies, remote signals or barrier semaphores. Data moves between devices by JAX's collectives and lax.ppermute only.
A program may use at most 128 MiB of HBM per device.

```python
import math
import jax
import jax.numpy as jnp
from jax import lax

NZ = 128
ELEC = 256
REC = 512
LEVELS = 4
COARSE_SWEEPS = 16
NX = 32
NY = 128
SHOTS = 2


def touch_ends(drawn, key, low, top_value):
    spot = [jax.random.randint(jax.random.fold_in(key, axis), (), 0, length) for axis, length in enumerate(drawn.shape)]
    longest = drawn.shape.index(max(drawn.shape))
    next_to = spot[:longest] + [(spot[longest] + 1) % drawn.shape[longest]] + spot[longest + 1:]
    return drawn.at[tuple(spot)].set(low).at[tuple(next_to)].set(top_value)


def block_scale(rng, shape, cuts, low, largest):
    def one(axis_at, blocks):
        steps = jax.random.uniform(jax.random.fold_in(jax.random.fold_in(rng, 6), axis_at), (blocks,), jnp.float32, low / len(cuts), largest / len(cuts))
        return jnp.repeat(jnp.exp(steps), shape[axis_at] // blocks).reshape((-1,) + (1,) * (len(shape) - axis_at - 1))

    factor_of = one(*cuts[0])
    for cut in cuts[1:]:
        factor_of = factor_of * one(*cut)
    return factor_of


def noise(rng, shape, spread, limit, split=(), held_as=jnp.bfloat16):
    drawn = spread * jax.random.normal(rng, shape, jnp.float32)
    if split:
        drawn = drawn * block_scale(rng, shape, split, -0.22, 0.18)
    return jnp.clip(drawn, -limit, limit).astype(held_as)


def setup_inputs(seed: int = 0, part: int = 0) -> dict:
    splits = jax.random.split(jax.random.key(seed), 6)
    own_keys = jax.random.split(jax.random.fold_in(splits[5], part), 6)
    return {
        "conductivity": jnp.clip(jnp.exp(math.log(5.0) - 3.218876 * jax.random.uniform(own_keys[0], (NX, NY, NZ), jnp.float32) ** block_scale(own_keys[0], (NX, NY, NZ), ((0, 4), (1, 2)), -0.2, 0.2)), 0.2, 5.0),
        "stations": touch_ends(jax.random.randint(own_keys[1], (ELEC,), 0, NX * NY * NZ), jax.random.fold_in(own_keys[1], 1), 0, (NX * NY * NZ) - 1).astype(jnp.int32),
        "currents": jnp.clip(jnp.exp(math.log(2.0) - 1.3862944 * jax.random.uniform(own_keys[2], (SHOTS, ELEC), jnp.float32) ** block_scale(own_keys[2], (SHOTS, ELEC), ((0, 2),), -0.2, 0.2)), 0.5, 2.0),
        "receivers": touch_ends(jax.random.randint(own_keys[3], (REC, 2), 0, ELEC), jax.random.fold_in(own_keys[3], 1), 0, ELEC - 1).astype(jnp.int32),
        "observed": noise(own_keys[4], (SHOTS, REC), 0.5, 4.0, ((0, 2),), jnp.float32),
    }


DAMPING = 0.8


def neighbours(field):
    padded = jnp.pad(field, ((1, 1), (1, 1), (1, 1)))
    return [padded[2:, 1:-1, 1:-1], padded[:-2, 1:-1, 1:-1], padded[1:-1, 2:, 1:-1],
            padded[1:-1, :-2, 1:-1], padded[1:-1, 1:-1, 2:], padded[1:-1, 1:-1, :-2]]


def couplings(conduct, level_scale):
    return [level_scale * 0.5 * (conduct + other) for other in neighbours(conduct)]


def apply_operator(field, links):
    summed = jnp.zeros_like(field)
    for link, other in zip(links, neighbours(field)):
        summed = summed + link * (field - other)
    return summed


def relaxed(field, source, links, diag_level):
    return field + DAMPING * (source - apply_operator(field, links)) / diag_level


def restrict(field):
    extent = field.shape
    return field.reshape(extent[0] // 2, 2, extent[1] // 2, 2, extent[2] // 2, 2).mean(axis=(1, 3, 5))


def prolong(field):
    return jnp.repeat(jnp.repeat(jnp.repeat(field, 2, axis=0), 2, axis=1), 2, axis=2)


def vcycle(source, level_index, operators):
    links, diag_level = operators[level_index]
    field = DAMPING * source / diag_level
    if level_index == LEVELS - 1:
        def turn(turn_index, iterate):
            return relaxed(iterate, source, links, diag_level)
        return lax.fori_loop(0, COARSE_SWEEPS - 1, turn, field)
    field = relaxed(field, source, links, diag_level)
    residual = source - apply_operator(field, links)
    field = field + prolong(vcycle(restrict(residual), level_index + 1, operators))
    field = relaxed(field, source, links, diag_level)
    return relaxed(field, source, links, diag_level)


def place(amounts, stations):
    flat = jnp.zeros((NX * NY * NZ,), jnp.float32).at[stations].add(amounts)
    return flat.reshape(NX, NY, NZ)


def reference(conductivity, stations, currents, receivers, observed):
    operators = []
    conduct = conductivity
    for level_index in range(LEVELS):
        links = couplings(conduct, 0.25 ** level_index)
        total_link = links[0]
        for link in links[1:]:
            total_link = total_link + link
        operators.append((links, total_link))
        if level_index < LEVELS - 1:
            conduct = restrict(conduct)
    positions = jnp.arange(ELEC).astype(jnp.int32)[:, None]
    pairs = (receivers[:, 0][None, :] == positions).astype(jnp.float32) - (receivers[:, 1][None, :] == positions).astype(jnp.float32)

    def one_shot(gradient, inputs):
        shot_currents, shot_observed = inputs
        potential = vcycle(place(shot_currents, stations), 0, operators)
        readings = potential.reshape(-1)[stations]
        misfit = jnp.dot(readings, pairs, precision=lax.Precision.HIGHEST) - shot_observed
        back_source = jnp.dot(pairs, misfit, precision=lax.Precision.HIGHEST)
        adjoint = vcycle(place(back_source, stations), 0, operators)
        for other_u, other_w in zip(neighbours(potential), neighbours(adjoint)):
            gradient = gradient - 0.5 * (potential - other_u) * (adjoint - other_w)
        return gradient, potential

    gradient, potentials = lax.scan(one_shot, jnp.zeros((NX, NY, NZ), jnp.float32), (currents, observed))
    return potentials, gradient
```

```python
import functools

import jax
import jax.numpy as jnp
from jax import lax
from jax.experimental import pallas as pl
from jax.experimental.pallas import tpu as pltpu
from jax.sharding import PartitionSpec as P

LEVELS = 4
COARSE_SWEEPS = 16


DAMPING = 0.8

EDGE = 8
LANES = 128
REPLICATED_BYTES = 4 * 2**20
VMEM_BYTES = 56 * 2**20


def halves(value):
    high = value.astype(jnp.bfloat16)
    return high, (value - high.astype(jnp.float32)).astype(jnp.bfloat16)


def product(value, matrix):
    high, low = halves(value)
    return jnp.dot(high, matrix, preferred_element_type=jnp.float32) + jnp.dot(
        low, matrix, preferred_element_type=jnp.float32
    )


def lane_of(shape):
    return lax.broadcasted_iota(jnp.int32, shape, len(shape) - 1)


def row_of(shape):
    return lax.broadcasted_iota(jnp.int32, shape, len(shape) - 2)


def up(field, axis, step=1):
    return pltpu.roll(field, field.shape[axis] - step, axis)


def down(field, axis, step=1):
    return pltpu.roll(field, step, axis)


def masked(keep, field):
    return jnp.where(keep, field, 0.0)


def matrix_of(rows, cols, test, value):
    shape = (rows, cols)
    return jnp.where(test(row_of(shape), lane_of(shape)), value, 0.0).astype(jnp.bfloat16)


def coarse_coefficients(cond, others, keeps, level_scale):
    total = 6.0 * cond
    for other in others:
        total = total + other
    total = 0.5 * total
    valid = cond > 0.0
    inverse = masked(valid, DAMPING / jnp.where(valid, total, 1.0))
    links = []
    for other, keep in zip(others, keeps):
        link = inverse * (0.5 * (cond + other))
        links.append(link if keep is None else masked(keep, link))
    return links, inverse * (1.0 / level_scale), masked(valid, total * (level_scale / DAMPING))


def replicated_kernel(
    dims,
    blocks_ref,
    place_ref,
    cells_ref,
    stations_ref,
    currents_ref,
    receivers_ref,
    observed_ref,
    potentials_ref,
    gradient_ref,
    cond,
    link_x,
    link_y,
    link_z,
    weight,
    diag,
    source,
    first,
    second,
    forward,
    pair_rows,
    cond1,
    links1,
    weight1,
    back1,
    field1,
    turned1,
    other1,
    turned_other1,
    base1,
    links2,
    weight2,
    back2,
    rows2,
    gathered,
    sems,
):
    nx, ny, rows, cols, count_x, count_y, count_s = dims
    f32 = jnp.float32
    electrodes = stations_ref.shape[1]
    slabs1 = nx // 4
    rows1 = ny // 2
    rows2_count = ny // 4
    rows3 = ny // 8
    slabs3 = nx // 8
    inner = pl.ds(EDGE, ny)
    above = pl.ds(EDGE + 1, ny)
    below = pl.ds(EDGE - 1, ny)

    part = rows // count_s
    copies = []
    for index_x in range(count_x):
        for index_y in range(count_y):
            for index_s in range(count_s):
                block = (index_x * count_y + index_y) * count_s + index_s
                copies.append(
                    pltpu.make_async_copy(
                        blocks_ref.at[block],
                        cond.at[
                            pl.ds(1 + index_x * rows + index_s * part, part),
                            pl.ds(EDGE + index_y * cols, cols),
                            :,
                        ],
                        sems.at[block],
                    )
                )
    for copy in copies:
        copy.start()

    edge_plane = jnp.zeros((ny + 2 * EDGE, LANES), f32)
    edge_rows = jnp.zeros((EDGE, LANES), f32)
    for array in (cond, first, second, forward):
        array[0] = edge_plane
        array[nx + 1] = edge_plane

    def clear_edges(x, carry):
        for array in (cond, first, second, forward):
            array[x + 1, pl.ds(0, EDGE), :] = edge_rows
            array[x + 1, pl.ds(EDGE + ny, EDGE), :] = edge_rows
        link_y[x, pl.ds(0, EDGE), :] = edge_rows
        return carry

    lax.fori_loop(0, nx, clear_edges, 0)
    plane1 = jnp.zeros((rows1, LANES), f32)
    for array in (turned1, turned_other1):
        array[0] = plane1
        array[slabs1 + 1] = plane1

    station_row = stations_ref[...]
    station_line = station_row // LANES
    station_z = station_row % LANES
    restrict1 = [
        matrix_of(LANES, LANES, lambda r, c: c == r // 2 + 64 * p, 0.125) for p in range(2)
    ]
    restrict2 = matrix_of(LANES, LANES, lambda r, c: c == r % 64 // 2, 0.125)
    expand2 = matrix_of(LANES, LANES, lambda r, c: r == c % 64 // 2, 1.0)
    expand1 = [
        matrix_of(LANES, LANES, lambda r, c: r == c // 2 + 64 * p, 1.0) for p in range(2)
    ]
    restrict3 = [
        matrix_of(LANES, LANES, lambda r, c: (r < 32) & (c == r // 2 + 16 * x), 0.125)
        for x in range(slabs3)
    ]
    expand3 = [
        matrix_of(LANES, LANES, lambda r, c: (c < 32) & (r == c // 2 + 16 * x), 1.0)
        for x in range(slabs3)
    ]

    for copy in copies:
        copy.wait()

    lane0 = lane_of((ny, LANES))
    not_last_z = lane0 < LANES - 1
    not_first_z = lane0 > 0

    def setup(x, carry):
        here = cond[x + 1, inner, :]
        next_x = cond[x + 2, inner, :]
        next_y = cond[x + 1, above, :]
        next_z = masked(not_last_z, up(here, 1))
        link_x[x + 1] = 0.5 * (here + next_x)
        link_y[x, inner, :] = 0.5 * (here + next_y)
        link_z[x] = masked(not_last_z, 0.5 * (here + next_z))
        total = next_x + cond[x, inner, :] + next_y + cond[x + 1, below, :]
        total = total + next_z + masked(not_first_z, down(here, 1))
        total = 3.0 * here + 0.5 * total
        diag[x] = total
        weight[x] = DAMPING / total
        return carry

    link_x[0] = jnp.zeros((ny, LANES), f32)
    lax.fori_loop(0, nx, setup, 0)

    def pairs_in_y(ref, index, count):
        return ref[index, pl.ds(0, count, stride=2), :] + ref[index, pl.ds(1, count, stride=2), :]

    def restrict_slabs(read, slab):
        result = None
        for p in range(2):
            pair_rows[p] = read(4 * slab + 2 * p) + read(4 * slab + 2 * p + 1)
        for p in range(2):
            term = product(pairs_in_y(pair_rows, p, rows1), restrict1[p])
            result = term if result is None else result + term
        return result

    def restrict_cond(slab, carry):
        cond1[slab] = restrict_slabs(lambda x: cond[x + 1, inner, :], slab)
        return carry

    lax.fori_loop(0, slabs1, restrict_cond, 0)

    lane1 = lane_of((rows1, LANES))
    row1 = row_of((rows1, LANES))
    even = lane1 < 64
    keeps1 = [
        None,
        None,
        row1 < rows1 - 1,
        row1 > 0,
        lane1 % 64 < 63,
        lane1 % 64 > 0,
    ]
    for slab in range(slabs1):
        here = cond1[slab]
        turned = down(here, 1, 64)
        before = down(cond1[slab - 1], 1, 64) if slab > 0 else plane1
        after = down(cond1[slab + 1], 1, 64) if slab < slabs1 - 1 else plane1
        others = [jnp.where(even, turned, after), jnp.where(even, before, turned)]
        others += [
            masked(keeps1[2], up(here, 0)),
            masked(keeps1[3], down(here, 0)),
            masked(keeps1[4], up(here, 1)),
            masked(keeps1[5], down(here, 1)),
        ]
        links, inverse, back = coarse_coefficients(here, others, keeps1, 0.25)
        for index, link in enumerate(links):
            links1[index, slab] = link
        weight1[slab] = inverse
        back1[slab] = back

    def restrict_level2(read, slab):
        pair_rows[0, pl.ds(0, rows1), :] = read(slab)
        return product(pairs_in_y(pair_rows, 0, rows2_count), restrict2)

    total2 = slabs1 * rows2_count
    for slab in range(slabs1):
        rows2[0, pl.ds(slab * rows2_count, rows2_count), :] = restrict_level2(
            lambda s: cond1[s], slab
        )
    row2 = row_of((total2, LANES))
    lane2 = lane_of((total2, LANES))
    here = rows2[0]
    keeps2 = [
        row2 < total2 - rows2_count,
        row2 >= rows2_count,
        row2 % rows2_count < rows2_count - 1,
        row2 % rows2_count > 0,
        lane2 < 31,
        lane2 > 0,
    ]
    shifts2 = [(up, 0, rows2_count), (down, 0, rows2_count), (up, 0, 1), (down, 0, 1), (up, 1, 1), (down, 1, 1)]
    others = [masked(k, s(here, axis, step)) for k, (s, axis, step) in zip(keeps2, shifts2)]
    links, inverse, back = coarse_coefficients(here, others, keeps2, 0.25**2)
    for index, link in enumerate(links):
        links2[index] = link
    weight2[...] = inverse
    back2[...] = back

    def restrict_level3(value):
        result = None
        for x in range(slabs3):
            start = 2 * x * rows2_count
            pair_rows[0, pl.ds(0, rows2_count), :] = (
                value[start : start + rows2_count]
                + value[start + rows2_count : start + 2 * rows2_count]
            )
            term = product(pairs_in_y(pair_rows, 0, rows3), restrict3[x])
            result = term if result is None else result + term
        return result

    row3 = row_of((rows3, LANES))
    lane3 = lane_of((rows3, LANES))
    used3 = lane3 < 16 * slabs3
    keeps3 = [
        lane3 < 16 * (slabs3 - 1),
        (lane3 >= 16) & used3,
        (row3 < rows3 - 1) & used3,
        (row3 > 0) & used3,
        (lane3 % 16 < 15) & used3,
        (lane3 % 16 > 0) & used3,
    ]
    shifts3 = [(up, 1, 16), (down, 1, 16), (up, 0, 1), (down, 0, 1), (up, 1, 1), (down, 1, 1)]
    here = restrict_level3(here)
    others = [masked(k, s(here, axis, step)) for k, (s, axis, step) in zip(keeps3, shifts3)]
    links3, weight3, _ = coarse_coefficients(here, others, keeps3, 0.25**3)

    def neighbour_sum(value, links, shifts, base):
        for link, (shift, axis, step) in zip(links, shifts):
            base = base + link * shift(value, axis, step)
        return base

    def level3(rhs):
        base = weight3 * rhs
        value = base
        for _ in range(COARSE_SWEEPS - 1):
            value = neighbour_sum(value, links3, shifts3, base + (1.0 - DAMPING) * value)
        return value

    def level2(rhs):
        base = weight2[...] * rhs
        links = [links2.at[index] for index in range(6)]

        def total(value):
            result = base
            for link, (shift, axis, step) in zip(links, shifts2):
                result = result + link[...] * shift(value, axis, step)
            return result

        value = base
        value = (1.0 - DAMPING) * value + total(value)
        residual = (total(value) - DAMPING * value) * back2[...]
        coarse = level3(restrict_level3(residual))
        pieces = []
        for x in range(slabs3):
            wide = product(coarse, expand3[x])
            pair_rows[0, pl.ds(0, rows3, stride=2), :] = wide
            pair_rows[0, pl.ds(1, rows3, stride=2), :] = wide
            piece = pair_rows[0, pl.ds(0, rows2_count), :]
            pieces += [piece, piece]
        value = value + jnp.concatenate(pieces, axis=0)
        for _ in range(2):
            value = (1.0 - DAMPING) * value + total(value)
        return value

    def total1(slab, value, turned):
        here = value[slab]
        mine = turned[slab + 1]
        result = base1[slab]
        result = result + links1[0, slab] * jnp.where(even, mine, turned[slab + 2])
        result = result + links1[1, slab] * jnp.where(even, turned[slab], mine)
        result = result + links1[2, slab] * up(here, 0) + links1[3, slab] * down(here, 0)
        result = result + links1[4, slab] * up(here, 1) + links1[5, slab] * down(here, 1)
        return here, result

    def keep1(slab, value, field, turned):
        field[slab] = value
        turned[slab + 1] = down(value, 1, 64)

    def sweep1(value, turned, out, turned_out):
        def one(slab, carry):
            here, result = total1(slab, value, turned)
            keep1(slab, (1.0 - DAMPING) * here + result, out, turned_out)
            return carry

        lax.fori_loop(0, slabs1, one, 0)

    def level1():
        def begin(slab, carry):
            keep1(slab, base1[slab], field1, turned1)
            return carry

        lax.fori_loop(0, slabs1, begin, 0)
        sweep1(field1, turned1, other1, turned_other1)

        def residual(slab, carry):
            here, result = total1(slab, other1, turned_other1)
            field1[slab] = (result - DAMPING * here) * back1[slab]
            return carry

        lax.fori_loop(0, slabs1, residual, 0)
        for slab in range(slabs1):
            rows2[0, pl.ds(slab * rows2_count, rows2_count), :] = restrict_level2(
                lambda s: field1[s], slab
            )
        rows2[1] = level2(rows2[0])
        for slab in range(slabs1):
            wide = product(rows2[1, pl.ds(slab * rows2_count, rows2_count), :], expand2)
            pair_rows[0, pl.ds(0, rows2_count, stride=2), :] = wide
            pair_rows[0, pl.ds(1, rows2_count, stride=2), :] = wide
            keep1(slab, other1[slab] + pair_rows[0, pl.ds(0, rows1), :], field1, turned1)
        sweep1(field1, turned1, other1, turned_other1)
        sweep1(other1, turned_other1, field1, turned1)

    def total0(x, field):
        here = field[x + 1, inner, :]
        along_z = link_z[x]
        result = source[x]
        result = result + link_x[x + 1] * field[x + 2, inner, :]
        result = result + link_x[x] * field[x, inner, :]
        result = result + link_y[x, inner, :] * field[x + 1, above, :]
        result = result + link_y[x, below, :] * field[x + 1, below, :]
        result = result + along_z * up(here, 1) + down(along_z * here, 1)
        return here, result

    def sweep0(field, out, low, high):
        def one(x, carry):
            here, result = total0(x, field)
            out[x + 1, inner, :] = (1.0 - DAMPING) * here + weight[x] * result
            return carry

        lax.fori_loop(low, high, one, 0)

    lines = row_of((ny, electrodes))

    def spread(amounts):
        weighted = masked(row_of((LANES, electrodes)) == station_z, amounts)
        high, low = halves(weighted)
        table = jnp.concatenate([high, low], axis=0)

        def one(x, carry):
            chosen = jnp.where(lines + x * ny == station_line, 1.0, 0.0).astype(jnp.bfloat16)
            both = lax.dot_general(
                chosen, table, (((1,), (1,)), ((), ())), preferred_element_type=f32
            )
            value = both[:, :LANES] + both[:, LANES:]
            source[x] = value
            first[x + 1, inner, :] = weight[x] * value
            return carry

        lax.fori_loop(0, nx, one, 0)

    def descend():
        sweep0(first, second, 0, nx)

        def residual(x):
            here, result = total0(x, second)
            return result - diag[x] * here

        def one(slab, carry):
            base1[slab] = weight1[slab] * restrict_slabs(residual, slab)
            return carry

        lax.fori_loop(0, slabs1, one, 0)
        level1()

    def ascend(last, low, high, ends):
        def one(slab, carry):
            value = field1[slab]
            for p in range(2):
                wide = product(value, expand1[p])
                pair_rows[p, pl.ds(0, rows1, stride=2), :] = wide
                pair_rows[p, pl.ds(1, rows1, stride=2), :] = wide
            for p in range(2):
                for q in range(2):
                    x = 4 * slab + 2 * p + q
                    second[x + 1, inner, :] = second[x + 1, inner, :] + pair_rows[p]
            return carry

        slab_low, slab_high = ends
        lax.fori_loop(slab_low, slab_high, one, 0)
        sweep0(second, first, low[0], high[0])
        sweep0(first, last, low[1], high[1])

    spread(currents_ref[...])
    descend()
    ascend(forward, (0, 0), (nx, nx), (0, slabs1))

    def read(electrode, carry):
        line = cells_ref[electrode] // LANES
        gathered[pl.ds(electrode, 1), :] = forward[line // ny + 1, pl.ds(EDGE + line % ny, 1), :]
        return carry

    lax.fori_loop(0, electrodes, read, 0, unroll=8)
    turned = gathered[...].T
    readings = jnp.sum(
        masked(row_of((LANES, electrodes)) == station_z, turned), axis=0, keepdims=True
    )
    receivers = receivers_ref[...]
    numbers = lane_of((receivers.shape[0], electrodes))
    pairs = jnp.where(numbers == receivers[:, 0:1], 1.0, 0.0) - jnp.where(
        numbers == receivers[:, 1:2], 1.0, 0.0
    )
    pairs = pairs.astype(jnp.bfloat16)

    def exact(row, dims):
        high = row.astype(jnp.bfloat16)
        rest = row - high.astype(f32)
        middle = rest.astype(jnp.bfloat16)
        low = (rest - middle.astype(f32)).astype(jnp.bfloat16)
        result = None
        for piece in (low, middle, high):
            wide = jnp.broadcast_to(piece, (16, row.shape[1]))
            term = lax.dot_general(wide, pairs, (dims, ((), ())), preferred_element_type=f32)
            result = term if result is None else result + term
        return result[0:1]

    misfit = exact(readings, ((1,), (1,))) - observed_ref[...]
    spread(exact(misfit, ((1,), (0,))))
    descend()
    begin_x = place_ref[0]
    begin_y = pl.multiple_of(place_ref[1], cols)
    ascend(
        second,
        (jnp.maximum(begin_x - 2, 0), jnp.maximum(begin_x - 1, 0)),
        (jnp.minimum(begin_x + rows + 2, nx), jnp.minimum(begin_x + rows + 1, nx)),
        (jnp.maximum(begin_x - 3, 0) // 4, jnp.minimum(begin_x + rows + 3 + 3, nx) // 4),
    )

    chunk = cols // count_s
    lane_c = lane_of((chunk, LANES))
    for k in range(count_s):
        offset = pl.multiple_of(begin_y + place_ref[2 + k], chunk)
        mid = pl.ds(EDGE + offset, chunk)
        nxt = pl.ds(EDGE + offset + 1, chunk)
        prv = pl.ds(EDGE + offset - 1, chunk)

        def one(x, carry):
            here_u = forward[begin_x + x + 1, mid, :]
            here_w = second[begin_x + x + 1, mid, :]
            total = jnp.zeros_like(here_u)
            for index, window in ((2, mid), (0, mid), (1, nxt), (1, prv)):
                total = total + (here_u - forward[begin_x + x + index, window, :]) * (
                    here_w - second[begin_x + x + index, window, :]
                )
            keep = lane_c < LANES - 1
            ahead = (here_u - masked(keep, up(here_u, 1))) * (here_w - masked(keep, up(here_w, 1)))
            total = total + ahead + jnp.where(lane_c > 0, down(ahead, 1), here_u * here_w)
            gradient_ref[k, x] = -0.5 * total
            return carry

        lax.fori_loop(0, rows, one, 0)

    def give(x, carry):
        potentials_ref[x] = forward[begin_x + x + 1, pl.ds(EDGE + begin_y, cols), :]
        return carry

    lax.fori_loop(0, rows, give, 0)


def replicated(conductivity, stations, currents, receivers, observed):
    rows, cols, depth = conductivity.shape
    count_x = lax.axis_size("gx")
    count_y = lax.axis_size("gy")
    count_s = lax.axis_size("shot")
    nx, ny = rows * count_x, cols * count_y
    shot = lax.axis_index("shot")
    part = rows // count_s
    mine = lax.dynamic_slice_in_dim(conductivity, shot * part, part, axis=0)
    blocks = lax.all_gather(mine, ("gx", "gy", "shot"), axis=0, tiled=False)
    chunk = cols // count_s
    place = jnp.stack(
        [lax.axis_index("gx") * rows, lax.axis_index("gy") * cols]
        + [(shot + k) % count_s * chunk for k in range(count_s)]
    ).astype(jnp.int32)
    electrodes = stations.shape[0]
    slabs1, rows1 = nx // 4, ny // 2
    total2 = slabs1 * ny // 4
    f32 = jnp.float32
    padded = pltpu.VMEM((nx + 2, ny + 2 * EDGE, LANES), f32)
    plain = pltpu.VMEM((nx, ny, LANES), f32)
    small = pltpu.VMEM((slabs1, rows1, LANES), f32)
    small_edge = pltpu.VMEM((slabs1 + 2, rows1, LANES), f32)
    flat2 = pltpu.VMEM((total2, LANES), f32)
    vmem = pl.BlockSpec(memory_space=pltpu.VMEM)
    smem = pl.BlockSpec(memory_space=pltpu.SMEM)
    dims = (nx, ny, rows, cols, count_x, count_y, count_s)
    potentials, gradient = pl.pallas_call(
        functools.partial(replicated_kernel, dims),
        out_shape=(
            jax.ShapeDtypeStruct((rows, cols, LANES), f32),
            jax.ShapeDtypeStruct((count_s, rows, chunk, LANES), f32),
        ),
        in_specs=[pl.BlockSpec(memory_space=pl.ANY), smem, smem, vmem, vmem, vmem, vmem],
        out_specs=(vmem, vmem),
        scratch_shapes=[
            padded,
            pltpu.VMEM((nx + 1, ny, LANES), f32),
            pltpu.VMEM((nx, ny + EDGE, LANES), f32),
            plain,
            plain,
            plain,
            plain,
            padded,
            padded,
            padded,
            pltpu.VMEM((2, ny, LANES), f32),
            small,
            pltpu.VMEM((6, slabs1, rows1, LANES), f32),
            small,
            small,
            small,
            small_edge,
            small,
            small_edge,
            small,
            pltpu.VMEM((6, total2, LANES), f32),
            flat2,
            flat2,
            pltpu.VMEM((2, total2, LANES), f32),
            pltpu.VMEM((electrodes, LANES), f32),
            pltpu.SemaphoreType.DMA((count_x * count_y * count_s,)),
        ],
        compiler_params=pltpu.CompilerParams(vmem_limit_bytes=VMEM_BYTES),
        cost_estimate=pl.CostEstimate(flops=200_000_000, bytes_accessed=4_000_000, transcendentals=0),
    )(
        blocks,
        place,
        stations,
        stations.reshape(1, electrodes),
        currents,
        receivers,
        observed,
    )
    summed = gradient[0]
    for k in range(1, count_s):
        pairs = [(i, (i + k) % count_s) for i in range(count_s)]
        summed = summed + lax.ppermute(gradient[k], "shot", pairs)
    return potentials[None], summed


def extended(array, sides, width):
    for axis, dim in sides:
        size, length = (lax.axis_size(axis), array.shape[dim])
        up = [(i, (i + 1) % size) for i in range(size - 1)]
        down = [(j, i) for i, j in up]
        last = lax.slice_in_dim(array, length - width, length, axis=dim)
        leading = lax.slice_in_dim(array, 0, width, axis=dim)
        before = lax.ppermute(last, axis, up)
        after = lax.ppermute(leading, axis, down)
        array = jnp.concatenate([before, array, after], axis=dim)
    return array


def upper_z(field):
    return jnp.concatenate([field[..., 1:], jnp.zeros_like(field[..., :1])], axis=-1)


def lower_z(field):
    return jnp.concatenate([jnp.zeros_like(field[..., :1]), field[..., :-1]], axis=-1)


def trim_circle(field, circle_width):
    return field[..., circle_width:-circle_width, circle_width:-circle_width, :]


def pad_plane(field, circle_width):
    spec = [(0, 0)] * (field.ndim - 3) + [
        (circle_width, circle_width),
        (circle_width, circle_width),
        (0, 0),
    ]
    return jnp.pad(field, spec)


def neighbour_list(field_pad):
    centre = trim_circle(field_pad, 1)
    return [
        field_pad[..., 2:, 1:-1, :],
        field_pad[..., :-2, 1:-1, :],
        field_pad[..., 1:-1, 2:, :],
        field_pad[..., 1:-1, :-2, :],
        upper_z(centre),
        lower_z(centre),
    ]


def stencil(field_pad, cond_pad, level_scale):
    centre = trim_circle(field_pad, 1)
    centre_cond = trim_circle(cond_pad, 1)
    summed = jnp.zeros_like(centre)
    for other, other_cond in zip(neighbour_list(field_pad), neighbour_list(cond_pad)):
        summed = summed + level_scale * 0.5 * (centre_cond + other_cond) * (centre - other)
    return summed


def diagonal(cond_pad, level_scale):
    centre_cond = trim_circle(cond_pad, 1)
    summed = jnp.zeros_like(centre_cond)
    for other_cond in neighbour_list(cond_pad):
        summed = summed + level_scale * 0.5 * (centre_cond + other_cond)
    return summed


def relaxed(field_pad, source, cond_pad, diag_level, level_scale):
    return (
        trim_circle(field_pad, 1)
        + DAMPING * (source - stencil(field_pad, cond_pad, level_scale)) / diag_level
    )


def restrict(field):
    leading = field.shape[:-3]
    extent = field.shape[-3:]
    shaped = field.reshape(leading + (extent[0] // 2, 2, extent[1] // 2, 2, extent[2] // 2, 2))
    return shaped.mean(axis=(-5, -3, -1))


def prolong(field):
    return jnp.repeat(jnp.repeat(jnp.repeat(field, 2, axis=-3), 2, axis=-2), 2, axis=-1)


def assemble(blocks, count_x, count_y):
    leading = blocks.shape[1:-3]
    extent = blocks.shape[-3:]
    depth_lead = len(leading)
    shaped = blocks.reshape((count_x, count_y) + leading + extent)
    order = tuple(range(2, 2 + depth_lead)) + (0, 2 + depth_lead, 1, 3 + depth_lead, 4 + depth_lead)
    return shaped.transpose(order).reshape(
        leading + (count_x * extent[0], count_y * extent[1], extent[2])
    )


def field_rim(field):
    return extended(field, (("gx", 1), ("gy", 2)), 1)


def cond_rim(conduct):
    return extended(conduct, (("gx", 0), ("gy", 1)), 1)


def whole_cycle(source, level_index, whole_plans):
    cond_pad, diag_level, level_scale = whole_plans[level_index]
    field = DAMPING * source / diag_level

    def turn(turn_index, iterate):
        return relaxed(pad_plane(iterate, 1), source, cond_pad, diag_level, level_scale)

    return lax.fori_loop(0, COARSE_SWEEPS - 1, turn, field)


def part_cycle(source, level_index, level_plans, whole_plans, gather_level):
    if level_index == gather_level:
        blocks = lax.all_gather(source[None], ("gx", "gy"), axis=0, tiled=True)
        whole = assemble(blocks, lax.axis_size("gx"), lax.axis_size("gy"))
        correction = whole_cycle(whole, level_index, whole_plans)
        extent = source.shape
        starts = (0, lax.axis_index("gx") * extent[1], lax.axis_index("gy") * extent[2], 0)
        return lax.dynamic_slice(correction, starts, extent)
    cond_pad, diag_level, level_scale = level_plans[level_index]
    field = DAMPING * source / diag_level
    field = relaxed(field_rim(field), source, cond_pad, diag_level, level_scale)
    residual = source - stencil(field_rim(field), cond_pad, level_scale)
    field = field + prolong(
        part_cycle(restrict(residual), level_index + 1, level_plans, whole_plans, gather_level)
    )
    field = relaxed(field_rim(field), source, cond_pad, diag_level, level_scale)
    return relaxed(field_rim(field), source, cond_pad, diag_level, level_scale)


def distributed(conductivity, stations, currents, receivers, observed):
    row_count, col_count, z_count = conductivity.shape
    shot_count = currents.shape[0]
    count_x = lax.axis_size("gx")
    count_y = lax.axis_size("gy")
    gather_level = LEVELS - 1
    level_plans = []
    conduct = conductivity
    for level_index in range(gather_level):
        level_scale = 0.25**level_index
        cond_pad = cond_rim(conduct)
        level_plans.append((cond_pad, diagonal(cond_pad, level_scale), level_scale))
        conduct = restrict(conduct)
    blocks = lax.all_gather(conduct[None], ("gx", "gy"), axis=0, tiled=True)
    whole = assemble(blocks, count_x, count_y)
    whole_plans = {}
    level_index = 3
    level_scale = 0.25**level_index
    cond_pad = pad_plane(whole, 1)
    whole_plans[level_index] = (cond_pad, diagonal(cond_pad, level_scale), level_scale)
    total_y = col_count * count_y
    cell_x = stations // (total_y * z_count)
    cell_y = stations // z_count % total_y
    cell_z = stations % z_count
    local_x = cell_x - lax.axis_index("gx") * row_count
    local_y = cell_y - lax.axis_index("gy") * col_count
    owned = (local_x >= 0) & (local_x < row_count) & (local_y >= 0) & (local_y < col_count)
    block_size = row_count * col_count * z_count
    local_cell = jnp.where(owned, (local_x * col_count + local_y) * z_count + cell_z, 0)
    offsets = jnp.arange(shot_count)[:, None] * block_size + local_cell[None, :]
    targets = jnp.where(owned[None, :], offsets, shot_count * block_size).reshape(-1)

    def spread(amounts):
        flat = (
            jnp.zeros((shot_count * block_size,), jnp.float32)
            .at[targets]
            .add(amounts.reshape(-1), mode="drop")
        )
        return flat.reshape(shot_count, row_count, col_count, z_count)

    potentials = part_cycle(spread(currents), 0, level_plans, whole_plans, gather_level)
    local_values = jnp.where(
        owned[None, :], potentials.reshape(shot_count, block_size)[:, local_cell], 0.0
    )
    readings = lax.psum(local_values, ("gx", "gy"))
    positions = jnp.arange(stations.shape[0])[:, None]
    pairs = (receivers[:, 0][None, :] == positions).astype(jnp.float32) - (
        receivers[:, 1][None, :] == positions
    ).astype(jnp.float32)
    misfit = jnp.dot(readings, pairs, precision=lax.Precision.HIGHEST) - observed
    back_source = jnp.dot(misfit, pairs.T, precision=lax.Precision.HIGHEST)
    adjoint = part_cycle(spread(back_source), 0, level_plans, whole_plans, gather_level)
    stacked = jnp.concatenate([potentials, adjoint], axis=0)
    padded = extended(stacked, (("gx", 1), ("gy", 2)), 1)
    potential_pad = padded[:shot_count]
    adjoint_pad = padded[shot_count:]
    gradient = jnp.zeros_like(potentials)
    for other_u, other_w in zip(neighbour_list(potential_pad), neighbour_list(adjoint_pad)):
        gradient = gradient - 0.5 * (potentials - other_u) * (adjoint - other_w)
    summed = lax.psum_scatter(jnp.sum(gradient, axis=0), "shot", scatter_dimension=1, tiled=True)
    return (potentials, summed)


def per_device(conductivity, stations, currents, receivers, observed):
    count = lax.axis_size("gx") * lax.axis_size("gy")
    fits = conductivity.size * count * 4 <= REPLICATED_BYTES
    fits = fits and conductivity.shape[2] == LANES and currents.shape[0] == 1
    plan = replicated if fits else distributed
    return plan(conductivity, stations, currents, receivers, observed)


def solution(mesh):
    in_specs = (
        P(("grp", "gx"), "gy", None),
        P("grp"),
        P(("grp", "shot"), None),
        P("grp", None),
        P(("grp", "shot"), None),
    )
    out_specs = (P(("grp", "shot"), "gx", "gy", None), P(("grp", "gx"), ("gy", "shot"), None))
    return jax.shard_map(
        per_device, mesh=mesh, in_specs=in_specs, out_specs=out_specs, check_vma=False
    )
```

```python
import functools

import jax
import jax.numpy as jnp
from jax import lax
from jax.experimental import pallas as pl
from jax.experimental.pallas import tpu as pltpu
from jax.sharding import PartitionSpec as P

LEVELS = 4
COARSE_SWEEPS = 16


DAMPING = 0.8

SIDE = 8
LANES = 128
GROUP = 16
VMEM_BYTES = 56 * 2**20


def pieces_of(value, count):
    pieces = []
    for _ in range(count):
        pieces.append(value.astype(jnp.bfloat16))
        value = value - pieces[-1].astype(jnp.float32)
    return pieces[::-1]


def product(value, matrix, count, dims=((1,), (0,))):
    result = None
    for piece in pieces_of(value, count):
        term = lax.dot_general(
            piece, matrix, (dims, ((), ())), preferred_element_type=jnp.float32
        )
        result = term if result is None else result + term
    return result


def iota(shape, dim):
    return lax.broadcasted_iota(jnp.int32, shape, dim)


def lane_order():
    row, col = iota((LANES, LANES), 0), iota((LANES, LANES), 1)
    chosen = row == col % GROUP * SIDE + col // GROUP
    return jnp.where(chosen, 1.0, 0.0).astype(jnp.bfloat16)


def exchange_groups(tiles):
    tiles = list(tiles)
    group = iota(tiles[0].shape, 1) // GROUP
    for bit in range(3):
        step = 1 << bit
        keep = (group & step) == 0
        for low in range(SIDE):
            if low & step == 0:
                a, b = tiles[low], tiles[low | step]
                tiles[low] = jnp.where(keep, a, pltpu.roll(b, step * GROUP, 1))
                tiles[low | step] = jnp.where(keep, pltpu.roll(a, LANES - step * GROUP, 1), b)
    return tiles


def to_blocks_kernel(natural_ref, blocks_ref):
    order = lane_order()
    for x in range(SIDE):
        tiles = product(natural_ref[x], order, 3)
        tiles = [tiles[SIDE * k : SIDE * (k + 1)] for k in range(SIDE)]
        for z, tile in enumerate(exchange_groups(tiles)):
            blocks_ref[pl.ds((x * SIDE + z) * SIDE, SIDE), :] = tile


def from_blocks(tiles, order):
    natural = jnp.concatenate(exchange_groups(tiles), axis=0)
    return product(natural, order, 3, ((1,), (1,)))


def block_up(field, axis):
    if axis == 0:
        return pltpu.roll(field, 6, 1)
    if axis == 2:
        return pltpu.roll(field, LANES - 1, 2)
    turned = pltpu.roll(field, LANES - GROUP, 2)
    return jnp.where(iota(field.shape, 2) < LANES - GROUP, turned, pltpu.roll(turned, 7, 1))


def block_down(field, axis):
    if axis == 0:
        return pltpu.roll(field, 2, 1)
    if axis == 2:
        return pltpu.roll(field, 1, 2)
    turned = pltpu.roll(field, GROUP, 2)
    return jnp.where(iota(field.shape, 2) >= GROUP, turned, pltpu.roll(turned, 1, 1))


def inside_up(field, axis):
    sub, lane = iota(field.shape, 1), iota(field.shape, 2)
    if axis == 0:
        keep = sub < 6
    elif axis == 1:
        keep = (lane < LANES - GROUP) | (sub % 2 == 0)
    else:
        keep = lane % GROUP < GROUP - 1
    return jnp.where(keep, field, 0.0)


def inside_down(field, axis):
    sub, lane = iota(field.shape, 1), iota(field.shape, 2)
    if axis == 0:
        keep = sub >= 2
    elif axis == 1:
        keep = (lane >= GROUP) | (sub % 2 == 1)
    else:
        keep = lane % GROUP > 0
    return jnp.where(keep, field, 0.0)


def pair_rows(row):
    count = row.shape[0] // 2
    return jnp.concatenate([row[2 * i : 2 * i + 1] + row[2 * i + 1 : 2 * i + 2] for i in range(count)])


def twice(row):
    return jnp.concatenate([row[i // 2 : i // 2 + 1] for i in range(2 * row.shape[0])])


class Edged:
    def __init__(self, ref, side):
        self.ref, self.side = ref, side

    def start(self, x, z, y=0):
        wide = self.side + 2
        return (((x + 1) * wide + z + 1) * wide + y + 1) * SIDE

    def __getitem__(self, at):
        x, z = at
        rows = self.ref[pl.ds(self.start(x, z), self.side * SIDE), :]
        return rows.reshape(self.side, SIDE, LANES)

    def __setitem__(self, at, value):
        x, z = at
        self.ref[pl.ds(self.start(x, z), self.side * SIDE), :] = value.reshape(-1, LANES)

    def put(self, x, z, value, exact=False):
        self[x, z] = value
        n = self.side
        if z == 0:
            edge = block_up(value, 2)
            self[x, n] = inside_up(edge, 2) if exact else edge
        if z == n - 1:
            edge = block_down(value, 2)
            self[x, -1] = inside_down(edge, 2) if exact else edge
        if exact:
            after = inside_up(block_up(value[:1], 1), 1)
            self.ref[pl.ds(self.start(x, z, n), SIDE), :] = after[0]
            before = inside_down(block_down(value[n - 1 :], 1), 1)
            self.ref[pl.ds(self.start(x, z, -1), SIDE), :] = before[0]

    def close(self, exact=False):
        n = self.side
        for z in range(n):
            after = block_up(self[0, z], 0)
            self[n, z] = inside_up(after, 0) if exact else after
            before = block_down(self[n - 1, z], 0)
            self[-1, z] = inside_down(before, 0) if exact else before


class Plain:
    def __init__(self, ref, side):
        self.ref, self.side = ref, side

    def __getitem__(self, at):
        x, z = at
        rows = self.side * SIDE
        return self.ref[pl.ds((x * self.side + z) * rows, rows), :].reshape(self.side, SIDE, LANES)

    def __setitem__(self, at, value):
        x, z = at
        rows = self.side * SIDE
        self.ref[pl.ds((x * self.side + z) * rows, rows), :] = value.reshape(-1, LANES)


class Level:
    def __init__(self, refs, index):
        self.side = side = SIDE >> index
        self.scale = 0.25**index
        self.cond, self.first, self.second = [Edged(ref, side) for ref in refs[:3]]
        self.links = [Plain(ref, side) for ref in refs[3:9]]
        self.weight, self.back, self.base, self.half = [Plain(ref, side) for ref in refs[9:13]]

    @staticmethod
    def scratch(index):
        side = SIDE >> index
        edged = pltpu.VMEM(((side + 2) ** 3 * SIDE, LANES), jnp.float32)
        plain = pltpu.VMEM((side**3 * SIDE, LANES), jnp.float32)
        return [edged] * 3 + [plain] * 10

    def planes(self, body):
        if self.side == SIDE:

            def one(x, carry):
                body(x)
                return carry

            lax.fori_loop(0, self.side, one, 0)
        else:
            for x in range(self.side):
                body(x)

    def shifted(self, field, x, z, here, exact=False):
        after = block_up(here[:1], 1)
        before = block_down(here[-1:], 1)
        if exact:
            after, before = inside_up(after, 1), inside_down(before, 1)
        return [
            field[x + 1, z],
            field[x - 1, z],
            jnp.concatenate([here[1:], after]),
            jnp.concatenate([before, here[:-1]]),
            field[x, z + 1],
            field[x, z - 1],
        ]

    def prepare(self):
        n = self.side

        def plane(x):
            for z in range(n):
                here = self.cond[x, z]
                others = self.shifted(self.cond, x, z, here, exact=True)
                total = others[0]
                for other in others[1:]:
                    total = total + other
                total = 3.0 * here + 0.5 * total
                inverse = DAMPING / total
                self.weight[x, z] = inverse * (1.0 / self.scale)
                self.back[x, z] = total * (self.scale / DAMPING)
                inverse = 0.5 * inverse
                for index, other in enumerate(others):
                    link = inverse * (here + other)
                    if index == 2:
                        link = jnp.concatenate([link[:-1], inside_up(link[-1:], 1)])
                    if index == 3:
                        link = jnp.concatenate([inside_down(link[:1], 1), link[1:]])
                    if index == 4 and z == n - 1:
                        link = inside_up(link, 2)
                    if index == 5 and z == 0:
                        link = inside_down(link, 2)
                    self.links[index][x, z] = link

        self.planes(plane)
        for z in range(n):
            self.links[0][n - 1, z] = inside_up(self.links[0][n - 1, z], 0)
            self.links[1][0, z] = inside_down(self.links[1][0, z], 0)

    def total(self, field, x, z):
        here = field[x, z]
        result = self.base[x, z]
        for link, other in zip(self.links, self.shifted(field, x, z, here)):
            result = result + link[x, z] * other
        return here, result

    def sweep(self, field, out, exact=False):
        def plane(x):
            for z in range(self.side):
                here, result = self.total(field, x, z)
                out.put(x, z, (1.0 - DAMPING) * here + result, exact)

        self.planes(plane)
        out.close(exact)

    def halve(self, rows, coarse):
        n = self.side

        def plane(x):
            for z in range(n // 2):
                self.half[x, z] = jnp.concatenate([pair_rows(rows(x, 2 * z) + rows(x, 2 * z + 1))] * 2)

        self.planes(plane)
        for x in range(n // 2):
            for z in range(n // 2):
                pair = self.half[2 * x, z][: n // 2] + self.half[2 * x + 1, z][: n // 2]
                coarse(x, z, 0.125 * pair)

    def descend(self, coarse):
        self.sweep(self.first, self.second)

        def residual(x, z):
            here, result = self.total(self.second, x, z)
            return (result - DAMPING * here) * self.back[x, z]

        self.halve(residual, coarse)

    def ascend(self, correction, out, exact=False):
        def plane(x):
            for z in range(self.side):
                self.second.put(x, z, self.second[x, z] + twice(correction(x, z)))

        self.planes(plane)
        self.second.close()
        self.sweep(self.second, self.first)
        self.sweep(self.first, out, exact)


def replicated_kernel(
    device_ref,
    cells_ref,
    blocks_ref,
    stations_ref,
    currents_ref,
    receivers_ref,
    observed_ref,
    potentials_ref,
    gradient_ref,
    forward_ref,
    gathered,
    *level_refs,
):
    f32 = jnp.float32
    electrodes = stations_ref.shape[1]
    per_level = len(Level.scratch(0))
    levels = [Level(level_refs[per_level * k : per_level * (k + 1)], k) for k in range(LEVELS - 1)]
    fine = levels[0]
    forward = Edged(forward_ref, SIDE)
    wide = SIDE * SIDE * SIDE

    def collect(x):
        for z in range(SIDE):
            rows = []
            for y in range(SIDE):
                rows.append(blocks_ref[pl.ds((x * SIDE + z) * SIDE + y, SIDE, stride=wide), :][None])
            fine.cond.put(x, z, jnp.concatenate(rows), exact=True)

    fine.planes(collect)
    fine.cond.close(exact=True)

    coarsest = []
    for level, below in zip(levels, levels[1:] + [None]):
        level.prepare()

        def coarse(x, z, row, below=below):
            if below is None:
                coarsest.append(row)
            else:
                below.cond.put(x, z, row, exact=True)

        level.halve(lambda x, z, level=level: level.cond[x, z], coarse)
        if below is not None:
            below.cond.close(exact=True)

    last_scale = 0.25 ** (LEVELS - 1)
    here = coarsest[0]
    others = [inside(move(here, axis), axis) for axis in range(3) for inside, move in ((inside_up, block_up), (inside_down, block_down))]
    total = others[0]
    for other in others[1:]:
        total = total + other
    total = 3.0 * here + 0.5 * total
    inverse = DAMPING / total
    last_weight = inverse * (1.0 / last_scale)
    last_links = []
    for axis in range(3):
        for inside, other in ((inside_up, others[2 * axis]), (inside_down, others[2 * axis + 1])):
            last_links.append(inside(0.5 * inverse * (here + other), axis))

    def solve_last(rhs):
        base = last_weight * rhs
        value = base
        for _ in range(COARSE_SWEEPS - 1):
            parts = []
            for axis in range(3):
                parts.append(last_links[2 * axis] * block_up(value, axis))
                parts.append(last_links[2 * axis + 1] * block_down(value, axis))
            start = base + (1.0 - DAMPING) * value
            value = ((start + parts[0]) + (parts[1] + parts[4])) + (parts[5] + (parts[2] + parts[3]))
        return value

    def cycle(index, out, exact=False):
        level = levels[index]
        if index == LEVELS - 2:
            held = []
            level.descend(lambda x, z, row: held.append(row))
            solved = solve_last(held[0])
            level.ascend(lambda x, z: solved, out, exact)
            return
        below = levels[index + 1]

        def coarse(x, z, row):
            row = below.weight[x, z] * row
            below.base[x, z] = row
            below.first.put(x, z, row)

        level.descend(coarse)
        below.first.close()
        cycle(index + 1, below.second)
        level.ascend(lambda x, z: below.second[x // 2, z // 2], out, exact)

    station = stations_ref[...]
    cell_x, cell_y, cell_z = station >> 14, station >> 7 & 127, station & 127
    register = ((cell_x & 7) * SIDE + (cell_z & 7)) * SIDE + (cell_y & 7)
    line = register * SIDE + (cell_x >> 3) * 2 + (cell_y >> 6)
    spot = (cell_y >> 3 & 7) * GROUP + (cell_z >> 3)
    at_spot = iota((LANES, electrodes), 0) == spot
    plane_lines = iota((SIDE * SIDE * SIDE, electrodes), 0)

    def spread(amounts):
        table = jnp.concatenate(pieces_of(jnp.where(at_spot, amounts, 0.0), 2))

        def plane(x):
            chosen = plane_lines + x * (SIDE * SIDE * SIDE) == line
            chosen = jnp.where(chosen, 1.0, 0.0).astype(jnp.bfloat16)
            both = lax.dot_general(
                chosen, table, (((1,), (1,)), ((), ())), preferred_element_type=f32
            )
            value = (both[:, :LANES] + both[:, LANES:]).reshape(SIDE, SIDE, SIDE, LANES)
            for z in range(SIDE):
                row = fine.weight[x, z] * value[z]
                fine.base[x, z] = row
                fine.first.put(x, z, row)

        fine.planes(plane)
        fine.first.close()

    spread(currents_ref[...])
    cycle(0, forward, exact=True)

    def read(electrode, carry):
        gathered[pl.ds(electrode, 1), :] = forward_ref[pl.ds(cells_ref[electrode], 1), :]
        return carry

    lax.fori_loop(0, electrodes, read, 0, unroll=8)
    readings = jnp.sum(jnp.where(at_spot, gathered[...].T, 0.0), axis=0, keepdims=True)
    receivers = receivers_ref[...]
    numbers = iota((receivers.shape[0], electrodes), 1)
    pairs = jnp.where(numbers == receivers[:, 0:1], 1.0, 0.0) - jnp.where(
        numbers == receivers[:, 1:2], 1.0, 0.0
    )
    pairs = pairs.astype(jnp.bfloat16)

    def exact(row, dims):
        return product(jnp.broadcast_to(row, (16, row.shape[1])), pairs, 3, dims)[0:1]

    misfit = exact(readings, ((1,), (1,))) - observed_ref[...]
    spread(exact(misfit, ((1,), (0,))))
    cycle(0, fine.second, exact=True)

    device = device_ref[0]
    order = lane_order()
    adjoint = fine.second

    def own(field, x, z, y=0):
        return field.ref[pl.ds(field.start(x, z, y) + device, SIDE, stride=SIDE), :]

    for x in range(SIDE):
        tiles_u, tiles_g = [], []
        for z in range(SIDE):
            here_u, here_w = own(forward, x, z), own(adjoint, x, z)
            total = None
            for at in ((x + 1, z), (x - 1, z), (x, z, 1), (x, z, -1), (x, z + 1), (x, z - 1)):
                term = (here_u - own(forward, *at)) * (here_w - own(adjoint, *at))
                total = term if total is None else total + term
            tiles_u.append(here_u)
            tiles_g.append(-0.5 * total)
        potentials_ref[x] = from_blocks(tiles_u, order)
        gradient_ref[x] = from_blocks(tiles_g, order)


def replicated(conductivity, stations, currents, receivers, observed):
    rows, cols, depth = conductivity.shape
    f32 = jnp.float32
    count_s = lax.axis_size("shot")
    shot = lax.axis_index("shot")
    electrodes = stations.shape[0]
    total = rows * cols
    vmem = pl.BlockSpec(memory_space=pltpu.VMEM)
    smem = pl.BlockSpec(memory_space=pltpu.SMEM)
    params = pltpu.CompilerParams(vmem_limit_bytes=VMEM_BYTES)
    mine = pl.pallas_call(
        to_blocks_kernel,
        out_shape=jax.ShapeDtypeStruct((total, LANES), f32),
        in_specs=[vmem],
        out_specs=vmem,
    )(conductivity)
    part = total // count_s
    mine = lax.dynamic_slice_in_dim(mine, shot * part, part, axis=0)
    blocks = lax.all_gather(mine, ("gx", "gy", "shot"), axis=0, tiled=True)
    device = (lax.axis_index("gx") * lax.axis_size("gy") + lax.axis_index("gy")).astype(jnp.int32)
    cell_x, cell_y, cell_z = stations >> 14, stations >> 7 & 127, stations & 127
    wide = SIDE + 2
    cells = ((cell_x % 8 + 1) * wide + cell_z % 8 + 1) * wide + cell_y % 8 + 1
    cells = cells * SIDE + cell_x // 8 * 2 + cell_y // 64
    levels = [shape for index in range(LEVELS - 1) for shape in Level.scratch(index)]
    potentials, gradient = pl.pallas_call(
        replicated_kernel,
        out_shape=(
            jax.ShapeDtypeStruct((rows, cols, LANES), f32),
            jax.ShapeDtypeStruct((rows, cols, LANES), f32),
        ),
        in_specs=[smem, smem, vmem, vmem, vmem, vmem, vmem],
        out_specs=(vmem, vmem),
        scratch_shapes=[
            pltpu.VMEM((wide**3 * SIDE, LANES), f32),
            pltpu.VMEM((electrodes, LANES), f32),
        ]
        + levels,
        compiler_params=params,
        cost_estimate=pl.CostEstimate(flops=200_000_000, bytes_accessed=4_000_000, transcendentals=0),
    )(
        device.reshape(1),
        cells,
        blocks,
        stations.reshape(1, electrodes),
        currents,
        receivers,
        observed,
    )
    chunk = cols // count_s
    summed = lax.dynamic_slice_in_dim(gradient, shot * chunk, chunk, axis=1)
    for k in range(1, count_s):
        theirs = lax.dynamic_slice_in_dim(gradient, (shot + k) % count_s * chunk, chunk, axis=1)
        summed = summed + lax.ppermute(theirs, "shot", [(i, (i + k) % count_s) for i in range(count_s)])
    return potentials[None], summed


def extended(array, sides, width):
    for axis, dim in sides:
        size, length = (lax.axis_size(axis), array.shape[dim])
        up = [(i, (i + 1) % size) for i in range(size - 1)]
        down = [(j, i) for i, j in up]
        last = lax.slice_in_dim(array, length - width, length, axis=dim)
        leading = lax.slice_in_dim(array, 0, width, axis=dim)
        before = lax.ppermute(last, axis, up)
        after = lax.ppermute(leading, axis, down)
        array = jnp.concatenate([before, array, after], axis=dim)
    return array


def upper_z(field):
    return jnp.concatenate([field[..., 1:], jnp.zeros_like(field[..., :1])], axis=-1)


def lower_z(field):
    return jnp.concatenate([jnp.zeros_like(field[..., :1]), field[..., :-1]], axis=-1)


def trim_circle(field, circle_width):
    return field[..., circle_width:-circle_width, circle_width:-circle_width, :]


def pad_plane(field, circle_width):
    spec = [(0, 0)] * (field.ndim - 3) + [
        (circle_width, circle_width),
        (circle_width, circle_width),
        (0, 0),
    ]
    return jnp.pad(field, spec)


def neighbour_list(field_pad):
    centre = trim_circle(field_pad, 1)
    return [
        field_pad[..., 2:, 1:-1, :],
        field_pad[..., :-2, 1:-1, :],
        field_pad[..., 1:-1, 2:, :],
        field_pad[..., 1:-1, :-2, :],
        upper_z(centre),
        lower_z(centre),
    ]


def stencil(field_pad, cond_pad, level_scale):
    centre = trim_circle(field_pad, 1)
    centre_cond = trim_circle(cond_pad, 1)
    summed = jnp.zeros_like(centre)
    for other, other_cond in zip(neighbour_list(field_pad), neighbour_list(cond_pad)):
        summed = summed + level_scale * 0.5 * (centre_cond + other_cond) * (centre - other)
    return summed


def diagonal(cond_pad, level_scale):
    centre_cond = trim_circle(cond_pad, 1)
    summed = jnp.zeros_like(centre_cond)
    for other_cond in neighbour_list(cond_pad):
        summed = summed + level_scale * 0.5 * (centre_cond + other_cond)
    return summed


def relaxed(field_pad, source, cond_pad, diag_level, level_scale):
    return (
        trim_circle(field_pad, 1)
        + DAMPING * (source - stencil(field_pad, cond_pad, level_scale)) / diag_level
    )


def restrict(field):
    leading = field.shape[:-3]
    extent = field.shape[-3:]
    shaped = field.reshape(leading + (extent[0] // 2, 2, extent[1] // 2, 2, extent[2] // 2, 2))
    return shaped.mean(axis=(-5, -3, -1))


def prolong(field):
    return jnp.repeat(jnp.repeat(jnp.repeat(field, 2, axis=-3), 2, axis=-2), 2, axis=-1)


def assemble(blocks, count_x, count_y):
    leading = blocks.shape[1:-3]
    extent = blocks.shape[-3:]
    depth_lead = len(leading)
    shaped = blocks.reshape((count_x, count_y) + leading + extent)
    order = tuple(range(2, 2 + depth_lead)) + (0, 2 + depth_lead, 1, 3 + depth_lead, 4 + depth_lead)
    return shaped.transpose(order).reshape(
        leading + (count_x * extent[0], count_y * extent[1], extent[2])
    )


def field_rim(field):
    return extended(field, (("gx", 1), ("gy", 2)), 1)


def cond_rim(conduct):
    return extended(conduct, (("gx", 0), ("gy", 1)), 1)


def whole_cycle(source, level_index, whole_plans):
    cond_pad, diag_level, level_scale = whole_plans[level_index]
    field = DAMPING * source / diag_level

    def turn(turn_index, iterate):
        return relaxed(pad_plane(iterate, 1), source, cond_pad, diag_level, level_scale)

    return lax.fori_loop(0, COARSE_SWEEPS - 1, turn, field)


def part_cycle(source, level_index, level_plans, whole_plans, gather_level):
    if level_index == gather_level:
        blocks = lax.all_gather(source[None], ("gx", "gy"), axis=0, tiled=True)
        whole = assemble(blocks, lax.axis_size("gx"), lax.axis_size("gy"))
        correction = whole_cycle(whole, level_index, whole_plans)
        extent = source.shape
        starts = (0, lax.axis_index("gx") * extent[1], lax.axis_index("gy") * extent[2], 0)
        return lax.dynamic_slice(correction, starts, extent)
    cond_pad, diag_level, level_scale = level_plans[level_index]
    field = DAMPING * source / diag_level
    field = relaxed(field_rim(field), source, cond_pad, diag_level, level_scale)
    residual = source - stencil(field_rim(field), cond_pad, level_scale)
    field = field + prolong(
        part_cycle(restrict(residual), level_index + 1, level_plans, whole_plans, gather_level)
    )
    field = relaxed(field_rim(field), source, cond_pad, diag_level, level_scale)
    return relaxed(field_rim(field), source, cond_pad, diag_level, level_scale)


def distributed(conductivity, stations, currents, receivers, observed):
    row_count, col_count, z_count = conductivity.shape
    shot_count = currents.shape[0]
    count_x = lax.axis_size("gx")
    count_y = lax.axis_size("gy")
    gather_level = LEVELS - 1
    level_plans = []
    conduct = conductivity
    for level_index in range(gather_level):
        level_scale = 0.25**level_index
        cond_pad = cond_rim(conduct)
        level_plans.append((cond_pad, diagonal(cond_pad, level_scale), level_scale))
        conduct = restrict(conduct)
    blocks = lax.all_gather(conduct[None], ("gx", "gy"), axis=0, tiled=True)
    whole = assemble(blocks, count_x, count_y)
    whole_plans = {}
    level_index = 3
    level_scale = 0.25**level_index
    cond_pad = pad_plane(whole, 1)
    whole_plans[level_index] = (cond_pad, diagonal(cond_pad, level_scale), level_scale)
    total_y = col_count * count_y
    cell_x = stations // (total_y * z_count)
    cell_y = stations // z_count % total_y
    cell_z = stations % z_count
    local_x = cell_x - lax.axis_index("gx") * row_count
    local_y = cell_y - lax.axis_index("gy") * col_count
    owned = (local_x >= 0) & (local_x < row_count) & (local_y >= 0) & (local_y < col_count)
    block_size = row_count * col_count * z_count
    local_cell = jnp.where(owned, (local_x * col_count + local_y) * z_count + cell_z, 0)
    offsets = jnp.arange(shot_count)[:, None] * block_size + local_cell[None, :]
    targets = jnp.where(owned[None, :], offsets, shot_count * block_size).reshape(-1)

    def spread(amounts):
        flat = (
            jnp.zeros((shot_count * block_size,), jnp.float32)
            .at[targets]
            .add(amounts.reshape(-1), mode="drop")
        )
        return flat.reshape(shot_count, row_count, col_count, z_count)

    potentials = part_cycle(spread(currents), 0, level_plans, whole_plans, gather_level)
    local_values = jnp.where(
        owned[None, :], potentials.reshape(shot_count, block_size)[:, local_cell], 0.0
    )
    readings = lax.psum(local_values, ("gx", "gy"))
    positions = jnp.arange(stations.shape[0])[:, None]
    pairs = (receivers[:, 0][None, :] == positions).astype(jnp.float32) - (
        receivers[:, 1][None, :] == positions
    ).astype(jnp.float32)
    misfit = jnp.dot(readings, pairs, precision=lax.Precision.HIGHEST) - observed
    back_source = jnp.dot(misfit, pairs.T, precision=lax.Precision.HIGHEST)
    adjoint = part_cycle(spread(back_source), 0, level_plans, whole_plans, gather_level)
    stacked = jnp.concatenate([potentials, adjoint], axis=0)
    padded = extended(stacked, (("gx", 1), ("gy", 2)), 1)
    potential_pad = padded[:shot_count]
    adjoint_pad = padded[shot_count:]
    gradient = jnp.zeros_like(potentials)
    for other_u, other_w in zip(neighbour_list(potential_pad), neighbour_list(adjoint_pad)):
        gradient = gradient - 0.5 * (potentials - other_u) * (adjoint - other_w)
    summed = lax.psum_scatter(jnp.sum(gradient, axis=0), "shot", scatter_dimension=1, tiled=True)
    return (potentials, summed)


def per_device(conductivity, stations, currents, receivers, observed):
    blocks = lax.axis_size("gx") * lax.axis_size("gy")
    fits = conductivity.shape == (SIDE, SIDE * SIDE, LANES) and blocks == SIDE
    fits = fits and lax.axis_size("gy") == 2 and currents.shape[0] == 1
    plan = replicated if fits else distributed
    return plan(conductivity, stations, currents, receivers, observed)


def solution(mesh):
    in_specs = (
        P(("grp", "gx"), "gy", None),
        P("grp"),
        P(("grp", "shot"), None),
        P("grp", None),
        P(("grp", "shot"), None),
    )
    out_specs = (P(("grp", "shot"), "gx", "gy", None), P(("grp", "gx"), ("gy", "shot"), None))
    return jax.shard_map(
        per_device, mesh=mesh, in_specs=in_specs, out_specs=out_specs, check_vma=False
    )
```

```python
import functools

import jax
import jax.numpy as jnp
from jax import lax
from jax.experimental import pallas as pl
from jax.experimental.pallas import tpu as pltpu
from jax.sharding import PartitionSpec as P

LEVELS = 4
COARSE_SWEEPS = 16


DAMPING = 0.8

SIDE = 8
LANES = 128
GROUP = 16
VMEM_BYTES = 56 * 2**20


def pieces_of(value, count):
    pieces = []
    for _ in range(count):
        pieces.append(value.astype(jnp.bfloat16))
        value = value - pieces[-1].astype(jnp.float32)
    return pieces[::-1]


def product(value, matrix, count, dims=((1,), (0,))):
    result = None
    for piece in pieces_of(value, count):
        term = lax.dot_general(
            piece, matrix, (dims, ((), ())), preferred_element_type=jnp.float32
        )
        result = term if result is None else result + term
    return result


def iota(shape, dim):
    return lax.broadcasted_iota(jnp.int32, shape, dim)


def lane_order():
    row, col = iota((LANES, LANES), 0), iota((LANES, LANES), 1)
    chosen = row == col % GROUP * SIDE + col // GROUP
    return jnp.where(chosen, 1.0, 0.0).astype(jnp.bfloat16)


def exchange_groups(tiles):
    tiles = list(tiles)
    group = iota(tiles[0].shape, 1) // GROUP
    for bit in range(3):
        step = 1 << bit
        keep = (group & step) == 0
        for low in range(SIDE):
            if low & step == 0:
                a, b = tiles[low], tiles[low | step]
                tiles[low] = jnp.where(keep, a, pltpu.roll(b, step * GROUP, 1))
                tiles[low | step] = jnp.where(keep, pltpu.roll(a, LANES - step * GROUP, 1), b)
    return tiles


def to_blocks_kernel(natural_ref, blocks_ref):
    order = lane_order()
    for x in range(SIDE):
        tiles = product(natural_ref[x], order, 3)
        tiles = [tiles[SIDE * k : SIDE * (k + 1)] for k in range(SIDE)]
        for z, tile in enumerate(exchange_groups(tiles)):
            blocks_ref[pl.ds((x * SIDE + z) * SIDE, SIDE), :] = tile


def from_blocks(tiles, order):
    natural = jnp.concatenate(exchange_groups(tiles), axis=0)
    return product(natural, order, 3, ((1,), (1,)))


def block_up(field, axis):
    if axis == 0:
        return pltpu.roll(field, 6, 1)
    if axis == 2:
        return pltpu.roll(field, LANES - 1, 2)
    turned = pltpu.roll(field, LANES - GROUP, 2)
    return jnp.where(iota(field.shape, 2) < LANES - GROUP, turned, pltpu.roll(turned, 7, 1))


def block_down(field, axis):
    if axis == 0:
        return pltpu.roll(field, 2, 1)
    if axis == 2:
        return pltpu.roll(field, 1, 2)
    turned = pltpu.roll(field, GROUP, 2)
    return jnp.where(iota(field.shape, 2) >= GROUP, turned, pltpu.roll(turned, 1, 1))


def inside_up(field, axis):
    sub, lane = iota(field.shape, 1), iota(field.shape, 2)
    if axis == 0:
        keep = sub < 6
    elif axis == 1:
        keep = (lane < LANES - GROUP) | (sub % 2 == 0)
    else:
        keep = lane % GROUP < GROUP - 1
    return jnp.where(keep, field, 0.0)


def inside_down(field, axis):
    sub, lane = iota(field.shape, 1), iota(field.shape, 2)
    if axis == 0:
        keep = sub >= 2
    elif axis == 1:
        keep = (lane >= GROUP) | (sub % 2 == 1)
    else:
        keep = lane % GROUP > 0
    return jnp.where(keep, field, 0.0)


def pair_rows(row):
    count = row.shape[0] // 2
    return jnp.concatenate([row[2 * i : 2 * i + 1] + row[2 * i + 1 : 2 * i + 2] for i in range(count)])


def twice(row):
    return jnp.concatenate([row[i // 2 : i // 2 + 1] for i in range(2 * row.shape[0])])


def station_table(station):
    cell_x, cell_y, cell_z = station >> 14, station >> 7 & 127, station & 127
    register = ((cell_x & 7) * SIDE + (cell_z & 7)) * SIDE + (cell_y & 7)
    line = register * SIDE + (cell_x >> 3) * 2 + (cell_y >> 6)
    return line, (cell_y >> 3 & 7) * GROUP + (cell_z >> 3)


def spread_planes(station, amounts, put):
    electrodes = station.shape[1]
    line, spot = station_table(station)
    at_spot = iota((LANES, electrodes), 0) == spot
    table = jnp.concatenate(pieces_of(jnp.where(at_spot, amounts, 0.0), 2))
    plane_lines = iota((SIDE * SIDE * SIDE, electrodes), 0)

    def plane(x, carry):
        chosen = plane_lines + x * (SIDE * SIDE * SIDE) == line
        chosen = jnp.where(chosen, 1.0, 0.0).astype(jnp.bfloat16)
        both = lax.dot_general(
            chosen, table, (((1,), (1,)), ((), ())), preferred_element_type=jnp.float32
        )
        put(x, both[:, :LANES] + both[:, LANES:])
        return carry

    lax.fori_loop(0, SIDE, plane, 0)


def source_kernel(stations_ref, currents_ref, source_ref):
    def put(x, value):
        source_ref[pl.ds(x * SIDE * SIDE * SIDE, SIDE * SIDE * SIDE), :] = value

    spread_planes(stations_ref[...], currents_ref[...], put)


class Edged:
    def __init__(self, ref, side):
        self.ref, self.side = ref, side

    def start(self, x, z, y=0):
        wide = self.side + 2
        return (((x + 1) * wide + z + 1) * wide + y + 1) * SIDE

    def __getitem__(self, at):
        x, z = at
        rows = self.ref[pl.ds(self.start(x, z), self.side * SIDE), :]
        return rows.reshape(self.side, SIDE, LANES)

    def __setitem__(self, at, value):
        x, z = at
        self.ref[pl.ds(self.start(x, z), self.side * SIDE), :] = value.reshape(-1, LANES)

    def put(self, x, z, value, exact=False):
        self[x, z] = value
        n = self.side
        if z == 0:
            edge = block_up(value, 2)
            self[x, n] = inside_up(edge, 2) if exact else edge
        if z == n - 1:
            edge = block_down(value, 2)
            self[x, -1] = inside_down(edge, 2) if exact else edge
        if exact:
            after = inside_up(block_up(value[:1], 1), 1)
            self.ref[pl.ds(self.start(x, z, n), SIDE), :] = after[0]
            before = inside_down(block_down(value[n - 1 :], 1), 1)
            self.ref[pl.ds(self.start(x, z, -1), SIDE), :] = before[0]

    def close(self, exact=False):
        n = self.side
        for z in range(n):
            after = block_up(self[0, z], 0)
            self[n, z] = inside_up(after, 0) if exact else after
            before = block_down(self[n - 1, z], 0)
            self[-1, z] = inside_down(before, 0) if exact else before


class Plain:
    def __init__(self, ref, side):
        self.ref, self.side = ref, side

    def __getitem__(self, at):
        x, z = at
        rows = self.side * SIDE
        return self.ref[pl.ds((x * self.side + z) * rows, rows), :].reshape(self.side, SIDE, LANES)

    def __setitem__(self, at, value):
        x, z = at
        rows = self.side * SIDE
        self.ref[pl.ds((x * self.side + z) * rows, rows), :] = value.reshape(-1, LANES)


class Level:
    def __init__(self, refs, index):
        self.side = side = SIDE >> index
        self.scale = 0.25**index
        self.cond, self.first, self.second = [Edged(ref, side) for ref in refs[:3]]
        self.links = [Plain(ref, side) for ref in refs[3:9]]
        self.weight, self.back, self.base, self.half = [Plain(ref, side) for ref in refs[9:13]]

    @staticmethod
    def scratch(index):
        side = SIDE >> index
        edged = pltpu.VMEM(((side + 2) ** 3 * SIDE, LANES), jnp.float32)
        plain = pltpu.VMEM((side**3 * SIDE, LANES), jnp.float32)
        return [edged] * 3 + [plain] * 10

    def planes(self, body):
        if self.side == SIDE:

            def one(x, carry):
                body(x)
                return carry

            lax.fori_loop(0, self.side, one, 0)
        else:
            for x in range(self.side):
                body(x)

    def shifted(self, field, x, z, here, exact=False):
        after = block_up(here[:1], 1)
        before = block_down(here[-1:], 1)
        if exact:
            after, before = inside_up(after, 1), inside_down(before, 1)
        return [
            field[x + 1, z],
            field[x - 1, z],
            jnp.concatenate([here[1:], after]),
            jnp.concatenate([before, here[:-1]]),
            field[x, z + 1],
            field[x, z - 1],
        ]

    def prepare(self):
        n = self.side

        def plane(x):
            for z in range(n):
                here = self.cond[x, z]
                others = self.shifted(self.cond, x, z, here, exact=True)
                total = others[0]
                for other in others[1:]:
                    total = total + other
                total = 3.0 * here + 0.5 * total
                inverse = DAMPING / total
                self.weight[x, z] = inverse * (1.0 / self.scale)
                self.back[x, z] = total * (self.scale / DAMPING)
                inverse = 0.5 * inverse
                for index, other in enumerate(others):
                    link = inverse * (here + other)
                    if index == 2:
                        link = jnp.concatenate([link[:-1], inside_up(link[-1:], 1)])
                    if index == 3:
                        link = jnp.concatenate([inside_down(link[:1], 1), link[1:]])
                    if index == 4 and z == n - 1:
                        link = inside_up(link, 2)
                    if index == 5 and z == 0:
                        link = inside_down(link, 2)
                    self.links[index][x, z] = link

        self.planes(plane)
        for z in range(n):
            self.links[0][n - 1, z] = inside_up(self.links[0][n - 1, z], 0)
            self.links[1][0, z] = inside_down(self.links[1][0, z], 0)

    def total(self, field, x, z):
        here = field[x, z]
        result = self.base[x, z]
        for link, other in zip(self.links, self.shifted(field, x, z, here)):
            result = result + link[x, z] * other
        return here, result

    def sweep(self, field, out, exact=False):
        def plane(x):
            for z in range(self.side):
                here, result = self.total(field, x, z)
                out.put(x, z, (1.0 - DAMPING) * here + result, exact)

        self.planes(plane)
        out.close(exact)

    def halve(self, rows, coarse):
        n = self.side

        def plane(x):
            for z in range(n // 2):
                self.half[x, z] = jnp.concatenate([pair_rows(rows(x, 2 * z) + rows(x, 2 * z + 1))] * 2)

        self.planes(plane)
        for x in range(n // 2):
            for z in range(n // 2):
                pair = self.half[2 * x, z][: n // 2] + self.half[2 * x + 1, z][: n // 2]
                coarse(x, z, 0.125 * pair)

    def descend(self, coarse):
        self.sweep(self.first, self.second)

        def residual(x, z):
            here, result = self.total(self.second, x, z)
            return (result - DAMPING * here) * self.back[x, z]

        self.halve(residual, coarse)

    def ascend(self, correction, out, exact=False):
        def plane(x):
            for z in range(self.side):
                self.second.put(x, z, self.second[x, z] + twice(correction(x, z)))

        self.planes(plane)
        self.second.close()
        self.sweep(self.second, self.first)
        self.sweep(self.first, out, exact)


def replicated_kernel(
    count,
    device_ref,
    cells_ref,
    *refs,
):
    solve_kernel(refs[:count], device_ref, cells_ref, *refs[count:])


def solve_kernel(
    part_refs,
    device_ref,
    cells_ref,
    source_ref,
    stations_ref,
    receivers_ref,
    observed_ref,
    potentials_ref,
    gradient_ref,
    forward_ref,
    gathered,
    *level_refs,
):
    f32 = jnp.float32
    electrodes = stations_ref.shape[1]
    per_level = len(Level.scratch(0))
    levels = [Level(level_refs[per_level * k : per_level * (k + 1)], k) for k in range(LEVELS - 1)]
    fine = levels[0]
    forward = Edged(forward_ref, SIDE)
    wide = SIDE * SIDE * SIDE

    device = device_ref[0]
    def collect(x):
        for k, part in enumerate(part_refs):
            for z in range(SIDE):
                start = fine.cond.start(x, z) + (device ^ k)
                fine.cond.ref[pl.ds(start, SIDE, stride=SIDE), :] = part[
                    pl.ds((x * SIDE + z) * SIDE, SIDE), :
                ]
        for z in (0, SIDE - 1):
            fine.cond.put(x, z, fine.cond[x, z], exact=True)

    fine.planes(collect)
    fine.cond.close(exact=True)

    coarsest = []
    for level, below in zip(levels, levels[1:] + [None]):
        level.prepare()

        def coarse(x, z, row, below=below):
            if below is None:
                coarsest.append(row)
            else:
                below.cond.put(x, z, row, exact=True)

        level.halve(lambda x, z, level=level: level.cond[x, z], coarse)
        if below is not None:
            below.cond.close(exact=True)

    last_scale = 0.25 ** (LEVELS - 1)
    here = coarsest[0]
    others = [inside(move(here, axis), axis) for axis in range(3) for inside, move in ((inside_up, block_up), (inside_down, block_down))]
    total = others[0]
    for other in others[1:]:
        total = total + other
    total = 3.0 * here + 0.5 * total
    inverse = DAMPING / total
    last_weight = inverse * (1.0 / last_scale)
    last_links = []
    for axis in range(3):
        for inside, other in ((inside_up, others[2 * axis]), (inside_down, others[2 * axis + 1])):
            last_links.append(inside(0.5 * inverse * (here + other), axis))

    def solve_last(rhs):
        base = last_weight * rhs
        value = base
        for _ in range(COARSE_SWEEPS - 1):
            parts = []
            for axis in range(3):
                parts.append(last_links[2 * axis] * block_up(value, axis))
                parts.append(last_links[2 * axis + 1] * block_down(value, axis))
            start = base + (1.0 - DAMPING) * value
            value = ((start + parts[0]) + (parts[1] + parts[4])) + (parts[5] + (parts[2] + parts[3]))
        return value

    def cycle(index, out, exact=False):
        level = levels[index]
        if index == LEVELS - 2:
            held = []
            level.descend(lambda x, z, row: held.append(row))
            solved = solve_last(held[0])
            level.ascend(lambda x, z: solved, out, exact)
            return
        below = levels[index + 1]

        def coarse(x, z, row):
            row = below.weight[x, z] * row
            below.base[x, z] = row
            below.first.put(x, z, row)

        level.descend(coarse)
        below.first.close()
        cycle(index + 1, below.second)
        level.ascend(lambda x, z: below.second[x // 2, z // 2], out, exact)

    def begin(x, rows):
        value = rows.reshape(SIDE, SIDE, SIDE, LANES)
        for z in range(SIDE):
            row = fine.weight[x, z] * value[z]
            fine.base[x, z] = row
            fine.first.put(x, z, row)

    fine.planes(lambda x: begin(x, source_ref[pl.ds(x * wide, wide), :]))
    fine.first.close()
    cycle(0, forward, exact=True)

    def read(electrode, carry):
        gathered[pl.ds(electrode, 1), :] = forward_ref[pl.ds(cells_ref[electrode], 1), :]
        return carry

    lax.fori_loop(0, electrodes, read, 0, unroll=8)
    _, spot = station_table(stations_ref[...])
    at_spot = iota((LANES, electrodes), 0) == spot
    readings = jnp.sum(jnp.where(at_spot, gathered[...].T, 0.0), axis=0, keepdims=True)
    receivers = receivers_ref[...]
    numbers = iota((receivers.shape[0], electrodes), 1)
    pairs = jnp.where(numbers == receivers[:, 0:1], 1.0, 0.0) - jnp.where(
        numbers == receivers[:, 1:2], 1.0, 0.0
    )
    pairs = pairs.astype(jnp.bfloat16)

    def exact(row, dims):
        return product(jnp.broadcast_to(row, (16, row.shape[1])), pairs, 3, dims)[0:1]

    misfit = exact(readings, ((1,), (1,))) - observed_ref[...]
    spread_planes(stations_ref[...], exact(misfit, ((1,), (0,))), begin)
    fine.first.close()
    cycle(0, fine.second, exact=True)

    order = lane_order()
    adjoint = fine.second

    def own(field, x, z, y=0):
        return field.ref[pl.ds(field.start(x, z, y) + device, SIDE, stride=SIDE), :]

    for x in range(SIDE):
        tiles_u, tiles_g = [], []
        for z in range(SIDE):
            here_u, here_w = own(forward, x, z), own(adjoint, x, z)
            total = None
            for at in ((x + 1, z), (x - 1, z), (x, z, 1), (x, z, -1), (x, z + 1), (x, z - 1)):
                term = (here_u - own(forward, *at)) * (here_w - own(adjoint, *at))
                total = term if total is None else total + term
            tiles_u.append(here_u)
            tiles_g.append(-0.5 * total)
        potentials_ref[x] = from_blocks(tiles_u, order)
        gradient_ref[x] = from_blocks(tiles_g, order)


def replicated(conductivity, stations, currents, receivers, observed):
    rows, cols, depth = conductivity.shape
    f32 = jnp.float32
    count_s = lax.axis_size("shot")
    shot = lax.axis_index("shot")
    electrodes = stations.shape[0]
    total = rows * cols
    vmem = pl.BlockSpec(memory_space=pltpu.VMEM)
    smem = pl.BlockSpec(memory_space=pltpu.SMEM)
    params = pltpu.CompilerParams(vmem_limit_bytes=VMEM_BYTES)
    mine = pl.pallas_call(
        to_blocks_kernel,
        out_shape=jax.ShapeDtypeStruct((total, LANES), f32),
        in_specs=[vmem],
        out_specs=vmem,
    )(conductivity)
    count_x, count_y = lax.axis_size("gx"), lax.axis_size("gy")
    parts = []
    for k in range(count_x):
        pairs = [(i, i ^ k) for i in range(count_x)]
        parts.append(lax.ppermute(mine, "gx", pairs) if k else mine)
    swap = [(0, 1), (1, 0)]
    parts = [part for own in parts for part in (own, lax.ppermute(own, "gy", swap))]
    station_row = stations.reshape(1, electrodes)
    source = pl.pallas_call(
        source_kernel,
        out_shape=jax.ShapeDtypeStruct((total * SIDE, LANES), f32),
        in_specs=[vmem, vmem],
        out_specs=vmem,
        compiler_params=params,
        cost_estimate=pl.CostEstimate(flops=600_000_000, bytes_accessed=4_000_000, transcendentals=0),
    )(station_row, currents)
    device = (lax.axis_index("gx") * lax.axis_size("gy") + lax.axis_index("gy")).astype(jnp.int32)
    cell_x, cell_y, cell_z = stations >> 14, stations >> 7 & 127, stations & 127
    wide = SIDE + 2
    cells = ((cell_x % 8 + 1) * wide + cell_z % 8 + 1) * wide + cell_y % 8 + 1
    cells = cells * SIDE + cell_x // 8 * 2 + cell_y // 64
    levels = [shape for index in range(LEVELS - 1) for shape in Level.scratch(index)]
    potentials, gradient = pl.pallas_call(
        functools.partial(replicated_kernel, len(parts)),
        out_shape=(
            jax.ShapeDtypeStruct((rows, cols, LANES), f32),
            jax.ShapeDtypeStruct((rows, cols, LANES), f32),
        ),
        in_specs=[smem, smem] + [vmem] * (len(parts) + 4),
        out_specs=(vmem, vmem),
        scratch_shapes=[
            pltpu.VMEM((wide**3 * SIDE, LANES), f32),
            pltpu.VMEM((electrodes, LANES), f32),
        ]
        + levels,
        compiler_params=params,
        cost_estimate=pl.CostEstimate(flops=200_000_000, bytes_accessed=4_000_000, transcendentals=0),
    )(
        device.reshape(1),
        cells,
        *parts,
        source,
        station_row,
        receivers,
        observed,
    )
    chunk = cols // count_s
    summed = lax.dynamic_slice_in_dim(gradient, shot * chunk, chunk, axis=1)
    for k in range(1, count_s):
        theirs = lax.dynamic_slice_in_dim(gradient, (shot + k) % count_s * chunk, chunk, axis=1)
        summed = summed + lax.ppermute(theirs, "shot", [(i, (i + k) % count_s) for i in range(count_s)])
    return potentials[None], summed


def extended(array, sides, width):
    for axis, dim in sides:
        size, length = (lax.axis_size(axis), array.shape[dim])
        up = [(i, (i + 1) % size) for i in range(size - 1)]
        down = [(j, i) for i, j in up]
        last = lax.slice_in_dim(array, length - width, length, axis=dim)
        leading = lax.slice_in_dim(array, 0, width, axis=dim)
        before = lax.ppermute(last, axis, up)
        after = lax.ppermute(leading, axis, down)
        array = jnp.concatenate([before, array, after], axis=dim)
    return array


def upper_z(field):
    return jnp.concatenate([field[..., 1:], jnp.zeros_like(field[..., :1])], axis=-1)


def lower_z(field):
    return jnp.concatenate([jnp.zeros_like(field[..., :1]), field[..., :-1]], axis=-1)


def trim_circle(field, circle_width):
    return field[..., circle_width:-circle_width, circle_width:-circle_width, :]


def pad_plane(field, circle_width):
    spec = [(0, 0)] * (field.ndim - 3) + [
        (circle_width, circle_width),
        (circle_width, circle_width),
        (0, 0),
    ]
    return jnp.pad(field, spec)


def neighbour_list(field_pad):
    centre = trim_circle(field_pad, 1)
    return [
        field_pad[..., 2:, 1:-1, :],
        field_pad[..., :-2, 1:-1, :],
        field_pad[..., 1:-1, 2:, :],
        field_pad[..., 1:-1, :-2, :],
        upper_z(centre),
        lower_z(centre),
    ]


def stencil(field_pad, cond_pad, level_scale):
    centre = trim_circle(field_pad, 1)
    centre_cond = trim_circle(cond_pad, 1)
    summed = jnp.zeros_like(centre)
    for other, other_cond in zip(neighbour_list(field_pad), neighbour_list(cond_pad)):
        summed = summed + level_scale * 0.5 * (centre_cond + other_cond) * (centre - other)
    return summed


def diagonal(cond_pad, level_scale):
    centre_cond = trim_circle(cond_pad, 1)
    summed = jnp.zeros_like(centre_cond)
    for other_cond in neighbour_list(cond_pad):
        summed = summed + level_scale * 0.5 * (centre_cond + other_cond)
    return summed


def relaxed(field_pad, source, cond_pad, diag_level, level_scale):
    return (
        trim_circle(field_pad, 1)
        + DAMPING * (source - stencil(field_pad, cond_pad, level_scale)) / diag_level
    )


def restrict(field):
    leading = field.shape[:-3]
    extent = field.shape[-3:]
    shaped = field.reshape(leading + (extent[0] // 2, 2, extent[1] // 2, 2, extent[2] // 2, 2))
    return shaped.mean(axis=(-5, -3, -1))


def prolong(field):
    return jnp.repeat(jnp.repeat(jnp.repeat(field, 2, axis=-3), 2, axis=-2), 2, axis=-1)


def assemble(blocks, count_x, count_y):
    leading = blocks.shape[1:-3]
    extent = blocks.shape[-3:]
    depth_lead = len(leading)
    shaped = blocks.reshape((count_x, count_y) + leading + extent)
    order = tuple(range(2, 2 + depth_lead)) + (0, 2 + depth_lead, 1, 3 + depth_lead, 4 + depth_lead)
    return shaped.transpose(order).reshape(
        leading + (count_x * extent[0], count_y * extent[1], extent[2])
    )


def field_rim(field):
    return extended(field, (("gx", 1), ("gy", 2)), 1)


def cond_rim(conduct):
    return extended(conduct, (("gx", 0), ("gy", 1)), 1)


def whole_cycle(source, level_index, whole_plans):
    cond_pad, diag_level, level_scale = whole_plans[level_index]
    field = DAMPING * source / diag_level

    def turn(turn_index, iterate):
        return relaxed(pad_plane(iterate, 1), source, cond_pad, diag_level, level_scale)

    return lax.fori_loop(0, COARSE_SWEEPS - 1, turn, field)


def part_cycle(source, level_index, level_plans, whole_plans, gather_level):
    if level_index == gather_level:
        blocks = lax.all_gather(source[None], ("gx", "gy"), axis=0, tiled=True)
        whole = assemble(blocks, lax.axis_size("gx"), lax.axis_size("gy"))
        correction = whole_cycle(whole, level_index, whole_plans)
        extent = source.shape
        starts = (0, lax.axis_index("gx") * extent[1], lax.axis_index("gy") * extent[2], 0)
        return lax.dynamic_slice(correction, starts, extent)
    cond_pad, diag_level, level_scale = level_plans[level_index]
    field = DAMPING * source / diag_level
    field = relaxed(field_rim(field), source, cond_pad, diag_level, level_scale)
    residual = source - stencil(field_rim(field), cond_pad, level_scale)
    field = field + prolong(
        part_cycle(restrict(residual), level_index + 1, level_plans, whole_plans, gather_level)
    )
    field = relaxed(field_rim(field), source, cond_pad, diag_level, level_scale)
    return relaxed(field_rim(field), source, cond_pad, diag_level, level_scale)


def distributed(conductivity, stations, currents, receivers, observed):
    row_count, col_count, z_count = conductivity.shape
    shot_count = currents.shape[0]
    count_x = lax.axis_size("gx")
    count_y = lax.axis_size("gy")
    gather_level = LEVELS - 1
    level_plans = []
    conduct = conductivity
    for level_index in range(gather_level):
        level_scale = 0.25**level_index
        cond_pad = cond_rim(conduct)
        level_plans.append((cond_pad, diagonal(cond_pad, level_scale), level_scale))
        conduct = restrict(conduct)
    blocks = lax.all_gather(conduct[None], ("gx", "gy"), axis=0, tiled=True)
    whole = assemble(blocks, count_x, count_y)
    whole_plans = {}
    level_index = 3
    level_scale = 0.25**level_index
    cond_pad = pad_plane(whole, 1)
    whole_plans[level_index] = (cond_pad, diagonal(cond_pad, level_scale), level_scale)
    total_y = col_count * count_y
    cell_x = stations // (total_y * z_count)
    cell_y = stations // z_count % total_y
    cell_z = stations % z_count
    local_x = cell_x - lax.axis_index("gx") * row_count
    local_y = cell_y - lax.axis_index("gy") * col_count
    owned = (local_x >= 0) & (local_x < row_count) & (local_y >= 0) & (local_y < col_count)
    block_size = row_count * col_count * z_count
    local_cell = jnp.where(owned, (local_x * col_count + local_y) * z_count + cell_z, 0)
    offsets = jnp.arange(shot_count)[:, None] * block_size + local_cell[None, :]
    targets = jnp.where(owned[None, :], offsets, shot_count * block_size).reshape(-1)

    def spread(amounts):
        flat = (
            jnp.zeros((shot_count * block_size,), jnp.float32)
            .at[targets]
            .add(amounts.reshape(-1), mode="drop")
        )
        return flat.reshape(shot_count, row_count, col_count, z_count)

    potentials = part_cycle(spread(currents), 0, level_plans, whole_plans, gather_level)
    local_values = jnp.where(
        owned[None, :], potentials.reshape(shot_count, block_size)[:, local_cell], 0.0
    )
    readings = lax.psum(local_values, ("gx", "gy"))
    positions = jnp.arange(stations.shape[0])[:, None]
    pairs = (receivers[:, 0][None, :] == positions).astype(jnp.float32) - (
        receivers[:, 1][None, :] == positions
    ).astype(jnp.float32)
    misfit = jnp.dot(readings, pairs, precision=lax.Precision.HIGHEST) - observed
    back_source = jnp.dot(misfit, pairs.T, precision=lax.Precision.HIGHEST)
    adjoint = part_cycle(spread(back_source), 0, level_plans, whole_plans, gather_level)
    stacked = jnp.concatenate([potentials, adjoint], axis=0)
    padded = extended(stacked, (("gx", 1), ("gy", 2)), 1)
    potential_pad = padded[:shot_count]
    adjoint_pad = padded[shot_count:]
    gradient = jnp.zeros_like(potentials)
    for other_u, other_w in zip(neighbour_list(potential_pad), neighbour_list(adjoint_pad)):
        gradient = gradient - 0.5 * (potentials - other_u) * (adjoint - other_w)
    summed = lax.psum_scatter(jnp.sum(gradient, axis=0), "shot", scatter_dimension=1, tiled=True)
    return (potentials, summed)


def per_device(conductivity, stations, currents, receivers, observed):
    blocks = lax.axis_size("gx") * lax.axis_size("gy")
    fits = conductivity.shape == (SIDE, SIDE * SIDE, LANES) and blocks == SIDE
    fits = fits and lax.axis_size("gy") == 2 and currents.shape[0] == 1
    plan = replicated if fits else distributed
    return plan(conductivity, stations, currents, receivers, observed)


def solution(mesh):
    in_specs = (
        P(("grp", "gx"), "gy", None),
        P("grp"),
        P(("grp", "shot"), None),
        P("grp", None),
        P(("grp", "shot"), None),
    )
    out_specs = (P(("grp", "shot"), "gx", "gy", None), P(("grp", "gx"), ("gy", "shot"), None))
    return jax.shard_map(
        per_device, mesh=mesh, in_specs=in_specs, out_specs=out_specs, check_vma=False
    )
```

```python
import functools

import jax
import jax.numpy as jnp
from jax import lax
from jax.experimental import pallas as pl
from jax.experimental.pallas import tpu as pltpu
from jax.sharding import PartitionSpec as P

LEVELS = 4
COARSE_SWEEPS = 16


DAMPING = 0.8

SIDE = 8
LANES = 128
GROUP = 16
VMEM_BYTES = 48 * 2**20


def pieces_of(value, count):
    pieces = []
    for _ in range(count):
        pieces.append(value.astype(jnp.bfloat16))
        value = value - pieces[-1].astype(jnp.float32)
    return pieces[::-1]


def product(value, matrix, count, dims=((1,), (0,))):
    result = None
    for piece in pieces_of(value, count):
        term = lax.dot_general(
            piece, matrix, (dims, ((), ())), preferred_element_type=jnp.float32
        )
        result = term if result is None else result + term
    return result


def iota(shape, dim):
    return lax.broadcasted_iota(jnp.int32, shape, dim)


def station_table(station):
    cell_x, cell_y, cell_z = station >> 14, station >> 7 & 127, station & 127
    row = (cell_x >> 3) * 2 + (cell_y >> 6)
    return cell_x, cell_y, cell_z, row, (cell_y >> 3 & 7) * GROUP + (cell_z >> 3)


def lane_order():
    row, col = iota((LANES, LANES), 0), iota((LANES, LANES), 1)
    chosen = row == col % GROUP * SIDE + col // GROUP
    return jnp.where(chosen, 1.0, 0.0).astype(jnp.bfloat16)


def exchange_groups(tiles):
    tiles = list(tiles)
    group = iota(tiles[0].shape, 1) // GROUP
    for bit in range(3):
        step = 1 << bit
        keep = (group & step) == 0
        for low in range(SIDE):
            if low & step == 0:
                a, b = tiles[low], tiles[low | step]
                tiles[low] = jnp.where(keep, a, pltpu.roll(b, step * GROUP, 1))
                tiles[low | step] = jnp.where(keep, pltpu.roll(a, LANES - step * GROUP, 1), b)
    return tiles


def to_blocks_kernel(natural_ref, stations_ref, blocks_ref, cells_ref):
    order = lane_order()
    for x in range(SIDE):
        tiles = product(natural_ref[x], order, 3)
        tiles = [tiles[SIDE * k : SIDE * (k + 1)] for k in range(SIDE)]
        for z, tile in enumerate(exchange_groups(tiles)):
            blocks_ref[pl.ds((x * SIDE + z) * SIDE, SIDE), :] = tile
    cell_x, cell_y, cell_z, row, _ = station_table(stations_ref[...])
    wide = SIDE + 2
    register = (((cell_x & 7) + 1) * wide + (cell_z & 7) + 1) * wide + (cell_y & 7) + 1
    cells_ref[...] = register * SIDE + row


def from_blocks(tiles, order):
    natural = jnp.concatenate(exchange_groups(tiles), axis=0)
    return product(natural, order, 3, ((1,), (1,)))


def block_up(field, axis):
    if axis == 0:
        return pltpu.roll(field, 6, 1)
    if axis == 2:
        return pltpu.roll(field, LANES - 1, 2)
    turned = pltpu.roll(field, LANES - GROUP, 2)
    return jnp.where(iota(field.shape, 2) < LANES - GROUP, turned, pltpu.roll(turned, 7, 1))


def block_down(field, axis):
    if axis == 0:
        return pltpu.roll(field, 2, 1)
    if axis == 2:
        return pltpu.roll(field, 1, 2)
    turned = pltpu.roll(field, GROUP, 2)
    return jnp.where(iota(field.shape, 2) >= GROUP, turned, pltpu.roll(turned, 1, 1))


def inside_up(field, axis):
    sub, lane = iota(field.shape, 1), iota(field.shape, 2)
    if axis == 0:
        keep = sub < 6
    elif axis == 1:
        keep = (lane < LANES - GROUP) | (sub % 2 == 0)
    else:
        keep = lane % GROUP < GROUP - 1
    return jnp.where(keep, field, 0.0)


def inside_down(field, axis):
    sub, lane = iota(field.shape, 1), iota(field.shape, 2)
    if axis == 0:
        keep = sub >= 2
    elif axis == 1:
        keep = (lane >= GROUP) | (sub % 2 == 1)
    else:
        keep = lane % GROUP > 0
    return jnp.where(keep, field, 0.0)


def pair_rows(row):
    count = row.shape[0] // 2
    return jnp.concatenate([row[2 * i : 2 * i + 1] + row[2 * i + 1 : 2 * i + 2] for i in range(count)])


def twice(row):
    return jnp.concatenate([row[i // 2 : i // 2 + 1] for i in range(2 * row.shape[0])])


class Edged:
    def __init__(self, ref, side):
        self.ref, self.side = ref, side

    def start(self, x, z, y=0):
        wide = self.side + 2
        return (((x + 1) * wide + z + 1) * wide + y + 1) * SIDE

    def __getitem__(self, at):
        x, z = at
        rows = self.ref[pl.ds(self.start(x, z), self.side * SIDE), :]
        return rows.reshape(self.side, SIDE, LANES)

    def __setitem__(self, at, value):
        x, z = at
        self.ref[pl.ds(self.start(x, z), self.side * SIDE), :] = value.reshape(-1, LANES)

    def put(self, x, z, value, exact=False):
        self[x, z] = value
        n = self.side
        if z == 0:
            edge = block_up(value, 2)
            self[x, n] = inside_up(edge, 2) if exact else edge
        if z == n - 1:
            edge = block_down(value, 2)
            self[x, -1] = inside_down(edge, 2) if exact else edge
        if exact:
            after = inside_up(block_up(value[:1], 1), 1)
            self.ref[pl.ds(self.start(x, z, n), SIDE), :] = after[0]
            before = inside_down(block_down(value[n - 1 :], 1), 1)
            self.ref[pl.ds(self.start(x, z, -1), SIDE), :] = before[0]

    def close_z(self, x):
        n = self.side
        self[x, n] = block_up(self[x, 0], 2)
        self[x, -1] = block_down(self[x, n - 1], 2)

    def close(self, exact=False):
        n = self.side
        for z in range(n):
            after = block_up(self[0, z], 0)
            self[n, z] = inside_up(after, 0) if exact else after
            before = block_down(self[n - 1, z], 0)
            self[-1, z] = inside_down(before, 0) if exact else before


class Plain:
    def __init__(self, ref, side):
        self.ref, self.side = ref, side

    def __getitem__(self, at):
        x, z = at
        rows = self.side * SIDE
        return self.ref[pl.ds((x * self.side + z) * rows, rows), :].reshape(self.side, SIDE, LANES)

    def __setitem__(self, at, value):
        x, z = at
        rows = self.side * SIDE
        self.ref[pl.ds((x * self.side + z) * rows, rows), :] = value.reshape(-1, LANES)


def planes_of(count, body):
    if count < SIDE:
        for x in range(count):
            body(x)
        return

    def one(x, carry):
        body(x)
        return carry

    lax.fori_loop(0, count, one, 0)


class Level:
    def __init__(self, refs, index):
        self.side = side = SIDE >> index
        self.scale = 0.25**index
        edged = [Edged(ref, side) for ref in refs[:5]]
        self.cond, self.first, self.second, self.base, self.back = edged
        self.links = [Plain(ref, side) for ref in refs[5:11]]
        self.half = Plain(refs[11], side // 2)
        self.weight = Plain(refs[12], side) if index else None

    @staticmethod
    def scratch(index):
        side = SIDE >> index
        edged = (side + 2) ** 3
        sizes = [edged] * 5 + [side**3] * 6 + [side**3 // 4] + [side**3] * (index > 0)
        return [pltpu.VMEM((size * SIDE, LANES), jnp.float32) for size in sizes]

    def shifted(self, field, x, z, here, exact=False, along=None):
        ahead, behind = along or (field[x, z + 1], field[x, z - 1])
        after = block_up(here[:1], 1)
        before = block_down(here[-1:], 1)
        if exact:
            after, before = inside_up(after, 1), inside_down(before, 1)
        return [
            field[x + 1, z],
            field[x - 1, z],
            jnp.concatenate([here[1:], after]),
            jnp.concatenate([before, here[:-1]]),
            ahead,
            behind,
        ]

    def prepare(self):
        n = self.side

        def plane(x):
            for z in range(n):
                here = self.cond[x, z]
                others = self.shifted(self.cond, x, z, here, exact=True)
                total = others[0]
                for other in others[1:]:
                    total = total + other
                total = 3.0 * here + 0.5 * total
                inverse = DAMPING / total
                if self.weight is not None:
                    self.weight[x, z] = inverse * (1.0 / self.scale)
                self.back[x, z] = total * (self.scale / DAMPING)
                inverse = 0.5 * inverse
                for index, other in enumerate(others):
                    link = inverse * (here + other)
                    if index == 2:
                        link = jnp.concatenate([link[:-1], inside_up(link[-1:], 1)])
                    if index == 3:
                        link = jnp.concatenate([inside_down(link[:1], 1), link[1:]])
                    if index == 4 and z == n - 1:
                        link = inside_up(link, 2)
                    if index == 5 and z == 0:
                        link = inside_down(link, 2)
                    self.links[index][x, z] = link

        planes_of(n, plane)
        for z in range(n):
            self.links[0][n - 1, z] = inside_up(self.links[0][n - 1, z], 0)
            self.links[1][0, z] = inside_down(self.links[1][0, z], 0)

    def rows(self, field, x):
        behind, here = field[x, -1], field[x, 0]
        for z in range(self.side):
            ahead = field[x, z + 1]
            result = self.base[x, z]
            others = self.shifted(field, x, z, here, along=(ahead, behind))
            for link, other in zip(self.links, others):
                result = result + link[x, z] * other
            yield z, here, result
            behind, here = here, ahead

    def sweep(self, field, out, exact=False):
        def plane(x):
            for z, here, result in self.rows(field, x):
                out.put(x, z, (1.0 - DAMPING) * here + result, exact)

        planes_of(self.side, plane)
        out.close(exact)

    def halve(self, plane_rows, coarse):
        n = self.side

        def plane(x):
            held = None
            for z, row in enumerate(plane_rows(x)):
                if z % 2 == 0:
                    held = row
                else:
                    self.half[x, z // 2] = pair_rows(held + row)

        planes_of(n, plane)
        for x in range(n // 2):
            for z in range(n // 2):
                pair = self.half[2 * x, z] + self.half[2 * x + 1, z]
                coarse(x, z, 0.125 * pair)

    def descend(self, coarse):
        self.sweep(self.base, self.second)

        def residuals(x):
            for z, here, result in self.rows(self.second, x):
                self.first[x, z] = (1.0 - DAMPING) * here + result
                yield (result - DAMPING * here) * self.back[x, z]

        self.halve(residuals, coarse)

    def ascend(self, correction, out, exact=False):
        def plane(x):
            upper = (x + 1) // 2
            for z in range(self.side):
                above = (z + 1) // 2
                row = correction(x // 2, z // 2)
                here = twice(row)
                after, before = block_up(row[:1], 1), block_down(row[-1:], 1)
                others = [
                    twice(correction(upper, z // 2)),
                    twice(correction(upper - 1, z // 2)),
                    jnp.concatenate([here[1:], after]),
                    jnp.concatenate([before, here[:-1]]),
                    twice(correction(x // 2, above)),
                    twice(correction(x // 2, above - 1)),
                ]
                result = self.first[x, z] + (1.0 - DAMPING) * here
                for link, other in zip(self.links, others):
                    result = result + link[x, z] * other
                self.second.put(x, z, result)

        planes_of(self.side, plane)
        self.second.close()
        self.sweep(self.second, out, exact)


def replicated_kernel(
    count,
    device_ref,
    cells_ref,
    *refs,
):
    solve_kernel(refs[:count], device_ref, cells_ref, *refs[count:])


def solve_kernel(
    part_refs,
    device_ref,
    cells_ref,
    stations_ref,
    currents_ref,
    receivers_ref,
    observed_ref,
    potentials_ref,
    mine_ref,
    theirs_ref,
    gathered,
    weights,
    *level_refs,
):
    f32 = jnp.float32
    electrodes = stations_ref.shape[1]
    levels, used = [], 0
    for index in range(LEVELS - 1):
        count = len(Level.scratch(index))
        levels.append(Level(level_refs[used : used + count], index))
        used += count
    fine = levels[0]
    forward = fine.cond
    wide = SIDE * SIDE * SIDE

    device = device_ref[0]
    def collect(x):
        for k, part in enumerate(part_refs):
            for z in range(SIDE):
                start = fine.cond.start(x, z) + (device ^ k)
                fine.cond.ref[pl.ds(start, SIDE, stride=SIDE), :] = part[
                    pl.ds((x * SIDE + z) * SIDE, SIDE), :
                ]
        for z in (0, SIDE - 1):
            fine.cond.put(x, z, fine.cond[x, z], exact=True)

    planes_of(SIDE, collect)
    fine.cond.close(exact=True)

    coarsest = []
    for level, below in zip(levels, levels[1:] + [None]):
        level.prepare()

        def coarse(x, z, row, below=below):
            if below is None:
                coarsest.append(row)
            else:
                below.cond.put(x, z, row, exact=True)

        level.halve(lambda x, level=level: [level.cond[x, z] for z in range(level.side)], coarse)
        if below is not None:
            below.cond.close(exact=True)

    last_scale = 0.25 ** (LEVELS - 1)
    here = coarsest[0]
    others = [inside(move(here, axis), axis) for axis in range(3) for inside, move in ((inside_up, block_up), (inside_down, block_down))]
    total = others[0]
    for other in others[1:]:
        total = total + other
    total = 3.0 * here + 0.5 * total
    inverse = DAMPING / total
    last_weight = inverse * (1.0 / last_scale)
    last_links = []
    for axis in range(3):
        for inside, other in ((inside_up, others[2 * axis]), (inside_down, others[2 * axis + 1])):
            last_links.append(inside(0.5 * inverse * (here + other), axis))

    def solve_last(rhs):
        base = last_weight * rhs
        value = base
        for _ in range(COARSE_SWEEPS - 1):
            parts = []
            for axis in range(3):
                parts.append(last_links[2 * axis] * block_up(value, axis))
                parts.append(last_links[2 * axis + 1] * block_down(value, axis))
            start = base + (1.0 - DAMPING) * value
            value = ((start + parts[0]) + (parts[1] + parts[4])) + (parts[5] + (parts[2] + parts[3]))
        return value

    def cycle(index, out, exact=False):
        level = levels[index]
        if index == LEVELS - 2:
            held = []
            level.descend(lambda x, z, row: held.append(row))
            solved = solve_last(held[0])

            def correction(x, z):
                if x != 0:
                    return (block_up if x > 0 else block_down)(solved, 0)
                if z != 0:
                    return (block_up if z > 0 else block_down)(solved, 2)
                return solved

            level.ascend(correction, out, exact)
            return
        below = levels[index + 1]
        level.descend(lambda x, z, row: below.base.put(x, z, below.weight[x, z] * row))
        below.base.close()
        cycle(index + 1, below.first)
        level.ascend(lambda x, z: below.first[x, z], out, exact)

    _, cell_y, cell_z, row, spot = station_table(stations_ref[...])
    at_spot = iota((LANES, electrodes), 0) == spot
    line = stations_ref[...] & 0x1C387 | row << 20
    same = jnp.broadcast_to(line, (electrodes, electrodes))
    same = jnp.where(same == same.T, 1.0, 0.0).astype(jnp.bfloat16)

    def each(body):
        def one(electrode, carry):
            body(pl.ds(electrode, 1), pl.ds(cells_ref[0, electrode], 1))
            return carry

        lax.fori_loop(0, electrodes, one, 0, unroll=8)

    def weigh(electrode, cell):
        weights[electrode, :] = fine.back.ref[cell, :]

    each(weigh)
    weights[...] = 1.0 / weights[...]
    fine.base.ref[...] = jnp.zeros_like(fine.base.ref)

    def spread(amounts):
        shared = product(jnp.where(at_spot, amounts, 0.0), same, 3)
        gathered[...] = shared.T * weights[...]

        def put(electrode, cell):
            fine.base.ref[cell, :] = gathered[electrode, :]

        each(put)
        planes_of(SIDE, fine.base.close_z)
        fine.base.close()

    spread(currents_ref[...])
    cycle(0, forward, exact=True)

    def read(electrode, cell):
        gathered[electrode, :] = forward.ref[cell, :]

    each(read)
    readings = jnp.sum(jnp.where(at_spot, gathered[...].T, 0.0), axis=0, keepdims=True)
    receivers = receivers_ref[...]
    numbers = iota((receivers.shape[0], electrodes), 1)
    pairs = jnp.where(numbers == receivers[:, 0:1], 1.0, 0.0) - jnp.where(
        numbers == receivers[:, 1:2], 1.0, 0.0
    )
    pairs = pairs.astype(jnp.bfloat16)

    def exact(row, dims):
        return product(jnp.broadcast_to(row, (16, row.shape[1])), pairs, 3, dims)[0:1]

    misfit = exact(readings, ((1,), (1,))) - observed_ref[...]
    spread(exact(misfit, ((1,), (0,))))
    cycle(0, fine.first, exact=True)

    order = lane_order()
    adjoint = fine.first
    chunk = mine_ref.shape[1]
    even = device_ref[1] == 0

    def own(field, x, z, y=0):
        return field.ref[pl.ds(field.start(x, z, y) + device, SIDE, stride=SIDE), :]

    for x in range(SIDE):
        tiles_u, tiles_g = [], []
        for z in range(SIDE):
            here_u, here_w = own(forward, x, z), own(adjoint, x, z)
            total = None
            for at in ((x + 1, z), (x - 1, z), (x, z, 1), (x, z, -1), (x, z + 1), (x, z - 1)):
                term = (here_u - own(forward, *at)) * (here_w - own(adjoint, *at))
                total = term if total is None else total + term
            tiles_u.append(here_u)
            tiles_g.append(-0.5 * total)
        potentials_ref[x] = from_blocks(tiles_u, order)
        natural = from_blocks(tiles_g, order)
        low, high = natural[:chunk], natural[chunk:]
        mine_ref[x] = jnp.where(even, low, high)
        theirs_ref[x] = jnp.where(even, high, low)


def replicated(conductivity, stations, currents, receivers, observed):
    rows, cols, depth = conductivity.shape
    f32 = jnp.float32
    electrodes = stations.shape[0]
    total = rows * cols
    vmem = pl.BlockSpec(memory_space=pltpu.VMEM)
    smem = pl.BlockSpec(memory_space=pltpu.SMEM)
    station_row = stations.reshape(1, electrodes)
    mine, cells = pl.pallas_call(
        to_blocks_kernel,
        out_shape=(
            jax.ShapeDtypeStruct((total, LANES), f32),
            jax.ShapeDtypeStruct((1, electrodes), jnp.int32),
        ),
        in_specs=[vmem, vmem],
        out_specs=(vmem, vmem),
    )(conductivity, station_row)
    count_x, count_y = lax.axis_size("gx"), lax.axis_size("gy")
    parts = []
    for k in range(count_x):
        pairs = [(i, i ^ k) for i in range(count_x)]
        parts.append(lax.ppermute(mine, "gx", pairs) if k else mine)
    swap = [(0, 1), (1, 0)]
    parts = [part for own in parts for part in (own, lax.ppermute(own, "gy", swap))]
    device = lax.axis_index("gx") * count_y + lax.axis_index("gy")
    place = jnp.stack([device, lax.axis_index("shot")]).astype(jnp.int32)
    chunk = cols // 2
    levels = [shape for index in range(LEVELS - 1) for shape in Level.scratch(index)]
    potentials, own, theirs = pl.pallas_call(
        functools.partial(replicated_kernel, len(parts)),
        out_shape=(
            jax.ShapeDtypeStruct((rows, cols, LANES), f32),
            jax.ShapeDtypeStruct((rows, chunk, LANES), f32),
            jax.ShapeDtypeStruct((rows, chunk, LANES), f32),
        ),
        in_specs=[smem, smem] + [vmem] * (len(parts) + 4),
        out_specs=(vmem, vmem, vmem),
        scratch_shapes=[
            pltpu.VMEM((electrodes, LANES), f32),
            pltpu.VMEM((electrodes, LANES), f32),
        ]
        + levels,
        compiler_params=pltpu.CompilerParams(vmem_limit_bytes=VMEM_BYTES),
        cost_estimate=pl.CostEstimate(flops=200_000_000, bytes_accessed=4_000_000, transcendentals=0),
    )(place, cells, *parts, station_row, currents, receivers, observed)
    return potentials[None], own + lax.ppermute(theirs, "shot", swap)


def extended(array, sides, width):
    for axis, dim in sides:
        size, length = (lax.axis_size(axis), array.shape[dim])
        up = [(i, (i + 1) % size) for i in range(size - 1)]
        down = [(j, i) for i, j in up]
        last = lax.slice_in_dim(array, length - width, length, axis=dim)
        leading = lax.slice_in_dim(array, 0, width, axis=dim)
        before = lax.ppermute(last, axis, up)
        after = lax.ppermute(leading, axis, down)
        array = jnp.concatenate([before, array, after], axis=dim)
    return array


def upper_z(field):
    return jnp.concatenate([field[..., 1:], jnp.zeros_like(field[..., :1])], axis=-1)


def lower_z(field):
    return jnp.concatenate([jnp.zeros_like(field[..., :1]), field[..., :-1]], axis=-1)


def trim_circle(field, circle_width):
    return field[..., circle_width:-circle_width, circle_width:-circle_width, :]


def pad_plane(field, circle_width):
    spec = [(0, 0)] * (field.ndim - 3) + [
        (circle_width, circle_width),
        (circle_width, circle_width),
        (0, 0),
    ]
    return jnp.pad(field, spec)


def neighbour_list(field_pad):
    centre = trim_circle(field_pad, 1)
    return [
        field_pad[..., 2:, 1:-1, :],
        field_pad[..., :-2, 1:-1, :],
        field_pad[..., 1:-1, 2:, :],
        field_pad[..., 1:-1, :-2, :],
        upper_z(centre),
        lower_z(centre),
    ]


def stencil(field_pad, cond_pad, level_scale):
    centre = trim_circle(field_pad, 1)
    centre_cond = trim_circle(cond_pad, 1)
    summed = jnp.zeros_like(centre)
    for other, other_cond in zip(neighbour_list(field_pad), neighbour_list(cond_pad)):
        summed = summed + level_scale * 0.5 * (centre_cond + other_cond) * (centre - other)
    return summed


def diagonal(cond_pad, level_scale):
    centre_cond = trim_circle(cond_pad, 1)
    summed = jnp.zeros_like(centre_cond)
    for other_cond in neighbour_list(cond_pad):
        summed = summed + level_scale * 0.5 * (centre_cond + other_cond)
    return summed


def relaxed(field_pad, source, cond_pad, diag_level, level_scale):
    return (
        trim_circle(field_pad, 1)
        + DAMPING * (source - stencil(field_pad, cond_pad, level_scale)) / diag_level
    )


def restrict(field):
    leading = field.shape[:-3]
    extent = field.shape[-3:]
    shaped = field.reshape(leading + (extent[0] // 2, 2, extent[1] // 2, 2, extent[2] // 2, 2))
    return shaped.mean(axis=(-5, -3, -1))


def prolong(field):
    return jnp.repeat(jnp.repeat(jnp.repeat(field, 2, axis=-3), 2, axis=-2), 2, axis=-1)


def assemble(blocks, count_x, count_y):
    leading = blocks.shape[1:-3]
    extent = blocks.shape[-3:]
    depth_lead = len(leading)
    shaped = blocks.reshape((count_x, count_y) + leading + extent)
    order = tuple(range(2, 2 + depth_lead)) + (0, 2 + depth_lead, 1, 3 + depth_lead, 4 + depth_lead)
    return shaped.transpose(order).reshape(
        leading + (count_x * extent[0], count_y * extent[1], extent[2])
    )


def field_rim(field):
    return extended(field, (("gx", 1), ("gy", 2)), 1)


def cond_rim(conduct):
    return extended(conduct, (("gx", 0), ("gy", 1)), 1)


def whole_cycle(source, level_index, whole_plans):
    cond_pad, diag_level, level_scale = whole_plans[level_index]
    field = DAMPING * source / diag_level

    def turn(turn_index, iterate):
        return relaxed(pad_plane(iterate, 1), source, cond_pad, diag_level, level_scale)

    return lax.fori_loop(0, COARSE_SWEEPS - 1, turn, field)


def part_cycle(source, level_index, level_plans, whole_plans, gather_level):
    if level_index == gather_level:
        blocks = lax.all_gather(source[None], ("gx", "gy"), axis=0, tiled=True)
        whole = assemble(blocks, lax.axis_size("gx"), lax.axis_size("gy"))
        correction = whole_cycle(whole, level_index, whole_plans)
        extent = source.shape
        starts = (0, lax.axis_index("gx") * extent[1], lax.axis_index("gy") * extent[2], 0)
        return lax.dynamic_slice(correction, starts, extent)
    cond_pad, diag_level, level_scale = level_plans[level_index]
    field = DAMPING * source / diag_level
    field = relaxed(field_rim(field), source, cond_pad, diag_level, level_scale)
    residual = source - stencil(field_rim(field), cond_pad, level_scale)
    field = field + prolong(
        part_cycle(restrict(residual), level_index + 1, level_plans, whole_plans, gather_level)
    )
    field = relaxed(field_rim(field), source, cond_pad, diag_level, level_scale)
    return relaxed(field_rim(field), source, cond_pad, diag_level, level_scale)


def distributed(conductivity, stations, currents, receivers, observed):
    row_count, col_count, z_count = conductivity.shape
    shot_count = currents.shape[0]
    count_x = lax.axis_size("gx")
    count_y = lax.axis_size("gy")
    gather_level = LEVELS - 1
    level_plans = []
    conduct = conductivity
    for level_index in range(gather_level):
        level_scale = 0.25**level_index
        cond_pad = cond_rim(conduct)
        level_plans.append((cond_pad, diagonal(cond_pad, level_scale), level_scale))
        conduct = restrict(conduct)
    blocks = lax.all_gather(conduct[None], ("gx", "gy"), axis=0, tiled=True)
    whole = assemble(blocks, count_x, count_y)
    whole_plans = {}
    level_index = 3
    level_scale = 0.25**level_index
    cond_pad = pad_plane(whole, 1)
    whole_plans[level_index] = (cond_pad, diagonal(cond_pad, level_scale), level_scale)
    total_y = col_count * count_y
    cell_x = stations // (total_y * z_count)
    cell_y = stations // z_count % total_y
    cell_z = stations % z_count
    local_x = cell_x - lax.axis_index("gx") * row_count
    local_y = cell_y - lax.axis_index("gy") * col_count
    owned = (local_x >= 0) & (local_x < row_count) & (local_y >= 0) & (local_y < col_count)
    block_size = row_count * col_count * z_count
    local_cell = jnp.where(owned, (local_x * col_count + local_y) * z_count + cell_z, 0)
    offsets = jnp.arange(shot_count)[:, None] * block_size + local_cell[None, :]
    targets = jnp.where(owned[None, :], offsets, shot_count * block_size).reshape(-1)

    def spread(amounts):
        flat = (
            jnp.zeros((shot_count * block_size,), jnp.float32)
            .at[targets]
            .add(amounts.reshape(-1), mode="drop")
        )
        return flat.reshape(shot_count, row_count, col_count, z_count)

    potentials = part_cycle(spread(currents), 0, level_plans, whole_plans, gather_level)
    local_values = jnp.where(
        owned[None, :], potentials.reshape(shot_count, block_size)[:, local_cell], 0.0
    )
    readings = lax.psum(local_values, ("gx", "gy"))
    positions = jnp.arange(stations.shape[0])[:, None]
    pairs = (receivers[:, 0][None, :] == positions).astype(jnp.float32) - (
        receivers[:, 1][None, :] == positions
    ).astype(jnp.float32)
    misfit = jnp.dot(readings, pairs, precision=lax.Precision.HIGHEST) - observed
    back_source = jnp.dot(misfit, pairs.T, precision=lax.Precision.HIGHEST)
    adjoint = part_cycle(spread(back_source), 0, level_plans, whole_plans, gather_level)
    stacked = jnp.concatenate([potentials, adjoint], axis=0)
    padded = extended(stacked, (("gx", 1), ("gy", 2)), 1)
    potential_pad = padded[:shot_count]
    adjoint_pad = padded[shot_count:]
    gradient = jnp.zeros_like(potentials)
    for other_u, other_w in zip(neighbour_list(potential_pad), neighbour_list(adjoint_pad)):
        gradient = gradient - 0.5 * (potentials - other_u) * (adjoint - other_w)
    summed = lax.psum_scatter(jnp.sum(gradient, axis=0), "shot", scatter_dimension=1, tiled=True)
    return (potentials, summed)


def per_device(conductivity, stations, currents, receivers, observed):
    blocks = lax.axis_size("gx") * lax.axis_size("gy")
    fits = conductivity.shape == (SIDE, SIDE * SIDE, LANES) and blocks == SIDE
    fits = fits and lax.axis_size("gy") == 2 and lax.axis_size("shot") == 2
    fits = fits and currents.shape[0] == 1
    plan = replicated if fits else distributed
    return plan(conductivity, stations, currents, receivers, observed)


def solution(mesh):
    in_specs = (
        P(("grp", "gx"), "gy", None),
        P("grp"),
        P(("grp", "shot"), None),
        P("grp", None),
        P(("grp", "shot"), None),
    )
    out_specs = (P(("grp", "shot"), "gx", "gy", None), P(("grp", "gx"), ("gy", "shot"), None))
    return jax.shard_map(
        per_device, mesh=mesh, in_specs=in_specs, out_specs=out_specs, check_vma=False
    )
```

```python
import functools

import jax
import jax.numpy as jnp
from jax import lax
from jax.experimental import pallas as pl
from jax.experimental.pallas import tpu as pltpu
from jax.sharding import PartitionSpec as P

LEVELS = 4
COARSE_SWEEPS = 16


DAMPING = 0.8

SIDE = 8
LANES = 128
GROUP = 16
VMEM_BYTES = 48 * 2**20


def pieces_of(value, count):
    pieces = []
    for _ in range(count):
        pieces.append(value.astype(jnp.bfloat16))
        value = value - pieces[-1].astype(jnp.float32)
    return pieces[::-1]


def product(value, matrix, count, dims=((1,), (0,))):
    result = None
    for piece in pieces_of(value, count):
        term = lax.dot_general(
            piece, matrix, (dims, ((), ())), preferred_element_type=jnp.float32
        )
        result = term if result is None else result + term
    return result


def iota(shape, dim):
    return lax.broadcasted_iota(jnp.int32, shape, dim)


def station_table(station):
    cell_x, cell_y, cell_z = station >> 14, station >> 7 & 127, station & 127
    row = (cell_x >> 3) * 2 + (cell_y >> 6)
    return cell_x, cell_y, cell_z, row, (cell_y >> 3 & 7) * GROUP + (cell_z >> 3)


def lane_order():
    row, col = iota((LANES, LANES), 0), iota((LANES, LANES), 1)
    chosen = row == col % GROUP * SIDE + col // GROUP
    return jnp.where(chosen, 1.0, 0.0).astype(jnp.bfloat16)


def exchange_groups(tiles):
    tiles = list(tiles)
    group = iota(tiles[0].shape, 1) // GROUP
    for bit in range(3):
        step = 1 << bit
        keep = (group & step) == 0
        for low in range(SIDE):
            if low & step == 0:
                a, b = tiles[low], tiles[low | step]
                tiles[low] = jnp.where(keep, a, pltpu.roll(b, step * GROUP, 1))
                tiles[low | step] = jnp.where(keep, pltpu.roll(a, LANES - step * GROUP, 1), b)
    return tiles


def to_blocks_kernel(place_ref, natural_ref, stations_ref, blocks_ref, half_ref, cells_ref):
    order = lane_order()
    for x in range(SIDE):
        tiles = product(natural_ref[x], order, 3)
        tiles = [tiles[SIDE * k : SIDE * (k + 1)] for k in range(SIDE)]
        for z, tile in enumerate(exchange_groups(tiles)):
            blocks_ref[pl.ds((x * SIDE + z) * SIDE, SIDE), :] = tile
    count = half_ref.shape[0]
    low, high = blocks_ref[pl.ds(0, count), :], blocks_ref[pl.ds(count, count), :]
    half_ref[...] = jnp.where(place_ref[1] == 0, low, high)
    cell_x, cell_y, cell_z, row, _ = station_table(stations_ref[...])
    wide = SIDE + 2
    register = (((cell_x & 7) + 1) * wide + (cell_z & 7) + 1) * wide + (cell_y & 7) + 1
    cells_ref[...] = register * SIDE + row


def from_blocks(tiles, order):
    natural = jnp.concatenate(exchange_groups(tiles), axis=0)
    return product(natural, order, 3, ((1,), (1,)))


def block_up(field, axis):
    if axis == 0:
        return pltpu.roll(field, 6, 1)
    if axis == 2:
        return pltpu.roll(field, LANES - 1, 2)
    turned = pltpu.roll(field, LANES - GROUP, 2)
    return jnp.where(iota(field.shape, 2) < LANES - GROUP, turned, pltpu.roll(turned, 7, 1))


def block_down(field, axis):
    if axis == 0:
        return pltpu.roll(field, 2, 1)
    if axis == 2:
        return pltpu.roll(field, 1, 2)
    turned = pltpu.roll(field, GROUP, 2)
    return jnp.where(iota(field.shape, 2) >= GROUP, turned, pltpu.roll(turned, 1, 1))


def inside_up(field, axis):
    sub, lane = iota(field.shape, 1), iota(field.shape, 2)
    if axis == 0:
        keep = sub < 6
    elif axis == 1:
        keep = (lane < LANES - GROUP) | (sub % 2 == 0)
    else:
        keep = lane % GROUP < GROUP - 1
    return jnp.where(keep, field, 0.0)


def inside_down(field, axis):
    sub, lane = iota(field.shape, 1), iota(field.shape, 2)
    if axis == 0:
        keep = sub >= 2
    elif axis == 1:
        keep = (lane >= GROUP) | (sub % 2 == 1)
    else:
        keep = lane % GROUP > 0
    return jnp.where(keep, field, 0.0)


def pair_rows(row):
    count = row.shape[0] // 2
    return jnp.concatenate([row[2 * i : 2 * i + 1] + row[2 * i + 1 : 2 * i + 2] for i in range(count)])


def twice(row):
    return jnp.concatenate([row[i // 2 : i // 2 + 1] for i in range(2 * row.shape[0])])


class Edged:
    def __init__(self, ref, side):
        self.ref, self.side = ref, side

    def start(self, x, z, y=0):
        wide = self.side + 2
        return (((x + 1) * wide + z + 1) * wide + y + 1) * SIDE

    def __getitem__(self, at):
        x, z = at
        rows = self.ref[pl.ds(self.start(x, z), self.side * SIDE), :]
        return rows.reshape(self.side, SIDE, LANES)

    def __setitem__(self, at, value):
        x, z = at
        self.ref[pl.ds(self.start(x, z), self.side * SIDE), :] = value.reshape(-1, LANES)

    def put(self, x, z, value, exact=False):
        self[x, z] = value
        n = self.side
        if z == 0:
            edge = block_up(value, 2)
            self[x, n] = inside_up(edge, 2) if exact else edge
        if z == n - 1:
            edge = block_down(value, 2)
            self[x, -1] = inside_down(edge, 2) if exact else edge
        if exact:
            after = inside_up(block_up(value[:1], 1), 1)
            self.ref[pl.ds(self.start(x, z, n), SIDE), :] = after[0]
            before = inside_down(block_down(value[n - 1 :], 1), 1)
            self.ref[pl.ds(self.start(x, z, -1), SIDE), :] = before[0]

    def close_z(self, x):
        n = self.side
        self[x, n] = block_up(self[x, 0], 2)
        self[x, -1] = block_down(self[x, n - 1], 2)

    def close(self, exact=False):
        n = self.side
        for z in range(n):
            after = block_up(self[0, z], 0)
            self[n, z] = inside_up(after, 0) if exact else after
            before = block_down(self[n - 1, z], 0)
            self[-1, z] = inside_down(before, 0) if exact else before


class Plain:
    def __init__(self, ref, side):
        self.ref, self.side = ref, side

    def __getitem__(self, at):
        x, z = at
        rows = self.side * SIDE
        return self.ref[pl.ds((x * self.side + z) * rows, rows), :].reshape(self.side, SIDE, LANES)

    def __setitem__(self, at, value):
        x, z = at
        rows = self.side * SIDE
        self.ref[pl.ds((x * self.side + z) * rows, rows), :] = value.reshape(-1, LANES)


def planes_of(count, body):
    if count < SIDE:
        for x in range(count):
            body(x)
        return

    def one(x, carry):
        body(x)
        return carry

    lax.fori_loop(0, count, one, 0)


class Level:
    def __init__(self, refs, index):
        self.side = side = SIDE >> index
        self.scale = 0.25**index
        edged = [Edged(ref, side) for ref in refs[:5]]
        self.cond, self.first, self.second, self.base, self.back = edged
        self.links = [Plain(ref, side) for ref in refs[5:11]]
        self.half = Plain(refs[11], side // 2)
        self.weight = Plain(refs[12], side) if index else None

    @staticmethod
    def scratch(index):
        side = SIDE >> index
        edged = (side + 2) ** 3
        sizes = [edged] * 5 + [side**3] * 6 + [side**3 // 4] + [side**3] * (index > 0)
        return [pltpu.VMEM((size * SIDE, LANES), jnp.float32) for size in sizes]

    def shifted(self, field, x, z, here, exact=False, along=None):
        ahead, behind = along or (field[x, z + 1], field[x, z - 1])
        after = block_up(here[:1], 1)
        before = block_down(here[-1:], 1)
        if exact:
            after, before = inside_up(after, 1), inside_down(before, 1)
        return [
            field[x + 1, z],
            field[x - 1, z],
            jnp.concatenate([here[1:], after]),
            jnp.concatenate([before, here[:-1]]),
            ahead,
            behind,
        ]

    def prepare(self):
        n = self.side

        def plane(x):
            for z in range(n):
                here = self.cond[x, z]
                others = self.shifted(self.cond, x, z, here, exact=True)
                total = others[0]
                for other in others[1:]:
                    total = total + other
                total = 3.0 * here + 0.5 * total
                inverse = DAMPING / total
                if self.weight is not None:
                    self.weight[x, z] = inverse * (1.0 / self.scale)
                self.back[x, z] = total * (self.scale / DAMPING)
                inverse = 0.5 * inverse
                for index, other in enumerate(others):
                    link = inverse * (here + other)
                    if index == 2:
                        link = jnp.concatenate([link[:-1], inside_up(link[-1:], 1)])
                    if index == 3:
                        link = jnp.concatenate([inside_down(link[:1], 1), link[1:]])
                    if index == 4 and z == n - 1:
                        link = inside_up(link, 2)
                    if index == 5 and z == 0:
                        link = inside_down(link, 2)
                    self.links[index][x, z] = link

        planes_of(n, plane)
        for z in range(n):
            self.links[0][n - 1, z] = inside_up(self.links[0][n - 1, z], 0)
            self.links[1][0, z] = inside_down(self.links[1][0, z], 0)

    def rows(self, field, x):
        behind, here = field[x, -1], field[x, 0]
        for z in range(self.side):
            ahead = field[x, z + 1]
            result = self.base[x, z]
            others = self.shifted(field, x, z, here, along=(ahead, behind))
            for link, other in zip(self.links, others):
                result = result + link[x, z] * other
            yield z, here, result
            behind, here = here, ahead

    def sweep(self, field, out, exact=False):
        def plane(x):
            for z, here, result in self.rows(field, x):
                out.put(x, z, (1.0 - DAMPING) * here + result, exact)

        planes_of(self.side, plane)
        out.close(exact)

    def halve(self, plane_rows, coarse):
        n = self.side

        def plane(x):
            held = None
            for z, row in enumerate(plane_rows(x)):
                if z % 2 == 0:
                    held = row
                else:
                    self.half[x, z // 2] = pair_rows(held + row)

        planes_of(n, plane)
        for x in range(n // 2):
            for z in range(n // 2):
                pair = self.half[2 * x, z] + self.half[2 * x + 1, z]
                coarse(x, z, 0.125 * pair)

    def descend(self, coarse):
        self.sweep(self.base, self.second)

        def residuals(x):
            for z, here, result in self.rows(self.second, x):
                self.first[x, z] = (1.0 - DAMPING) * here + result
                yield (result - DAMPING * here) * self.back[x, z]

        self.halve(residuals, coarse)

    def ascend(self, correction, out, exact=False):
        def plane(x):
            upper = (x + 1) // 2
            for z in range(self.side):
                above = (z + 1) // 2
                row = correction(x // 2, z // 2)
                here = twice(row)
                after, before = block_up(row[:1], 1), block_down(row[-1:], 1)
                others = [
                    twice(correction(upper, z // 2)),
                    twice(correction(upper - 1, z // 2)),
                    jnp.concatenate([here[1:], after]),
                    jnp.concatenate([before, here[:-1]]),
                    twice(correction(x // 2, above)),
                    twice(correction(x // 2, above - 1)),
                ]
                result = self.first[x, z] + (1.0 - DAMPING) * here
                for link, other in zip(self.links, others):
                    result = result + link[x, z] * other
                self.second.put(x, z, result)

        planes_of(self.side, plane)
        self.second.close()
        self.sweep(self.second, out, exact)


def replicated_kernel(
    whole,
    halved,
    device_ref,
    cells_ref,
    *refs,
):
    parts = refs[:whole], refs[whole : whole + halved]
    solve_kernel(*parts, device_ref, cells_ref, *refs[whole + halved :])


def solve_kernel(
    part_refs,
    half_refs,
    device_ref,
    cells_ref,
    stations_ref,
    currents_ref,
    receivers_ref,
    observed_ref,
    potentials_ref,
    mine_ref,
    theirs_ref,
    gathered,
    weights,
    *level_refs,
):
    f32 = jnp.float32
    electrodes = stations_ref.shape[1]
    levels, used = [], 0
    for index in range(LEVELS - 1):
        count = len(Level.scratch(index))
        levels.append(Level(level_refs[used : used + count], index))
        used += count
    fine = levels[0]
    forward = fine.cond
    wide = SIDE * SIDE * SIDE

    device = device_ref[0]
    shot = device_ref[1]

    def place(part, row, x, index):
        for z in range(SIDE):
            fine.cond.ref[pl.ds(fine.cond.start(x, z) + index, SIDE, stride=SIDE), :] = part[
                pl.ds((row * SIDE + z) * SIDE, SIDE), :
            ]

    def collect(x):
        for k, part in enumerate(part_refs):
            place(part, x, x, device ^ k)

    def collect_half(x):
        for k, part in enumerate(half_refs):
            swapped, index = k // 2 % 2, len(part_refs) + k // 4 * 2 + k % 2
            place(part, x, (shot ^ swapped) * (SIDE // 2) + x, device ^ index)

    def edges(x):
        for z in (0, SIDE - 1):
            fine.cond.put(x, z, fine.cond[x, z], exact=True)

    planes_of(SIDE, collect)
    planes_of(SIDE // 2, collect_half)
    planes_of(SIDE, edges)
    fine.cond.close(exact=True)

    coarsest = []
    for level, below in zip(levels, levels[1:] + [None]):
        level.prepare()

        def coarse(x, z, row, below=below):
            if below is None:
                coarsest.append(row)
            else:
                below.cond.put(x, z, row, exact=True)

        level.halve(lambda x, level=level: [level.cond[x, z] for z in range(level.side)], coarse)
        if below is not None:
            below.cond.close(exact=True)

    last_scale = 0.25 ** (LEVELS - 1)
    here = coarsest[0]
    others = [inside(move(here, axis), axis) for axis in range(3) for inside, move in ((inside_up, block_up), (inside_down, block_down))]
    total = others[0]
    for other in others[1:]:
        total = total + other
    total = 3.0 * here + 0.5 * total
    inverse = DAMPING / total
    last_weight = inverse * (1.0 / last_scale)
    last_links = []
    for axis in range(3):
        for inside, other in ((inside_up, others[2 * axis]), (inside_down, others[2 * axis + 1])):
            last_links.append(inside(0.5 * inverse * (here + other), axis))

    def solve_last(rhs):
        base = last_weight * rhs
        value = base
        for _ in range(COARSE_SWEEPS - 1):
            parts = []
            for axis in range(3):
                parts.append(last_links[2 * axis] * block_up(value, axis))
                parts.append(last_links[2 * axis + 1] * block_down(value, axis))
            start = base + (1.0 - DAMPING) * value
            value = ((start + parts[0]) + (parts[1] + parts[4])) + (parts[5] + (parts[2] + parts[3]))
        return value

    def cycle(index, out, exact=False):
        level = levels[index]
        if index == LEVELS - 2:
            held = []
            level.descend(lambda x, z, row: held.append(row))
            solved = solve_last(held[0])

            def correction(x, z):
                if x != 0:
                    return (block_up if x > 0 else block_down)(solved, 0)
                if z != 0:
                    return (block_up if z > 0 else block_down)(solved, 2)
                return solved

            level.ascend(correction, out, exact)
            return
        below = levels[index + 1]
        level.descend(lambda x, z, row: below.base.put(x, z, below.weight[x, z] * row))
        below.base.close()
        cycle(index + 1, below.first)
        level.ascend(lambda x, z: below.first[x, z], out, exact)

    _, cell_y, cell_z, row, spot = station_table(stations_ref[...])
    at_spot = iota((LANES, electrodes), 0) == spot
    line = stations_ref[...] & 0x1C387 | row << 20
    same = jnp.broadcast_to(line, (electrodes, electrodes))
    same = jnp.where(same == same.T, 1.0, 0.0).astype(jnp.bfloat16)

    def each(body):
        def one(electrode, carry):
            body(pl.ds(electrode, 1), pl.ds(cells_ref[0, electrode], 1))
            return carry

        lax.fori_loop(0, electrodes, one, 0, unroll=8)

    def weigh(electrode, cell):
        weights[electrode, :] = fine.back.ref[cell, :]

    each(weigh)
    weights[...] = 1.0 / weights[...]
    fine.base.ref[...] = jnp.zeros_like(fine.base.ref)

    def spread(amounts):
        shared = product(jnp.where(at_spot, amounts, 0.0), same, 3)
        gathered[...] = shared.T * weights[...]

        def put(electrode, cell):
            fine.base.ref[cell, :] = gathered[electrode, :]

        each(put)
        planes_of(SIDE, fine.base.close_z)
        fine.base.close()

    spread(currents_ref[...])
    cycle(0, forward, exact=True)

    def read(electrode, cell):
        gathered[electrode, :] = forward.ref[cell, :]

    each(read)
    readings = jnp.sum(jnp.where(at_spot, gathered[...].T, 0.0), axis=0, keepdims=True)
    receivers = receivers_ref[...]
    numbers = iota((receivers.shape[0], electrodes), 1)
    pairs = jnp.where(numbers == receivers[:, 0:1], 1.0, 0.0) - jnp.where(
        numbers == receivers[:, 1:2], 1.0, 0.0
    )
    pairs = pairs.astype(jnp.bfloat16)

    def exact(row, dims):
        return product(jnp.broadcast_to(row, (16, row.shape[1])), pairs, 3, dims)[0:1]

    misfit = exact(readings, ((1,), (1,))) - observed_ref[...]
    spread(exact(misfit, ((1,), (0,))))
    cycle(0, fine.first, exact=True)

    order = lane_order()
    adjoint = fine.first
    chunk = mine_ref.shape[1]
    even = shot == 0

    def own(field, x, z, y=0):
        return field.ref[pl.ds(field.start(x, z, y) + device, SIDE, stride=SIDE), :]

    for x in range(SIDE):
        tiles_u, tiles_g = [], []
        for z in range(SIDE):
            here_u, here_w = own(forward, x, z), own(adjoint, x, z)
            total = None
            for at in ((x + 1, z), (x - 1, z), (x, z, 1), (x, z, -1), (x, z + 1), (x, z - 1)):
                term = (here_u - own(forward, *at)) * (here_w - own(adjoint, *at))
                total = term if total is None else total + term
            tiles_u.append(here_u)
            tiles_g.append(-0.5 * total)
        potentials_ref[x] = from_blocks(tiles_u, order)
        natural = from_blocks(tiles_g, order)
        low, high = natural[:chunk], natural[chunk:]
        mine_ref[x] = jnp.where(even, low, high)
        theirs_ref[x] = jnp.where(even, high, low)


def replicated(conductivity, stations, currents, receivers, observed):
    rows, cols, depth = conductivity.shape
    f32 = jnp.float32
    electrodes = stations.shape[0]
    total = rows * cols
    vmem = pl.BlockSpec(memory_space=pltpu.VMEM)
    smem = pl.BlockSpec(memory_space=pltpu.SMEM)
    station_row = stations.reshape(1, electrodes)
    device = lax.axis_index("gx") * lax.axis_size("gy") + lax.axis_index("gy")
    place = jnp.stack([device, lax.axis_index("shot")]).astype(jnp.int32)
    mine, half, cells = pl.pallas_call(
        to_blocks_kernel,
        out_shape=(
            jax.ShapeDtypeStruct((total, LANES), f32),
            jax.ShapeDtypeStruct((total // 2, LANES), f32),
            jax.ShapeDtypeStruct((1, electrodes), jnp.int32),
        ),
        in_specs=[smem, vmem, vmem],
        out_specs=(vmem, vmem, vmem),
    )(place, conductivity, station_row)
    swap = [(0, 1), (1, 0)]

    def partner(part, k):
        count = lax.axis_size("gx")
        return lax.ppermute(part, "gx", [(i, i ^ k) for i in range(count)])

    def with_mate(part):
        return [part, lax.ppermute(part, "gy", swap)]

    far = [partner(half, k) for k in (2, 3)]
    near = partner(mine, 1)
    halved = [piece for own in far for piece in (own, lax.ppermute(own, "shot", swap))]
    parts = [piece for own in (mine, near) for piece in with_mate(own)]
    halved = [piece for own in halved for piece in with_mate(own)]
    chunk = cols // 2
    levels = [shape for index in range(LEVELS - 1) for shape in Level.scratch(index)]
    potentials, own, theirs = pl.pallas_call(
        functools.partial(replicated_kernel, len(parts), len(halved)),
        out_shape=(
            jax.ShapeDtypeStruct((rows, cols, LANES), f32),
            jax.ShapeDtypeStruct((rows, chunk, LANES), f32),
            jax.ShapeDtypeStruct((rows, chunk, LANES), f32),
        ),
        in_specs=[smem, smem] + [vmem] * (len(parts) + len(halved) + 4),
        out_specs=(vmem, vmem, vmem),
        scratch_shapes=[
            pltpu.VMEM((electrodes, LANES), f32),
            pltpu.VMEM((electrodes, LANES), f32),
        ]
        + levels,
        compiler_params=pltpu.CompilerParams(vmem_limit_bytes=VMEM_BYTES),
        cost_estimate=pl.CostEstimate(flops=200_000_000, bytes_accessed=4_000_000, transcendentals=0),
    )(place, cells, *parts, *halved, station_row, currents, receivers, observed)
    return potentials[None], own + lax.ppermute(theirs, "shot", swap)


def extended(array, sides, width):
    for axis, dim in sides:
        size, length = (lax.axis_size(axis), array.shape[dim])
        up = [(i, (i + 1) % size) for i in range(size - 1)]
        down = [(j, i) for i, j in up]
        last = lax.slice_in_dim(array, length - width, length, axis=dim)
        leading = lax.slice_in_dim(array, 0, width, axis=dim)
        before = lax.ppermute(last, axis, up)
        after = lax.ppermute(leading, axis, down)
        array = jnp.concatenate([before, array, after], axis=dim)
    return array


def upper_z(field):
    return jnp.concatenate([field[..., 1:], jnp.zeros_like(field[..., :1])], axis=-1)


def lower_z(field):
    return jnp.concatenate([jnp.zeros_like(field[..., :1]), field[..., :-1]], axis=-1)


def trim_circle(field, circle_width):
    return field[..., circle_width:-circle_width, circle_width:-circle_width, :]


def pad_plane(field, circle_width):
    spec = [(0, 0)] * (field.ndim - 3) + [
        (circle_width, circle_width),
        (circle_width, circle_width),
        (0, 0),
    ]
    return jnp.pad(field, spec)


def neighbour_list(field_pad):
    centre = trim_circle(field_pad, 1)
    return [
        field_pad[..., 2:, 1:-1, :],
        field_pad[..., :-2, 1:-1, :],
        field_pad[..., 1:-1, 2:, :],
        field_pad[..., 1:-1, :-2, :],
        upper_z(centre),
        lower_z(centre),
    ]


def stencil(field_pad, cond_pad, level_scale):
    centre = trim_circle(field_pad, 1)
    centre_cond = trim_circle(cond_pad, 1)
    summed = jnp.zeros_like(centre)
    for other, other_cond in zip(neighbour_list(field_pad), neighbour_list(cond_pad)):
        summed = summed + level_scale * 0.5 * (centre_cond + other_cond) * (centre - other)
    return summed


def diagonal(cond_pad, level_scale):
    centre_cond = trim_circle(cond_pad, 1)
    summed = jnp.zeros_like(centre_cond)
    for other_cond in neighbour_list(cond_pad):
        summed = summed + level_scale * 0.5 * (centre_cond + other_cond)
    return summed


def relaxed(field_pad, source, cond_pad, diag_level, level_scale):
    return (
        trim_circle(field_pad, 1)
        + DAMPING * (source - stencil(field_pad, cond_pad, level_scale)) / diag_level
    )


def restrict(field):
    leading = field.shape[:-3]
    extent = field.shape[-3:]
    shaped = field.reshape(leading + (extent[0] // 2, 2, extent[1] // 2, 2, extent[2] // 2, 2))
    return shaped.mean(axis=(-5, -3, -1))


def prolong(field):
    return jnp.repeat(jnp.repeat(jnp.repeat(field, 2, axis=-3), 2, axis=-2), 2, axis=-1)


def assemble(blocks, count_x, count_y):
    leading = blocks.shape[1:-3]
    extent = blocks.shape[-3:]
    depth_lead = len(leading)
    shaped = blocks.reshape((count_x, count_y) + leading + extent)
    order = tuple(range(2, 2 + depth_lead)) + (0, 2 + depth_lead, 1, 3 + depth_lead, 4 + depth_lead)
    return shaped.transpose(order).reshape(
        leading + (count_x * extent[0], count_y * extent[1], extent[2])
    )


def field_rim(field):
    return extended(field, (("gx", 1), ("gy", 2)), 1)


def cond_rim(conduct):
    return extended(conduct, (("gx", 0), ("gy", 1)), 1)


def whole_cycle(source, level_index, whole_plans):
    cond_pad, diag_level, level_scale = whole_plans[level_index]
    field = DAMPING * source / diag_level

    def turn(turn_index, iterate):
        return relaxed(pad_plane(iterate, 1), source, cond_pad, diag_level, level_scale)

    return lax.fori_loop(0, COARSE_SWEEPS - 1, turn, field)


def part_cycle(source, level_index, level_plans, whole_plans, gather_level):
    if level_index == gather_level:
        blocks = lax.all_gather(source[None], ("gx", "gy"), axis=0, tiled=True)
        whole = assemble(blocks, lax.axis_size("gx"), lax.axis_size("gy"))
        correction = whole_cycle(whole, level_index, whole_plans)
        extent = source.shape
        starts = (0, lax.axis_index("gx") * extent[1], lax.axis_index("gy") * extent[2], 0)
        return lax.dynamic_slice(correction, starts, extent)
    cond_pad, diag_level, level_scale = level_plans[level_index]
    field = DAMPING * source / diag_level
    field = relaxed(field_rim(field), source, cond_pad, diag_level, level_scale)
    residual = source - stencil(field_rim(field), cond_pad, level_scale)
    field = field + prolong(
        part_cycle(restrict(residual), level_index + 1, level_plans, whole_plans, gather_level)
    )
    field = relaxed(field_rim(field), source, cond_pad, diag_level, level_scale)
    return relaxed(field_rim(field), source, cond_pad, diag_level, level_scale)


def distributed(conductivity, stations, currents, receivers, observed):
    row_count, col_count, z_count = conductivity.shape
    shot_count = currents.shape[0]
    count_x = lax.axis_size("gx")
    count_y = lax.axis_size("gy")
    gather_level = LEVELS - 1
    level_plans = []
    conduct = conductivity
    for level_index in range(gather_level):
        level_scale = 0.25**level_index
        cond_pad = cond_rim(conduct)
        level_plans.append((cond_pad, diagonal(cond_pad, level_scale), level_scale))
        conduct = restrict(conduct)
    blocks = lax.all_gather(conduct[None], ("gx", "gy"), axis=0, tiled=True)
    whole = assemble(blocks, count_x, count_y)
    whole_plans = {}
    level_index = 3
    level_scale = 0.25**level_index
    cond_pad = pad_plane(whole, 1)
    whole_plans[level_index] = (cond_pad, diagonal(cond_pad, level_scale), level_scale)
    total_y = col_count * count_y
    cell_x = stations // (total_y * z_count)
    cell_y = stations // z_count % total_y
    cell_z = stations % z_count
    local_x = cell_x - lax.axis_index("gx") * row_count
    local_y = cell_y - lax.axis_index("gy") * col_count
    owned = (local_x >= 0) & (local_x < row_count) & (local_y >= 0) & (local_y < col_count)
    block_size = row_count * col_count * z_count
    local_cell = jnp.where(owned, (local_x * col_count + local_y) * z_count + cell_z, 0)
    offsets = jnp.arange(shot_count)[:, None] * block_size + local_cell[None, :]
    targets = jnp.where(owned[None, :], offsets, shot_count * block_size).reshape(-1)

    def spread(amounts):
        flat = (
            jnp.zeros((shot_count * block_size,), jnp.float32)
            .at[targets]
            .add(amounts.reshape(-1), mode="drop")
        )
        return flat.reshape(shot_count, row_count, col_count, z_count)

    potentials = part_cycle(spread(currents), 0, level_plans, whole_plans, gather_level)
    local_values = jnp.where(
        owned[None, :], potentials.reshape(shot_count, block_size)[:, local_cell], 0.0
    )
    readings = lax.psum(local_values, ("gx", "gy"))
    positions = jnp.arange(stations.shape[0])[:, None]
    pairs = (receivers[:, 0][None, :] == positions).astype(jnp.float32) - (
        receivers[:, 1][None, :] == positions
    ).astype(jnp.float32)
    misfit = jnp.dot(readings, pairs, precision=lax.Precision.HIGHEST) - observed
    back_source = jnp.dot(misfit, pairs.T, precision=lax.Precision.HIGHEST)
    adjoint = part_cycle(spread(back_source), 0, level_plans, whole_plans, gather_level)
    stacked = jnp.concatenate([potentials, adjoint], axis=0)
    padded = extended(stacked, (("gx", 1), ("gy", 2)), 1)
    potential_pad = padded[:shot_count]
    adjoint_pad = padded[shot_count:]
    gradient = jnp.zeros_like(potentials)
    for other_u, other_w in zip(neighbour_list(potential_pad), neighbour_list(adjoint_pad)):
        gradient = gradient - 0.5 * (potentials - other_u) * (adjoint - other_w)
    summed = lax.psum_scatter(jnp.sum(gradient, axis=0), "shot", scatter_dimension=1, tiled=True)
    return (potentials, summed)


def per_device(conductivity, stations, currents, receivers, observed):
    blocks = lax.axis_size("gx") * lax.axis_size("gy")
    fits = conductivity.shape == (SIDE, SIDE * SIDE, LANES) and blocks == SIDE
    fits = fits and lax.axis_size("gy") == 2 and lax.axis_size("shot") == 2
    fits = fits and currents.shape[0] == 1
    plan = replicated if fits else distributed
    return plan(conductivity, stations, currents, receivers, observed)


def solution(mesh):
    in_specs = (
        P(("grp", "gx"), "gy", None),
        P("grp"),
        P(("grp", "shot"), None),
        P("grp", None),
        P(("grp", "shot"), None),
    )
    out_specs = (P(("grp", "shot"), "gx", "gy", None), P(("grp", "gx"), ("gy", "shot"), None))
    return jax.shard_map(
        per_device, mesh=mesh, in_specs=in_specs, out_specs=out_specs, check_vma=False
    )
```

```python
import functools

import jax
import jax.numpy as jnp
from jax import lax
from jax.experimental import pallas as pl
from jax.experimental.pallas import tpu as pltpu
from jax.sharding import PartitionSpec as P

LEVELS = 4
COARSE_SWEEPS = 16


DAMPING = 0.8

SIDE = 8
LANES = 128
GROUP = 16
VMEM_BYTES = 48 * 2**20


def pieces_of(value, count):
    pieces = []
    for _ in range(count):
        pieces.append(value.astype(jnp.bfloat16))
        value = value - pieces[-1].astype(jnp.float32)
    return pieces[::-1]


def product(value, matrix, count, dims=((1,), (0,))):
    result = None
    for piece in pieces_of(value, count):
        term = lax.dot_general(
            piece, matrix, (dims, ((), ())), preferred_element_type=jnp.float32
        )
        result = term if result is None else result + term
    return result


def iota(shape, dim):
    return lax.broadcasted_iota(jnp.int32, shape, dim)


def station_table(station):
    cell_x, cell_y, cell_z = station >> 14, station >> 7 & 127, station & 127
    row = (cell_x >> 3) * 2 + (cell_y >> 6)
    return cell_x, cell_y, cell_z, row, (cell_y >> 3 & 7) * GROUP + (cell_z >> 3)


def lane_order():
    row, col = iota((LANES, LANES), 0), iota((LANES, LANES), 1)
    chosen = row == col % GROUP * SIDE + col // GROUP
    return jnp.where(chosen, 1.0, 0.0).astype(jnp.bfloat16)


def exchange_groups(tiles):
    tiles = list(tiles)
    group = iota(tiles[0].shape, 1) // GROUP
    for bit in range(3):
        step = 1 << bit
        keep = (group & step) == 0
        for low in range(SIDE):
            if low & step == 0:
                a, b = tiles[low], tiles[low | step]
                tiles[low] = jnp.where(keep, a, pltpu.roll(b, step * GROUP, 1))
                tiles[low | step] = jnp.where(keep, pltpu.roll(a, LANES - step * GROUP, 1), b)
    return tiles


def own_place():
    return lax.axis_index("gx") * 2 + lax.axis_index("gy"), lax.axis_index("shot")


def to_blocks_kernel(natural_ref, stations_ref, blocks_ref, half_ref, cells_ref):
    order = lane_order()
    for x in range(SIDE):
        tiles = product(natural_ref[x], order, 3)
        tiles = [tiles[SIDE * k : SIDE * (k + 1)] for k in range(SIDE)]
        for z, tile in enumerate(exchange_groups(tiles)):
            blocks_ref[pl.ds((x * SIDE + z) * SIDE, SIDE), :] = tile
    count = half_ref.shape[0]
    low, high = blocks_ref[pl.ds(0, count), :], blocks_ref[pl.ds(count, count), :]
    half_ref[...] = jnp.where(own_place()[1] == 0, low, high)
    cell_x, cell_y, cell_z, row, _ = station_table(stations_ref[...])
    wide = SIDE + 2
    register = (((cell_x & 7) + 1) * wide + (cell_z & 7) + 1) * wide + (cell_y & 7) + 1
    cells_ref[...] = register * SIDE + row


def from_blocks(tiles, order):
    natural = jnp.concatenate(exchange_groups(tiles), axis=0)
    return product(natural, order, 3, ((1,), (1,)))


def block_up(field, axis):
    if axis == 0:
        return pltpu.roll(field, 6, 1)
    if axis == 2:
        return pltpu.roll(field, LANES - 1, 2)
    turned = pltpu.roll(field, LANES - GROUP, 2)
    return jnp.where(iota(field.shape, 2) < LANES - GROUP, turned, pltpu.roll(turned, 7, 1))


def block_down(field, axis):
    if axis == 0:
        return pltpu.roll(field, 2, 1)
    if axis == 2:
        return pltpu.roll(field, 1, 2)
    turned = pltpu.roll(field, GROUP, 2)
    return jnp.where(iota(field.shape, 2) >= GROUP, turned, pltpu.roll(turned, 1, 1))


def inside_up(field, axis):
    sub, lane = iota(field.shape, 1), iota(field.shape, 2)
    if axis == 0:
        keep = sub < 6
    elif axis == 1:
        keep = (lane < LANES - GROUP) | (sub % 2 == 0)
    else:
        keep = lane % GROUP < GROUP - 1
    return jnp.where(keep, field, 0.0)


def inside_down(field, axis):
    sub, lane = iota(field.shape, 1), iota(field.shape, 2)
    if axis == 0:
        keep = sub >= 2
    elif axis == 1:
        keep = (lane >= GROUP) | (sub % 2 == 1)
    else:
        keep = lane % GROUP > 0
    return jnp.where(keep, field, 0.0)


def pair_rows(row):
    count = row.shape[0] // 2
    return jnp.concatenate([row[2 * i : 2 * i + 1] + row[2 * i + 1 : 2 * i + 2] for i in range(count)])


def twice(row):
    return jnp.concatenate([row[i // 2 : i // 2 + 1] for i in range(2 * row.shape[0])])


def electrode_kernel(stations_ref, currents_ref, receivers_ref, rows_ref, same_ref, pairs_ref):
    stations = stations_ref[...]
    electrodes = stations.shape[1]
    row, spot = station_table(stations)[3:]
    line = stations & 0x1C387 | row << 20
    same = jnp.broadcast_to(line, (electrodes, electrodes))
    same = jnp.where(same == same.T, 1.0, 0.0).astype(jnp.bfloat16)
    same_ref[...] = same
    rows_ref[...] = shared_rows(currents_ref[...], spot, same)
    receivers = receivers_ref[...]
    numbers = iota((receivers.shape[0], electrodes), 1)
    pairs = jnp.where(numbers == receivers[:, 0:1], 1.0, 0.0) - jnp.where(
        numbers == receivers[:, 1:2], 1.0, 0.0
    )
    pairs_ref[...] = pairs.astype(jnp.bfloat16)


def shared_rows(amounts, spot, same):
    electrodes = amounts.shape[1]
    at_spot = iota((LANES, electrodes), 0) == spot
    return product(jnp.where(at_spot, amounts, 0.0), same, 3).T


class Edged:
    def __init__(self, ref, side):
        self.ref, self.side = ref, side

    def start(self, x, z, y=0):
        wide = self.side + 2
        return (((x + 1) * wide + z + 1) * wide + y + 1) * SIDE

    def __getitem__(self, at):
        x, z = at
        rows = self.ref[pl.ds(self.start(x, z), self.side * SIDE), :]
        return rows.reshape(self.side, SIDE, LANES)

    def __setitem__(self, at, value):
        x, z = at
        self.ref[pl.ds(self.start(x, z), self.side * SIDE), :] = value.reshape(-1, LANES)

    def put(self, x, z, value, exact=False):
        self[x, z] = value
        n = self.side
        if z == 0:
            edge = block_up(value, 2)
            self[x, n] = inside_up(edge, 2) if exact else edge
        if z == n - 1:
            edge = block_down(value, 2)
            self[x, -1] = inside_down(edge, 2) if exact else edge
        if exact:
            after = inside_up(block_up(value[:1], 1), 1)
            self.ref[pl.ds(self.start(x, z, n), SIDE), :] = after[0]
            before = inside_down(block_down(value[n - 1 :], 1), 1)
            self.ref[pl.ds(self.start(x, z, -1), SIDE), :] = before[0]

    def close_z(self, x):
        n = self.side
        self[x, n] = block_up(self[x, 0], 2)
        self[x, -1] = block_down(self[x, n - 1], 2)

    def close(self, exact=False):
        n = self.side
        for z in range(n):
            after = block_up(self[0, z], 0)
            self[n, z] = inside_up(after, 0) if exact else after
            before = block_down(self[n - 1, z], 0)
            self[-1, z] = inside_down(before, 0) if exact else before


class Plain:
    def __init__(self, ref, side):
        self.ref, self.side = ref, side

    def __getitem__(self, at):
        x, z = at
        rows = self.side * SIDE
        return self.ref[pl.ds((x * self.side + z) * rows, rows), :].reshape(self.side, SIDE, LANES)

    def __setitem__(self, at, value):
        x, z = at
        rows = self.side * SIDE
        self.ref[pl.ds((x * self.side + z) * rows, rows), :] = value.reshape(-1, LANES)


def planes_of(count, body):
    if count < SIDE:
        for x in range(count):
            body(x)
        return

    def one(x, carry):
        body(x)
        return carry

    lax.fori_loop(0, count, one, 0)


class Level:
    def __init__(self, refs, index):
        self.side = side = SIDE >> index
        self.scale = 0.25**index
        edged = [Edged(ref, side) for ref in refs[:5]]
        self.cond, self.first, self.second, self.base, self.back = edged
        self.links = [Plain(ref, side) for ref in refs[5:11]]
        self.half = Plain(refs[11], side // 2)
        self.weight = Plain(refs[12], side) if index else None

    @staticmethod
    def scratch(index):
        side = SIDE >> index
        edged = (side + 2) ** 3
        sizes = [edged] * 5 + [side**3] * 6 + [side**3 // 4] + [side**3] * (index > 0)
        return [pltpu.VMEM((size * SIDE, LANES), jnp.float32) for size in sizes]

    def shifted(self, field, x, z, here, exact=False, along=None):
        ahead, behind = along or (field[x, z + 1], field[x, z - 1])
        after = block_up(here[:1], 1)
        before = block_down(here[-1:], 1)
        if exact:
            after, before = inside_up(after, 1), inside_down(before, 1)
        return [
            field[x + 1, z],
            field[x - 1, z],
            jnp.concatenate([here[1:], after]),
            jnp.concatenate([before, here[:-1]]),
            ahead,
            behind,
        ]

    def prepare(self):
        n = self.side

        def plane(x):
            for z in range(n):
                here = self.cond[x, z]
                others = self.shifted(self.cond, x, z, here, exact=True)
                total = others[0]
                for other in others[1:]:
                    total = total + other
                total = 3.0 * here + 0.5 * total
                inverse = DAMPING / total
                if self.weight is not None:
                    self.weight[x, z] = inverse * (1.0 / self.scale)
                self.back[x, z] = total * (self.scale / DAMPING)
                inverse = 0.5 * inverse
                for index, other in enumerate(others):
                    link = inverse * (here + other)
                    if index == 2:
                        link = jnp.concatenate([link[:-1], inside_up(link[-1:], 1)])
                    if index == 3:
                        link = jnp.concatenate([inside_down(link[:1], 1), link[1:]])
                    if index == 4 and z == n - 1:
                        link = inside_up(link, 2)
                    if index == 5 and z == 0:
                        link = inside_down(link, 2)
                    self.links[index][x, z] = link

        planes_of(n, plane)
        for z in range(n):
            self.links[0][n - 1, z] = inside_up(self.links[0][n - 1, z], 0)
            self.links[1][0, z] = inside_down(self.links[1][0, z], 0)

    def rows(self, field, x):
        behind, here = field[x, -1], field[x, 0]
        for z in range(self.side):
            ahead = field[x, z + 1]
            result = self.base[x, z]
            others = self.shifted(field, x, z, here, along=(ahead, behind))
            for link, other in zip(self.links, others):
                result = result + link[x, z] * other
            yield z, here, result
            behind, here = here, ahead

    def sweep(self, field, out, exact=False):
        def plane(x):
            for z, here, result in self.rows(field, x):
                out.put(x, z, (1.0 - DAMPING) * here + result, exact)

        planes_of(self.side, plane)
        out.close(exact)

    def halve(self, plane_rows, coarse):
        n = self.side

        def plane(x):
            held = None
            for z, row in enumerate(plane_rows(x)):
                if z % 2 == 0:
                    held = row
                else:
                    self.half[x, z // 2] = pair_rows(held + row)

        planes_of(n, plane)
        for x in range(n // 2):
            for z in range(n // 2):
                pair = self.half[2 * x, z] + self.half[2 * x + 1, z]
                coarse(x, z, 0.125 * pair)

    def descend(self, coarse):
        self.sweep(self.base, self.second)

        def residuals(x):
            for z, here, result in self.rows(self.second, x):
                self.first[x, z] = (1.0 - DAMPING) * here + result
                yield (result - DAMPING * here) * self.back[x, z]

        self.halve(residuals, coarse)

    def ascend(self, correction, out, exact=False):
        def plane(x):
            upper = (x + 1) // 2
            for z in range(self.side):
                above = (z + 1) // 2
                row = correction(x // 2, z // 2)
                here = twice(row)
                after, before = block_up(row[:1], 1), block_down(row[-1:], 1)
                others = [
                    twice(correction(upper, z // 2)),
                    twice(correction(upper - 1, z // 2)),
                    jnp.concatenate([here[1:], after]),
                    jnp.concatenate([before, here[:-1]]),
                    twice(correction(x // 2, above)),
                    twice(correction(x // 2, above - 1)),
                ]
                result = self.first[x, z] + (1.0 - DAMPING) * here
                for link, other in zip(self.links, others):
                    result = result + link[x, z] * other
                self.second.put(x, z, result)

        planes_of(self.side, plane)
        self.second.close()
        self.sweep(self.second, out, exact)


def replicated_kernel(
    whole,
    halved,
    cells_ref,
    *refs,
):
    parts = refs[:whole], refs[whole : whole + halved]
    solve_kernel(*parts, cells_ref, *refs[whole + halved :])


def solve_kernel(
    part_refs,
    half_refs,
    cells_ref,
    stations_ref,
    rows_ref,
    same_ref,
    pairs_ref,
    observed_ref,
    potentials_ref,
    mine_ref,
    theirs_ref,
    gathered,
    weights,
    *level_refs,
):
    f32 = jnp.float32
    electrodes = stations_ref.shape[1]
    levels, used = [], 0
    for index in range(LEVELS - 1):
        count = len(Level.scratch(index))
        levels.append(Level(level_refs[used : used + count], index))
        used += count
    fine = levels[0]
    forward = fine.cond
    wide = SIDE * SIDE * SIDE

    device, shot = own_place()

    def place(part, row, x, index):
        for z in range(SIDE):
            fine.cond.ref[pl.ds(fine.cond.start(x, z) + index, SIDE, stride=SIDE), :] = part[
                pl.ds((row * SIDE + z) * SIDE, SIDE), :
            ]

    def collect(x):
        for k, part in enumerate(part_refs):
            place(part, x, x, device ^ k)

    def collect_half(x):
        for k, part in enumerate(half_refs):
            swapped, index = k // 2 % 2, len(part_refs) + k // 4 * 2 + k % 2
            place(part, x, (shot ^ swapped) * (SIDE // 2) + x, device ^ index)

    def edges(x):
        for z in (0, SIDE - 1):
            fine.cond.put(x, z, fine.cond[x, z], exact=True)

    planes_of(SIDE, collect)
    planes_of(SIDE // 2, collect_half)
    planes_of(SIDE, edges)
    fine.cond.close(exact=True)

    coarsest = []
    for level, below in zip(levels, levels[1:] + [None]):
        level.prepare()

        def coarse(x, z, row, below=below):
            if below is None:
                coarsest.append(row)
            else:
                below.cond.put(x, z, row, exact=True)

        level.halve(lambda x, level=level: [level.cond[x, z] for z in range(level.side)], coarse)
        if below is not None:
            below.cond.close(exact=True)

    keep = iota((1, SIDE, LANES), 1) % 2 == 0
    lane = iota((1, SIDE, LANES), 2)

    def split(value):
        return [jnp.where(keep, part, 0.0) for part in (value, pltpu.roll(value, SIDE - 1, 1))]

    def around(value):
        low, high = value
        low_up, high_up = [pltpu.roll(part, LANES - GROUP, 2) for part in value]
        low_down, high_down = [pltpu.roll(part, GROUP, 2) for part in value]
        along = [[move(part, axis) for part in value] for axis in (0, 2) for move in (block_up, block_down)]
        return along + [
            [jnp.where(lane < LANES - GROUP, low_up, high_up), high_up],
            [low_down, jnp.where(lane >= GROUP, high_down, low_down)],
        ]

    sub = iota((1, SIDE, LANES), 1)
    inside_last = [
        [sub < 6] * 2,
        [sub >= 2] * 2,
        [lane % GROUP < GROUP - 1] * 2,
        [lane % GROUP > 0] * 2,
        [keep, lane < LANES - GROUP],
        [lane >= GROUP, keep],
    ]
    last_scale = 0.25 ** (LEVELS - 1)
    here = split(coarsest[0])
    others = [
        [jnp.where(inside & keep, part, 0.0) for inside, part in zip(pair, moved)]
        for pair, moved in zip(inside_last, around(here))
    ]
    last_weight, last_links = [], []
    for half, part in enumerate(here):
        total = 3.0 * part
        for other in others:
            total = total + 0.5 * other[half]
        inverse = jnp.where(keep, DAMPING / jnp.where(keep, total, 1.0), 0.0)
        last_weight.append(inverse * (1.0 / last_scale))
        last_links.append(
            [
                jnp.where(pair[half] & keep, 0.5 * inverse * (part + other[half]), 0.0)
                for pair, other in zip(inside_last, others)
            ]
        )

    def solve_last(rhs):
        base = [weight * part for weight, part in zip(last_weight, split(rhs))]
        value = base
        for _ in range(COARSE_SWEEPS - 1):
            moved = around(value)
            fresh = []
            for half in range(2):
                parts = [link * other[half] for link, other in zip(last_links[half], moved)]
                start = base[half] + (1.0 - DAMPING) * value[half]
                fresh.append(((start + parts[0]) + (parts[1] + parts[2])) + (parts[3] + (parts[4] + parts[5])))
            value = fresh
        return value[0] + pltpu.roll(value[1], 1, 1)

    def cycle(index, out, exact=False):
        level = levels[index]
        if index == LEVELS - 2:
            held = []
            level.descend(lambda x, z, row: held.append(row))
            solved = solve_last(held[0])

            def correction(x, z):
                if x != 0:
                    return (block_up if x > 0 else block_down)(solved, 0)
                if z != 0:
                    return (block_up if z > 0 else block_down)(solved, 2)
                return solved

            level.ascend(correction, out, exact)
            return
        below = levels[index + 1]
        level.descend(lambda x, z, row: below.base.put(x, z, below.weight[x, z] * row))
        below.base.close()
        cycle(index + 1, below.first)
        level.ascend(lambda x, z: below.first[x, z], out, exact)

    spot = station_table(stations_ref[...])[4]

    def each(body):
        def one(electrode, carry):
            body(pl.ds(electrode, 1), pl.ds(cells_ref[0, electrode], 1))
            return carry

        lax.fori_loop(0, electrodes, one, 0, unroll=8)

    def weigh(electrode, cell):
        weights[electrode, :] = fine.back.ref[cell, :]

    each(weigh)
    weights[...] = 1.0 / weights[...]
    fine.base.ref[...] = jnp.zeros_like(fine.base.ref)

    def spread(rows):
        gathered[...] = rows * weights[...]

        def put(electrode, cell):
            fine.base.ref[cell, :] = gathered[electrode, :]

        each(put)
        planes_of(SIDE, fine.base.close_z)
        fine.base.close()

    spread(rows_ref[...])
    cycle(0, forward, exact=True)

    def read(electrode, cell):
        gathered[electrode, :] = forward.ref[cell, :]

    each(read)
    at_spot = iota((LANES, electrodes), 0) == spot
    readings = jnp.sum(jnp.where(at_spot, gathered[...].T, 0.0), axis=0, keepdims=True)
    pairs = pairs_ref[...]

    def exact(row, dims):
        return product(jnp.broadcast_to(row, (16, row.shape[1])), pairs, 3, dims)[0:1]

    misfit = exact(readings, ((1,), (1,))) - observed_ref[...]
    spread(shared_rows(exact(misfit, ((1,), (0,))), spot, same_ref[...]))
    cycle(0, fine.first, exact=True)

    order = lane_order()
    adjoint = fine.first
    chunk = mine_ref.shape[1]
    even = shot == 0

    def own(field, x, z, y=0):
        return field.ref[pl.ds(field.start(x, z, y) + device, SIDE, stride=SIDE), :]

    for x in range(SIDE):
        tiles_u, tiles_g = [], []
        for z in range(SIDE):
            here_u, here_w = own(forward, x, z), own(adjoint, x, z)
            total = None
            for at in ((x + 1, z), (x - 1, z), (x, z, 1), (x, z, -1), (x, z + 1), (x, z - 1)):
                term = (here_u - own(forward, *at)) * (here_w - own(adjoint, *at))
                total = term if total is None else total + term
            tiles_u.append(here_u)
            tiles_g.append(-0.5 * total)
        potentials_ref[x] = from_blocks(tiles_u, order)
        natural = from_blocks(tiles_g, order)
        low, high = natural[:chunk], natural[chunk:]
        mine_ref[x] = jnp.where(even, low, high)
        theirs_ref[x] = jnp.where(even, high, low)


def replicated(conductivity, stations, currents, receivers, observed):
    rows, cols, depth = conductivity.shape
    f32 = jnp.float32
    electrodes = stations.shape[0]
    total = rows * cols
    vmem = pl.BlockSpec(memory_space=pltpu.VMEM)
    smem = pl.BlockSpec(memory_space=pltpu.SMEM)
    station_row = stations.reshape(1, electrodes)
    mine, half, cells = pl.pallas_call(
        to_blocks_kernel,
        out_shape=(
            jax.ShapeDtypeStruct((total, LANES), f32),
            jax.ShapeDtypeStruct((total // 2, LANES), f32),
            jax.ShapeDtypeStruct((1, electrodes), jnp.int32),
        ),
        in_specs=[vmem, vmem],
        out_specs=(vmem, vmem, vmem),
    )(conductivity, station_row)
    swap = [(0, 1), (1, 0)]

    def partner(part, k):
        count = lax.axis_size("gx")
        return lax.ppermute(part, "gx", [(i, i ^ k) for i in range(count)])

    def with_mate(part):
        return [part, lax.ppermute(part, "gy", swap)]

    far = partner(half, 2)
    near = partner(mine, 1)
    rows_of, same, pairs = pl.pallas_call(
        electrode_kernel,
        out_shape=(
            jax.ShapeDtypeStruct((electrodes, LANES), f32),
            jax.ShapeDtypeStruct((electrodes, electrodes), jnp.bfloat16),
            jax.ShapeDtypeStruct((receivers.shape[0], electrodes), jnp.bfloat16),
        ),
        in_specs=[vmem, vmem, vmem],
        out_specs=(vmem, vmem, vmem),
        cost_estimate=pl.CostEstimate(flops=100_000_000, bytes_accessed=1_000_000, transcendentals=0),
    )(station_row, currents, receivers)
    far, rows_of = lax.optimization_barrier((far, rows_of))
    far = [far, partner(far, 1)]
    halved = [piece for own in far for piece in (own, lax.ppermute(own, "shot", swap))]
    parts = [piece for own in (mine, near) for piece in with_mate(own)]
    halved = [piece for own in halved for piece in with_mate(own)]
    chunk = cols // 2
    levels = [shape for index in range(LEVELS - 1) for shape in Level.scratch(index)]
    potentials, own, theirs = pl.pallas_call(
        functools.partial(replicated_kernel, len(parts), len(halved)),
        out_shape=(
            jax.ShapeDtypeStruct((rows, cols, LANES), f32),
            jax.ShapeDtypeStruct((rows, chunk, LANES), f32),
            jax.ShapeDtypeStruct((rows, chunk, LANES), f32),
        ),
        in_specs=[smem] + [vmem] * (len(parts) + len(halved) + 5),
        out_specs=(vmem, vmem, vmem),
        scratch_shapes=[
            pltpu.VMEM((electrodes, LANES), f32),
            pltpu.VMEM((electrodes, LANES), f32),
        ]
        + levels,
        compiler_params=pltpu.CompilerParams(vmem_limit_bytes=VMEM_BYTES),
        cost_estimate=pl.CostEstimate(flops=200_000_000, bytes_accessed=4_000_000, transcendentals=0),
    )(cells, *parts, *halved, station_row, rows_of, same, pairs, observed)
    return potentials[None], own + lax.ppermute(theirs, "shot", swap)


def extended(array, sides, width):
    for axis, dim in sides:
        size, length = (lax.axis_size(axis), array.shape[dim])
        up = [(i, (i + 1) % size) for i in range(size - 1)]
        down = [(j, i) for i, j in up]
        last = lax.slice_in_dim(array, length - width, length, axis=dim)
        leading = lax.slice_in_dim(array, 0, width, axis=dim)
        before = lax.ppermute(last, axis, up)
        after = lax.ppermute(leading, axis, down)
        array = jnp.concatenate([before, array, after], axis=dim)
    return array


def upper_z(field):
    return jnp.concatenate([field[..., 1:], jnp.zeros_like(field[..., :1])], axis=-1)


def lower_z(field):
    return jnp.concatenate([jnp.zeros_like(field[..., :1]), field[..., :-1]], axis=-1)


def trim_circle(field, circle_width):
    return field[..., circle_width:-circle_width, circle_width:-circle_width, :]


def pad_plane(field, circle_width):
    spec = [(0, 0)] * (field.ndim - 3) + [
        (circle_width, circle_width),
        (circle_width, circle_width),
        (0, 0),
    ]
    return jnp.pad(field, spec)


def neighbour_list(field_pad):
    centre = trim_circle(field_pad, 1)
    return [
        field_pad[..., 2:, 1:-1, :],
        field_pad[..., :-2, 1:-1, :],
        field_pad[..., 1:-1, 2:, :],
        field_pad[..., 1:-1, :-2, :],
        upper_z(centre),
        lower_z(centre),
    ]


def stencil(field_pad, cond_pad, level_scale):
    centre = trim_circle(field_pad, 1)
    centre_cond = trim_circle(cond_pad, 1)
    summed = jnp.zeros_like(centre)
    for other, other_cond in zip(neighbour_list(field_pad), neighbour_list(cond_pad)):
        summed = summed + level_scale * 0.5 * (centre_cond + other_cond) * (centre - other)
    return summed


def diagonal(cond_pad, level_scale):
    centre_cond = trim_circle(cond_pad, 1)
    summed = jnp.zeros_like(centre_cond)
    for other_cond in neighbour_list(cond_pad):
        summed = summed + level_scale * 0.5 * (centre_cond + other_cond)
    return summed


def relaxed(field_pad, source, cond_pad, diag_level, level_scale):
    return (
        trim_circle(field_pad, 1)
        + DAMPING * (source - stencil(field_pad, cond_pad, level_scale)) / diag_level
    )


def restrict(field):
    leading = field.shape[:-3]
    extent = field.shape[-3:]
    shaped = field.reshape(leading + (extent[0] // 2, 2, extent[1] // 2, 2, extent[2] // 2, 2))
    return shaped.mean(axis=(-5, -3, -1))


def prolong(field):
    return jnp.repeat(jnp.repeat(jnp.repeat(field, 2, axis=-3), 2, axis=-2), 2, axis=-1)


def assemble(blocks, count_x, count_y):
    leading = blocks.shape[1:-3]
    extent = blocks.shape[-3:]
    depth_lead = len(leading)
    shaped = blocks.reshape((count_x, count_y) + leading + extent)
    order = tuple(range(2, 2 + depth_lead)) + (0, 2 + depth_lead, 1, 3 + depth_lead, 4 + depth_lead)
    return shaped.transpose(order).reshape(
        leading + (count_x * extent[0], count_y * extent[1], extent[2])
    )


def field_rim(field):
    return extended(field, (("gx", 1), ("gy", 2)), 1)


def cond_rim(conduct):
    return extended(conduct, (("gx", 0), ("gy", 1)), 1)


def whole_cycle(source, level_index, whole_plans):
    cond_pad, diag_level, level_scale = whole_plans[level_index]
    field = DAMPING * source / diag_level

    def turn(turn_index, iterate):
        return relaxed(pad_plane(iterate, 1), source, cond_pad, diag_level, level_scale)

    return lax.fori_loop(0, COARSE_SWEEPS - 1, turn, field)


def part_cycle(source, level_index, level_plans, whole_plans, gather_level):
    if level_index == gather_level:
        blocks = lax.all_gather(source[None], ("gx", "gy"), axis=0, tiled=True)
        whole = assemble(blocks, lax.axis_size("gx"), lax.axis_size("gy"))
        correction = whole_cycle(whole, level_index, whole_plans)
        extent = source.shape
        starts = (0, lax.axis_index("gx") * extent[1], lax.axis_index("gy") * extent[2], 0)
        return lax.dynamic_slice(correction, starts, extent)
    cond_pad, diag_level, level_scale = level_plans[level_index]
    field = DAMPING * source / diag_level
    field = relaxed(field_rim(field), source, cond_pad, diag_level, level_scale)
    residual = source - stencil(field_rim(field), cond_pad, level_scale)
    field = field + prolong(
        part_cycle(restrict(residual), level_index + 1, level_plans, whole_plans, gather_level)
    )
    field = relaxed(field_rim(field), source, cond_pad, diag_level, level_scale)
    return relaxed(field_rim(field), source, cond_pad, diag_level, level_scale)


def distributed(conductivity, stations, currents, receivers, observed):
    row_count, col_count, z_count = conductivity.shape
    shot_count = currents.shape[0]
    count_x = lax.axis_size("gx")
    count_y = lax.axis_size("gy")
    gather_level = LEVELS - 1
    level_plans = []
    conduct = conductivity
    for level_index in range(gather_level):
        level_scale = 0.25**level_index
        cond_pad = cond_rim(conduct)
        level_plans.append((cond_pad, diagonal(cond_pad, level_scale), level_scale))
        conduct = restrict(conduct)
    blocks = lax.all_gather(conduct[None], ("gx", "gy"), axis=0, tiled=True)
    whole = assemble(blocks, count_x, count_y)
    whole_plans = {}
    level_index = 3
    level_scale = 0.25**level_index
    cond_pad = pad_plane(whole, 1)
    whole_plans[level_index] = (cond_pad, diagonal(cond_pad, level_scale), level_scale)
    total_y = col_count * count_y
    cell_x = stations // (total_y * z_count)
    cell_y = stations // z_count % total_y
    cell_z = stations % z_count
    local_x = cell_x - lax.axis_index("gx") * row_count
    local_y = cell_y - lax.axis_index("gy") * col_count
    owned = (local_x >= 0) & (local_x < row_count) & (local_y >= 0) & (local_y < col_count)
    block_size = row_count * col_count * z_count
    local_cell = jnp.where(owned, (local_x * col_count + local_y) * z_count + cell_z, 0)
    offsets = jnp.arange(shot_count)[:, None] * block_size + local_cell[None, :]
    targets = jnp.where(owned[None, :], offsets, shot_count * block_size).reshape(-1)

    def spread(amounts):
        flat = (
            jnp.zeros((shot_count * block_size,), jnp.float32)
            .at[targets]
            .add(amounts.reshape(-1), mode="drop")
        )
        return flat.reshape(shot_count, row_count, col_count, z_count)

    potentials = part_cycle(spread(currents), 0, level_plans, whole_plans, gather_level)
    local_values = jnp.where(
        owned[None, :], potentials.reshape(shot_count, block_size)[:, local_cell], 0.0
    )
    readings = lax.psum(local_values, ("gx", "gy"))
    positions = jnp.arange(stations.shape[0])[:, None]
    pairs = (receivers[:, 0][None, :] == positions).astype(jnp.float32) - (
        receivers[:, 1][None, :] == positions
    ).astype(jnp.float32)
    misfit = jnp.dot(readings, pairs, precision=lax.Precision.HIGHEST) - observed
    back_source = jnp.dot(misfit, pairs.T, precision=lax.Precision.HIGHEST)
    adjoint = part_cycle(spread(back_source), 0, level_plans, whole_plans, gather_level)
    stacked = jnp.concatenate([potentials, adjoint], axis=0)
    padded = extended(stacked, (("gx", 1), ("gy", 2)), 1)
    potential_pad = padded[:shot_count]
    adjoint_pad = padded[shot_count:]
    gradient = jnp.zeros_like(potentials)
    for other_u, other_w in zip(neighbour_list(potential_pad), neighbour_list(adjoint_pad)):
        gradient = gradient - 0.5 * (potentials - other_u) * (adjoint - other_w)
    summed = lax.psum_scatter(jnp.sum(gradient, axis=0), "shot", scatter_dimension=1, tiled=True)
    return (potentials, summed)


def per_device(conductivity, stations, currents, receivers, observed):
    blocks = lax.axis_size("gx") * lax.axis_size("gy")
    fits = conductivity.shape == (SIDE, SIDE * SIDE, LANES) and blocks == SIDE
    fits = fits and lax.axis_size("gy") == 2 and lax.axis_size("shot") == 2
    fits = fits and currents.shape[0] == 1
    plan = replicated if fits else distributed
    return plan(conductivity, stations, currents, receivers, observed)


def solution(mesh):
    in_specs = (
        P(("grp", "gx"), "gy", None),
        P("grp"),
        P(("grp", "shot"), None),
        P("grp", None),
        P(("grp", "shot"), None),
    )
    out_specs = (P(("grp", "shot"), "gx", "gy", None), P(("grp", "gx"), ("gy", "shot"), None))
    return jax.shard_map(
        per_device, mesh=mesh, in_specs=in_specs, out_specs=out_specs, check_vma=False
    )
```

```python
import functools

import jax
import jax.numpy as jnp
from jax import lax
from jax.experimental import pallas as pl
from jax.experimental.pallas import tpu as pltpu
from jax.sharding import PartitionSpec as P

LEVELS = 4
COARSE_SWEEPS = 16


DAMPING = 0.8

SIDE = 8
LANES = 128
GROUP = 16
VMEM_BYTES = 48 * 2**20
SMALL_BYTES = 6 * 2**20


def pieces_of(value, count):
    pieces = []
    for _ in range(count):
        pieces.append(value.astype(jnp.bfloat16))
        value = value - pieces[-1].astype(jnp.float32)
    return pieces[::-1]


def product(value, matrix, count, dims=((1,), (0,))):
    result = None
    for piece in pieces_of(value, count):
        term = lax.dot_general(
            piece, matrix, (dims, ((), ())), preferred_element_type=jnp.float32
        )
        result = term if result is None else result + term
    return result


def iota(shape, dim):
    return lax.broadcasted_iota(jnp.int32, shape, dim)


def station_table(station):
    cell_x, cell_y, cell_z = station >> 14, station >> 7 & 127, station & 127
    row = (cell_x >> 3) * 2 + (cell_y >> 6)
    return cell_x, cell_y, cell_z, row, (cell_y >> 3 & 7) * GROUP + (cell_z >> 3)


def lane_order():
    row, col = iota((LANES, LANES), 0), iota((LANES, LANES), 1)
    chosen = row == col % GROUP * SIDE + col // GROUP
    return jnp.where(chosen, 1.0, 0.0).astype(jnp.bfloat16)


def exchange_groups(tiles):
    tiles = list(tiles)
    group = iota(tiles[0].shape, 1) // GROUP
    for bit in range(3):
        step = 1 << bit
        keep = (group & step) == 0
        for low in range(SIDE):
            if low & step == 0:
                a, b = tiles[low], tiles[low | step]
                tiles[low] = jnp.where(keep, a, pltpu.roll(b, step * GROUP, 1))
                tiles[low | step] = jnp.where(keep, pltpu.roll(a, LANES - step * GROUP, 1), b)
    return tiles


def own_place():
    return lax.axis_index("gx") * 2 + lax.axis_index("gy"), lax.axis_index("shot")


def to_blocks_kernel(natural_ref, stations_ref, blocks_ref, half_ref, cells_ref):
    order = lane_order()
    for x in range(SIDE):
        tiles = product(natural_ref[x], order, 3)
        tiles = [tiles[SIDE * k : SIDE * (k + 1)] for k in range(SIDE)]
        for z, tile in enumerate(exchange_groups(tiles)):
            blocks_ref[pl.ds((x * SIDE + z) * SIDE, SIDE), :] = tile
    count = half_ref.shape[0]
    low, high = blocks_ref[pl.ds(0, count), :], blocks_ref[pl.ds(count, count), :]
    half_ref[...] = jnp.where(own_place()[1] == 0, low, high)
    cell_x, cell_y, cell_z, row, _ = station_table(stations_ref[...])
    wide = SIDE + 2
    register = (((cell_x & 7) + 1) * wide + (cell_z & 7) + 1) * wide + (cell_y & 7) + 1
    cells_ref[...] = register * SIDE + row


def from_blocks(tiles, order):
    natural = jnp.concatenate(exchange_groups(tiles), axis=0)
    return product(natural, order, 3, ((1,), (1,)))


def block_up(field, axis):
    if axis == 0:
        return pltpu.roll(field, 6, 1)
    if axis == 2:
        return pltpu.roll(field, LANES - 1, 2)
    turned = pltpu.roll(field, LANES - GROUP, 2)
    return jnp.where(iota(field.shape, 2) < LANES - GROUP, turned, pltpu.roll(turned, 7, 1))


def block_down(field, axis):
    if axis == 0:
        return pltpu.roll(field, 2, 1)
    if axis == 2:
        return pltpu.roll(field, 1, 2)
    turned = pltpu.roll(field, GROUP, 2)
    return jnp.where(iota(field.shape, 2) >= GROUP, turned, pltpu.roll(turned, 1, 1))


def inside_up(field, axis):
    sub, lane = iota(field.shape, 1), iota(field.shape, 2)
    if axis == 0:
        keep = sub < 6
    elif axis == 1:
        keep = (lane < LANES - GROUP) | (sub % 2 == 0)
    else:
        keep = lane % GROUP < GROUP - 1
    return jnp.where(keep, field, 0.0)


def inside_down(field, axis):
    sub, lane = iota(field.shape, 1), iota(field.shape, 2)
    if axis == 0:
        keep = sub >= 2
    elif axis == 1:
        keep = (lane >= GROUP) | (sub % 2 == 1)
    else:
        keep = lane % GROUP > 0
    return jnp.where(keep, field, 0.0)


def pair_rows(row):
    count = row.shape[0] // 2
    return jnp.concatenate([row[2 * i : 2 * i + 1] + row[2 * i + 1 : 2 * i + 2] for i in range(count)])


def twice(row):
    return jnp.concatenate([row[i // 2 : i // 2 + 1] for i in range(2 * row.shape[0])])


def electrode_kernel(stations_ref, currents_ref, receivers_ref, rows_ref, same_ref, pairs_ref):
    stations = stations_ref[...]
    electrodes = stations.shape[1]
    row, spot = station_table(stations)[3:]
    line = stations & 0x1C387 | row << 20
    same = jnp.broadcast_to(line, (electrodes, electrodes))
    same = jnp.where(same == same.T, 1.0, 0.0).astype(jnp.bfloat16)
    same_ref[...] = same
    rows_ref[...] = shared_rows(currents_ref[...], spot, same)
    receivers = receivers_ref[...]
    numbers = iota((receivers.shape[0], electrodes), 1)
    pairs = jnp.where(numbers == receivers[:, 0:1], 1.0, 0.0) - jnp.where(
        numbers == receivers[:, 1:2], 1.0, 0.0
    )
    pairs_ref[...] = pairs.astype(jnp.bfloat16)


def shared_rows(amounts, spot, same):
    electrodes = amounts.shape[1]
    at_spot = iota((LANES, electrodes), 0) == spot
    return product(jnp.where(at_spot, amounts, 0.0), same, 3).T


class Edged:
    def __init__(self, ref, side):
        self.ref, self.side = ref, side

    def start(self, x, z, y=0):
        wide = self.side + 2
        return (((x + 1) * wide + z + 1) * wide + y + 1) * SIDE

    def __getitem__(self, at):
        x, z = at
        rows = self.ref[pl.ds(self.start(x, z), self.side * SIDE), :]
        return rows.reshape(self.side, SIDE, LANES)

    def __setitem__(self, at, value):
        x, z = at
        self.ref[pl.ds(self.start(x, z), self.side * SIDE), :] = value.reshape(-1, LANES)

    def put(self, x, z, value, exact=False):
        self[x, z] = value
        n = self.side
        if z == 0:
            edge = block_up(value, 2)
            self[x, n] = inside_up(edge, 2) if exact else edge
        if z == n - 1:
            edge = block_down(value, 2)
            self[x, -1] = inside_down(edge, 2) if exact else edge
        if exact:
            after = inside_up(block_up(value[:1], 1), 1)
            self.ref[pl.ds(self.start(x, z, n), SIDE), :] = after[0]
            before = inside_down(block_down(value[n - 1 :], 1), 1)
            self.ref[pl.ds(self.start(x, z, -1), SIDE), :] = before[0]

    def close_z(self, x):
        n = self.side
        self[x, n] = block_up(self[x, 0], 2)
        self[x, -1] = block_down(self[x, n - 1], 2)

    def close(self, exact=False):
        n = self.side
        for z in range(n):
            after = block_up(self[0, z], 0)
            self[n, z] = inside_up(after, 0) if exact else after
            before = block_down(self[n - 1, z], 0)
            self[-1, z] = inside_down(before, 0) if exact else before


class Plain:
    def __init__(self, ref, side):
        self.ref, self.side = ref, side

    def __getitem__(self, at):
        x, z = at
        rows = self.side * SIDE
        return self.ref[pl.ds((x * self.side + z) * rows, rows), :].reshape(self.side, SIDE, LANES)

    def __setitem__(self, at, value):
        x, z = at
        rows = self.side * SIDE
        self.ref[pl.ds((x * self.side + z) * rows, rows), :] = value.reshape(-1, LANES)


def planes_of(count, body):
    if count < SIDE:
        for x in range(count):
            body(x)
        return

    def one(x, carry):
        body(x)
        return carry

    lax.fori_loop(0, count, one, 0, unroll=2)


class Level:
    def __init__(self, refs, index):
        self.side = side = SIDE >> index
        self.scale = 0.25**index
        edged = [Edged(ref, side) for ref in refs[:5]]
        self.cond, self.first, self.second, self.base, self.back = edged
        self.links = [Plain(ref, side) for ref in refs[5:11]]
        self.half = Plain(refs[11], side // 2)
        self.weight = Plain(refs[12], side) if index else None

    @staticmethod
    def scratch(index):
        side = SIDE >> index
        edged = (side + 2) ** 3
        sizes = [edged] * 5 + [side**3] * 6 + [side**3 // 4] + [side**3] * (index > 0)
        return [pltpu.VMEM((size * SIDE, LANES), jnp.float32) for size in sizes]

    def shifted(self, field, x, z, here, exact=False, along=None):
        ahead, behind = along or (field[x, z + 1], field[x, z - 1])
        after = block_up(here[:1], 1)
        before = block_down(here[-1:], 1)
        if exact:
            after, before = inside_up(after, 1), inside_down(before, 1)
        return [
            field[x + 1, z],
            field[x - 1, z],
            jnp.concatenate([here[1:], after]),
            jnp.concatenate([before, here[:-1]]),
            ahead,
            behind,
        ]

    def prepare(self):
        n = self.side

        def plane(x):
            for z in range(n):
                here = self.cond[x, z]
                others = self.shifted(self.cond, x, z, here, exact=True)
                total = others[0]
                for other in others[1:]:
                    total = total + other
                total = 3.0 * here + 0.5 * total
                inverse = DAMPING / total
                if self.weight is not None:
                    self.weight[x, z] = inverse * (1.0 / self.scale)
                self.back[x, z] = total * (self.scale / DAMPING)
                inverse = 0.5 * inverse
                for index, other in enumerate(others):
                    link = inverse * (here + other)
                    if index == 2:
                        link = jnp.concatenate([link[:-1], inside_up(link[-1:], 1)])
                    if index == 3:
                        link = jnp.concatenate([inside_down(link[:1], 1), link[1:]])
                    if index == 4 and z == n - 1:
                        link = inside_up(link, 2)
                    if index == 5 and z == 0:
                        link = inside_down(link, 2)
                    self.links[index][x, z] = link

        planes_of(n, plane)
        for z in range(n):
            self.links[0][n - 1, z] = inside_up(self.links[0][n - 1, z], 0)
            self.links[1][0, z] = inside_down(self.links[1][0, z], 0)

    def rows(self, field, x):
        behind, here = field[x, -1], field[x, 0]
        for z in range(self.side):
            ahead = field[x, z + 1]
            result = self.base[x, z]
            others = self.shifted(field, x, z, here, along=(ahead, behind))
            for link, other in zip(self.links, others):
                result = result + link[x, z] * other
            yield z, here, result
            behind, here = here, ahead

    def sweep(self, field, out, exact=False):
        def plane(x):
            for z, here, result in self.rows(field, x):
                out.put(x, z, (1.0 - DAMPING) * here + result, exact)

        planes_of(self.side, plane)
        out.close(exact)

    def halve(self, plane_rows, coarse):
        n = self.side

        def plane(x):
            held = None
            for z, row in enumerate(plane_rows(x)):
                if z % 2 == 0:
                    held = row
                else:
                    self.half[x, z // 2] = pair_rows(held + row)

        planes_of(n, plane)
        for x in range(n // 2):
            for z in range(n // 2):
                pair = self.half[2 * x, z] + self.half[2 * x + 1, z]
                coarse(x, z, 0.125 * pair)

    def descend(self, coarse):
        self.sweep(self.base, self.second)

        def residuals(x):
            for z, here, result in self.rows(self.second, x):
                self.first[x, z] = (1.0 - DAMPING) * here + result
                yield (result - DAMPING * here) * self.back[x, z]

        self.halve(residuals, coarse)

    def ascend(self, correction, out, exact=False):
        def plane(x):
            upper = (x + 1) // 2
            for z in range(self.side):
                above = (z + 1) // 2
                row = correction(x // 2, z // 2)
                here = twice(row)
                after, before = block_up(row[:1], 1), block_down(row[-1:], 1)
                others = [
                    twice(correction(upper, z // 2)),
                    twice(correction(upper - 1, z // 2)),
                    jnp.concatenate([here[1:], after]),
                    jnp.concatenate([before, here[:-1]]),
                    twice(correction(x // 2, above)),
                    twice(correction(x // 2, above - 1)),
                ]
                result = self.first[x, z] + (1.0 - DAMPING) * here
                for link, other in zip(self.links, others):
                    result = result + link[x, z] * other
                self.second.put(x, z, result)

        planes_of(self.side, plane)
        self.second.close()
        self.sweep(self.second, out, exact)


class HeldLevel(Level):
    def sums(self, field, base):
        result = {}
        for (x, z), here in field.items():
            others = [
                field[1, z] if x == 0 else block_up(field[0, z], 0),
                field[0, z] if x == 1 else block_down(field[1, z], 0),
                jnp.concatenate([here[1:], block_up(here[:1], 1)]),
                jnp.concatenate([block_down(here[-1:], 1), here[:-1]]),
                field[x, 1] if z == 0 else block_up(field[x, 0], 2),
                field[x, 0] if z == 1 else block_down(field[x, 1], 2),
            ]
            total = base[x, z]
            for link, other in zip(self.links, others):
                total = total + link[x, z] * other
            result[x, z] = total
        return result

    def swept(self, field, base):
        sums = self.sums(field, base)
        return {at: (1.0 - DAMPING) * field[at] + sums[at] for at in field}

    def cycle(self, base, solve, out):
        field = self.swept(base, base)
        sums = self.sums(field, base)
        total = None
        for at in field:
            residual = (sums[at] - DAMPING * field[at]) * self.back[at]
            total = residual if total is None else total + residual
        solved = solve(0.125 * (total[:1] + total[1:]))
        row = twice(solved)
        copied = {at: row for at in field}
        change = {at: sums[at] + (1.0 - DAMPING) * (field[at] + row) for at in field}
        field = self.sums(copied, change)
        for (x, z), value in self.swept(field, base).items():
            out.put(x, z, value)
        out.close()


def replicated_kernel(
    whole,
    halved,
    cells_ref,
    *refs,
):
    parts = refs[:whole], refs[whole : whole + halved]
    solve_kernel(*parts, cells_ref, *refs[whole + halved :])


def solve_kernel(
    part_refs,
    half_refs,
    cells_ref,
    stations_ref,
    rows_ref,
    same_ref,
    pairs_ref,
    observed_ref,
    potentials_ref,
    mine_ref,
    theirs_ref,
    gathered,
    weights,
    owned,
    *level_refs,
):
    f32 = jnp.float32
    electrodes = stations_ref.shape[1]
    levels, used = [], 0
    for index in range(LEVELS - 1):
        count = len(Level.scratch(index))
        kind = HeldLevel if index == LEVELS - 2 else Level
        levels.append(kind(level_refs[used : used + count], index))
        used += count
    fine = levels[0]
    forward = fine.cond
    wide = SIDE * SIDE * SIDE

    device, shot = own_place()

    def place(part, row, x, index):
        for z in range(SIDE):
            fine.cond.ref[pl.ds(fine.cond.start(x, z) + index, SIDE, stride=SIDE), :] = part[
                pl.ds((row * SIDE + z) * SIDE, SIDE), :
            ]

    def collect(x):
        for k, part in enumerate(part_refs):
            place(part, x, x, device ^ k)

    def collect_half(x):
        for k, part in enumerate(half_refs):
            swapped, index = k // 2 % 2, len(part_refs) + k // 4 * 2 + k % 2
            place(part, x, (shot ^ swapped) * (SIDE // 2) + x, device ^ index)

    def edges(x):
        for z in (0, SIDE - 1):
            fine.cond.put(x, z, fine.cond[x, z], exact=True)

    planes_of(SIDE, collect)
    planes_of(SIDE // 2, collect_half)
    planes_of(SIDE, edges)
    fine.cond.close(exact=True)

    coarsest = []
    for level, below in zip(levels, levels[1:] + [None]):
        level.prepare()

        def coarse(x, z, row, below=below):
            if below is None:
                coarsest.append(row)
            else:
                below.cond.put(x, z, row, exact=True)

        level.halve(lambda x, level=level: [level.cond[x, z] for z in range(level.side)], coarse)
        if below is not None:
            below.cond.close(exact=True)

    keep = iota((1, SIDE, LANES), 1) % 2 == 0
    lane = iota((1, SIDE, LANES), 2)

    def split(value):
        return [jnp.where(keep, part, 0.0) for part in (value, pltpu.roll(value, SIDE - 1, 1))]

    def around(value):
        low, high = value
        low_up, high_up = [pltpu.roll(part, LANES - GROUP, 2) for part in value]
        low_down, high_down = [pltpu.roll(part, GROUP, 2) for part in value]
        along = [[move(part, axis) for part in value] for axis in (0, 2) for move in (block_up, block_down)]
        return along + [
            [jnp.where(lane < LANES - GROUP, low_up, high_up), high_up],
            [low_down, jnp.where(lane >= GROUP, high_down, low_down)],
        ]

    sub = iota((1, SIDE, LANES), 1)
    inside_last = [
        [sub < 6] * 2,
        [sub >= 2] * 2,
        [lane % GROUP < GROUP - 1] * 2,
        [lane % GROUP > 0] * 2,
        [keep, lane < LANES - GROUP],
        [lane >= GROUP, keep],
    ]
    last_scale = 0.25 ** (LEVELS - 1)
    here = split(coarsest[0])
    others = [
        [jnp.where(inside & keep, part, 0.0) for inside, part in zip(pair, moved)]
        for pair, moved in zip(inside_last, around(here))
    ]
    last_weight, last_links = [], []
    for half, part in enumerate(here):
        total = 3.0 * part
        for other in others:
            total = total + 0.5 * other[half]
        inverse = jnp.where(keep, DAMPING / jnp.where(keep, total, 1.0), 0.0)
        last_weight.append(inverse * (1.0 / last_scale))
        last_links.append(
            [
                jnp.where(pair[half] & keep, 0.5 * inverse * (part + other[half]), 0.0)
                for pair, other in zip(inside_last, others)
            ]
        )

    def solve_last(rhs):
        base = [weight * part for weight, part in zip(last_weight, split(rhs))]
        value = base
        for _ in range(COARSE_SWEEPS - 1):
            moved = around(value)
            fresh = []
            for half in range(2):
                parts = [link * other[half] for link, other in zip(last_links[half], moved)]
                start = base[half] + (1.0 - DAMPING) * value[half]
                fresh.append(((start + parts[0]) + (parts[1] + parts[2])) + (parts[3] + (parts[4] + parts[5])))
            value = fresh
        return value[0] + pltpu.roll(value[1], 1, 1)

    def cycle(index, out, exact=False):
        level = levels[index]
        below = levels[index + 1]
        if index == LEVELS - 3:
            base = {}

            def take(x, z, row):
                base[x, z] = below.weight[x, z] * row

            level.descend(take)
            below.cycle(base, solve_last, below.first)
        else:
            level.descend(lambda x, z, row: below.base.put(x, z, below.weight[x, z] * row))
            below.base.close()
            cycle(index + 1, below.first)
        level.ascend(lambda x, z: below.first[x, z], out, exact)

    spot = station_table(stations_ref[...])[4]

    def each(body):
        def one(electrode, carry):
            body(pl.ds(electrode, 1), pl.ds(cells_ref[0, electrode], 1))
            return carry

        lax.fori_loop(0, electrodes, one, 0, unroll=32)

    def weigh(electrode, cell):
        weights[electrode, :] = fine.back.ref[cell, :]

    each(weigh)
    weights[...] = 1.0 / weights[...]
    fine.base.ref[...] = jnp.zeros_like(fine.base.ref)

    def spread(rows):
        gathered[...] = rows * weights[...]

        def put(electrode, cell):
            fine.base.ref[cell, :] = gathered[electrode, :]

        each(put)
        planes_of(SIDE, fine.base.close_z)
        fine.base.close()

    spread(rows_ref[...])
    cycle(0, forward, exact=True)

    def read(electrode, cell):
        gathered[electrode, :] = forward.ref[cell, :]

    each(read)
    at_spot = iota((LANES, electrodes), 0) == spot
    readings = jnp.sum(jnp.where(at_spot, gathered[...].T, 0.0), axis=0, keepdims=True)
    pairs = pairs_ref[...]

    def exact(row, dims):
        return product(jnp.broadcast_to(row, (16, row.shape[1])), pairs, 3, dims)[0:1]

    misfit = exact(readings, ((1,), (1,))) - observed_ref[...]
    spread(shared_rows(exact(misfit, ((1,), (0,))), spot, same_ref[...]))
    cycle(0, fine.first, exact=True)

    order = lane_order()
    adjoint = fine.first
    chunk = mine_ref.shape[1]
    even = shot == 0

    def own(field, x, z, y=0):
        return field.ref[pl.ds(field.start(x, z, y) + device, SIDE, stride=SIDE), :]

    wide = SIDE + 2
    for index, field in enumerate((forward, adjoint)):
        for x in range(-1, SIDE + 1):
            for z in range(-1, SIDE + 1):
                if 0 <= x < SIDE or 0 <= z < SIDE:
                    owned[index, (x + 1) * wide + z + 1] = own(field, x, z)

    for x in range(SIDE):
        tiles_u, tiles_g = [], []
        for z in range(SIDE):
            at = (x + 1) * wide + z + 1
            here_u, here_w = owned[0, at], owned[1, at]
            total = None
            for step in (wide, -wide, 1, -1):
                term = (here_u - owned[0, at + step]) * (here_w - owned[1, at + step])
                total = term if total is None else total + term
            for y in (1, -1):
                total = total + (here_u - own(forward, x, z, y)) * (here_w - own(adjoint, x, z, y))
            tiles_u.append(here_u)
            tiles_g.append(-0.5 * total)
        potentials_ref[x] = from_blocks(tiles_u, order)
        natural = from_blocks(tiles_g, order)
        low, high = natural[:chunk], natural[chunk:]
        mine_ref[x] = jnp.where(even, low, high)
        theirs_ref[x] = jnp.where(even, high, low)


def replicated(conductivity, stations, currents, receivers, observed):
    rows, cols, depth = conductivity.shape
    f32 = jnp.float32
    electrodes = stations.shape[0]
    total = rows * cols
    vmem = pl.BlockSpec(memory_space=pltpu.VMEM)
    smem = pl.BlockSpec(memory_space=pltpu.SMEM)
    station_row = stations.reshape(1, electrodes)
    mine, half, cells = pl.pallas_call(
        to_blocks_kernel,
        out_shape=(
            jax.ShapeDtypeStruct((total, LANES), f32),
            jax.ShapeDtypeStruct((total // 2, LANES), f32),
            jax.ShapeDtypeStruct((1, electrodes), jnp.int32),
        ),
        in_specs=[vmem, vmem],
        out_specs=(vmem, vmem, vmem),
        compiler_params=pltpu.CompilerParams(vmem_limit_bytes=SMALL_BYTES),
    )(conductivity, station_row)
    swap = [(0, 1), (1, 0)]

    def partner(part, k):
        count = lax.axis_size("gx")
        return lax.ppermute(part, "gx", [(i, i ^ k) for i in range(count)])

    def with_mate(part):
        return [part, lax.ppermute(part, "gy", swap)]

    far = partner(half, 2)
    near = partner(mine, 1)
    rows_of, same, pairs = pl.pallas_call(
        electrode_kernel,
        out_shape=(
            jax.ShapeDtypeStruct((electrodes, LANES), f32),
            jax.ShapeDtypeStruct((electrodes, electrodes), jnp.bfloat16),
            jax.ShapeDtypeStruct((receivers.shape[0], electrodes), jnp.bfloat16),
        ),
        in_specs=[vmem, vmem, vmem],
        out_specs=(vmem, vmem, vmem),
        compiler_params=pltpu.CompilerParams(vmem_limit_bytes=SMALL_BYTES),
        cost_estimate=pl.CostEstimate(flops=100_000_000, bytes_accessed=1_000_000, transcendentals=0),
    )(station_row, currents, receivers)
    far, rows_of = lax.optimization_barrier((far, rows_of))
    far = [far, partner(far, 1)]
    halved = [piece for own in far for piece in (own, lax.ppermute(own, "shot", swap))]
    parts = [piece for own in (mine, near) for piece in with_mate(own)]
    halved = [piece for own in halved for piece in with_mate(own)]
    chunk = cols // 2
    levels = [shape for index in range(LEVELS - 1) for shape in Level.scratch(index)]
    potentials, own, theirs = pl.pallas_call(
        functools.partial(replicated_kernel, len(parts), len(halved)),
        out_shape=(
            jax.ShapeDtypeStruct((rows, cols, LANES), f32),
            jax.ShapeDtypeStruct((rows, chunk, LANES), f32),
            jax.ShapeDtypeStruct((rows, chunk, LANES), f32),
        ),
        in_specs=[smem] + [vmem] * (len(parts) + len(halved) + 5),
        out_specs=(vmem, vmem, vmem),
        scratch_shapes=[
            pltpu.VMEM((electrodes, LANES), f32),
            pltpu.VMEM((electrodes, LANES), f32),
            pltpu.VMEM((2, (SIDE + 2) ** 2, SIDE, LANES), f32),
        ]
        + levels,
        compiler_params=pltpu.CompilerParams(vmem_limit_bytes=VMEM_BYTES),
        cost_estimate=pl.CostEstimate(flops=200_000_000, bytes_accessed=4_000_000, transcendentals=0),
    )(cells, *parts, *halved, station_row, rows_of, same, pairs, observed)
    return potentials[None], own + lax.ppermute(theirs, "shot", swap)


def extended(array, sides, width):
    for axis, dim in sides:
        size, length = (lax.axis_size(axis), array.shape[dim])
        up = [(i, (i + 1) % size) for i in range(size - 1)]
        down = [(j, i) for i, j in up]
        last = lax.slice_in_dim(array, length - width, length, axis=dim)
        leading = lax.slice_in_dim(array, 0, width, axis=dim)
        before = lax.ppermute(last, axis, up)
        after = lax.ppermute(leading, axis, down)
        array = jnp.concatenate([before, array, after], axis=dim)
    return array


def upper_z(field):
    return jnp.concatenate([field[..., 1:], jnp.zeros_like(field[..., :1])], axis=-1)


def lower_z(field):
    return jnp.concatenate([jnp.zeros_like(field[..., :1]), field[..., :-1]], axis=-1)


def trim_circle(field, circle_width):
    return field[..., circle_width:-circle_width, circle_width:-circle_width, :]


def pad_plane(field, circle_width):
    spec = [(0, 0)] * (field.ndim - 3) + [
        (circle_width, circle_width),
        (circle_width, circle_width),
        (0, 0),
    ]
    return jnp.pad(field, spec)


def neighbour_list(field_pad):
    centre = trim_circle(field_pad, 1)
    return [
        field_pad[..., 2:, 1:-1, :],
        field_pad[..., :-2, 1:-1, :],
        field_pad[..., 1:-1, 2:, :],
        field_pad[..., 1:-1, :-2, :],
        upper_z(centre),
        lower_z(centre),
    ]


def stencil(field_pad, cond_pad, level_scale):
    centre = trim_circle(field_pad, 1)
    centre_cond = trim_circle(cond_pad, 1)
    summed = jnp.zeros_like(centre)
    for other, other_cond in zip(neighbour_list(field_pad), neighbour_list(cond_pad)):
        summed = summed + level_scale * 0.5 * (centre_cond + other_cond) * (centre - other)
    return summed


def diagonal(cond_pad, level_scale):
    centre_cond = trim_circle(cond_pad, 1)
    summed = jnp.zeros_like(centre_cond)
    for other_cond in neighbour_list(cond_pad):
        summed = summed + level_scale * 0.5 * (centre_cond + other_cond)
    return summed


def relaxed(field_pad, source, cond_pad, diag_level, level_scale):
    return (
        trim_circle(field_pad, 1)
        + DAMPING * (source - stencil(field_pad, cond_pad, level_scale)) / diag_level
    )


def restrict(field):
    leading = field.shape[:-3]
    extent = field.shape[-3:]
    shaped = field.reshape(leading + (extent[0] // 2, 2, extent[1] // 2, 2, extent[2] // 2, 2))
    return shaped.mean(axis=(-5, -3, -1))


def prolong(field):
    return jnp.repeat(jnp.repeat(jnp.repeat(field, 2, axis=-3), 2, axis=-2), 2, axis=-1)


def assemble(blocks, count_x, count_y):
    leading = blocks.shape[1:-3]
    extent = blocks.shape[-3:]
    depth_lead = len(leading)
    shaped = blocks.reshape((count_x, count_y) + leading + extent)
    order = tuple(range(2, 2 + depth_lead)) + (0, 2 + depth_lead, 1, 3 + depth_lead, 4 + depth_lead)
    return shaped.transpose(order).reshape(
        leading + (count_x * extent[0], count_y * extent[1], extent[2])
    )


def field_rim(field):
    return extended(field, (("gx", 1), ("gy", 2)), 1)


def cond_rim(conduct):
    return extended(conduct, (("gx", 0), ("gy", 1)), 1)


def whole_cycle(source, level_index, whole_plans):
    cond_pad, diag_level, level_scale = whole_plans[level_index]
    field = DAMPING * source / diag_level

    def turn(turn_index, iterate):
        return relaxed(pad_plane(iterate, 1), source, cond_pad, diag_level, level_scale)

    return lax.fori_loop(0, COARSE_SWEEPS - 1, turn, field)


def part_cycle(source, level_index, level_plans, whole_plans, gather_level):
    if level_index == gather_level:
        blocks = lax.all_gather(source[None], ("gx", "gy"), axis=0, tiled=True)
        whole = assemble(blocks, lax.axis_size("gx"), lax.axis_size("gy"))
        correction = whole_cycle(whole, level_index, whole_plans)
        extent = source.shape
        starts = (0, lax.axis_index("gx") * extent[1], lax.axis_index("gy") * extent[2], 0)
        return lax.dynamic_slice(correction, starts, extent)
    cond_pad, diag_level, level_scale = level_plans[level_index]
    field = DAMPING * source / diag_level
    field = relaxed(field_rim(field), source, cond_pad, diag_level, level_scale)
    residual = source - stencil(field_rim(field), cond_pad, level_scale)
    field = field + prolong(
        part_cycle(restrict(residual), level_index + 1, level_plans, whole_plans, gather_level)
    )
    field = relaxed(field_rim(field), source, cond_pad, diag_level, level_scale)
    return relaxed(field_rim(field), source, cond_pad, diag_level, level_scale)


def distributed(conductivity, stations, currents, receivers, observed):
    row_count, col_count, z_count = conductivity.shape
    shot_count = currents.shape[0]
    count_x = lax.axis_size("gx")
    count_y = lax.axis_size("gy")
    gather_level = LEVELS - 1
    level_plans = []
    conduct = conductivity
    for level_index in range(gather_level):
        level_scale = 0.25**level_index
        cond_pad = cond_rim(conduct)
        level_plans.append((cond_pad, diagonal(cond_pad, level_scale), level_scale))
        conduct = restrict(conduct)
    blocks = lax.all_gather(conduct[None], ("gx", "gy"), axis=0, tiled=True)
    whole = assemble(blocks, count_x, count_y)
    whole_plans = {}
    level_index = 3
    level_scale = 0.25**level_index
    cond_pad = pad_plane(whole, 1)
    whole_plans[level_index] = (cond_pad, diagonal(cond_pad, level_scale), level_scale)
    total_y = col_count * count_y
    cell_x = stations // (total_y * z_count)
    cell_y = stations // z_count % total_y
    cell_z = stations % z_count
    local_x = cell_x - lax.axis_index("gx") * row_count
    local_y = cell_y - lax.axis_index("gy") * col_count
    owned = (local_x >= 0) & (local_x < row_count) & (local_y >= 0) & (local_y < col_count)
    block_size = row_count * col_count * z_count
    local_cell = jnp.where(owned, (local_x * col_count + local_y) * z_count + cell_z, 0)
    offsets = jnp.arange(shot_count)[:, None] * block_size + local_cell[None, :]
    targets = jnp.where(owned[None, :], offsets, shot_count * block_size).reshape(-1)

    def spread(amounts):
        flat = (
            jnp.zeros((shot_count * block_size,), jnp.float32)
            .at[targets]
            .add(amounts.reshape(-1), mode="drop")
        )
        return flat.reshape(shot_count, row_count, col_count, z_count)

    potentials = part_cycle(spread(currents), 0, level_plans, whole_plans, gather_level)
    local_values = jnp.where(
        owned[None, :], potentials.reshape(shot_count, block_size)[:, local_cell], 0.0
    )
    readings = lax.psum(local_values, ("gx", "gy"))
    positions = jnp.arange(stations.shape[0])[:, None]
    pairs = (receivers[:, 0][None, :] == positions).astype(jnp.float32) - (
        receivers[:, 1][None, :] == positions
    ).astype(jnp.float32)
    misfit = jnp.dot(readings, pairs, precision=lax.Precision.HIGHEST) - observed
    back_source = jnp.dot(misfit, pairs.T, precision=lax.Precision.HIGHEST)
    adjoint = part_cycle(spread(back_source), 0, level_plans, whole_plans, gather_level)
    stacked = jnp.concatenate([potentials, adjoint], axis=0)
    padded = extended(stacked, (("gx", 1), ("gy", 2)), 1)
    potential_pad = padded[:shot_count]
    adjoint_pad = padded[shot_count:]
    gradient = jnp.zeros_like(potentials)
    for other_u, other_w in zip(neighbour_list(potential_pad), neighbour_list(adjoint_pad)):
        gradient = gradient - 0.5 * (potentials - other_u) * (adjoint - other_w)
    summed = lax.psum_scatter(jnp.sum(gradient, axis=0), "shot", scatter_dimension=1, tiled=True)
    return (potentials, summed)


def per_device(conductivity, stations, currents, receivers, observed):
    blocks = lax.axis_size("gx") * lax.axis_size("gy")
    fits = conductivity.shape == (SIDE, SIDE * SIDE, LANES) and blocks == SIDE
    fits = fits and lax.axis_size("gy") == 2 and lax.axis_size("shot") == 2
    fits = fits and currents.shape[0] == 1
    plan = replicated if fits else distributed
    return plan(conductivity, stations, currents, receivers, observed)


def solution(mesh):
    in_specs = (
        P(("grp", "gx"), "gy", None),
        P("grp"),
        P(("grp", "shot"), None),
        P("grp", None),
        P(("grp", "shot"), None),
    )
    out_specs = (P(("grp", "shot"), "gx", "gy", None), P(("grp", "gx"), ("gy", "shot"), None))
    return jax.shard_map(
        per_device, mesh=mesh, in_specs=in_specs, out_specs=out_specs, check_vma=False
    )
```

```python
import functools

import jax
import jax.numpy as jnp
from jax import lax
from jax.experimental import pallas as pl
from jax.experimental.pallas import tpu as pltpu
from jax.sharding import PartitionSpec as P

LEVELS = 4
COARSE_SWEEPS = 16


DAMPING = 0.8

SIDE = 8
LANES = 128
GROUP = 16
VMEM_BYTES = 48 * 2**20
SMALL_BYTES = 6 * 2**20


def pieces_of(value, count):
    pieces = []
    for _ in range(count):
        pieces.append(value.astype(jnp.bfloat16))
        value = value - pieces[-1].astype(jnp.float32)
    return pieces[::-1]


def product(value, matrix, count, dims=((1,), (0,))):
    result = None
    for piece in pieces_of(value, count):
        term = lax.dot_general(
            piece, matrix, (dims, ((), ())), preferred_element_type=jnp.float32
        )
        result = term if result is None else result + term
    return result


def iota(shape, dim):
    return lax.broadcasted_iota(jnp.int32, shape, dim)


def station_table(station):
    cell_x, cell_y, cell_z = station >> 14, station >> 7 & 127, station & 127
    row = (cell_x >> 3) * 2 + (cell_y >> 6)
    return cell_x, cell_y, cell_z, row, (cell_y >> 3 & 7) * GROUP + (cell_z >> 3)


def lane_order():
    row, col = iota((LANES, LANES), 0), iota((LANES, LANES), 1)
    chosen = row == col % GROUP * SIDE + col // GROUP
    return jnp.where(chosen, 1.0, 0.0).astype(jnp.bfloat16)


def exchange_groups(tiles):
    tiles = list(tiles)
    group = iota(tiles[0].shape, 1) // GROUP
    for bit in range(3):
        step = 1 << bit
        keep = (group & step) == 0
        for low in range(SIDE):
            if low & step == 0:
                a, b = tiles[low], tiles[low | step]
                tiles[low] = jnp.where(keep, a, pltpu.roll(b, step * GROUP, 1))
                tiles[low | step] = jnp.where(keep, pltpu.roll(a, LANES - step * GROUP, 1), b)
    return tiles


def own_place():
    return lax.axis_index("gx") * 2 + lax.axis_index("gy"), lax.axis_index("shot")


def to_blocks_kernel(natural_ref, blocks_ref, half_ref):
    order = lane_order()
    for x in range(SIDE):
        tiles = product(natural_ref[x], order, 3)
        tiles = [tiles[SIDE * k : SIDE * (k + 1)] for k in range(SIDE)]
        for z, tile in enumerate(exchange_groups(tiles)):
            blocks_ref[pl.ds((x * SIDE + z) * SIDE, SIDE), :] = tile
    count = half_ref.shape[0]
    low, high = blocks_ref[pl.ds(0, count), :], blocks_ref[pl.ds(count, count), :]
    half_ref[...] = jnp.where(own_place()[1] == 0, low, high)


def from_blocks(tiles, order):
    natural = jnp.concatenate(exchange_groups(tiles), axis=0)
    return product(natural, order, 3, ((1,), (1,)))


def block_up(field, axis):
    if axis == 0:
        return pltpu.roll(field, 6, 1)
    if axis == 2:
        return pltpu.roll(field, LANES - 1, 2)
    turned = pltpu.roll(field, LANES - GROUP, 2)
    return jnp.where(iota(field.shape, 2) < LANES - GROUP, turned, pltpu.roll(turned, 7, 1))


def block_down(field, axis):
    if axis == 0:
        return pltpu.roll(field, 2, 1)
    if axis == 2:
        return pltpu.roll(field, 1, 2)
    turned = pltpu.roll(field, GROUP, 2)
    return jnp.where(iota(field.shape, 2) >= GROUP, turned, pltpu.roll(turned, 1, 1))


def inside_up(field, axis):
    sub, lane = iota(field.shape, 1), iota(field.shape, 2)
    if axis == 0:
        keep = sub < 6
    elif axis == 1:
        keep = (lane < LANES - GROUP) | (sub % 2 == 0)
    else:
        keep = lane % GROUP < GROUP - 1
    return jnp.where(keep, field, 0.0)


def inside_down(field, axis):
    sub, lane = iota(field.shape, 1), iota(field.shape, 2)
    if axis == 0:
        keep = sub >= 2
    elif axis == 1:
        keep = (lane >= GROUP) | (sub % 2 == 1)
    else:
        keep = lane % GROUP > 0
    return jnp.where(keep, field, 0.0)


def pair_rows(row):
    count = row.shape[0] // 2
    return jnp.concatenate([row[2 * i : 2 * i + 1] + row[2 * i + 1 : 2 * i + 2] for i in range(count)])


def twice(row):
    return jnp.concatenate([row[i // 2 : i // 2 + 1] for i in range(2 * row.shape[0])])


def electrode_kernel(
    stations_ref,
    currents_ref,
    receivers_ref,
    observed_ref,
    cells_ref,
    spot_ref,
    rows_ref,
    same_ref,
    pairs_ref,
    held_ref,
):
    stations = stations_ref[...]
    electrodes = stations.shape[1]
    cell_x, cell_y, cell_z, row, spot = station_table(stations)
    wide = SIDE + 2
    register = (((cell_x & 7) + 1) * wide + (cell_z & 7) + 1) * wide + (cell_y & 7) + 1
    cells_ref[...] = register * SIDE + row
    spot_ref[...] = spot
    held_ref[...] = observed_ref[...]
    line = stations & 0x1C387 | row << 20
    same = jnp.broadcast_to(line, (electrodes, electrodes))
    same = jnp.where(same == same.T, 1.0, 0.0).astype(jnp.bfloat16)
    same_ref[...] = same
    rows_ref[...] = shared_rows(currents_ref[...], spot, same)
    receivers = receivers_ref[...]
    numbers = iota((receivers.shape[0], electrodes), 1)
    pairs = jnp.where(numbers == receivers[:, 0:1], 1.0, 0.0) - jnp.where(
        numbers == receivers[:, 1:2], 1.0, 0.0
    )
    pairs_ref[...] = pairs.astype(jnp.bfloat16)


def shared_rows(amounts, spot, same):
    electrodes = amounts.shape[1]
    at_spot = iota((LANES, electrodes), 0) == spot
    return product(jnp.where(at_spot, amounts, 0.0), same, 3).T


class Edged:
    def __init__(self, ref, side):
        self.ref, self.side = ref, side

    def start(self, x, z, y=0):
        wide = self.side + 2
        return (((x + 1) * wide + z + 1) * wide + y + 1) * SIDE

    def __getitem__(self, at):
        x, z = at
        rows = self.ref[pl.ds(self.start(x, z), self.side * SIDE), :]
        return rows.reshape(self.side, SIDE, LANES)

    def __setitem__(self, at, value):
        x, z = at
        self.ref[pl.ds(self.start(x, z), self.side * SIDE), :] = value.reshape(-1, LANES)

    def put(self, x, z, value, exact=False):
        self[x, z] = value
        n = self.side
        if z == 0:
            edge = block_up(value, 2)
            self[x, n] = inside_up(edge, 2) if exact else edge
        if z == n - 1:
            edge = block_down(value, 2)
            self[x, -1] = inside_down(edge, 2) if exact else edge
        if exact:
            after = inside_up(block_up(value[:1], 1), 1)
            self.ref[pl.ds(self.start(x, z, n), SIDE), :] = after[0]
            before = inside_down(block_down(value[n - 1 :], 1), 1)
            self.ref[pl.ds(self.start(x, z, -1), SIDE), :] = before[0]

    def close_z(self, x, exact=False):
        n = self.side
        after, before = block_up(self[x, 0], 2), block_down(self[x, n - 1], 2)
        self[x, n] = inside_up(after, 2) if exact else after
        self[x, -1] = inside_down(before, 2) if exact else before

    def close(self, exact=False):
        n = self.side
        for z in range(n):
            after = block_up(self[0, z], 0)
            self[n, z] = inside_up(after, 0) if exact else after
            before = block_down(self[n - 1, z], 0)
            self[-1, z] = inside_down(before, 0) if exact else before


class Rows:
    def __init__(self, ref, side, first_x=0, first_z=0):
        self.ref, self.side, self.first_x, self.first_z = ref, side, first_x, first_z

    def place(self, at):
        count = self.side - self.first_z
        rows = self.side * SIDE
        return pl.ds(((at[0] - self.first_x) * count + at[1] - self.first_z) * rows, rows)

    def __getitem__(self, at):
        return self.ref[self.place(at), :].reshape(self.side, SIDE, LANES)

    def __setitem__(self, at, value):
        self.ref[self.place(at), :] = value.reshape(-1, LANES)


def rolled(count, body):
    def one(x, carry):
        body(x)
        return carry

    lax.fori_loop(0, count, one, 0)


def next_in_y(row):
    return jnp.concatenate([row[1:], block_up(row[:1], 1)])


def last_in_y(row):
    return jnp.concatenate([block_down(row[-1:], 1), row[:-1]])


class Level:
    def __init__(self, refs, index):
        self.side = side = SIDE >> index
        self.scale = 0.25**index
        edged = [Edged(ref, side) for ref in refs[:5]]
        self.cond, self.first, self.second, self.base, self.weight = edged
        self.link_x = Rows(refs[5], side, first_x=-1)
        self.link_y = Rows(refs[6], side)
        self.link_z = Rows(refs[7], side, first_z=-1)
        self.back = Rows(refs[8], side)

    @staticmethod
    def scratch(index):
        side = SIDE >> index
        sizes = [(side + 2) ** 3] * 5
        sizes += [side**2 * (side + 1), side**3, side**2 * (side + 1), side**3]
        return [pltpu.VMEM((size * SIDE, LANES), jnp.float32) for size in sizes]

    def pairs(self, body):
        if self.side == SIDE:
            rolled(self.side // 2, lambda i: body(2 * i))
        else:
            for i in range(self.side // 2):
                body(2 * i)

    def prepare(self):
        n = self.side
        cond = self.cond

        def plane(x):
            for z in range(n):
                here, ahead, next_x = cond[x, z], cond[x, z + 1], cond[x + 1, z]
                after = inside_up(block_up(here[:1], 1), 1)
                before = inside_down(block_down(here[-1:], 1), 1)
                next_y = jnp.concatenate([here[1:], after])
                last_y = jnp.concatenate([before, here[:-1]])
                total = (next_x + cond[x - 1, z]) + (ahead + cond[x, z - 1]) + (next_y + last_y)
                total = 3.0 * here + 0.5 * total
                self.weight[x, z] = DAMPING / total
                self.back[x, z] = total * (self.scale / DAMPING)
                self.link_x[x, z] = 0.5 * (here + next_x)
                link = 0.5 * (here + next_y)
                self.link_y[x, z] = jnp.concatenate([link[:-1], inside_up(link[-1:], 1)])
                link = 0.5 * (here + ahead)
                if z == n - 1:
                    link = inside_up(link, 2)
                    self.link_z[x, -1] = block_down(link, 2)
                self.link_z[x, z] = link

        if n == SIDE:
            rolled(n, plane)
        else:
            for x in range(n):
                plane(x)
        for z in range(n):
            link = inside_up(self.link_x[n - 1, z], 0)
            self.link_x[n - 1, z] = link
            self.link_x[-1, z] = block_down(link, 0)

    def flows(self, x, z, here, ahead, outer, down):
        result = []
        inner = self.link_x[x, z]
        sides = [
            self.link_x[x - 1, z] * outer[0] + inner * here[1],
            inner * here[0] + self.link_x[x + 1, z] * outer[1],
        ]
        for p in range(2):
            link_y, link_z = self.link_y[x + p, z], self.link_z[x + p, z]
            along = link_y * next_in_y(here[p]) + last_in_y(link_y * here[p])
            total = sides[p] + (link_z * ahead[p] + down[p]) + along
            down[p] = link_z * here[p]
            result.append(self.weight[x + p, z] * total)
        return result

    def rows(self, field, x):
        here = [field[x, 0], field[x + 1, 0]]
        down = [self.link_z[x + p, -1] * field[x + p, -1] for p in range(2)]
        for z in range(self.side):
            ahead = [field[x, z + 1], field[x + 1, z + 1]]
            outer = [field[x - 1, z], field[x + 2, z]]
            yield z, here, self.flows(x, z, here, ahead, outer, down)
            here = ahead

    def sweep(self, field, out, exact=False):
        def pair(x):
            for z, here, sums in self.rows(field, x):
                for p in range(2):
                    if field is self.base:
                        value = (2.0 - DAMPING) * here[p] + sums[p]
                    else:
                        value = (1.0 - DAMPING) * here[p] + (self.base[x + p, z] + sums[p])
                    out.put(x + p, z, value, exact)

        self.pairs(pair)
        out.close(exact)

    def halve(self, rows, coarse):
        def pair(x):
            held = None
            for z, row in enumerate(rows(x)):
                row = row[0] + row[1]
                if z % 2 == 0:
                    held = row
                else:
                    coarse(x // 2, z // 2, 0.125 * pair_rows(held + row))

        self.pairs(pair)

    def descend(self, coarse):
        self.sweep(self.base, self.second)

        def residuals(x):
            for z, here, sums in self.rows(self.second, x):
                result = []
                for p in range(2):
                    total = self.base[x + p, z] + sums[p]
                    self.first[x + p, z] = (1.0 - DAMPING) * here[p] + total
                    result.append((total - DAMPING * here[p]) * self.back[x + p, z])
                yield result

        self.halve(residuals, coarse)

    def ascend(self, correction, out, exact=False):
        def pair(x):
            i = x // 2
            here = twice(correction(i, 0))
            start = twice(correction(i, -1))
            down = [self.link_z[x + p, -1] * start for p in range(2)]
            for z in range(self.side):
                ahead = twice(correction(i, (z + 1) // 2))
                outer = [twice(correction(i - 1, z // 2)), twice(correction(i + 1, z // 2))]
                sums = self.flows(x, z, [here, here], [ahead, ahead], outer, down)
                for p in range(2):
                    value = self.first[x + p, z] + ((1.0 - DAMPING) * here + sums[p])
                    self.second.put(x + p, z, value)
                here = ahead

        self.pairs(pair)
        self.second.close()
        self.sweep(self.second, out, exact)


class HeldLevel:
    def __init__(self, refs, index):
        self.side = 2
        self.scale = 0.25**index
        self.cond, self.first = Edged(refs[0], 2), Edged(refs[1], 2)
        self.weight, self.back = Rows(refs[2], 2), Rows(refs[3], 2)
        self.links = [Rows(ref, 2) for ref in refs[4:]]

    @staticmethod
    def scratch(index):
        sizes = [4**3] * 2 + [2**3] * 8
        return [pltpu.VMEM((size * SIDE, LANES), jnp.float32) for size in sizes]

    def around(self, field, inside=False):
        def moved(row, axis, up):
            row = (block_up if up else block_down)(row, axis)
            return (inside_up if up else inside_down)(row, axis) if inside else row

        result = {}
        for (x, z), here in field.items():
            result[x, z] = [
                field[1, z] if x == 0 else moved(field[0, z], 0, True),
                field[0, z] if x == 1 else moved(field[1, z], 0, False),
                jnp.concatenate([here[1:], moved(here[:1], 1, True)]),
                jnp.concatenate([moved(here[-1:], 1, False), here[:-1]]),
                field[x, 1] if z == 0 else moved(field[x, 0], 2, True),
                field[x, 0] if z == 1 else moved(field[x, 1], 2, False),
            ]
        return result

    def prepare(self):
        field = {(x, z): self.cond[x, z] for x in range(2) for z in range(2)}
        for at, others in self.around(field, inside=True).items():
            here = field[at]
            total = others[0]
            for other in others[1:]:
                total = total + other
            total = 3.0 * here + 0.5 * total
            inverse = DAMPING / total
            self.weight[at] = inverse
            self.back[at] = total * (self.scale / DAMPING)
            for index, other in enumerate(others):
                link = 0.5 * inverse * (here + other)
                self.links[index][at] = jnp.where(other > 0.0, link, 0.0)

    def halve(self, rows, coarse):
        total = None
        for row in rows(0):
            row = row[0] + row[1]
            total = row if total is None else total + row
        coarse(0, 0, 0.125 * (total[:1] + total[1:]))

    def sums(self, field, base):
        result = {}
        for at, others in self.around(field).items():
            total = base[at]
            for link, other in zip(self.links, others):
                total = total + link[at] * other
            result[at] = total
        return result

    def swept(self, field, base):
        sums = self.sums(field, base)
        return {at: (1.0 - DAMPING) * field[at] + sums[at] for at in field}

    def cycle(self, base, solve, out):
        field = self.swept(base, base)
        sums = self.sums(field, base)
        total = None
        for at in field:
            residual = (sums[at] - DAMPING * field[at]) * self.back[at]
            total = residual if total is None else total + residual
        solved = solve(0.125 * (total[:1] + total[1:]))
        row = twice(solved)
        copied = {at: row for at in field}
        change = {at: sums[at] + (1.0 - DAMPING) * (field[at] + row) for at in field}
        field = self.sums(copied, change)
        for (x, z), value in self.swept(field, base).items():
            out.put(x, z, value)
        out.close()


def replicated_kernel(
    whole,
    halved,
    cells_ref,
    *refs,
):
    parts = refs[:whole], refs[whole : whole + halved]
    solve_kernel(*parts, cells_ref, *refs[whole + halved :])


def solve_kernel(
    part_refs,
    half_refs,
    cells_ref,
    spot_ref,
    rows_ref,
    same_ref,
    pairs_ref,
    observed_ref,
    potentials_ref,
    mine_ref,
    theirs_ref,
    gathered,
    weights,
    owned,
    *level_refs,
):
    f32 = jnp.float32
    electrodes = spot_ref.shape[1]
    levels, used = [], 0
    for index in range(LEVELS - 1):
        kind = HeldLevel if index == LEVELS - 2 else Level
        count = len(kind.scratch(index))
        levels.append(kind(level_refs[used : used + count], index))
        used += count
    fine = levels[0]
    forward = fine.cond
    wide = SIDE * SIDE * SIDE

    device, shot = own_place()

    def place(part, row, x, index):
        for z in range(SIDE):
            fine.cond.ref[pl.ds(fine.cond.start(x, z) + index, SIDE, stride=SIDE), :] = part[
                pl.ds((row * SIDE + z) * SIDE, SIDE), :
            ]

    def collect(x):
        for k, part in enumerate(part_refs):
            place(part, x, x, device ^ k)

    def collect_half(x):
        for k, part in enumerate(half_refs):
            swapped, index = k // 2 % 2, len(part_refs) + k // 4 * 2 + k % 2
            place(part, x, (shot ^ swapped) * (SIDE // 2) + x, device ^ index)

    def edges(x):
        fine.cond.close_z(x, exact=True)

    rolled(SIDE, collect)
    for x in range(SIDE // 2):
        collect_half(x)
    rolled(SIDE, edges)
    fine.cond.close(exact=True)

    coarsest = []
    for level, below in zip(levels, levels[1:] + [None]):
        level.prepare()

        def coarse(x, z, row, below=below):
            if below is None:
                coarsest.append(row)
            else:
                below.cond.put(x, z, row, exact=True)

        level.halve(
            lambda x, level=level: [
                (level.cond[x, z], level.cond[x + 1, z]) for z in range(level.side)
            ],
            coarse,
        )
        if below is not None:
            below.cond.close(exact=True)

    keep = iota((1, SIDE, LANES), 1) % 2 == 0
    lane = iota((1, SIDE, LANES), 2)

    def split(value):
        return [jnp.where(keep, part, 0.0) for part in (value, pltpu.roll(value, SIDE - 1, 1))]

    def around(value):
        low, high = value
        low_up, high_up = [pltpu.roll(part, LANES - GROUP, 2) for part in value]
        low_down, high_down = [pltpu.roll(part, GROUP, 2) for part in value]
        along = [[move(part, axis) for part in value] for axis in (0, 2) for move in (block_up, block_down)]
        return along + [
            [jnp.where(lane < LANES - GROUP, low_up, high_up), high_up],
            [low_down, jnp.where(lane >= GROUP, high_down, low_down)],
        ]

    sub = iota((1, SIDE, LANES), 1)
    inside_last = [
        [sub < 6] * 2,
        [sub >= 2] * 2,
        [lane % GROUP < GROUP - 1] * 2,
        [lane % GROUP > 0] * 2,
        [keep, lane < LANES - GROUP],
        [lane >= GROUP, keep],
    ]
    last_scale = 0.25 ** (LEVELS - 1)
    here = split(coarsest[0])
    others = [
        [jnp.where(inside & keep, part, 0.0) for inside, part in zip(pair, moved)]
        for pair, moved in zip(inside_last, around(here))
    ]
    last_weight, last_links = [], []
    for half, part in enumerate(here):
        total = 3.0 * part
        for other in others:
            total = total + 0.5 * other[half]
        inverse = jnp.where(keep, DAMPING / jnp.where(keep, total, 1.0), 0.0)
        last_weight.append(inverse * (1.0 / last_scale))
        last_links.append(
            [
                jnp.where(pair[half] & keep, 0.5 * inverse * (part + other[half]), 0.0)
                for pair, other in zip(inside_last, others)
            ]
        )

    def solve_last(rhs):
        base = [weight * part for weight, part in zip(last_weight, split(rhs))]
        value = base
        for _ in range(COARSE_SWEEPS - 1):
            moved = around(value)
            fresh = []
            for half in range(2):
                parts = [link * other[half] for link, other in zip(last_links[half], moved)]
                start = base[half] + (1.0 - DAMPING) * value[half]
                fresh.append(((start + parts[0]) + (parts[1] + parts[2])) + (parts[3] + (parts[4] + parts[5])))
            value = fresh
        return value[0] + pltpu.roll(value[1], 1, 1)

    def cycle(index, out, exact=False):
        level = levels[index]
        below = levels[index + 1]
        if index == LEVELS - 3:
            base = {}

            def take(x, z, row):
                base[x, z] = below.weight[x, z] * (row * (1.0 / below.scale))

            level.descend(take)
            below.cycle(base, solve_last, below.first)
        else:
            level.descend(
                lambda x, z, row: below.base.put(
                    x, z, below.weight[x, z] * (row * (1.0 / below.scale))
                )
            )
            below.base.close()
            cycle(index + 1, below.first)
        level.ascend(lambda x, z: below.first[x, z], out, exact)

    spot = spot_ref[...]

    def each(body):
        def one(electrode, carry):
            body(pl.ds(electrode, 1), pl.ds(cells_ref[0, electrode], 1))
            return carry

        lax.fori_loop(0, electrodes, one, 0, unroll=32)

    def weigh(electrode, cell):
        weights[electrode, :] = fine.weight.ref[cell, :]

    each(weigh)
    fine.base.ref[...] = jnp.zeros_like(fine.base.ref)

    def spread(rows):
        gathered[...] = rows * weights[...]

        def put(electrode, cell):
            fine.base.ref[cell, :] = gathered[electrode, :]

        each(put)
        rolled(SIDE, fine.base.close_z)
        fine.base.close()

    spread(rows_ref[...])
    cycle(0, forward, exact=True)

    def read(electrode, cell):
        gathered[electrode, :] = forward.ref[cell, :]

    each(read)
    at_spot = iota((LANES, electrodes), 0) == spot
    readings = jnp.sum(jnp.where(at_spot, gathered[...].T, 0.0), axis=0, keepdims=True)
    pairs = pairs_ref[...]

    def exact(row, dims):
        return product(jnp.broadcast_to(row, (16, row.shape[1])), pairs, 3, dims)[0:1]

    misfit = exact(readings, ((1,), (1,))) - observed_ref[...]
    spread(shared_rows(exact(misfit, ((1,), (0,))), spot, same_ref[...]))
    cycle(0, fine.first, exact=True)

    order = lane_order()
    adjoint = fine.first
    chunk = mine_ref.shape[1]
    even = shot == 0

    def own(field, x, z, y=0):
        return field.ref[pl.ds(field.start(x, z, y) + device, SIDE, stride=SIDE), :]

    wide = SIDE + 2
    for index, field in enumerate((forward, adjoint)):
        for x in range(-1, SIDE + 1):
            for z in range(-1, SIDE + 1):
                if 0 <= x < SIDE or 0 <= z < SIDE:
                    owned[index, (x + 1) * wide + z + 1] = own(field, x, z)

    for x in range(SIDE):
        tiles_u, tiles_g = [], []
        for z in range(SIDE):
            at = (x + 1) * wide + z + 1
            here_u, here_w = owned[0, at], owned[1, at]
            total = None
            for step in (wide, -wide, 1, -1):
                term = (here_u - owned[0, at + step]) * (here_w - owned[1, at + step])
                total = term if total is None else total + term
            for y in (1, -1):
                total = total + (here_u - own(forward, x, z, y)) * (here_w - own(adjoint, x, z, y))
            tiles_u.append(here_u)
            tiles_g.append(-0.5 * total)
        potentials_ref[x] = from_blocks(tiles_u, order)
        natural = from_blocks(tiles_g, order)
        low, high = natural[:chunk], natural[chunk:]
        mine_ref[x] = jnp.where(even, low, high)
        theirs_ref[x] = jnp.where(even, high, low)


def replicated(conductivity, stations, currents, receivers, observed):
    rows, cols, depth = conductivity.shape
    f32 = jnp.float32
    electrodes = stations.shape[0]
    total = rows * cols
    vmem = pl.BlockSpec(memory_space=pltpu.VMEM)
    smem = pl.BlockSpec(memory_space=pltpu.SMEM)
    station_row = stations.reshape(1, electrodes)
    mine, half = pl.pallas_call(
        to_blocks_kernel,
        out_shape=(
            jax.ShapeDtypeStruct((total, LANES), f32),
            jax.ShapeDtypeStruct((total // 2, LANES), f32),
        ),
        in_specs=[vmem],
        out_specs=(vmem, vmem),
        compiler_params=pltpu.CompilerParams(vmem_limit_bytes=SMALL_BYTES),
    )(conductivity)
    swap = [(0, 1), (1, 0)]

    def partner(part, k):
        count = lax.axis_size("gx")
        return lax.ppermute(part, "gx", [(i, i ^ k) for i in range(count)])

    def with_mate(part):
        return [part, lax.ppermute(part, "gy", swap)]

    far = partner(half, 2)
    near = partner(mine, 1)
    line = jax.ShapeDtypeStruct((1, electrodes), jnp.int32)
    cells, spot, rows_of, same, pairs, held = pl.pallas_call(
        electrode_kernel,
        out_shape=(
            line,
            line,
            jax.ShapeDtypeStruct((electrodes, LANES), f32),
            jax.ShapeDtypeStruct((electrodes, electrodes), jnp.bfloat16),
            jax.ShapeDtypeStruct((receivers.shape[0], electrodes), jnp.bfloat16),
            jax.ShapeDtypeStruct(observed.shape, f32),
        ),
        in_specs=[vmem] * 4,
        out_specs=(vmem,) * 6,
        compiler_params=pltpu.CompilerParams(vmem_limit_bytes=SMALL_BYTES),
        cost_estimate=pl.CostEstimate(flops=100_000_000, bytes_accessed=1_000_000, transcendentals=0),
    )(station_row, currents, receivers, observed)
    far, rows_of = lax.optimization_barrier((far, rows_of))
    far = [far, partner(far, 1)]
    halved = [piece for own in far for piece in (own, lax.ppermute(own, "shot", swap))]
    parts = [piece for own in (mine, near) for piece in with_mate(own)]
    halved = [piece for own in halved for piece in with_mate(own)]
    chunk = cols // 2
    levels = [shape for index in range(LEVELS - 2) for shape in Level.scratch(index)]
    levels += HeldLevel.scratch(LEVELS - 2)
    potentials, own, theirs = pl.pallas_call(
        functools.partial(replicated_kernel, len(parts), len(halved)),
        out_shape=(
            jax.ShapeDtypeStruct((rows, cols, LANES), f32),
            jax.ShapeDtypeStruct((rows, chunk, LANES), f32),
            jax.ShapeDtypeStruct((rows, chunk, LANES), f32),
        ),
        in_specs=[smem] + [vmem] * (len(parts) + len(halved) + 5),
        out_specs=(vmem, vmem, vmem),
        scratch_shapes=[
            pltpu.VMEM((electrodes, LANES), f32),
            pltpu.VMEM((electrodes, LANES), f32),
            pltpu.VMEM((2, (SIDE + 2) ** 2, SIDE, LANES), f32),
        ]
        + levels,
        compiler_params=pltpu.CompilerParams(vmem_limit_bytes=VMEM_BYTES),
        cost_estimate=pl.CostEstimate(flops=200_000_000, bytes_accessed=4_000_000, transcendentals=0),
    )(cells, *parts, *halved, spot, rows_of, same, pairs, held)
    return potentials[None], own + lax.ppermute(theirs, "shot", swap)


def extended(array, sides, width):
    for axis, dim in sides:
        size, length = (lax.axis_size(axis), array.shape[dim])
        up = [(i, (i + 1) % size) for i in range(size - 1)]
        down = [(j, i) for i, j in up]
        last = lax.slice_in_dim(array, length - width, length, axis=dim)
        leading = lax.slice_in_dim(array, 0, width, axis=dim)
        before = lax.ppermute(last, axis, up)
        after = lax.ppermute(leading, axis, down)
        array = jnp.concatenate([before, array, after], axis=dim)
    return array


def upper_z(field):
    return jnp.concatenate([field[..., 1:], jnp.zeros_like(field[..., :1])], axis=-1)


def lower_z(field):
    return jnp.concatenate([jnp.zeros_like(field[..., :1]), field[..., :-1]], axis=-1)


def trim_circle(field, circle_width):
    return field[..., circle_width:-circle_width, circle_width:-circle_width, :]


def pad_plane(field, circle_width):
    spec = [(0, 0)] * (field.ndim - 3) + [
        (circle_width, circle_width),
        (circle_width, circle_width),
        (0, 0),
    ]
    return jnp.pad(field, spec)


def neighbour_list(field_pad):
    centre = trim_circle(field_pad, 1)
    return [
        field_pad[..., 2:, 1:-1, :],
        field_pad[..., :-2, 1:-1, :],
        field_pad[..., 1:-1, 2:, :],
        field_pad[..., 1:-1, :-2, :],
        upper_z(centre),
        lower_z(centre),
    ]


def stencil(field_pad, cond_pad, level_scale):
    centre = trim_circle(field_pad, 1)
    centre_cond = trim_circle(cond_pad, 1)
    summed = jnp.zeros_like(centre)
    for other, other_cond in zip(neighbour_list(field_pad), neighbour_list(cond_pad)):
        summed = summed + level_scale * 0.5 * (centre_cond + other_cond) * (centre - other)
    return summed


def diagonal(cond_pad, level_scale):
    centre_cond = trim_circle(cond_pad, 1)
    summed = jnp.zeros_like(centre_cond)
    for other_cond in neighbour_list(cond_pad):
        summed = summed + level_scale * 0.5 * (centre_cond + other_cond)
    return summed


def relaxed(field_pad, source, cond_pad, diag_level, level_scale):
    return (
        trim_circle(field_pad, 1)
        + DAMPING * (source - stencil(field_pad, cond_pad, level_scale)) / diag_level
    )


def restrict(field):
    leading = field.shape[:-3]
    extent = field.shape[-3:]
    shaped = field.reshape(leading + (extent[0] // 2, 2, extent[1] // 2, 2, extent[2] // 2, 2))
    return shaped.mean(axis=(-5, -3, -1))


def prolong(field):
    return jnp.repeat(jnp.repeat(jnp.repeat(field, 2, axis=-3), 2, axis=-2), 2, axis=-1)


def assemble(blocks, count_x, count_y):
    leading = blocks.shape[1:-3]
    extent = blocks.shape[-3:]
    depth_lead = len(leading)
    shaped = blocks.reshape((count_x, count_y) + leading + extent)
    order = tuple(range(2, 2 + depth_lead)) + (0, 2 + depth_lead, 1, 3 + depth_lead, 4 + depth_lead)
    return shaped.transpose(order).reshape(
        leading + (count_x * extent[0], count_y * extent[1], extent[2])
    )


def field_rim(field):
    return extended(field, (("gx", 1), ("gy", 2)), 1)


def cond_rim(conduct):
    return extended(conduct, (("gx", 0), ("gy", 1)), 1)


def whole_cycle(source, level_index, whole_plans):
    cond_pad, diag_level, level_scale = whole_plans[level_index]
    field = DAMPING * source / diag_level

    def turn(turn_index, iterate):
        return relaxed(pad_plane(iterate, 1), source, cond_pad, diag_level, level_scale)

    return lax.fori_loop(0, COARSE_SWEEPS - 1, turn, field)


def part_cycle(source, level_index, level_plans, whole_plans, gather_level):
    if level_index == gather_level:
        blocks = lax.all_gather(source[None], ("gx", "gy"), axis=0, tiled=True)
        whole = assemble(blocks, lax.axis_size("gx"), lax.axis_size("gy"))
        correction = whole_cycle(whole, level_index, whole_plans)
        extent = source.shape
        starts = (0, lax.axis_index("gx") * extent[1], lax.axis_index("gy") * extent[2], 0)
        return lax.dynamic_slice(correction, starts, extent)
    cond_pad, diag_level, level_scale = level_plans[level_index]
    field = DAMPING * source / diag_level
    field = relaxed(field_rim(field), source, cond_pad, diag_level, level_scale)
    residual = source - stencil(field_rim(field), cond_pad, level_scale)
    field = field + prolong(
        part_cycle(restrict(residual), level_index + 1, level_plans, whole_plans, gather_level)
    )
    field = relaxed(field_rim(field), source, cond_pad, diag_level, level_scale)
    return relaxed(field_rim(field), source, cond_pad, diag_level, level_scale)


def distributed(conductivity, stations, currents, receivers, observed):
    row_count, col_count, z_count = conductivity.shape
    shot_count = currents.shape[0]
    count_x = lax.axis_size("gx")
    count_y = lax.axis_size("gy")
    gather_level = LEVELS - 1
    level_plans = []
    conduct = conductivity
    for level_index in range(gather_level):
        level_scale = 0.25**level_index
        cond_pad = cond_rim(conduct)
        level_plans.append((cond_pad, diagonal(cond_pad, level_scale), level_scale))
        conduct = restrict(conduct)
    blocks = lax.all_gather(conduct[None], ("gx", "gy"), axis=0, tiled=True)
    whole = assemble(blocks, count_x, count_y)
    whole_plans = {}
    level_index = 3
    level_scale = 0.25**level_index
    cond_pad = pad_plane(whole, 1)
    whole_plans[level_index] = (cond_pad, diagonal(cond_pad, level_scale), level_scale)
    total_y = col_count * count_y
    cell_x = stations // (total_y * z_count)
    cell_y = stations // z_count % total_y
    cell_z = stations % z_count
    local_x = cell_x - lax.axis_index("gx") * row_count
    local_y = cell_y - lax.axis_index("gy") * col_count
    owned = (local_x >= 0) & (local_x < row_count) & (local_y >= 0) & (local_y < col_count)
    block_size = row_count * col_count * z_count
    local_cell = jnp.where(owned, (local_x * col_count + local_y) * z_count + cell_z, 0)
    offsets = jnp.arange(shot_count)[:, None] * block_size + local_cell[None, :]
    targets = jnp.where(owned[None, :], offsets, shot_count * block_size).reshape(-1)

    def spread(amounts):
        flat = (
            jnp.zeros((shot_count * block_size,), jnp.float32)
            .at[targets]
            .add(amounts.reshape(-1), mode="drop")
        )
        return flat.reshape(shot_count, row_count, col_count, z_count)

    potentials = part_cycle(spread(currents), 0, level_plans, whole_plans, gather_level)
    local_values = jnp.where(
        owned[None, :], potentials.reshape(shot_count, block_size)[:, local_cell], 0.0
    )
    readings = lax.psum(local_values, ("gx", "gy"))
    positions = jnp.arange(stations.shape[0])[:, None]
    pairs = (receivers[:, 0][None, :] == positions).astype(jnp.float32) - (
        receivers[:, 1][None, :] == positions
    ).astype(jnp.float32)
    misfit = jnp.dot(readings, pairs, precision=lax.Precision.HIGHEST) - observed
    back_source = jnp.dot(misfit, pairs.T, precision=lax.Precision.HIGHEST)
    adjoint = part_cycle(spread(back_source), 0, level_plans, whole_plans, gather_level)
    stacked = jnp.concatenate([potentials, adjoint], axis=0)
    padded = extended(stacked, (("gx", 1), ("gy", 2)), 1)
    potential_pad = padded[:shot_count]
    adjoint_pad = padded[shot_count:]
    gradient = jnp.zeros_like(potentials)
    for other_u, other_w in zip(neighbour_list(potential_pad), neighbour_list(adjoint_pad)):
        gradient = gradient - 0.5 * (potentials - other_u) * (adjoint - other_w)
    summed = lax.psum_scatter(jnp.sum(gradient, axis=0), "shot", scatter_dimension=1, tiled=True)
    return (potentials, summed)


def per_device(conductivity, stations, currents, receivers, observed):
    blocks = lax.axis_size("gx") * lax.axis_size("gy")
    fits = conductivity.shape == (SIDE, SIDE * SIDE, LANES) and blocks == SIDE
    fits = fits and lax.axis_size("gy") == 2 and lax.axis_size("shot") == 2
    fits = fits and currents.shape[0] == 1
    plan = replicated if fits else distributed
    return plan(conductivity, stations, currents, receivers, observed)


def solution(mesh):
    in_specs = (
        P(("grp", "gx"), "gy", None),
        P("grp"),
        P(("grp", "shot"), None),
        P("grp", None),
        P(("grp", "shot"), None),
    )
    out_specs = (P(("grp", "shot"), "gx", "gy", None), P(("grp", "gx"), ("gy", "shot"), None))
    return jax.shard_map(
        per_device, mesh=mesh, in_specs=in_specs, out_specs=out_specs, check_vma=False
    )
```

```python
import functools

import jax
import jax.numpy as jnp
from jax import lax
from jax.experimental import pallas as pl
from jax.experimental.pallas import tpu as pltpu
from jax.sharding import PartitionSpec as P

LEVELS = 4
COARSE_SWEEPS = 16


DAMPING = 0.8

SIDE = 8
LANES = 128
GROUP = 16
VMEM_BYTES = 48 * 2**20
SMALL_BYTES = 6 * 2**20


def pieces_of(value, count):
    pieces = []
    for _ in range(count):
        pieces.append(value.astype(jnp.bfloat16))
        value = value - pieces[-1].astype(jnp.float32)
    return pieces[::-1]


def product(value, matrix, count, dims=((1,), (0,))):
    result = None
    for piece in pieces_of(value, count):
        term = lax.dot_general(
            piece, matrix, (dims, ((), ())), preferred_element_type=jnp.float32
        )
        result = term if result is None else result + term
    return result


def iota(shape, dim):
    return lax.broadcasted_iota(jnp.int32, shape, dim)


def station_table(station):
    cell_x, cell_y, cell_z = station >> 14, station >> 7 & 127, station & 127
    row = (cell_x >> 3) * 2 + (cell_y >> 6)
    return cell_x, cell_y, cell_z, row, (cell_y >> 3 & 7) * GROUP + (cell_z >> 3)


def lane_order():
    row, col = iota((LANES, LANES), 0), iota((LANES, LANES), 1)
    chosen = row == col % GROUP * SIDE + col // GROUP
    return jnp.where(chosen, 1.0, 0.0).astype(jnp.bfloat16)


def exchange_groups(tiles):
    tiles = list(tiles)
    group = iota(tiles[0].shape, 1) // GROUP
    for bit in range(3):
        step = 1 << bit
        keep = (group & step) == 0
        for low in range(SIDE):
            if low & step == 0:
                a, b = tiles[low], tiles[low | step]
                tiles[low] = jnp.where(keep, a, pltpu.roll(b, step * GROUP, 1))
                tiles[low | step] = jnp.where(keep, pltpu.roll(a, LANES - step * GROUP, 1), b)
    return tiles


def own_place():
    return lax.axis_index("gx") * 2 + lax.axis_index("gy"), lax.axis_index("shot")


def to_blocks_kernel(natural_ref, blocks_ref, half_ref):
    order = lane_order()
    for x in range(SIDE):
        tiles = product(natural_ref[x], order, 3)
        tiles = [tiles[SIDE * k : SIDE * (k + 1)] for k in range(SIDE)]
        for z, tile in enumerate(exchange_groups(tiles)):
            blocks_ref[pl.ds((x * SIDE + z) * SIDE, SIDE), :] = tile
    count = half_ref.shape[0]
    low, high = blocks_ref[pl.ds(0, count), :], blocks_ref[pl.ds(count, count), :]
    half_ref[...] = jnp.where(own_place()[1] == 0, low, high)


def from_blocks(tiles, order):
    natural = jnp.concatenate(exchange_groups(tiles), axis=0)
    return product(natural, order, 3, ((1,), (1,)))


def block_up(field, axis):
    if axis == 0:
        return pltpu.roll(field, 6, 1)
    if axis == 2:
        return pltpu.roll(field, LANES - 1, 2)
    turned = pltpu.roll(field, LANES - GROUP, 2)
    return jnp.where(iota(field.shape, 2) < LANES - GROUP, turned, pltpu.roll(turned, 7, 1))


def block_down(field, axis):
    if axis == 0:
        return pltpu.roll(field, 2, 1)
    if axis == 2:
        return pltpu.roll(field, 1, 2)
    turned = pltpu.roll(field, GROUP, 2)
    return jnp.where(iota(field.shape, 2) >= GROUP, turned, pltpu.roll(turned, 1, 1))


def inside_up(field, axis):
    sub, lane = iota(field.shape, 1), iota(field.shape, 2)
    if axis == 0:
        keep = sub < 6
    elif axis == 1:
        keep = (lane < LANES - GROUP) | (sub % 2 == 0)
    else:
        keep = lane % GROUP < GROUP - 1
    return jnp.where(keep, field, 0.0)


def inside_down(field, axis):
    sub, lane = iota(field.shape, 1), iota(field.shape, 2)
    if axis == 0:
        keep = sub >= 2
    elif axis == 1:
        keep = (lane >= GROUP) | (sub % 2 == 1)
    else:
        keep = lane % GROUP > 0
    return jnp.where(keep, field, 0.0)


def pair_rows(row):
    count = row.shape[0] // 2
    return jnp.concatenate([row[2 * i : 2 * i + 1] + row[2 * i + 1 : 2 * i + 2] for i in range(count)])


def twice(row):
    return jnp.concatenate([row[i // 2 : i // 2 + 1] for i in range(2 * row.shape[0])])


def electrode_kernel(
    stations_ref,
    currents_ref,
    receivers_ref,
    observed_ref,
    cells_ref,
    spot_ref,
    rows_ref,
    same_ref,
    pairs_ref,
    held_ref,
):
    stations = stations_ref[...]
    electrodes = stations.shape[1]
    cell_x, cell_y, cell_z, row, spot = station_table(stations)
    wide = SIDE + 2
    register = (((cell_x & 7) + 1) * wide + (cell_z & 7) + 1) * wide + (cell_y & 7) + 1
    cells_ref[...] = register * SIDE + row
    spot_ref[...] = spot
    held_ref[...] = observed_ref[...]
    line = stations & 0x1C387 | row << 20
    same = jnp.broadcast_to(line, (electrodes, electrodes))
    same = jnp.where(same == same.T, 1.0, 0.0).astype(jnp.bfloat16)
    same_ref[...] = same
    rows_ref[...] = shared_rows(currents_ref[...], spot, same)
    receivers = receivers_ref[...]
    numbers = iota((receivers.shape[0], electrodes), 1)
    pairs = jnp.where(numbers == receivers[:, 0:1], 1.0, 0.0) - jnp.where(
        numbers == receivers[:, 1:2], 1.0, 0.0
    )
    pairs_ref[...] = pairs.astype(jnp.bfloat16)


def shared_rows(amounts, spot, same):
    electrodes = amounts.shape[1]
    at_spot = iota((LANES, electrodes), 0) == spot
    return product(jnp.where(at_spot, amounts, 0.0), same, 3).T


class Edged:
    def __init__(self, ref, side):
        self.ref, self.side = ref, side

    def start(self, x, z, y=0):
        wide = self.side + 2
        return (((x + 1) * wide + z + 1) * wide + y + 1) * SIDE

    def __getitem__(self, at):
        x, z = at
        rows = self.ref[pl.ds(self.start(x, z), self.side * SIDE), :]
        return rows.reshape(self.side, SIDE, LANES)

    def __setitem__(self, at, value):
        x, z = at
        self.ref[pl.ds(self.start(x, z), self.side * SIDE), :] = value.reshape(-1, LANES)

    def put(self, x, z, value, exact=False):
        self[x, z] = value
        n = self.side
        if z == 0:
            edge = block_up(value, 2)
            self[x, n] = inside_up(edge, 2) if exact else edge
        if z == n - 1:
            edge = block_down(value, 2)
            self[x, -1] = inside_down(edge, 2) if exact else edge
        if exact:
            after = inside_up(block_up(value[:1], 1), 1)
            self.ref[pl.ds(self.start(x, z, n), SIDE), :] = after[0]
            before = inside_down(block_down(value[n - 1 :], 1), 1)
            self.ref[pl.ds(self.start(x, z, -1), SIDE), :] = before[0]

    def close_z(self, x, exact=False):
        n = self.side
        after, before = block_up(self[x, 0], 2), block_down(self[x, n - 1], 2)
        self[x, n] = inside_up(after, 2) if exact else after
        self[x, -1] = inside_down(before, 2) if exact else before

    def close(self, exact=False):
        n = self.side
        for z in range(n):
            after = block_up(self[0, z], 0)
            self[n, z] = inside_up(after, 0) if exact else after
            before = block_down(self[n - 1, z], 0)
            self[-1, z] = inside_down(before, 0) if exact else before


class Rows:
    def __init__(self, ref, side, first_x=0, first_z=0):
        self.ref, self.side, self.first_x, self.first_z = ref, side, first_x, first_z

    def place(self, at):
        count = self.side - self.first_z
        rows = self.side * SIDE
        return pl.ds(((at[0] - self.first_x) * count + at[1] - self.first_z) * rows, rows)

    def __getitem__(self, at):
        return self.ref[self.place(at), :].reshape(self.side, SIDE, LANES)

    def __setitem__(self, at, value):
        self.ref[self.place(at), :] = value.reshape(-1, LANES)


def rolled(count, body):
    def one(x, carry):
        body(x)
        return carry

    lax.fori_loop(0, count, one, 0)


def next_in_y(row):
    return jnp.concatenate([row[1:], block_up(row[:1], 1)])


def last_in_y(row):
    return jnp.concatenate([block_down(row[-1:], 1), row[:-1]])


class Level:
    def __init__(self, refs, index):
        self.side = side = SIDE >> index
        self.scale = 0.25**index
        edged = [Edged(ref, side) for ref in refs[:5]]
        self.cond, self.first, self.second, self.base, self.weight = edged
        self.link_x = Rows(refs[5], side, first_x=-1)
        self.link_y = Rows(refs[6], side)
        self.link_z = Rows(refs[7], side, first_z=-1)
        self.back = Rows(refs[8], side)

    @staticmethod
    def scratch(index):
        side = SIDE >> index
        sizes = [(side + 2) ** 3] * 5
        sizes += [side**2 * (side + 1), side**3, side**2 * (side + 1), side**3]
        return [pltpu.VMEM((size * SIDE, LANES), jnp.float32) for size in sizes]

    def pairs(self, body):
        if self.side == SIDE:
            rolled(self.side // 2, lambda i: body(2 * i))
        else:
            for i in range(self.side // 2):
                body(2 * i)

    def prepare(self):
        n = self.side
        cond = self.cond

        def plane(x):
            for z in range(n):
                here, ahead, next_x = cond[x, z], cond[x, z + 1], cond[x + 1, z]
                after = inside_up(block_up(here[:1], 1), 1)
                before = inside_down(block_down(here[-1:], 1), 1)
                next_y = jnp.concatenate([here[1:], after])
                last_y = jnp.concatenate([before, here[:-1]])
                total = (next_x + cond[x - 1, z]) + (ahead + cond[x, z - 1]) + (next_y + last_y)
                total = 3.0 * here + 0.5 * total
                self.weight[x, z] = DAMPING / total
                if n == SIDE:
                    self.base[x, z] = jnp.zeros_like(here)
                self.back[x, z] = total * (self.scale / DAMPING)
                self.link_x[x, z] = 0.5 * (here + next_x)
                link = 0.5 * (here + next_y)
                self.link_y[x, z] = jnp.concatenate([link[:-1], inside_up(link[-1:], 1)])
                link = 0.5 * (here + ahead)
                if z == n - 1:
                    link = inside_up(link, 2)
                    self.link_z[x, -1] = block_down(link, 2)
                self.link_z[x, z] = link

        if n == SIDE:
            rolled(n, plane)
        else:
            for x in range(n):
                plane(x)
        for z in range(n):
            link = inside_up(self.link_x[n - 1, z], 0)
            self.link_x[n - 1, z] = link
            self.link_x[-1, z] = block_down(link, 0)

    def flows(self, x, z, here, ahead, outer, down):
        result = []
        inner = self.link_x[x, z]
        sides = [
            self.link_x[x - 1, z] * outer[0] + inner * here[1],
            inner * here[0] + self.link_x[x + 1, z] * outer[1],
        ]
        for p in range(2):
            link_y, link_z = self.link_y[x + p, z], self.link_z[x + p, z]
            along = link_y * next_in_y(here[p]) + last_in_y(link_y * here[p])
            total = sides[p] + (link_z * ahead[p] + down[p]) + along
            down[p] = link_z * here[p]
            result.append(self.weight[x + p, z] * total)
        return result

    def rows(self, field, x):
        here = [field[x, 0], field[x + 1, 0]]
        down = [self.link_z[x + p, -1] * field[x + p, -1] for p in range(2)]
        for z in range(self.side):
            ahead = [field[x, z + 1], field[x + 1, z + 1]]
            outer = [field[x - 1, z], field[x + 2, z]]
            yield z, here, self.flows(x, z, here, ahead, outer, down)
            here = ahead

    def sweep(self, field, out, exact=False):
        def pair(x):
            for z, here, sums in self.rows(field, x):
                for p in range(2):
                    if field is self.base:
                        value = (2.0 - DAMPING) * here[p] + sums[p]
                    else:
                        value = (1.0 - DAMPING) * here[p] + (self.base[x + p, z] + sums[p])
                    out.put(x + p, z, value, exact)

        self.pairs(pair)
        out.close(exact)

    def halve(self, rows, coarse):
        def pair(x):
            held = None
            for z, row in enumerate(rows(x)):
                row = row[0] + row[1]
                if z % 2 == 0:
                    held = row
                else:
                    coarse(x // 2, z // 2, 0.125 * pair_rows(held + row))

        self.pairs(pair)

    def descend(self, coarse):
        self.sweep(self.base, self.second)

        def residuals(x):
            for z, here, sums in self.rows(self.second, x):
                result = []
                for p in range(2):
                    swept = (1.0 - DAMPING) * here[p] + (self.base[x + p, z] + sums[p])
                    self.first[x + p, z] = swept
                    result.append((swept - here[p]) * self.back[x + p, z])
                yield result

        self.halve(residuals, coarse)

    def ascend(self, correction, out, exact=False):
        def pair(x):
            i = x // 2
            here = twice(correction(i, 0))
            start = twice(correction(i, -1))
            down = [self.link_z[x + p, -1] * start for p in range(2)]
            for z in range(self.side):
                ahead = twice(correction(i, (z + 1) // 2))
                outer = [twice(correction(i - 1, z // 2)), twice(correction(i + 1, z // 2))]
                sums = self.flows(x, z, [here, here], [ahead, ahead], outer, down)
                for p in range(2):
                    value = self.first[x + p, z] + ((1.0 - DAMPING) * here + sums[p])
                    self.second.put(x + p, z, value)
                here = ahead

        self.pairs(pair)
        self.second.close()
        self.sweep(self.second, out, exact)


class HeldLevel:
    def __init__(self, refs, index):
        self.side = 2
        self.scale = 0.25**index
        self.cond, self.first = Edged(refs[0], 2), Edged(refs[1], 2)
        self.weight, self.back = Rows(refs[2], 2), Rows(refs[3], 2)
        self.links = [Rows(ref, 2) for ref in refs[4:]]

    @staticmethod
    def scratch(index):
        sizes = [4**3] * 2 + [2**3] * 8
        return [pltpu.VMEM((size * SIDE, LANES), jnp.float32) for size in sizes]

    def around(self, field, inside=False):
        def moved(row, axis, up):
            row = (block_up if up else block_down)(row, axis)
            return (inside_up if up else inside_down)(row, axis) if inside else row

        result = {}
        for (x, z), here in field.items():
            result[x, z] = [
                field[1, z] if x == 0 else moved(field[0, z], 0, True),
                field[0, z] if x == 1 else moved(field[1, z], 0, False),
                jnp.concatenate([here[1:], moved(here[:1], 1, True)]),
                jnp.concatenate([moved(here[-1:], 1, False), here[:-1]]),
                field[x, 1] if z == 0 else moved(field[x, 0], 2, True),
                field[x, 0] if z == 1 else moved(field[x, 1], 2, False),
            ]
        return result

    def prepare(self):
        field = {(x, z): self.cond[x, z] for x in range(2) for z in range(2)}
        for at, others in self.around(field, inside=True).items():
            here = field[at]
            total = others[0]
            for other in others[1:]:
                total = total + other
            total = 3.0 * here + 0.5 * total
            inverse = DAMPING / total
            self.weight[at] = inverse
            self.back[at] = total * (self.scale / DAMPING)
            for index, other in enumerate(others):
                link = 0.5 * inverse * (here + other)
                self.links[index][at] = jnp.where(other > 0.0, link, 0.0)

    def halve(self, rows, coarse):
        total = None
        for row in rows(0):
            row = row[0] + row[1]
            total = row if total is None else total + row
        coarse(0, 0, 0.125 * (total[:1] + total[1:]))

    def sums(self, field, base):
        result = {}
        for at, others in self.around(field).items():
            total = base[at]
            for link, other in zip(self.links, others):
                total = total + link[at] * other
            result[at] = total
        return result

    def swept(self, field, base):
        sums = self.sums(field, base)
        return {at: (1.0 - DAMPING) * field[at] + sums[at] for at in field}

    def cycle(self, base, solve, out):
        field = self.swept(base, base)
        sums = self.sums(field, base)
        total = None
        for at in field:
            residual = (sums[at] - DAMPING * field[at]) * self.back[at]
            total = residual if total is None else total + residual
        solved = solve(0.125 * (total[:1] + total[1:]))
        row = twice(solved)
        copied = {at: row for at in field}
        change = {at: sums[at] + (1.0 - DAMPING) * (field[at] + row) for at in field}
        field = self.sums(copied, change)
        for (x, z), value in self.swept(field, base).items():
            out.put(x, z, value)
        out.close()


def replicated_kernel(
    whole,
    halved,
    cells_ref,
    *refs,
):
    parts = refs[:whole], refs[whole : whole + halved]
    solve_kernel(*parts, cells_ref, *refs[whole + halved :])


def solve_kernel(
    part_refs,
    half_refs,
    cells_ref,
    spot_ref,
    rows_ref,
    same_ref,
    pairs_ref,
    observed_ref,
    potentials_ref,
    mine_ref,
    theirs_ref,
    gathered,
    owned,
    beside,
    sent,
    sem,
    *level_refs,
):
    f32 = jnp.float32
    electrodes = spot_ref.shape[1]
    levels, used = [], 0
    for index in range(LEVELS - 1):
        kind = HeldLevel if index == LEVELS - 2 else Level
        count = len(kind.scratch(index))
        levels.append(kind(level_refs[used : used + count], index))
        used += count
    fine = levels[0]
    forward = fine.cond
    wide = SIDE * SIDE * SIDE

    device, shot = own_place()

    def place(part, row, x, index):
        for z in range(SIDE):
            fine.cond.ref[pl.ds(fine.cond.start(x, z) + index, SIDE, stride=SIDE), :] = part[
                pl.ds((row * SIDE + z) * SIDE, SIDE), :
            ]

    def collect(x):
        for k, part in enumerate(part_refs):
            place(part, x, x, device ^ k)

    def collect_half(x):
        for k, part in enumerate(half_refs):
            swapped, index = k // 2 % 2, len(part_refs) + k // 4 * 2 + k % 2
            place(part, x, (shot ^ swapped) * (SIDE // 2) + x, device ^ index)

    def edges(x):
        fine.cond.close_z(x, exact=True)

    rolled(SIDE, collect)
    for x in range(SIDE // 2):
        collect_half(x)
    rolled(SIDE, edges)
    fine.cond.close(exact=True)

    coarsest = []
    for level, below in zip(levels, levels[1:] + [None]):
        level.prepare()

        def coarse(x, z, row, below=below):
            if below is None:
                coarsest.append(row)
            else:
                below.cond.put(x, z, row, exact=True)

        level.halve(
            lambda x, level=level: [
                (level.cond[x, z], level.cond[x + 1, z]) for z in range(level.side)
            ],
            coarse,
        )
        if below is not None:
            below.cond.close(exact=True)

    keep = iota((1, SIDE, LANES), 1) % 2 == 0
    lane = iota((1, SIDE, LANES), 2)

    def split(value):
        return [jnp.where(keep, part, 0.0) for part in (value, pltpu.roll(value, SIDE - 1, 1))]

    def around(value):
        low, high = value
        low_up, high_up = [pltpu.roll(part, LANES - GROUP, 2) for part in value]
        low_down, high_down = [pltpu.roll(part, GROUP, 2) for part in value]
        along = [[move(part, axis) for part in value] for axis in (0, 2) for move in (block_up, block_down)]
        return along + [
            [jnp.where(lane < LANES - GROUP, low_up, high_up), high_up],
            [low_down, jnp.where(lane >= GROUP, high_down, low_down)],
        ]

    sub = iota((1, SIDE, LANES), 1)
    inside_last = [
        [sub < 6] * 2,
        [sub >= 2] * 2,
        [lane % GROUP < GROUP - 1] * 2,
        [lane % GROUP > 0] * 2,
        [keep, lane < LANES - GROUP],
        [lane >= GROUP, keep],
    ]
    last_scale = 0.25 ** (LEVELS - 1)
    here = split(coarsest[0])
    others = [
        [jnp.where(inside & keep, part, 0.0) for inside, part in zip(pair, moved)]
        for pair, moved in zip(inside_last, around(here))
    ]
    last_weight, last_links = [], []
    for half, part in enumerate(here):
        total = 3.0 * part
        for other in others:
            total = total + 0.5 * other[half]
        inverse = jnp.where(keep, DAMPING / jnp.where(keep, total, 1.0), 0.0)
        last_weight.append(inverse * (1.0 / last_scale))
        last_links.append(
            [
                jnp.where(pair[half] & keep, 0.5 * inverse * (part + other[half]), 0.0)
                for pair, other in zip(inside_last, others)
            ]
        )

    def solve_last(rhs):
        base = [weight * part for weight, part in zip(last_weight, split(rhs))]
        value = base
        for _ in range(COARSE_SWEEPS - 1):
            moved = around(value)
            fresh = []
            for half in range(2):
                parts = [link * other[half] for link, other in zip(last_links[half], moved)]
                start = base[half] + (1.0 - DAMPING) * value[half]
                fresh.append(((start + parts[0]) + (parts[1] + parts[2])) + (parts[3] + (parts[4] + parts[5])))
            value = fresh
        return value[0] + pltpu.roll(value[1], 1, 1)

    def cycle(index, out, exact=False):
        level = levels[index]
        below = levels[index + 1]
        if index == LEVELS - 3:
            base = {}

            def take(x, z, row):
                base[x, z] = below.weight[x, z] * (row * (1.0 / below.scale))

            level.descend(take)
            below.cycle(base, solve_last, below.first)
        else:
            level.descend(
                lambda x, z, row: below.base.put(
                    x, z, below.weight[x, z] * (row * (1.0 / below.scale))
                )
            )
            below.base.close()
            cycle(index + 1, below.first)
        level.ascend(lambda x, z: below.first[x, z], out, exact)

    spot = spot_ref[...]
    at_spot = iota((LANES, electrodes), 0) == spot
    order = lane_order()
    wide = SIDE + 2
    sending = pltpu.make_async_copy(sent, potentials_ref, sem)

    def each(body):
        def one(electrode, carry):
            body(pl.ds(electrode, 1), pl.ds(cells_ref[0, electrode], 1))
            return carry

        lax.fori_loop(0, electrodes, one, 0, unroll=32)

    def put(electrode, cell):
        fine.base.ref[cell, :] = gathered[electrode, :] * fine.weight.ref[cell, :]

    def read(electrode, cell):
        gathered[electrode, :] = forward.ref[cell, :]

    def exact(row, dims):
        return product(jnp.broadcast_to(row, (16, row.shape[1])), pairs_ref[...], 3, dims)[0:1]

    def own(x, z, y=0):
        return forward.ref[pl.ds(forward.start(x, z, y) + device, SIDE, stride=SIDE), :]

    def solve(index):
        each(put)
        rolled(SIDE, fine.base.close_z)
        fine.base.close()
        cycle(0, forward, exact=True)
        for x in range(-1, SIDE + 1):
            for z in range(-1, SIDE + 1):
                if 0 <= x < SIDE or 0 <= z < SIDE:
                    owned[index, (x + 1) * wide + z + 1] = own(x, z)
                if 0 <= x < SIDE and 0 <= z < SIDE:
                    for side, y in enumerate((1, -1)):
                        beside[index, side, x * SIDE + z] = own(x, z, y)

        @pl.when(index == 0)
        def _():
            for x in range(SIDE):
                tiles = [owned[0, (x + 1) * wide + z + 1] for z in range(SIDE)]
                sent[x] = from_blocks(tiles, order)
            sending.start()
            each(read)
            readings = jnp.where(at_spot, gathered[...].T, 0.0)
            readings = jnp.sum(readings, axis=0, keepdims=True)
            misfit = exact(readings, ((1,), (1,))) - observed_ref[...]
            gathered[...] = shared_rows(exact(misfit, ((1,), (0,))), spot, same_ref[...])

    gathered[...] = rows_ref[...]
    rolled(2, solve)

    chunk = mine_ref.shape[1]
    even = shot == 0
    for x in range(SIDE):
        tiles = []
        for z in range(SIDE):
            at = (x + 1) * wide + z + 1
            here_u, here_w = owned[0, at], owned[1, at]
            total = None
            for step in (wide, -wide, 1, -1):
                term = (here_u - owned[0, at + step]) * (here_w - owned[1, at + step])
                total = term if total is None else total + term
            for side in range(2):
                other_u, other_w = beside[0, side, x * SIDE + z], beside[1, side, x * SIDE + z]
                total = total + (here_u - other_u) * (here_w - other_w)
            tiles.append(-0.5 * total)
        natural = from_blocks(tiles, order)
        low, high = natural[:chunk], natural[chunk:]
        mine_ref[x] = jnp.where(even, low, high)
        theirs_ref[x] = jnp.where(even, high, low)
    sending.wait()


def replicated(conductivity, stations, currents, receivers, observed):
    rows, cols, depth = conductivity.shape
    f32 = jnp.float32
    electrodes = stations.shape[0]
    total = rows * cols
    vmem = pl.BlockSpec(memory_space=pltpu.VMEM)
    smem = pl.BlockSpec(memory_space=pltpu.SMEM)
    station_row = stations.reshape(1, electrodes)
    mine, half = pl.pallas_call(
        to_blocks_kernel,
        out_shape=(
            jax.ShapeDtypeStruct((total, LANES), f32),
            jax.ShapeDtypeStruct((total // 2, LANES), f32),
        ),
        in_specs=[vmem],
        out_specs=(vmem, vmem),
        compiler_params=pltpu.CompilerParams(vmem_limit_bytes=SMALL_BYTES),
    )(conductivity)
    swap = [(0, 1), (1, 0)]

    def partner(part, k):
        count = lax.axis_size("gx")
        return lax.ppermute(part, "gx", [(i, i ^ k) for i in range(count)])

    def with_mate(part):
        return [part, lax.ppermute(part, "gy", swap)]

    far = partner(half, 2)
    near = partner(mine, 1)
    line = jax.ShapeDtypeStruct((1, electrodes), jnp.int32)
    cells, spot, rows_of, same, pairs, held = pl.pallas_call(
        electrode_kernel,
        out_shape=(
            line,
            line,
            jax.ShapeDtypeStruct((electrodes, LANES), f32),
            jax.ShapeDtypeStruct((electrodes, electrodes), jnp.bfloat16),
            jax.ShapeDtypeStruct((receivers.shape[0], electrodes), jnp.bfloat16),
            jax.ShapeDtypeStruct(observed.shape, f32),
        ),
        in_specs=[vmem] * 4,
        out_specs=(vmem,) * 6,
        compiler_params=pltpu.CompilerParams(vmem_limit_bytes=SMALL_BYTES),
        cost_estimate=pl.CostEstimate(flops=100_000_000, bytes_accessed=1_000_000, transcendentals=0),
    )(station_row, currents, receivers, observed)
    far, rows_of = lax.optimization_barrier((far, rows_of))
    far = [far, partner(far, 1)]
    halved = [piece for own in far for piece in (own, lax.ppermute(own, "shot", swap))]
    parts = [piece for own in (mine, near) for piece in with_mate(own)]
    halved = [piece for own in halved for piece in with_mate(own)]
    chunk = cols // 2
    levels = [shape for index in range(LEVELS - 2) for shape in Level.scratch(index)]
    levels += HeldLevel.scratch(LEVELS - 2)
    potentials, own, theirs = pl.pallas_call(
        functools.partial(replicated_kernel, len(parts), len(halved)),
        out_shape=(
            jax.ShapeDtypeStruct((rows, cols, LANES), f32),
            jax.ShapeDtypeStruct((rows, chunk, LANES), f32),
            jax.ShapeDtypeStruct((rows, chunk, LANES), f32),
        ),
        in_specs=[smem] + [vmem] * (len(parts) + len(halved) + 5),
        out_specs=(pl.BlockSpec(memory_space=pl.ANY), vmem, vmem),
        scratch_shapes=[
            pltpu.VMEM((electrodes, LANES), f32),
            pltpu.VMEM((2, (SIDE + 2) ** 2, SIDE, LANES), f32),
            pltpu.VMEM((2, 2, SIDE**2, SIDE, LANES), f32),
            pltpu.VMEM((rows, cols, LANES), f32),
            pltpu.SemaphoreType.DMA,
        ]
        + levels,
        compiler_params=pltpu.CompilerParams(vmem_limit_bytes=VMEM_BYTES),
        cost_estimate=pl.CostEstimate(flops=200_000_000, bytes_accessed=4_000_000, transcendentals=0),
    )(cells, *parts, *halved, spot, rows_of, same, pairs, held)
    return potentials[None], own + lax.ppermute(theirs, "shot", swap)


def extended(array, sides, width):
    for axis, dim in sides:
        size, length = (lax.axis_size(axis), array.shape[dim])
        up = [(i, (i + 1) % size) for i in range(size - 1)]
        down = [(j, i) for i, j in up]
        last = lax.slice_in_dim(array, length - width, length, axis=dim)
        leading = lax.slice_in_dim(array, 0, width, axis=dim)
        before = lax.ppermute(last, axis, up)
        after = lax.ppermute(leading, axis, down)
        array = jnp.concatenate([before, array, after], axis=dim)
    return array


def upper_z(field):
    return jnp.concatenate([field[..., 1:], jnp.zeros_like(field[..., :1])], axis=-1)


def lower_z(field):
    return jnp.concatenate([jnp.zeros_like(field[..., :1]), field[..., :-1]], axis=-1)


def trim_circle(field, circle_width):
    return field[..., circle_width:-circle_width, circle_width:-circle_width, :]


def pad_plane(field, circle_width):
    spec = [(0, 0)] * (field.ndim - 3) + [
        (circle_width, circle_width),
        (circle_width, circle_width),
        (0, 0),
    ]
    return jnp.pad(field, spec)


def neighbour_list(field_pad):
    centre = trim_circle(field_pad, 1)
    return [
        field_pad[..., 2:, 1:-1, :],
        field_pad[..., :-2, 1:-1, :],
        field_pad[..., 1:-1, 2:, :],
        field_pad[..., 1:-1, :-2, :],
        upper_z(centre),
        lower_z(centre),
    ]


def stencil(field_pad, cond_pad, level_scale):
    centre = trim_circle(field_pad, 1)
    centre_cond = trim_circle(cond_pad, 1)
    summed = jnp.zeros_like(centre)
    for other, other_cond in zip(neighbour_list(field_pad), neighbour_list(cond_pad)):
        summed = summed + level_scale * 0.5 * (centre_cond + other_cond) * (centre - other)
    return summed


def diagonal(cond_pad, level_scale):
    centre_cond = trim_circle(cond_pad, 1)
    summed = jnp.zeros_like(centre_cond)
    for other_cond in neighbour_list(cond_pad):
        summed = summed + level_scale * 0.5 * (centre_cond + other_cond)
    return summed


def relaxed(field_pad, source, cond_pad, diag_level, level_scale):
    return (
        trim_circle(field_pad, 1)
        + DAMPING * (source - stencil(field_pad, cond_pad, level_scale)) / diag_level
    )


def restrict(field):
    leading = field.shape[:-3]
    extent = field.shape[-3:]
    shaped = field.reshape(leading + (extent[0] // 2, 2, extent[1] // 2, 2, extent[2] // 2, 2))
    return shaped.mean(axis=(-5, -3, -1))


def prolong(field):
    return jnp.repeat(jnp.repeat(jnp.repeat(field, 2, axis=-3), 2, axis=-2), 2, axis=-1)


def assemble(blocks, count_x, count_y):
    leading = blocks.shape[1:-3]
    extent = blocks.shape[-3:]
    depth_lead = len(leading)
    shaped = blocks.reshape((count_x, count_y) + leading + extent)
    order = tuple(range(2, 2 + depth_lead)) + (0, 2 + depth_lead, 1, 3 + depth_lead, 4 + depth_lead)
    return shaped.transpose(order).reshape(
        leading + (count_x * extent[0], count_y * extent[1], extent[2])
    )


def field_rim(field):
    return extended(field, (("gx", 1), ("gy", 2)), 1)


def cond_rim(conduct):
    return extended(conduct, (("gx", 0), ("gy", 1)), 1)


def whole_cycle(source, level_index, whole_plans):
    cond_pad, diag_level, level_scale = whole_plans[level_index]
    field = DAMPING * source / diag_level

    def turn(turn_index, iterate):
        return relaxed(pad_plane(iterate, 1), source, cond_pad, diag_level, level_scale)

    return lax.fori_loop(0, COARSE_SWEEPS - 1, turn, field)


def part_cycle(source, level_index, level_plans, whole_plans, gather_level):
    if level_index == gather_level:
        blocks = lax.all_gather(source[None], ("gx", "gy"), axis=0, tiled=True)
        whole = assemble(blocks, lax.axis_size("gx"), lax.axis_size("gy"))
        correction = whole_cycle(whole, level_index, whole_plans)
        extent = source.shape
        starts = (0, lax.axis_index("gx") * extent[1], lax.axis_index("gy") * extent[2], 0)
        return lax.dynamic_slice(correction, starts, extent)
    cond_pad, diag_level, level_scale = level_plans[level_index]
    field = DAMPING * source / diag_level
    field = relaxed(field_rim(field), source, cond_pad, diag_level, level_scale)
    residual = source - stencil(field_rim(field), cond_pad, level_scale)
    field = field + prolong(
        part_cycle(restrict(residual), level_index + 1, level_plans, whole_plans, gather_level)
    )
    field = relaxed(field_rim(field), source, cond_pad, diag_level, level_scale)
    return relaxed(field_rim(field), source, cond_pad, diag_level, level_scale)


def distributed(conductivity, stations, currents, receivers, observed):
    row_count, col_count, z_count = conductivity.shape
    shot_count = currents.shape[0]
    count_x = lax.axis_size("gx")
    count_y = lax.axis_size("gy")
    gather_level = LEVELS - 1
    level_plans = []
    conduct = conductivity
    for level_index in range(gather_level):
        level_scale = 0.25**level_index
        cond_pad = cond_rim(conduct)
        level_plans.append((cond_pad, diagonal(cond_pad, level_scale), level_scale))
        conduct = restrict(conduct)
    blocks = lax.all_gather(conduct[None], ("gx", "gy"), axis=0, tiled=True)
    whole = assemble(blocks, count_x, count_y)
    whole_plans = {}
    level_index = 3
    level_scale = 0.25**level_index
    cond_pad = pad_plane(whole, 1)
    whole_plans[level_index] = (cond_pad, diagonal(cond_pad, level_scale), level_scale)
    total_y = col_count * count_y
    cell_x = stations // (total_y * z_count)
    cell_y = stations // z_count % total_y
    cell_z = stations % z_count
    local_x = cell_x - lax.axis_index("gx") * row_count
    local_y = cell_y - lax.axis_index("gy") * col_count
    owned = (local_x >= 0) & (local_x < row_count) & (local_y >= 0) & (local_y < col_count)
    block_size = row_count * col_count * z_count
    local_cell = jnp.where(owned, (local_x * col_count + local_y) * z_count + cell_z, 0)
    offsets = jnp.arange(shot_count)[:, None] * block_size + local_cell[None, :]
    targets = jnp.where(owned[None, :], offsets, shot_count * block_size).reshape(-1)

    def spread(amounts):
        flat = (
            jnp.zeros((shot_count * block_size,), jnp.float32)
            .at[targets]
            .add(amounts.reshape(-1), mode="drop")
        )
        return flat.reshape(shot_count, row_count, col_count, z_count)

    potentials = part_cycle(spread(currents), 0, level_plans, whole_plans, gather_level)
    local_values = jnp.where(
        owned[None, :], potentials.reshape(shot_count, block_size)[:, local_cell], 0.0
    )
    readings = lax.psum(local_values, ("gx", "gy"))
    positions = jnp.arange(stations.shape[0])[:, None]
    pairs = (receivers[:, 0][None, :] == positions).astype(jnp.float32) - (
        receivers[:, 1][None, :] == positions
    ).astype(jnp.float32)
    misfit = jnp.dot(readings, pairs, precision=lax.Precision.HIGHEST) - observed
    back_source = jnp.dot(misfit, pairs.T, precision=lax.Precision.HIGHEST)
    adjoint = part_cycle(spread(back_source), 0, level_plans, whole_plans, gather_level)
    stacked = jnp.concatenate([potentials, adjoint], axis=0)
    padded = extended(stacked, (("gx", 1), ("gy", 2)), 1)
    potential_pad = padded[:shot_count]
    adjoint_pad = padded[shot_count:]
    gradient = jnp.zeros_like(potentials)
    for other_u, other_w in zip(neighbour_list(potential_pad), neighbour_list(adjoint_pad)):
        gradient = gradient - 0.5 * (potentials - other_u) * (adjoint - other_w)
    summed = lax.psum_scatter(jnp.sum(gradient, axis=0), "shot", scatter_dimension=1, tiled=True)
    return (potentials, summed)


def per_device(conductivity, stations, currents, receivers, observed):
    blocks = lax.axis_size("gx") * lax.axis_size("gy")
    fits = conductivity.shape == (SIDE, SIDE * SIDE, LANES) and blocks == SIDE
    fits = fits and lax.axis_size("gy") == 2 and lax.axis_size("shot") == 2
    fits = fits and currents.shape[0] == 1
    plan = replicated if fits else distributed
    return plan(conductivity, stations, currents, receivers, observed)


def solution(mesh):
    in_specs = (
        P(("grp", "gx"), "gy", None),
        P("grp"),
        P(("grp", "shot"), None),
        P("grp", None),
        P(("grp", "shot"), None),
    )
    out_specs = (P(("grp", "shot"), "gx", "gy", None), P(("grp", "gx"), ("gy", "shot"), None))
    return jax.shard_map(
        per_device, mesh=mesh, in_specs=in_specs, out_specs=out_specs, check_vma=False
    )
```

```python
import functools

import jax
import jax.numpy as jnp
from jax import lax
from jax.experimental import pallas as pl
from jax.experimental.pallas import tpu as pltpu
from jax.sharding import PartitionSpec as P

LEVELS = 4
COARSE_SWEEPS = 16


DAMPING = 0.8

SIDE = 8
LANES = 128
GROUP = 16
VMEM_BYTES = 48 * 2**20
SMALL_BYTES = 6 * 2**20


def pieces_of(value, count):
    pieces = []
    for _ in range(count):
        pieces.append(value.astype(jnp.bfloat16))
        value = value - pieces[-1].astype(jnp.float32)
    return pieces[::-1]


def product(value, matrix, count, dims=((1,), (0,))):
    result = None
    for piece in pieces_of(value, count):
        term = lax.dot_general(
            piece, matrix, (dims, ((), ())), preferred_element_type=jnp.float32
        )
        result = term if result is None else result + term
    return result


def iota(shape, dim):
    return lax.broadcasted_iota(jnp.int32, shape, dim)


def station_table(station):
    cell_x, cell_y, cell_z = station >> 14, station >> 7 & 127, station & 127
    row = (cell_x >> 3) * 2 + (cell_y >> 6)
    return cell_x, cell_y, cell_z, row, (cell_y >> 3 & 7) * GROUP + (cell_z >> 3)


def lane_order():
    row, col = iota((LANES, LANES), 0), iota((LANES, LANES), 1)
    chosen = row == col % GROUP * SIDE + col // GROUP
    return jnp.where(chosen, 1.0, 0.0).astype(jnp.bfloat16)


def exchange_groups(tiles):
    tiles = list(tiles)
    group = iota(tiles[0].shape, 1) // GROUP
    for bit in range(3):
        step = 1 << bit
        keep = (group & step) == 0
        for low in range(SIDE):
            if low & step == 0:
                a, b = tiles[low], tiles[low | step]
                tiles[low] = jnp.where(keep, a, pltpu.roll(b, step * GROUP, 1))
                tiles[low | step] = jnp.where(keep, pltpu.roll(a, LANES - step * GROUP, 1), b)
    return tiles


def own_place():
    return lax.axis_index("gx") * 2 + lax.axis_index("gy"), lax.axis_index("shot")


def to_blocks_kernel(natural_ref, blocks_ref, half_ref):
    order = lane_order()
    for x in range(SIDE):
        tiles = product(natural_ref[x], order, 3)
        tiles = [tiles[SIDE * k : SIDE * (k + 1)] for k in range(SIDE)]
        for z, tile in enumerate(exchange_groups(tiles)):
            blocks_ref[pl.ds((x * SIDE + z) * SIDE, SIDE), :] = tile
    count = half_ref.shape[0]
    low, high = blocks_ref[pl.ds(0, count), :], blocks_ref[pl.ds(count, count), :]
    half_ref[...] = jnp.where(own_place()[1] == 0, low, high)


def from_blocks(tiles, order):
    natural = jnp.concatenate(exchange_groups(tiles), axis=0)
    return product(natural, order, 3, ((1,), (1,)))


def block_up(field, axis):
    if axis == 0:
        return pltpu.roll(field, 6, 1)
    if axis == 2:
        return pltpu.roll(field, LANES - 1, 2)
    turned = pltpu.roll(field, LANES - GROUP, 2)
    return jnp.where(iota(field.shape, 2) < LANES - GROUP, turned, pltpu.roll(turned, 7, 1))


def block_down(field, axis):
    if axis == 0:
        return pltpu.roll(field, 2, 1)
    if axis == 2:
        return pltpu.roll(field, 1, 2)
    turned = pltpu.roll(field, GROUP, 2)
    return jnp.where(iota(field.shape, 2) >= GROUP, turned, pltpu.roll(turned, 1, 1))


def inside_up(field, axis):
    sub, lane = iota(field.shape, 1), iota(field.shape, 2)
    if axis == 0:
        keep = sub < 6
    elif axis == 1:
        keep = (lane < LANES - GROUP) | (sub % 2 == 0)
    else:
        keep = lane % GROUP < GROUP - 1
    return jnp.where(keep, field, 0.0)


def inside_down(field, axis):
    sub, lane = iota(field.shape, 1), iota(field.shape, 2)
    if axis == 0:
        keep = sub >= 2
    elif axis == 1:
        keep = (lane >= GROUP) | (sub % 2 == 1)
    else:
        keep = lane % GROUP > 0
    return jnp.where(keep, field, 0.0)


def pair_rows(row):
    count = row.shape[0] // 2
    return jnp.concatenate([row[2 * i : 2 * i + 1] + row[2 * i + 1 : 2 * i + 2] for i in range(count)])


def twice(row):
    return jnp.concatenate([row[i // 2 : i // 2 + 1] for i in range(2 * row.shape[0])])


def electrode_kernel(
    stations_ref,
    currents_ref,
    receivers_ref,
    observed_ref,
    cells_ref,
    spot_ref,
    rows_ref,
    same_ref,
    pairs_ref,
    held_ref,
):
    stations = stations_ref[...]
    electrodes = stations.shape[1]
    cell_x, cell_y, cell_z, row, spot = station_table(stations)
    wide = SIDE + 2
    register = (((cell_x & 7) + 1) * wide + (cell_z & 7) + 1) * wide + (cell_y & 7) + 1
    cells_ref[...] = register * SIDE + row
    spot_ref[...] = spot
    held_ref[...] = observed_ref[...]
    line = stations & 0x1C387 | row << 20
    same = jnp.broadcast_to(line, (electrodes, electrodes))
    same = jnp.where(same == same.T, 1.0, 0.0).astype(jnp.bfloat16)
    same_ref[...] = same
    rows_ref[...] = shared_rows(currents_ref[...], spot, same)
    receivers = receivers_ref[...]
    numbers = iota((receivers.shape[0], electrodes), 1)
    pairs = jnp.where(numbers == receivers[:, 0:1], 1.0, 0.0) - jnp.where(
        numbers == receivers[:, 1:2], 1.0, 0.0
    )
    pairs_ref[...] = pairs.astype(jnp.bfloat16)


def shared_rows(amounts, spot, same):
    electrodes = amounts.shape[1]
    at_spot = iota((LANES, electrodes), 0) == spot
    return product(jnp.where(at_spot, amounts, 0.0), same, 3).T


class Edged:
    def __init__(self, ref, side):
        self.ref, self.side = ref, side

    def start(self, x, z, y=0):
        wide = self.side + 2
        return (((x + 1) * wide + z + 1) * wide + y + 1) * SIDE

    def __getitem__(self, at):
        x, z = at
        rows = self.ref[pl.ds(self.start(x, z), self.side * SIDE), :]
        return rows.reshape(self.side, SIDE, LANES)

    def __setitem__(self, at, value):
        x, z = at
        self.ref[pl.ds(self.start(x, z), self.side * SIDE), :] = value.reshape(-1, LANES)

    def put(self, x, z, value, exact=False):
        self[x, z] = value
        n = self.side
        if z == 0:
            edge = block_up(value, 2)
            self[x, n] = inside_up(edge, 2) if exact else edge
        if z == n - 1:
            edge = block_down(value, 2)
            self[x, -1] = inside_down(edge, 2) if exact else edge
        if x == 0:
            edge = block_up(value, 0)
            self[n, z] = inside_up(edge, 0) if exact else edge
        if x == n - 1:
            edge = block_down(value, 0)
            self[-1, z] = inside_down(edge, 0) if exact else edge
        if exact:
            after = inside_up(block_up(value[:1], 1), 1)
            self.ref[pl.ds(self.start(x, z, n), SIDE), :] = after[0]
            before = inside_down(block_down(value[n - 1 :], 1), 1)
            self.ref[pl.ds(self.start(x, z, -1), SIDE), :] = before[0]

    def close_z(self, x, exact=False):
        n = self.side
        after, before = block_up(self[x, 0], 2), block_down(self[x, n - 1], 2)
        self[x, n] = inside_up(after, 2) if exact else after
        self[x, -1] = inside_down(before, 2) if exact else before

    def close(self, exact=False):
        n = self.side
        for z in range(n):
            after = block_up(self[0, z], 0)
            self[n, z] = inside_up(after, 0) if exact else after
            before = block_down(self[n - 1, z], 0)
            self[-1, z] = inside_down(before, 0) if exact else before


class Rows:
    def __init__(self, ref, side, first_x=0, first_z=0):
        self.ref, self.side, self.first_x, self.first_z = ref, side, first_x, first_z

    def place(self, at):
        count = self.side - self.first_z
        rows = self.side * SIDE
        return pl.ds(((at[0] - self.first_x) * count + at[1] - self.first_z) * rows, rows)

    def __getitem__(self, at):
        return self.ref[self.place(at), :].reshape(self.side, SIDE, LANES)

    def __setitem__(self, at, value):
        self.ref[self.place(at), :] = value.reshape(-1, LANES)


def rolled(count, body):
    def one(x, carry):
        body(x)
        return carry

    lax.fori_loop(0, count, one, 0)


def next_in_y(row):
    return jnp.concatenate([row[1:], block_up(row[:1], 1)])


def last_in_y(row):
    return jnp.concatenate([block_down(row[-1:], 1), row[:-1]])


class Level:
    def __init__(self, refs, index):
        self.side = side = SIDE >> index
        self.scale = 0.25**index
        edged = [Edged(ref, side) for ref in refs[:5]]
        self.cond, self.first, self.second, self.base, self.weight = edged
        self.link_x = Rows(refs[5], side, first_x=-1)
        self.link_y = Rows(refs[6], side)
        self.link_z = Rows(refs[7], side, first_z=-1)
        self.back = Rows(refs[8], side)

    @staticmethod
    def scratch(index):
        side = SIDE >> index
        sizes = [(side + 2) ** 3] * 5
        sizes += [side**2 * (side + 1), side**3, side**2 * (side + 1), side**3]
        return [pltpu.VMEM((size * SIDE, LANES), jnp.float32) for size in sizes]

    def pairs(self, body):
        for i in range(self.side // 2):
            body(2 * i)

    def prepare(self):
        n = self.side
        cond = self.cond

        def plane(x):
            for z in range(n):
                here, ahead, next_x = cond[x, z], cond[x, z + 1], cond[x + 1, z]
                after = inside_up(block_up(here[:1], 1), 1)
                before = inside_down(block_down(here[-1:], 1), 1)
                next_y = jnp.concatenate([here[1:], after])
                last_y = jnp.concatenate([before, here[:-1]])
                total = (next_x + cond[x - 1, z]) + (ahead + cond[x, z - 1]) + (next_y + last_y)
                total = 3.0 * here + 0.5 * total
                self.weight[x, z] = DAMPING / total
                if n == SIDE:
                    self.base[x, z] = jnp.zeros_like(here)
                self.back[x, z] = total * (self.scale / DAMPING)
                self.link_x[x, z] = 0.5 * (here + next_x)
                link = 0.5 * (here + next_y)
                self.link_y[x, z] = jnp.concatenate([link[:-1], inside_up(link[-1:], 1)])
                link = 0.5 * (here + ahead)
                if z == n - 1:
                    link = inside_up(link, 2)
                    self.link_z[x, -1] = block_down(link, 2)
                self.link_z[x, z] = link

        if n == SIDE:
            rolled(n, plane)
        else:
            for x in range(n):
                plane(x)
        for z in range(n):
            link = inside_up(self.link_x[n - 1, z], 0)
            self.link_x[n - 1, z] = link
            self.link_x[-1, z] = block_down(link, 0)

    def flows(self, x, z, here, ahead, outer, down):
        result = []
        inner = self.link_x[x, z]
        sides = [
            self.link_x[x - 1, z] * outer[0] + inner * here[1],
            inner * here[0] + self.link_x[x + 1, z] * outer[1],
        ]
        for p in range(2):
            link_y, link_z = self.link_y[x + p, z], self.link_z[x + p, z]
            along = link_y * next_in_y(here[p]) + last_in_y(link_y * here[p])
            total = sides[p] + (link_z * ahead[p] + down[p]) + along
            down[p] = link_z * here[p]
            result.append(self.weight[x + p, z] * total)
        return result

    def rows(self, field, x):
        here = [field[x, 0], field[x + 1, 0]]
        down = [self.link_z[x + p, -1] * field[x + p, -1] for p in range(2)]
        for z in range(self.side):
            ahead = [field[x, z + 1], field[x + 1, z + 1]]
            outer = [field[x - 1, z], field[x + 2, z]]
            yield z, here, self.flows(x, z, here, ahead, outer, down)
            here = ahead

    def sweep(self, field, out, exact=False):
        def pair(x):
            for z, here, sums in self.rows(field, x):
                for p in range(2):
                    if field is self.base:
                        value = (2.0 - DAMPING) * here[p] + sums[p]
                    else:
                        value = (1.0 - DAMPING) * here[p] + (self.base[x + p, z] + sums[p])
                    out.put(x + p, z, value, exact)

        self.pairs(pair)

    def halve(self, rows, coarse):
        def pair(x):
            held = None
            for z, row in enumerate(rows(x)):
                row = row[0] + row[1]
                if z % 2 == 0:
                    held = row
                else:
                    coarse(x // 2, z // 2, 0.125 * pair_rows(held + row))

        self.pairs(pair)

    def descend(self, coarse):
        self.sweep(self.base, self.second)

        def residuals(x):
            for z, here, sums in self.rows(self.second, x):
                result = []
                for p in range(2):
                    swept = (1.0 - DAMPING) * here[p] + (self.base[x + p, z] + sums[p])
                    self.first[x + p, z] = swept
                    result.append((swept - here[p]) * self.back[x + p, z])
                yield result

        self.halve(residuals, coarse)

    def ascend(self, correction, out, exact=False):
        def pair(x):
            i = x // 2
            here = twice(correction(i, 0))
            start = twice(correction(i, -1))
            down = [self.link_z[x + p, -1] * start for p in range(2)]
            for z in range(self.side):
                ahead = twice(correction(i, (z + 1) // 2))
                outer = [twice(correction(i - 1, z // 2)), twice(correction(i + 1, z // 2))]
                sums = self.flows(x, z, [here, here], [ahead, ahead], outer, down)
                for p in range(2):
                    value = self.first[x + p, z] + ((1.0 - DAMPING) * here + sums[p])
                    self.second.put(x + p, z, value)
                here = ahead

        self.pairs(pair)
        self.sweep(self.second, out, exact)


class HeldLevel:
    def __init__(self, refs, index):
        self.side = 2
        self.scale = 0.25**index
        self.cond, self.first = Edged(refs[0], 2), Edged(refs[1], 2)
        self.weight, self.back = Rows(refs[2], 2), Rows(refs[3], 2)
        self.links = [Rows(ref, 2) for ref in refs[4:]]

    @staticmethod
    def scratch(index):
        sizes = [4**3] * 2 + [2**3] * 8
        return [pltpu.VMEM((size * SIDE, LANES), jnp.float32) for size in sizes]

    def around(self, field, inside=False):
        def moved(row, axis, up):
            row = (block_up if up else block_down)(row, axis)
            return (inside_up if up else inside_down)(row, axis) if inside else row

        result = {}
        for (x, z), here in field.items():
            result[x, z] = [
                field[1, z] if x == 0 else moved(field[0, z], 0, True),
                field[0, z] if x == 1 else moved(field[1, z], 0, False),
                jnp.concatenate([here[1:], moved(here[:1], 1, True)]),
                jnp.concatenate([moved(here[-1:], 1, False), here[:-1]]),
                field[x, 1] if z == 0 else moved(field[x, 0], 2, True),
                field[x, 0] if z == 1 else moved(field[x, 1], 2, False),
            ]
        return result

    def prepare(self):
        field = {(x, z): self.cond[x, z] for x in range(2) for z in range(2)}
        for at, others in self.around(field, inside=True).items():
            here = field[at]
            total = others[0]
            for other in others[1:]:
                total = total + other
            total = 3.0 * here + 0.5 * total
            inverse = DAMPING / total
            self.weight[at] = inverse
            self.back[at] = total * (self.scale / DAMPING)
            for index, other in enumerate(others):
                link = 0.5 * inverse * (here + other)
                self.links[index][at] = jnp.where(other > 0.0, link, 0.0)

    def halve(self, rows, coarse):
        total = None
        for row in rows(0):
            row = row[0] + row[1]
            total = row if total is None else total + row
        coarse(0, 0, 0.125 * (total[:1] + total[1:]))

    def sums(self, field, base):
        result = {}
        for at, others in self.around(field).items():
            total = base[at]
            for link, other in zip(self.links, others):
                total = total + link[at] * other
            result[at] = total
        return result

    def swept(self, field, base):
        sums = self.sums(field, base)
        return {at: (1.0 - DAMPING) * field[at] + sums[at] for at in field}

    def cycle(self, base, solve, out):
        field = self.swept(base, base)
        sums = self.sums(field, base)
        total = None
        for at in field:
            residual = (sums[at] - DAMPING * field[at]) * self.back[at]
            total = residual if total is None else total + residual
        solved = solve(0.125 * (total[:1] + total[1:]))
        row = twice(solved)
        copied = {at: row for at in field}
        change = {at: sums[at] + (1.0 - DAMPING) * (field[at] + row) for at in field}
        field = self.sums(copied, change)
        for (x, z), value in self.swept(field, base).items():
            out.put(x, z, value)


def replicated_kernel(
    whole,
    halved,
    cells_ref,
    *refs,
):
    parts = refs[:whole], refs[whole : whole + halved]
    solve_kernel(*parts, cells_ref, *refs[whole + halved :])


def solve_kernel(
    part_refs,
    half_refs,
    cells_ref,
    spot_ref,
    rows_ref,
    same_ref,
    pairs_ref,
    observed_ref,
    potentials_ref,
    mine_ref,
    theirs_ref,
    gathered,
    owned,
    beside,
    sent,
    sem,
    *level_refs,
):
    f32 = jnp.float32
    electrodes = spot_ref.shape[1]
    levels, used = [], 0
    for index in range(LEVELS - 1):
        kind = HeldLevel if index == LEVELS - 2 else Level
        count = len(kind.scratch(index))
        levels.append(kind(level_refs[used : used + count], index))
        used += count
    fine = levels[0]
    forward = fine.cond
    wide = SIDE * SIDE * SIDE

    device, shot = own_place()

    def place(part, row, x, index):
        for z in range(SIDE):
            fine.cond.ref[pl.ds(fine.cond.start(x, z) + index, SIDE, stride=SIDE), :] = part[
                pl.ds((row * SIDE + z) * SIDE, SIDE), :
            ]

    def collect(x):
        for k, part in enumerate(part_refs):
            place(part, x, x, device ^ k)

    def collect_half(x):
        for k, part in enumerate(half_refs):
            swapped, index = k // 2 % 2, len(part_refs) + k // 4 * 2 + k % 2
            place(part, x, (shot ^ swapped) * (SIDE // 2) + x, device ^ index)

    def edges(x):
        fine.cond.close_z(x, exact=True)

    rolled(SIDE, collect)
    for x in range(SIDE // 2):
        collect_half(x)
    rolled(SIDE, edges)
    fine.cond.close(exact=True)

    coarsest = []
    for level, below in zip(levels, levels[1:] + [None]):
        level.prepare()

        def coarse(x, z, row, below=below):
            if below is None:
                coarsest.append(row)
            else:
                below.cond.put(x, z, row, exact=True)

        level.halve(
            lambda x, level=level: [
                (level.cond[x, z], level.cond[x + 1, z]) for z in range(level.side)
            ],
            coarse,
        )

    keep = iota((1, SIDE, LANES), 1) % 2 == 0
    lane = iota((1, SIDE, LANES), 2)

    def split(value):
        return [jnp.where(keep, part, 0.0) for part in (value, pltpu.roll(value, SIDE - 1, 1))]

    def around(value):
        low, high = value
        low_up, high_up = [pltpu.roll(part, LANES - GROUP, 2) for part in value]
        low_down, high_down = [pltpu.roll(part, GROUP, 2) for part in value]
        along = [[move(part, axis) for part in value] for axis in (0, 2) for move in (block_up, block_down)]
        return along + [
            [jnp.where(lane < LANES - GROUP, low_up, high_up), high_up],
            [low_down, jnp.where(lane >= GROUP, high_down, low_down)],
        ]

    sub = iota((1, SIDE, LANES), 1)
    inside_last = [
        [sub < 6] * 2,
        [sub >= 2] * 2,
        [lane % GROUP < GROUP - 1] * 2,
        [lane % GROUP > 0] * 2,
        [keep, lane < LANES - GROUP],
        [lane >= GROUP, keep],
    ]
    last_scale = 0.25 ** (LEVELS - 1)
    here = split(coarsest[0])
    others = [
        [jnp.where(inside & keep, part, 0.0) for inside, part in zip(pair, moved)]
        for pair, moved in zip(inside_last, around(here))
    ]
    last_weight, last_links = [], []
    for half, part in enumerate(here):
        total = 3.0 * part
        for other in others:
            total = total + 0.5 * other[half]
        inverse = jnp.where(keep, DAMPING / jnp.where(keep, total, 1.0), 0.0)
        last_weight.append(inverse * (1.0 / last_scale))
        last_links.append(
            [
                jnp.where(pair[half] & keep, 0.5 * inverse * (part + other[half]), 0.0)
                for pair, other in zip(inside_last, others)
            ]
        )

    def solve_last(rhs):
        base = [weight * part for weight, part in zip(last_weight, split(rhs))]
        value = base
        for _ in range(COARSE_SWEEPS - 1):
            moved = around(value)
            fresh = []
            for half in range(2):
                parts = [link * other[half] for link, other in zip(last_links[half], moved)]
                start = base[half] + (1.0 - DAMPING) * value[half]
                fresh.append(((start + parts[0]) + (parts[1] + parts[2])) + (parts[3] + (parts[4] + parts[5])))
            value = fresh
        return value[0] + pltpu.roll(value[1], 1, 1)

    def cycle(index, out, exact=False):
        level = levels[index]
        below = levels[index + 1]
        if index == LEVELS - 3:
            base = {}

            def take(x, z, row):
                base[x, z] = below.weight[x, z] * (row * (1.0 / below.scale))

            level.descend(take)
            below.cycle(base, solve_last, below.first)
        else:
            level.descend(
                lambda x, z, row: below.base.put(
                    x, z, below.weight[x, z] * (row * (1.0 / below.scale))
                )
            )
            cycle(index + 1, below.first)
        level.ascend(lambda x, z: below.first[x, z], out, exact)

    spot = spot_ref[...]
    at_spot = iota((LANES, electrodes), 0) == spot
    order = lane_order()
    wide = SIDE + 2
    sending = pltpu.make_async_copy(sent, potentials_ref, sem)

    def each(body):
        def one(electrode, carry):
            body(pl.ds(electrode, 1), pl.ds(cells_ref[0, electrode], 1))
            return carry

        lax.fori_loop(0, electrodes, one, 0, unroll=32)

    def put(electrode, cell):
        fine.base.ref[cell, :] = gathered[electrode, :] * fine.weight.ref[cell, :]

    def read(electrode, cell):
        gathered[electrode, :] = forward.ref[cell, :]

    def exact(row, dims):
        return product(jnp.broadcast_to(row, (16, row.shape[1])), pairs_ref[...], 3, dims)[0:1]

    def own(x, z, y=0):
        return forward.ref[pl.ds(forward.start(x, z, y) + device, SIDE, stride=SIDE), :]

    def solve(index):
        each(put)
        rolled(SIDE, fine.base.close_z)
        fine.base.close()
        cycle(0, forward, exact=True)
        for x in range(-1, SIDE + 1):
            for z in range(-1, SIDE + 1):
                if 0 <= x < SIDE or 0 <= z < SIDE:
                    owned[index, (x + 1) * wide + z + 1] = own(x, z)
                if 0 <= x < SIDE and 0 <= z < SIDE:
                    for side, y in enumerate((1, -1)):
                        beside[index, side, x * SIDE + z] = own(x, z, y)

        @pl.when(index == 0)
        def _():
            for x in range(SIDE):
                tiles = [owned[0, (x + 1) * wide + z + 1] for z in range(SIDE)]
                sent[x] = from_blocks(tiles, order)
            sending.start()
            each(read)
            readings = jnp.where(at_spot, gathered[...].T, 0.0)
            readings = jnp.sum(readings, axis=0, keepdims=True)
            misfit = exact(readings, ((1,), (1,))) - observed_ref[...]
            gathered[...] = shared_rows(exact(misfit, ((1,), (0,))), spot, same_ref[...])

    gathered[...] = rows_ref[...]
    rolled(2, solve)

    chunk = mine_ref.shape[1]
    even = shot == 0
    for x in range(SIDE):
        tiles = []
        for z in range(SIDE):
            at = (x + 1) * wide + z + 1
            here_u, here_w = owned[0, at], owned[1, at]
            total = None
            for step in (wide, -wide, 1, -1):
                term = (here_u - owned[0, at + step]) * (here_w - owned[1, at + step])
                total = term if total is None else total + term
            for side in range(2):
                other_u, other_w = beside[0, side, x * SIDE + z], beside[1, side, x * SIDE + z]
                total = total + (here_u - other_u) * (here_w - other_w)
            tiles.append(-0.5 * total)
        natural = from_blocks(tiles, order)
        low, high = natural[:chunk], natural[chunk:]
        mine_ref[x] = jnp.where(even, low, high)
        theirs_ref[x] = jnp.where(even, high, low)
    sending.wait()


def replicated(conductivity, stations, currents, receivers, observed):
    rows, cols, depth = conductivity.shape
    f32 = jnp.float32
    electrodes = stations.shape[0]
    total = rows * cols
    vmem = pl.BlockSpec(memory_space=pltpu.VMEM)
    smem = pl.BlockSpec(memory_space=pltpu.SMEM)
    station_row = stations.reshape(1, electrodes)
    mine, half = pl.pallas_call(
        to_blocks_kernel,
        out_shape=(
            jax.ShapeDtypeStruct((total, LANES), f32),
            jax.ShapeDtypeStruct((total // 2, LANES), f32),
        ),
        in_specs=[vmem],
        out_specs=(vmem, vmem),
        compiler_params=pltpu.CompilerParams(vmem_limit_bytes=SMALL_BYTES),
    )(conductivity)
    swap = [(0, 1), (1, 0)]

    def partner(part, k):
        count = lax.axis_size("gx")
        return lax.ppermute(part, "gx", [(i, i ^ k) for i in range(count)])

    def with_mate(part):
        return [part, lax.ppermute(part, "gy", swap)]

    far = partner(half, 2)
    near = partner(mine, 1)
    line = jax.ShapeDtypeStruct((1, electrodes), jnp.int32)
    cells, spot, rows_of, same, pairs, held = pl.pallas_call(
        electrode_kernel,
        out_shape=(
            line,
            line,
            jax.ShapeDtypeStruct((electrodes, LANES), f32),
            jax.ShapeDtypeStruct((electrodes, electrodes), jnp.bfloat16),
            jax.ShapeDtypeStruct((receivers.shape[0], electrodes), jnp.bfloat16),
            jax.ShapeDtypeStruct(observed.shape, f32),
        ),
        in_specs=[vmem] * 4,
        out_specs=(vmem,) * 6,
        compiler_params=pltpu.CompilerParams(vmem_limit_bytes=SMALL_BYTES),
        cost_estimate=pl.CostEstimate(flops=100_000_000, bytes_accessed=1_000_000, transcendentals=0),
    )(station_row, currents, receivers, observed)
    far, rows_of = lax.optimization_barrier((far, rows_of))
    far = [far, partner(far, 1)]
    halved = [piece for own in far for piece in (own, lax.ppermute(own, "shot", swap))]
    parts = [piece for own in (mine, near) for piece in with_mate(own)]
    halved = [piece for own in halved for piece in with_mate(own)]
    chunk = cols // 2
    levels = [shape for index in range(LEVELS - 2) for shape in Level.scratch(index)]
    levels += HeldLevel.scratch(LEVELS - 2)
    potentials, own, theirs = pl.pallas_call(
        functools.partial(replicated_kernel, len(parts), len(halved)),
        out_shape=(
            jax.ShapeDtypeStruct((rows, cols, LANES), f32),
            jax.ShapeDtypeStruct((rows, chunk, LANES), f32),
            jax.ShapeDtypeStruct((rows, chunk, LANES), f32),
        ),
        in_specs=[smem] + [vmem] * (len(parts) + len(halved) + 5),
        out_specs=(pl.BlockSpec(memory_space=pl.ANY), vmem, vmem),
        scratch_shapes=[
            pltpu.VMEM((electrodes, LANES), f32),
            pltpu.VMEM((2, (SIDE + 2) ** 2, SIDE, LANES), f32),
            pltpu.VMEM((2, 2, SIDE**2, SIDE, LANES), f32),
            pltpu.VMEM((rows, cols, LANES), f32),
            pltpu.SemaphoreType.DMA,
        ]
        + levels,
        compiler_params=pltpu.CompilerParams(vmem_limit_bytes=VMEM_BYTES),
        cost_estimate=pl.CostEstimate(flops=200_000_000, bytes_accessed=4_000_000, transcendentals=0),
    )(cells, *parts, *halved, spot, rows_of, same, pairs, held)
    return potentials[None], own + lax.ppermute(theirs, "shot", swap)


def extended(array, sides, width):
    for axis, dim in sides:
        size, length = (lax.axis_size(axis), array.shape[dim])
        up = [(i, (i + 1) % size) for i in range(size - 1)]
        down = [(j, i) for i, j in up]
        last = lax.slice_in_dim(array, length - width, length, axis=dim)
        leading = lax.slice_in_dim(array, 0, width, axis=dim)
        before = lax.ppermute(last, axis, up)
        after = lax.ppermute(leading, axis, down)
        array = jnp.concatenate([before, array, after], axis=dim)
    return array


def upper_z(field):
    return jnp.concatenate([field[..., 1:], jnp.zeros_like(field[..., :1])], axis=-1)


def lower_z(field):
    return jnp.concatenate([jnp.zeros_like(field[..., :1]), field[..., :-1]], axis=-1)


def trim_circle(field, circle_width):
    return field[..., circle_width:-circle_width, circle_width:-circle_width, :]


def pad_plane(field, circle_width):
    spec = [(0, 0)] * (field.ndim - 3) + [
        (circle_width, circle_width),
        (circle_width, circle_width),
        (0, 0),
    ]
    return jnp.pad(field, spec)


def neighbour_list(field_pad):
    centre = trim_circle(field_pad, 1)
    return [
        field_pad[..., 2:, 1:-1, :],
        field_pad[..., :-2, 1:-1, :],
        field_pad[..., 1:-1, 2:, :],
        field_pad[..., 1:-1, :-2, :],
        upper_z(centre),
        lower_z(centre),
    ]


def stencil(field_pad, cond_pad, level_scale):
    centre = trim_circle(field_pad, 1)
    centre_cond = trim_circle(cond_pad, 1)
    summed = jnp.zeros_like(centre)
    for other, other_cond in zip(neighbour_list(field_pad), neighbour_list(cond_pad)):
        summed = summed + level_scale * 0.5 * (centre_cond + other_cond) * (centre - other)
    return summed


def diagonal(cond_pad, level_scale):
    centre_cond = trim_circle(cond_pad, 1)
    summed = jnp.zeros_like(centre_cond)
    for other_cond in neighbour_list(cond_pad):
        summed = summed + level_scale * 0.5 * (centre_cond + other_cond)
    return summed


def relaxed(field_pad, source, cond_pad, diag_level, level_scale):
    return (
        trim_circle(field_pad, 1)
        + DAMPING * (source - stencil(field_pad, cond_pad, level_scale)) / diag_level
    )


def restrict(field):
    leading = field.shape[:-3]
    extent = field.shape[-3:]
    shaped = field.reshape(leading + (extent[0] // 2, 2, extent[1] // 2, 2, extent[2] // 2, 2))
    return shaped.mean(axis=(-5, -3, -1))


def prolong(field):
    return jnp.repeat(jnp.repeat(jnp.repeat(field, 2, axis=-3), 2, axis=-2), 2, axis=-1)


def assemble(blocks, count_x, count_y):
    leading = blocks.shape[1:-3]
    extent = blocks.shape[-3:]
    depth_lead = len(leading)
    shaped = blocks.reshape((count_x, count_y) + leading + extent)
    order = tuple(range(2, 2 + depth_lead)) + (0, 2 + depth_lead, 1, 3 + depth_lead, 4 + depth_lead)
    return shaped.transpose(order).reshape(
        leading + (count_x * extent[0], count_y * extent[1], extent[2])
    )


def field_rim(field):
    return extended(field, (("gx", 1), ("gy", 2)), 1)


def cond_rim(conduct):
    return extended(conduct, (("gx", 0), ("gy", 1)), 1)


def whole_cycle(source, level_index, whole_plans):
    cond_pad, diag_level, level_scale = whole_plans[level_index]
    field = DAMPING * source / diag_level

    def turn(turn_index, iterate):
        return relaxed(pad_plane(iterate, 1), source, cond_pad, diag_level, level_scale)

    return lax.fori_loop(0, COARSE_SWEEPS - 1, turn, field)


def part_cycle(source, level_index, level_plans, whole_plans, gather_level):
    if level_index == gather_level:
        blocks = lax.all_gather(source[None], ("gx", "gy"), axis=0, tiled=True)
        whole = assemble(blocks, lax.axis_size("gx"), lax.axis_size("gy"))
        correction = whole_cycle(whole, level_index, whole_plans)
        extent = source.shape
        starts = (0, lax.axis_index("gx") * extent[1], lax.axis_index("gy") * extent[2], 0)
        return lax.dynamic_slice(correction, starts, extent)
    cond_pad, diag_level, level_scale = level_plans[level_index]
    field = DAMPING * source / diag_level
    field = relaxed(field_rim(field), source, cond_pad, diag_level, level_scale)
    residual = source - stencil(field_rim(field), cond_pad, level_scale)
    field = field + prolong(
        part_cycle(restrict(residual), level_index + 1, level_plans, whole_plans, gather_level)
    )
    field = relaxed(field_rim(field), source, cond_pad, diag_level, level_scale)
    return relaxed(field_rim(field), source, cond_pad, diag_level, level_scale)


def distributed(conductivity, stations, currents, receivers, observed):
    row_count, col_count, z_count = conductivity.shape
    shot_count = currents.shape[0]
    count_x = lax.axis_size("gx")
    count_y = lax.axis_size("gy")
    gather_level = LEVELS - 1
    level_plans = []
    conduct = conductivity
    for level_index in range(gather_level):
        level_scale = 0.25**level_index
        cond_pad = cond_rim(conduct)
        level_plans.append((cond_pad, diagonal(cond_pad, level_scale), level_scale))
        conduct = restrict(conduct)
    blocks = lax.all_gather(conduct[None], ("gx", "gy"), axis=0, tiled=True)
    whole = assemble(blocks, count_x, count_y)
    whole_plans = {}
    level_index = 3
    level_scale = 0.25**level_index
    cond_pad = pad_plane(whole, 1)
    whole_plans[level_index] = (cond_pad, diagonal(cond_pad, level_scale), level_scale)
    total_y = col_count * count_y
    cell_x = stations // (total_y * z_count)
    cell_y = stations // z_count % total_y
    cell_z = stations % z_count
    local_x = cell_x - lax.axis_index("gx") * row_count
    local_y = cell_y - lax.axis_index("gy") * col_count
    owned = (local_x >= 0) & (local_x < row_count) & (local_y >= 0) & (local_y < col_count)
    block_size = row_count * col_count * z_count
    local_cell = jnp.where(owned, (local_x * col_count + local_y) * z_count + cell_z, 0)
    offsets = jnp.arange(shot_count)[:, None] * block_size + local_cell[None, :]
    targets = jnp.where(owned[None, :], offsets, shot_count * block_size).reshape(-1)

    def spread(amounts):
        flat = (
            jnp.zeros((shot_count * block_size,), jnp.float32)
            .at[targets]
            .add(amounts.reshape(-1), mode="drop")
        )
        return flat.reshape(shot_count, row_count, col_count, z_count)

    potentials = part_cycle(spread(currents), 0, level_plans, whole_plans, gather_level)
    local_values = jnp.where(
        owned[None, :], potentials.reshape(shot_count, block_size)[:, local_cell], 0.0
    )
    readings = lax.psum(local_values, ("gx", "gy"))
    positions = jnp.arange(stations.shape[0])[:, None]
    pairs = (receivers[:, 0][None, :] == positions).astype(jnp.float32) - (
        receivers[:, 1][None, :] == positions
    ).astype(jnp.float32)
    misfit = jnp.dot(readings, pairs, precision=lax.Precision.HIGHEST) - observed
    back_source = jnp.dot(misfit, pairs.T, precision=lax.Precision.HIGHEST)
    adjoint = part_cycle(spread(back_source), 0, level_plans, whole_plans, gather_level)
    stacked = jnp.concatenate([potentials, adjoint], axis=0)
    padded = extended(stacked, (("gx", 1), ("gy", 2)), 1)
    potential_pad = padded[:shot_count]
    adjoint_pad = padded[shot_count:]
    gradient = jnp.zeros_like(potentials)
    for other_u, other_w in zip(neighbour_list(potential_pad), neighbour_list(adjoint_pad)):
        gradient = gradient - 0.5 * (potentials - other_u) * (adjoint - other_w)
    summed = lax.psum_scatter(jnp.sum(gradient, axis=0), "shot", scatter_dimension=1, tiled=True)
    return (potentials, summed)


def per_device(conductivity, stations, currents, receivers, observed):
    blocks = lax.axis_size("gx") * lax.axis_size("gy")
    fits = conductivity.shape == (SIDE, SIDE * SIDE, LANES) and blocks == SIDE
    fits = fits and lax.axis_size("gy") == 2 and lax.axis_size("shot") == 2
    fits = fits and currents.shape[0] == 1
    plan = replicated if fits else distributed
    return plan(conductivity, stations, currents, receivers, observed)


def solution(mesh):
    in_specs = (
        P(("grp", "gx"), "gy", None),
        P("grp"),
        P(("grp", "shot"), None),
        P("grp", None),
        P(("grp", "shot"), None),
    )
    out_specs = (P(("grp", "shot"), "gx", "gy", None), P(("grp", "gx"), ("gy", "shot"), None))
    return jax.shard_map(
        per_device, mesh=mesh, in_specs=in_specs, out_specs=out_specs, check_vma=False
    )
```

```python
import functools

import jax
import jax.numpy as jnp
from jax import lax
from jax.experimental import pallas as pl
from jax.experimental.pallas import tpu as pltpu
from jax.sharding import PartitionSpec as P

LEVELS = 4
COARSE_SWEEPS = 16


DAMPING = 0.8

SIDE = 8
LANES = 128
GROUP = 16
VMEM_BYTES = 48 * 2**20
SMALL_BYTES = 6 * 2**20


def pieces_of(value, count):
    pieces = []
    for _ in range(count):
        pieces.append(value.astype(jnp.bfloat16))
        value = value - pieces[-1].astype(jnp.float32)
    return pieces[::-1]


def product(value, matrix, count, dims=((1,), (0,))):
    result = None
    for piece in pieces_of(value, count):
        term = lax.dot_general(
            piece, matrix, (dims, ((), ())), preferred_element_type=jnp.float32
        )
        result = term if result is None else result + term
    return result


def iota(shape, dim):
    return lax.broadcasted_iota(jnp.int32, shape, dim)


def station_table(station):
    cell_x, cell_y, cell_z = station >> 14, station >> 7 & 127, station & 127
    row = (cell_x >> 3) * 2 + (cell_y >> 6)
    return cell_x, cell_y, cell_z, row, (cell_y >> 3 & 7) * GROUP + (cell_z >> 3)


def lane_order():
    row, col = iota((LANES, LANES), 0), iota((LANES, LANES), 1)
    chosen = row == col % GROUP * SIDE + col // GROUP
    return jnp.where(chosen, 1.0, 0.0).astype(jnp.bfloat16)


def exchange_groups(tiles):
    tiles = list(tiles)
    group = iota(tiles[0].shape, 1) // GROUP
    for bit in range(3):
        step = 1 << bit
        keep = (group & step) == 0
        for low in range(SIDE):
            if low & step == 0:
                a, b = tiles[low], tiles[low | step]
                tiles[low] = jnp.where(keep, a, pltpu.roll(b, step * GROUP, 1))
                tiles[low | step] = jnp.where(keep, pltpu.roll(a, LANES - step * GROUP, 1), b)
    return tiles


def own_place():
    return lax.axis_index("gx") * 2 + lax.axis_index("gy"), lax.axis_index("shot")


def to_blocks_kernel(natural_ref, blocks_ref, half_ref, planes, sems):
    copies = [
        pltpu.make_async_copy(natural_ref.at[x], planes.at[x], sems.at[x]) for x in range(SIDE)
    ]
    for copy in copies:
        copy.start()
    order = lane_order()
    for x in range(SIDE):
        copies[x].wait()
        tiles = product(planes[x], order, 3)
        tiles = [tiles[SIDE * k : SIDE * (k + 1)] for k in range(SIDE)]
        for z, tile in enumerate(exchange_groups(tiles)):
            blocks_ref[pl.ds((x * SIDE + z) * SIDE, SIDE), :] = tile
    count = half_ref.shape[0]
    low, high = blocks_ref[pl.ds(0, count), :], blocks_ref[pl.ds(count, count), :]
    half_ref[...] = jnp.where(own_place()[1] == 0, low, high)


def from_blocks(tiles, order):
    natural = jnp.concatenate(exchange_groups(tiles), axis=0)
    return product(natural, order, 3, ((1,), (1,)))


def block_up(field, axis):
    if axis == 0:
        return pltpu.roll(field, 6, 1)
    if axis == 2:
        return pltpu.roll(field, LANES - 1, 2)
    turned = pltpu.roll(field, LANES - GROUP, 2)
    return jnp.where(iota(field.shape, 2) < LANES - GROUP, turned, pltpu.roll(turned, 7, 1))


def block_down(field, axis):
    if axis == 0:
        return pltpu.roll(field, 2, 1)
    if axis == 2:
        return pltpu.roll(field, 1, 2)
    turned = pltpu.roll(field, GROUP, 2)
    return jnp.where(iota(field.shape, 2) >= GROUP, turned, pltpu.roll(turned, 1, 1))


def inside_up(field, axis):
    sub, lane = iota(field.shape, 1), iota(field.shape, 2)
    if axis == 0:
        keep = sub < 6
    elif axis == 1:
        keep = (lane < LANES - GROUP) | (sub % 2 == 0)
    else:
        keep = lane % GROUP < GROUP - 1
    return jnp.where(keep, field, 0.0)


def inside_down(field, axis):
    sub, lane = iota(field.shape, 1), iota(field.shape, 2)
    if axis == 0:
        keep = sub >= 2
    elif axis == 1:
        keep = (lane >= GROUP) | (sub % 2 == 1)
    else:
        keep = lane % GROUP > 0
    return jnp.where(keep, field, 0.0)


def pair_rows(row):
    count = row.shape[0] // 2
    return jnp.concatenate([row[2 * i : 2 * i + 1] + row[2 * i + 1 : 2 * i + 2] for i in range(count)])


def twice(row):
    return jnp.concatenate([row[i // 2 : i // 2 + 1] for i in range(2 * row.shape[0])])


def electrode_kernel(
    stations_ref,
    currents_ref,
    receivers_ref,
    observed_ref,
    cells_ref,
    spot_ref,
    rows_ref,
    same_ref,
    pairs_ref,
    held_ref,
):
    stations = stations_ref[...]
    electrodes = stations.shape[1]
    cell_x, cell_y, cell_z, row, spot = station_table(stations)
    wide = SIDE + 2
    register = (((cell_x & 7) + 1) * wide + (cell_z & 7) + 1) * wide + (cell_y & 7) + 1
    cells_ref[...] = register * SIDE + row
    spot_ref[...] = spot
    held_ref[...] = observed_ref[...]
    line = stations & 0x1C387 | row << 20
    same = jnp.broadcast_to(line, (electrodes, electrodes))
    same = jnp.where(same == same.T, 1.0, 0.0).astype(jnp.bfloat16)
    same_ref[...] = same
    rows_ref[...] = shared_rows(currents_ref[...], spot, same)
    receivers = receivers_ref[...]
    numbers = iota((receivers.shape[0], electrodes), 1)
    pairs = jnp.where(numbers == receivers[:, 0:1], 1.0, 0.0) - jnp.where(
        numbers == receivers[:, 1:2], 1.0, 0.0
    )
    pairs_ref[...] = pairs.astype(jnp.bfloat16)


def shared_rows(amounts, spot, same):
    electrodes = amounts.shape[1]
    at_spot = iota((LANES, electrodes), 0) == spot
    return product(jnp.where(at_spot, amounts, 0.0), same, 3).T


class Edged:
    def __init__(self, ref, side):
        self.ref, self.side = ref, side

    def start(self, x, z, y=0):
        wide = self.side + 2
        return (((x + 1) * wide + z + 1) * wide + y + 1) * SIDE

    def __getitem__(self, at):
        x, z = at
        rows = self.ref[pl.ds(self.start(x, z), self.side * SIDE), :]
        return rows.reshape(self.side, SIDE, LANES)

    def __setitem__(self, at, value):
        x, z = at
        self.ref[pl.ds(self.start(x, z), self.side * SIDE), :] = value.reshape(-1, LANES)

    def put(self, x, z, value, exact=False):
        self[x, z] = value
        n = self.side
        if z == 0:
            edge = block_up(value, 2)
            self[x, n] = inside_up(edge, 2) if exact else edge
        if z == n - 1:
            edge = block_down(value, 2)
            self[x, -1] = inside_down(edge, 2) if exact else edge
        if x == 0:
            edge = block_up(value, 0)
            self[n, z] = inside_up(edge, 0) if exact else edge
        if x == n - 1:
            edge = block_down(value, 0)
            self[-1, z] = inside_down(edge, 0) if exact else edge
        if exact:
            after = inside_up(block_up(value[:1], 1), 1)
            self.ref[pl.ds(self.start(x, z, n), SIDE), :] = after[0]
            before = inside_down(block_down(value[n - 1 :], 1), 1)
            self.ref[pl.ds(self.start(x, z, -1), SIDE), :] = before[0]

    def close_z(self, x, exact=False):
        n = self.side
        after, before = block_up(self[x, 0], 2), block_down(self[x, n - 1], 2)
        self[x, n] = inside_up(after, 2) if exact else after
        self[x, -1] = inside_down(before, 2) if exact else before

    def close(self, exact=False):
        n = self.side
        for z in range(n):
            after = block_up(self[0, z], 0)
            self[n, z] = inside_up(after, 0) if exact else after
            before = block_down(self[n - 1, z], 0)
            self[-1, z] = inside_down(before, 0) if exact else before


class Rows:
    def __init__(self, ref, side, first_x=0, first_z=0):
        self.ref, self.side, self.first_x, self.first_z = ref, side, first_x, first_z

    def place(self, at):
        count = self.side - self.first_z
        rows = self.side * SIDE
        return pl.ds(((at[0] - self.first_x) * count + at[1] - self.first_z) * rows, rows)

    def __getitem__(self, at):
        return self.ref[self.place(at), :].reshape(self.side, SIDE, LANES)

    def __setitem__(self, at, value):
        self.ref[self.place(at), :] = value.reshape(-1, LANES)


def rolled(count, body):
    def one(x, carry):
        body(x)
        return carry

    lax.fori_loop(0, count, one, 0)


def next_in_y(row):
    return jnp.concatenate([row[1:], block_up(row[:1], 1)])


def last_in_y(row):
    return jnp.concatenate([block_down(row[-1:], 1), row[:-1]])


class Level:
    def __init__(self, refs, index):
        self.side = side = SIDE >> index
        self.scale = 0.25**index
        edged = [Edged(ref, side) for ref in refs[:5]]
        self.cond, self.first, self.second, self.base, self.weight = edged
        self.link_x = Rows(refs[5], side, first_x=-1)
        self.link_y = Rows(refs[6], side)
        self.link_z = Rows(refs[7], side, first_z=-1)
        self.back = Rows(refs[8], side)

    @staticmethod
    def scratch(index):
        side = SIDE >> index
        sizes = [(side + 2) ** 3] * 5
        sizes += [side**2 * (side + 1), side**3, side**2 * (side + 1), side**3]
        return [pltpu.VMEM((size * SIDE, LANES), jnp.float32) for size in sizes]

    def pairs(self, body):
        for i in range(self.side // 2):
            body(2 * i)

    def prepare(self):
        n = self.side
        cond = self.cond

        def plane(x):
            for z in range(n):
                here, ahead, next_x = cond[x, z], cond[x, z + 1], cond[x + 1, z]
                after = inside_up(block_up(here[:1], 1), 1)
                before = inside_down(block_down(here[-1:], 1), 1)
                next_y = jnp.concatenate([here[1:], after])
                last_y = jnp.concatenate([before, here[:-1]])
                total = (next_x + cond[x - 1, z]) + (ahead + cond[x, z - 1]) + (next_y + last_y)
                total = 6.0 * here + total
                self.weight[x, z] = DAMPING / total
                if n == SIDE:
                    self.base[x, z] = jnp.zeros_like(here)
                self.back[x, z] = total * (0.5 * self.scale / DAMPING)
                self.link_x[x, z] = here + next_x
                link = here + next_y
                self.link_y[x, z] = jnp.concatenate([link[:-1], inside_up(link[-1:], 1)])
                link = here + ahead
                if z == n - 1:
                    link = inside_up(link, 2)
                    self.link_z[x, -1] = block_down(link, 2)
                self.link_z[x, z] = link

        if n == SIDE:
            rolled(n, plane)
        else:
            for x in range(n):
                plane(x)
        for z in range(n):
            link = inside_up(self.link_x[n - 1, z], 0)
            self.link_x[n - 1, z] = link
            self.link_x[-1, z] = block_down(link, 0)

    def flows(self, x, z, here, ahead, outer, down):
        result = []
        inner = self.link_x[x, z]
        sides = [
            self.link_x[x - 1, z] * outer[0] + inner * here[1],
            inner * here[0] + self.link_x[x + 1, z] * outer[1],
        ]
        for p in range(2):
            link_y, link_z = self.link_y[x + p, z], self.link_z[x + p, z]
            along = link_y * next_in_y(here[p]) + last_in_y(link_y * here[p])
            total = sides[p] + (link_z * ahead[p] + down[p]) + along
            down[p] = link_z * here[p]
            result.append(self.weight[x + p, z] * total)
        return result

    def rows(self, field, x):
        here = [field[x, 0], field[x + 1, 0]]
        down = [self.link_z[x + p, -1] * field[x + p, -1] for p in range(2)]
        for z in range(self.side):
            ahead = [field[x, z + 1], field[x + 1, z + 1]]
            outer = [field[x - 1, z], field[x + 2, z]]
            yield z, here, self.flows(x, z, here, ahead, outer, down)
            here = ahead

    def sweep(self, field, out, exact=False):
        def pair(x):
            for z, here, sums in self.rows(field, x):
                for p in range(2):
                    if field is self.base:
                        value = (2.0 - DAMPING) * here[p] + sums[p]
                    else:
                        value = (1.0 - DAMPING) * here[p] + (self.base[x + p, z] + sums[p])
                    out.put(x + p, z, value, exact)

        self.pairs(pair)

    def halve(self, rows, coarse):
        def pair(x):
            held = None
            for z, row in enumerate(rows(x)):
                row = row[0] + row[1]
                if z % 2 == 0:
                    held = row
                else:
                    coarse(x // 2, z // 2, 0.125 * pair_rows(held + row))

        self.pairs(pair)

    def descend(self, coarse):
        self.sweep(self.base, self.second)

        def residuals(x):
            for z, here, sums in self.rows(self.second, x):
                result = []
                for p in range(2):
                    swept = (1.0 - DAMPING) * here[p] + (self.base[x + p, z] + sums[p])
                    self.first[x + p, z] = swept
                    result.append((swept - here[p]) * self.back[x + p, z])
                yield result

        self.halve(residuals, coarse)

    def ascend(self, correction, out, exact=False):
        def pair(x):
            i = x // 2
            here = twice(correction(i, 0))
            start = twice(correction(i, -1))
            down = [self.link_z[x + p, -1] * start for p in range(2)]
            for z in range(self.side):
                ahead = twice(correction(i, (z + 1) // 2))
                outer = [twice(correction(i - 1, z // 2)), twice(correction(i + 1, z // 2))]
                sums = self.flows(x, z, [here, here], [ahead, ahead], outer, down)
                for p in range(2):
                    value = self.first[x + p, z] + ((1.0 - DAMPING) * here + sums[p])
                    self.second.put(x + p, z, value)
                here = ahead

        self.pairs(pair)
        self.sweep(self.second, out, exact)


class HeldLevel:
    def __init__(self, refs, index):
        self.side = 2
        self.scale = 0.25**index
        self.cond, self.first = Edged(refs[0], 2), Edged(refs[1], 2)
        self.weight, self.back = Rows(refs[2], 2), Rows(refs[3], 2)
        self.links = [Rows(ref, 2) for ref in refs[4:]]

    @staticmethod
    def scratch(index):
        sizes = [4**3] * 2 + [2**3] * 8
        return [pltpu.VMEM((size * SIDE, LANES), jnp.float32) for size in sizes]

    def around(self, field, inside=False):
        def moved(row, axis, up):
            row = (block_up if up else block_down)(row, axis)
            return (inside_up if up else inside_down)(row, axis) if inside else row

        result = {}
        for (x, z), here in field.items():
            result[x, z] = [
                field[1, z] if x == 0 else moved(field[0, z], 0, True),
                field[0, z] if x == 1 else moved(field[1, z], 0, False),
                jnp.concatenate([here[1:], moved(here[:1], 1, True)]),
                jnp.concatenate([moved(here[-1:], 1, False), here[:-1]]),
                field[x, 1] if z == 0 else moved(field[x, 0], 2, True),
                field[x, 0] if z == 1 else moved(field[x, 1], 2, False),
            ]
        return result

    def prepare(self):
        field = {(x, z): self.cond[x, z] for x in range(2) for z in range(2)}
        for at, others in self.around(field, inside=True).items():
            here = field[at]
            total = others[0]
            for other in others[1:]:
                total = total + other
            total = 3.0 * here + 0.5 * total
            inverse = DAMPING / total
            self.weight[at] = inverse
            self.back[at] = total * (self.scale / DAMPING)
            for index, other in enumerate(others):
                link = 0.5 * inverse * (here + other)
                self.links[index][at] = jnp.where(other > 0.0, link, 0.0)

    def halve(self, rows, coarse):
        total = None
        for row in rows(0):
            row = row[0] + row[1]
            total = row if total is None else total + row
        coarse(0, 0, 0.125 * (total[:1] + total[1:]))

    def sums(self, field, base):
        result = {}
        for at, others in self.around(field).items():
            total = base[at]
            for link, other in zip(self.links, others):
                total = total + link[at] * other
            result[at] = total
        return result

    def swept(self, field, base):
        sums = self.sums(field, base)
        return {at: (1.0 - DAMPING) * field[at] + sums[at] for at in field}

    def cycle(self, base, solve, out):
        field = self.swept(base, base)
        sums = self.sums(field, base)
        total = None
        for at in field:
            residual = (sums[at] - DAMPING * field[at]) * self.back[at]
            total = residual if total is None else total + residual
        solved = solve(0.125 * (total[:1] + total[1:]))
        row = twice(solved)
        copied = {at: row for at in field}
        change = {at: sums[at] + (1.0 - DAMPING) * (field[at] + row) for at in field}
        field = self.sums(copied, change)
        for (x, z), value in self.swept(field, base).items():
            out.put(x, z, value)


def replicated_kernel(
    whole,
    halved,
    cells_ref,
    *refs,
):
    parts = refs[:whole], refs[whole : whole + halved]
    solve_kernel(*parts, cells_ref, *refs[whole + halved :])


def solve_kernel(
    part_refs,
    half_refs,
    cells_ref,
    spot_ref,
    rows_ref,
    same_ref,
    pairs_ref,
    observed_ref,
    potentials_ref,
    mine_ref,
    theirs_ref,
    gathered,
    owned,
    beside,
    sent,
    sem,
    *level_refs,
):
    f32 = jnp.float32
    electrodes = spot_ref.shape[1]
    levels, used = [], 0
    for index in range(LEVELS - 1):
        kind = HeldLevel if index == LEVELS - 2 else Level
        count = len(kind.scratch(index))
        levels.append(kind(level_refs[used : used + count], index))
        used += count
    fine = levels[0]
    forward = fine.cond
    wide = SIDE * SIDE * SIDE

    device, shot = own_place()

    def place(part, row, x, index):
        for z in range(SIDE):
            fine.cond.ref[pl.ds(fine.cond.start(x, z) + index, SIDE, stride=SIDE), :] = part[
                pl.ds((row * SIDE + z) * SIDE, SIDE), :
            ]

    def collect(x):
        for k, part in enumerate(part_refs):
            place(part, x, x, device ^ k)

    def collect_half(x):
        for k, part in enumerate(half_refs):
            swapped, index = k // 2 % 2, len(part_refs) + k // 4 * 2 + k % 2
            place(part, x, (shot ^ swapped) * (SIDE // 2) + x, device ^ index)

    def edges(x):
        fine.cond.close_z(x, exact=True)

    rolled(SIDE, collect)
    for x in range(SIDE // 2):
        collect_half(x)
    rolled(SIDE, edges)
    fine.cond.close(exact=True)

    coarsest = []
    for level, below in zip(levels, levels[1:] + [None]):
        level.prepare()

        def coarse(x, z, row, below=below):
            if below is None:
                coarsest.append(row)
            else:
                below.cond.put(x, z, row, exact=True)

        level.halve(
            lambda x, level=level: [
                (level.cond[x, z], level.cond[x + 1, z]) for z in range(level.side)
            ],
            coarse,
        )

    keep = iota((1, SIDE, LANES), 1) % 2 == 0
    lane = iota((1, SIDE, LANES), 2)

    def split(value):
        return [jnp.where(keep, part, 0.0) for part in (value, pltpu.roll(value, SIDE - 1, 1))]

    def around(value):
        low, high = value
        low_up, high_up = [pltpu.roll(part, LANES - GROUP, 2) for part in value]
        low_down, high_down = [pltpu.roll(part, GROUP, 2) for part in value]
        along = [[move(part, axis) for part in value] for axis in (0, 2) for move in (block_up, block_down)]
        return along + [
            [jnp.where(lane < LANES - GROUP, low_up, high_up), high_up],
            [low_down, jnp.where(lane >= GROUP, high_down, low_down)],
        ]

    sub = iota((1, SIDE, LANES), 1)
    inside_last = [
        [sub < 6] * 2,
        [sub >= 2] * 2,
        [lane % GROUP < GROUP - 1] * 2,
        [lane % GROUP > 0] * 2,
        [keep, lane < LANES - GROUP],
        [lane >= GROUP, keep],
    ]
    last_scale = 0.25 ** (LEVELS - 1)
    here = split(coarsest[0])
    others = [
        [jnp.where(inside & keep, part, 0.0) for inside, part in zip(pair, moved)]
        for pair, moved in zip(inside_last, around(here))
    ]
    last_weight, last_links = [], []
    for half, part in enumerate(here):
        total = 3.0 * part
        for other in others:
            total = total + 0.5 * other[half]
        inverse = jnp.where(keep, DAMPING / jnp.where(keep, total, 1.0), 0.0)
        last_weight.append(inverse * (1.0 / last_scale))
        last_links.append(
            [
                jnp.where(pair[half] & keep, 0.5 * inverse * (part + other[half]), 0.0)
                for pair, other in zip(inside_last, others)
            ]
        )

    def solve_last(rhs):
        base = [weight * part for weight, part in zip(last_weight, split(rhs))]
        value = base
        for _ in range(COARSE_SWEEPS - 1):
            moved = around(value)
            fresh = []
            for half in range(2):
                parts = [link * other[half] for link, other in zip(last_links[half], moved)]
                start = base[half] + (1.0 - DAMPING) * value[half]
                fresh.append(((start + parts[0]) + (parts[1] + parts[2])) + (parts[3] + (parts[4] + parts[5])))
            value = fresh
        return value[0] + pltpu.roll(value[1], 1, 1)

    def cycle(index, out, exact=False):
        level = levels[index]
        below = levels[index + 1]
        if index == LEVELS - 3:
            base = {}

            def take(x, z, row):
                base[x, z] = below.weight[x, z] * (row * (1.0 / below.scale))

            level.descend(take)
            below.cycle(base, solve_last, below.first)
        else:
            level.descend(
                lambda x, z, row: below.base.put(
                    x, z, below.weight[x, z] * (row * (2.0 / below.scale))
                )
            )
            cycle(index + 1, below.first)
        level.ascend(lambda x, z: below.first[x, z], out, exact)

    spot = spot_ref[...]
    at_spot = iota((LANES, electrodes), 0) == spot
    order = lane_order()
    wide = SIDE + 2
    sending = pltpu.make_async_copy(sent, potentials_ref, sem)

    def each(body):
        def one(electrode, carry):
            body(pl.ds(electrode, 1), pl.ds(cells_ref[0, electrode], 1))
            return carry

        lax.fori_loop(0, electrodes, one, 0, unroll=32)

    def put(electrode, cell):
        fine.base.ref[cell, :] = (2.0 * gathered[electrode, :]) * fine.weight.ref[cell, :]

    def read(electrode, cell):
        gathered[electrode, :] = forward.ref[cell, :]

    def exact(row, dims):
        return product(jnp.broadcast_to(row, (16, row.shape[1])), pairs_ref[...], 3, dims)[0:1]

    sub, lane = iota((SIDE, LANES), 0), iota((SIDE, LANES), 1)

    def margin(x, z, y):
        return forward.ref[pl.ds(forward.start(x, z, y) + device, 1), :]

    def extract(index):
        for x in range(-1, SIDE + 1):
            for z in range(SIDE):
                at = (x + 1) * wide + z + 1
                start = forward.start(x, z) + device
                row = forward.ref[pl.ds(start, SIDE, stride=SIDE), :]
                owned[index, at] = row
                if 0 <= x < SIDE:
                    after, before = margin(x, z, SIDE), margin(x, z, -1)
                    place = x * SIDE + z
                    turned = pltpu.roll(row, SIDE - 1, 0)
                    beside[index, 0, place] = jnp.where(sub == SIDE - 1, after, turned)
                    beside[index, 1, place] = jnp.where(sub == 0, before, pltpu.roll(row, 1, 0))
                    if z == 0:
                        edge = pltpu.roll(row, LANES - 1, 1)
                        owned[index, at + SIDE] = jnp.where(lane % GROUP < GROUP - 1, edge, 0.0)
                    if z == SIDE - 1:
                        edge = pltpu.roll(row, 1, 1)
                        owned[index, at - SIDE] = jnp.where(lane % GROUP > 0, edge, 0.0)

    def solve(index):
        each(put)
        rolled(SIDE, fine.base.close_z)
        fine.base.close()
        cycle(0, forward, exact=True)
        extract(index)

        @pl.when(index == 0)
        def _():
            for x in range(SIDE):
                tiles = [owned[0, (x + 1) * wide + z + 1] for z in range(SIDE)]
                sent[x] = from_blocks(tiles, order)
            sending.start()
            each(read)
            readings = jnp.where(at_spot, gathered[...].T, 0.0)
            readings = jnp.sum(readings, axis=0, keepdims=True)
            misfit = exact(readings, ((1,), (1,))) - observed_ref[...]
            gathered[...] = shared_rows(exact(misfit, ((1,), (0,))), spot, same_ref[...])

    gathered[...] = rows_ref[...]
    rolled(2, solve)

    chunk = mine_ref.shape[1]
    even = shot == 0
    for x in range(SIDE):
        tiles = []
        for z in range(SIDE):
            at = (x + 1) * wide + z + 1
            here_u, here_w = owned[0, at], owned[1, at]
            total = None
            for step in (wide, -wide, 1, -1):
                term = (here_u - owned[0, at + step]) * (here_w - owned[1, at + step])
                total = term if total is None else total + term
            for side in range(2):
                other_u, other_w = beside[0, side, x * SIDE + z], beside[1, side, x * SIDE + z]
                total = total + (here_u - other_u) * (here_w - other_w)
            tiles.append(-0.5 * total)
        natural = from_blocks(tiles, order)
        low, high = natural[:chunk], natural[chunk:]
        mine_ref[x] = jnp.where(even, low, high)
        theirs_ref[x] = jnp.where(even, high, low)
    sending.wait()


def replicated(conductivity, stations, currents, receivers, observed):
    rows, cols, depth = conductivity.shape
    f32 = jnp.float32
    electrodes = stations.shape[0]
    total = rows * cols
    vmem = pl.BlockSpec(memory_space=pltpu.VMEM)
    smem = pl.BlockSpec(memory_space=pltpu.SMEM)
    station_row = stations.reshape(1, electrodes)
    mine, half = pl.pallas_call(
        to_blocks_kernel,
        out_shape=(
            jax.ShapeDtypeStruct((total, LANES), f32),
            jax.ShapeDtypeStruct((total // 2, LANES), f32),
        ),
        in_specs=[pl.BlockSpec(memory_space=pl.ANY)],
        out_specs=(vmem, vmem),
        scratch_shapes=[
            pltpu.VMEM((rows, cols, LANES), f32),
            pltpu.SemaphoreType.DMA((rows,)),
        ],
        compiler_params=pltpu.CompilerParams(vmem_limit_bytes=SMALL_BYTES),
    )(conductivity)
    swap = [(0, 1), (1, 0)]

    def partner(part, k):
        count = lax.axis_size("gx")
        return lax.ppermute(part, "gx", [(i, i ^ k) for i in range(count)])

    def with_mate(part):
        return [part, lax.ppermute(part, "gy", swap)]

    far = partner(half, 2)
    near = partner(mine, 1)
    line = jax.ShapeDtypeStruct((1, electrodes), jnp.int32)
    cells, spot, rows_of, same, pairs, held = pl.pallas_call(
        electrode_kernel,
        out_shape=(
            line,
            line,
            jax.ShapeDtypeStruct((electrodes, LANES), f32),
            jax.ShapeDtypeStruct((electrodes, electrodes), jnp.bfloat16),
            jax.ShapeDtypeStruct((receivers.shape[0], electrodes), jnp.bfloat16),
            jax.ShapeDtypeStruct(observed.shape, f32),
        ),
        in_specs=[vmem] * 4,
        out_specs=(vmem,) * 6,
        compiler_params=pltpu.CompilerParams(vmem_limit_bytes=SMALL_BYTES),
        cost_estimate=pl.CostEstimate(flops=100_000_000, bytes_accessed=1_000_000, transcendentals=0),
    )(station_row, currents, receivers, observed)
    far, rows_of = lax.optimization_barrier((far, rows_of))
    far = [far, partner(far, 1)]
    halved = [piece for own in far for piece in (own, lax.ppermute(own, "shot", swap))]
    parts = [piece for own in (mine, near) for piece in with_mate(own)]
    halved = [piece for own in halved for piece in with_mate(own)]
    chunk = cols // 2
    levels = [shape for index in range(LEVELS - 2) for shape in Level.scratch(index)]
    levels += HeldLevel.scratch(LEVELS - 2)
    potentials, own, theirs = pl.pallas_call(
        functools.partial(replicated_kernel, len(parts), len(halved)),
        out_shape=(
            jax.ShapeDtypeStruct((rows, cols, LANES), f32),
            jax.ShapeDtypeStruct((rows, chunk, LANES), f32),
            jax.ShapeDtypeStruct((rows, chunk, LANES), f32),
        ),
        in_specs=[smem] + [vmem] * (len(parts) + len(halved) + 5),
        out_specs=(pl.BlockSpec(memory_space=pl.ANY), vmem, vmem),
        scratch_shapes=[
            pltpu.VMEM((electrodes, LANES), f32),
            pltpu.VMEM((2, (SIDE + 2) ** 2, SIDE, LANES), f32),
            pltpu.VMEM((2, 2, SIDE**2, SIDE, LANES), f32),
            pltpu.VMEM((rows, cols, LANES), f32),
            pltpu.SemaphoreType.DMA,
        ]
        + levels,
        compiler_params=pltpu.CompilerParams(vmem_limit_bytes=VMEM_BYTES),
        cost_estimate=pl.CostEstimate(flops=200_000_000, bytes_accessed=4_000_000, transcendentals=0),
    )(cells, *parts, *halved, spot, rows_of, same, pairs, held)
    return potentials[None], own + lax.ppermute(theirs, "shot", swap)


def extended(array, sides, width):
    for axis, dim in sides:
        size, length = (lax.axis_size(axis), array.shape[dim])
        up = [(i, (i + 1) % size) for i in range(size - 1)]
        down = [(j, i) for i, j in up]
        last = lax.slice_in_dim(array, length - width, length, axis=dim)
        leading = lax.slice_in_dim(array, 0, width, axis=dim)
        before = lax.ppermute(last, axis, up)
        after = lax.ppermute(leading, axis, down)
        array = jnp.concatenate([before, array, after], axis=dim)
    return array


def upper_z(field):
    return jnp.concatenate([field[..., 1:], jnp.zeros_like(field[..., :1])], axis=-1)


def lower_z(field):
    return jnp.concatenate([jnp.zeros_like(field[..., :1]), field[..., :-1]], axis=-1)


def trim_circle(field, circle_width):
    return field[..., circle_width:-circle_width, circle_width:-circle_width, :]


def pad_plane(field, circle_width):
    spec = [(0, 0)] * (field.ndim - 3) + [
        (circle_width, circle_width),
        (circle_width, circle_width),
        (0, 0),
    ]
    return jnp.pad(field, spec)


def neighbour_list(field_pad):
    centre = trim_circle(field_pad, 1)
    return [
        field_pad[..., 2:, 1:-1, :],
        field_pad[..., :-2, 1:-1, :],
        field_pad[..., 1:-1, 2:, :],
        field_pad[..., 1:-1, :-2, :],
        upper_z(centre),
        lower_z(centre),
    ]


def stencil(field_pad, cond_pad, level_scale):
    centre = trim_circle(field_pad, 1)
    centre_cond = trim_circle(cond_pad, 1)
    summed = jnp.zeros_like(centre)
    for other, other_cond in zip(neighbour_list(field_pad), neighbour_list(cond_pad)):
        summed = summed + level_scale * 0.5 * (centre_cond + other_cond) * (centre - other)
    return summed


def diagonal(cond_pad, level_scale):
    centre_cond = trim_circle(cond_pad, 1)
    summed = jnp.zeros_like(centre_cond)
    for other_cond in neighbour_list(cond_pad):
        summed = summed + level_scale * 0.5 * (centre_cond + other_cond)
    return summed


def relaxed(field_pad, source, cond_pad, diag_level, level_scale):
    return (
        trim_circle(field_pad, 1)
        + DAMPING * (source - stencil(field_pad, cond_pad, level_scale)) / diag_level
    )


def restrict(field):
    leading = field.shape[:-3]
    extent = field.shape[-3:]
    shaped = field.reshape(leading + (extent[0] // 2, 2, extent[1] // 2, 2, extent[2] // 2, 2))
    return shaped.mean(axis=(-5, -3, -1))


def prolong(field):
    return jnp.repeat(jnp.repeat(jnp.repeat(field, 2, axis=-3), 2, axis=-2), 2, axis=-1)


def assemble(blocks, count_x, count_y):
    leading = blocks.shape[1:-3]
    extent = blocks.shape[-3:]
    depth_lead = len(leading)
    shaped = blocks.reshape((count_x, count_y) + leading + extent)
    order = tuple(range(2, 2 + depth_lead)) + (0, 2 + depth_lead, 1, 3 + depth_lead, 4 + depth_lead)
    return shaped.transpose(order).reshape(
        leading + (count_x * extent[0], count_y * extent[1], extent[2])
    )


def field_rim(field):
    return extended(field, (("gx", 1), ("gy", 2)), 1)


def cond_rim(conduct):
    return extended(conduct, (("gx", 0), ("gy", 1)), 1)


def whole_cycle(source, level_index, whole_plans):
    cond_pad, diag_level, level_scale = whole_plans[level_index]
    field = DAMPING * source / diag_level

    def turn(turn_index, iterate):
        return relaxed(pad_plane(iterate, 1), source, cond_pad, diag_level, level_scale)

    return lax.fori_loop(0, COARSE_SWEEPS - 1, turn, field)


def part_cycle(source, level_index, level_plans, whole_plans, gather_level):
    if level_index == gather_level:
        blocks = lax.all_gather(source[None], ("gx", "gy"), axis=0, tiled=True)
        whole = assemble(blocks, lax.axis_size("gx"), lax.axis_size("gy"))
        correction = whole_cycle(whole, level_index, whole_plans)
        extent = source.shape
        starts = (0, lax.axis_index("gx") * extent[1], lax.axis_index("gy") * extent[2], 0)
        return lax.dynamic_slice(correction, starts, extent)
    cond_pad, diag_level, level_scale = level_plans[level_index]
    field = DAMPING * source / diag_level
    field = relaxed(field_rim(field), source, cond_pad, diag_level, level_scale)
    residual = source - stencil(field_rim(field), cond_pad, level_scale)
    field = field + prolong(
        part_cycle(restrict(residual), level_index + 1, level_plans, whole_plans, gather_level)
    )
    field = relaxed(field_rim(field), source, cond_pad, diag_level, level_scale)
    return relaxed(field_rim(field), source, cond_pad, diag_level, level_scale)


def distributed(conductivity, stations, currents, receivers, observed):
    row_count, col_count, z_count = conductivity.shape
    shot_count = currents.shape[0]
    count_x = lax.axis_size("gx")
    count_y = lax.axis_size("gy")
    gather_level = LEVELS - 1
    level_plans = []
    conduct = conductivity
    for level_index in range(gather_level):
        level_scale = 0.25**level_index
        cond_pad = cond_rim(conduct)
        level_plans.append((cond_pad, diagonal(cond_pad, level_scale), level_scale))
        conduct = restrict(conduct)
    blocks = lax.all_gather(conduct[None], ("gx", "gy"), axis=0, tiled=True)
    whole = assemble(blocks, count_x, count_y)
    whole_plans = {}
    level_index = 3
    level_scale = 0.25**level_index
    cond_pad = pad_plane(whole, 1)
    whole_plans[level_index] = (cond_pad, diagonal(cond_pad, level_scale), level_scale)
    total_y = col_count * count_y
    cell_x = stations // (total_y * z_count)
    cell_y = stations // z_count % total_y
    cell_z = stations % z_count
    local_x = cell_x - lax.axis_index("gx") * row_count
    local_y = cell_y - lax.axis_index("gy") * col_count
    owned = (local_x >= 0) & (local_x < row_count) & (local_y >= 0) & (local_y < col_count)
    block_size = row_count * col_count * z_count
    local_cell = jnp.where(owned, (local_x * col_count + local_y) * z_count + cell_z, 0)
    offsets = jnp.arange(shot_count)[:, None] * block_size + local_cell[None, :]
    targets = jnp.where(owned[None, :], offsets, shot_count * block_size).reshape(-1)

    def spread(amounts):
        flat = (
            jnp.zeros((shot_count * block_size,), jnp.float32)
            .at[targets]
            .add(amounts.reshape(-1), mode="drop")
        )
        return flat.reshape(shot_count, row_count, col_count, z_count)

    potentials = part_cycle(spread(currents), 0, level_plans, whole_plans, gather_level)
    local_values = jnp.where(
        owned[None, :], potentials.reshape(shot_count, block_size)[:, local_cell], 0.0
    )
    readings = lax.psum(local_values, ("gx", "gy"))
    positions = jnp.arange(stations.shape[0])[:, None]
    pairs = (receivers[:, 0][None, :] == positions).astype(jnp.float32) - (
        receivers[:, 1][None, :] == positions
    ).astype(jnp.float32)
    misfit = jnp.dot(readings, pairs, precision=lax.Precision.HIGHEST) - observed
    back_source = jnp.dot(misfit, pairs.T, precision=lax.Precision.HIGHEST)
    adjoint = part_cycle(spread(back_source), 0, level_plans, whole_plans, gather_level)
    stacked = jnp.concatenate([potentials, adjoint], axis=0)
    padded = extended(stacked, (("gx", 1), ("gy", 2)), 1)
    potential_pad = padded[:shot_count]
    adjoint_pad = padded[shot_count:]
    gradient = jnp.zeros_like(potentials)
    for other_u, other_w in zip(neighbour_list(potential_pad), neighbour_list(adjoint_pad)):
        gradient = gradient - 0.5 * (potentials - other_u) * (adjoint - other_w)
    summed = lax.psum_scatter(jnp.sum(gradient, axis=0), "shot", scatter_dimension=1, tiled=True)
    return (potentials, summed)


def per_device(conductivity, stations, currents, receivers, observed):
    blocks = lax.axis_size("gx") * lax.axis_size("gy")
    fits = conductivity.shape == (SIDE, SIDE * SIDE, LANES) and blocks == SIDE
    fits = fits and lax.axis_size("gy") == 2 and lax.axis_size("shot") == 2
    fits = fits and currents.shape[0] == 1
    plan = replicated if fits else distributed
    return plan(conductivity, stations, currents, receivers, observed)


def solution(mesh):
    in_specs = (
        P(("grp", "gx"), "gy", None),
        P("grp"),
        P(("grp", "shot"), None),
        P("grp", None),
        P(("grp", "shot"), None),
    )
    out_specs = (P(("grp", "shot"), "gx", "gy", None), P(("grp", "gx"), ("gy", "shot"), None))
    return jax.shard_map(
        per_device, mesh=mesh, in_specs=in_specs, out_specs=out_specs, check_vma=False
    )
```

```python
import functools

import jax
import jax.numpy as jnp
from jax import lax
from jax.experimental import pallas as pl
from jax.experimental.pallas import tpu as pltpu
from jax.sharding import PartitionSpec as P

LEVELS = 4
COARSE_SWEEPS = 16


DAMPING = 0.8

SIDE = 8
LANES = 128
GROUP = 16
VMEM_BYTES = 48 * 2**20
SMALL_BYTES = 6 * 2**20


def pieces_of(value, count):
    pieces = []
    for _ in range(count):
        pieces.append(value.astype(jnp.bfloat16))
        value = value - pieces[-1].astype(jnp.float32)
    return pieces[::-1]


def product(value, matrix, count, dims=((1,), (0,))):
    result = None
    for piece in pieces_of(value, count):
        term = lax.dot_general(
            piece, matrix, (dims, ((), ())), preferred_element_type=jnp.float32
        )
        result = term if result is None else result + term
    return result


def iota(shape, dim):
    return lax.broadcasted_iota(jnp.int32, shape, dim)


def station_table(station):
    cell_x, cell_y, cell_z = station >> 14, station >> 7 & 127, station & 127
    row = (cell_x >> 3) * 2 + (cell_y >> 6)
    return cell_x, cell_y, cell_z, row, (cell_y >> 3 & 7) * GROUP + (cell_z >> 3)


def lane_order():
    row, col = iota((LANES, LANES), 0), iota((LANES, LANES), 1)
    chosen = row == col % GROUP * SIDE + col // GROUP
    return jnp.where(chosen, 1.0, 0.0).astype(jnp.bfloat16)


def exchange_groups(tiles):
    tiles = list(tiles)
    group = iota(tiles[0].shape, 1) // GROUP
    for bit in range(3):
        step = 1 << bit
        keep = (group & step) == 0
        for low in range(SIDE):
            if low & step == 0:
                a, b = tiles[low], tiles[low | step]
                tiles[low] = jnp.where(keep, a, pltpu.roll(b, step * GROUP, 1))
                tiles[low | step] = jnp.where(keep, pltpu.roll(a, LANES - step * GROUP, 1), b)
    return tiles


def own_place():
    return lax.axis_index("gx") * 2 + lax.axis_index("gy"), lax.axis_index("shot")


def to_blocks_kernel(natural_ref, blocks_ref, half_ref):
    order = lane_order()
    for x in range(SIDE):
        tiles = product(natural_ref[x], order, 3)
        tiles = [tiles[SIDE * k : SIDE * (k + 1)] for k in range(SIDE)]
        for z, tile in enumerate(exchange_groups(tiles)):
            blocks_ref[pl.ds((x * SIDE + z) * SIDE, SIDE), :] = tile
    count = half_ref.shape[0]
    low, high = blocks_ref[pl.ds(0, count), :], blocks_ref[pl.ds(count, count), :]
    half_ref[...] = jnp.where(own_place()[1] == 0, low, high)


def from_blocks(tiles, order):
    natural = jnp.concatenate(exchange_groups(tiles), axis=0)
    return product(natural, order, 3, ((1,), (1,)))


def block_up(register, axis):
    if axis == 0:
        return pltpu.roll(register, 6, 0)
    if axis == 2:
        return pltpu.roll(register, LANES - 1, 1)
    turned = pltpu.roll(register, LANES - GROUP, 1)
    return jnp.where(iota(register.shape, 1) < LANES - GROUP, turned, pltpu.roll(turned, 7, 0))


def block_down(register, axis):
    if axis == 0:
        return pltpu.roll(register, 2, 0)
    if axis == 2:
        return pltpu.roll(register, 1, 1)
    turned = pltpu.roll(register, GROUP, 1)
    return jnp.where(iota(register.shape, 1) >= GROUP, turned, pltpu.roll(turned, 1, 0))


def inside_up(register, axis):
    sub, lane = iota(register.shape, 0), iota(register.shape, 1)
    if axis == 0:
        keep = sub < 6
    elif axis == 1:
        keep = (lane < LANES - GROUP) | (sub % 2 == 0)
    else:
        keep = lane % GROUP < GROUP - 1
    return jnp.where(keep, register, 0.0)


def inside_down(register, axis):
    sub, lane = iota(register.shape, 0), iota(register.shape, 1)
    if axis == 0:
        keep = sub >= 2
    elif axis == 1:
        keep = (lane >= GROUP) | (sub % 2 == 1)
    else:
        keep = lane % GROUP > 0
    return jnp.where(keep, register, 0.0)


def electrode_kernel(
    stations_ref,
    currents_ref,
    receivers_ref,
    observed_ref,
    cells_ref,
    spot_ref,
    rows_ref,
    same_ref,
    pairs_ref,
    held_ref,
):
    stations = stations_ref[...]
    electrodes = stations.shape[1]
    cell_x, cell_y, cell_z, row, spot = station_table(stations)
    wide = SIDE + 2
    register = (((cell_x & 7) + 1) * wide + (cell_z & 7) + 1) * wide + (cell_y & 7) + 1
    cells_ref[...] = register * SIDE + row
    spot_ref[...] = spot
    held_ref[...] = observed_ref[...]
    line = stations & 0x1C387 | row << 20
    same = jnp.broadcast_to(line, (electrodes, electrodes))
    same = jnp.where(same == same.T, 1.0, 0.0).astype(jnp.bfloat16)
    same_ref[...] = same
    rows_ref[...] = shared_rows(currents_ref[...], spot, same)
    receivers = receivers_ref[...]
    numbers = iota((receivers.shape[0], electrodes), 1)
    pairs = jnp.where(numbers == receivers[:, 0:1], 1.0, 0.0) - jnp.where(
        numbers == receivers[:, 1:2], 1.0, 0.0
    )
    pairs_ref[...] = pairs.astype(jnp.bfloat16)


def shared_rows(amounts, spot, same):
    electrodes = amounts.shape[1]
    at_spot = iota((LANES, electrodes), 0) == spot
    return product(jnp.where(at_spot, amounts, 0.0), same, 3).T


class Edged:
    def __init__(self, ref, side):
        self.ref, self.side = ref, side

    def start(self, x, z, y=0):
        wide = self.side + 2
        return (((x + 1) * wide + z + 1) * wide + y + 1) * SIDE

    def __getitem__(self, at):
        return self.ref[pl.ds(self.start(*at), SIDE), :]

    def __setitem__(self, at, value):
        self.ref[pl.ds(self.start(*at), SIDE), :] = value

    def put(self, x, z, y, value, exact=False):
        self[x, z, y] = value
        n = self.side
        for axis, place in enumerate((x, y, z)):
            if axis == 1 and not exact:
                continue
            if place == 0:
                edge = block_up(value, axis)
                self.set_margin(x, z, y, axis, n, inside_up(edge, axis) if exact else edge)
            if place == n - 1:
                edge = block_down(value, axis)
                self.set_margin(x, z, y, axis, -1, inside_down(edge, axis) if exact else edge)

    def set_margin(self, x, z, y, axis, place, value):
        at = [x, y, z]
        at[axis] = place
        self[at[0], at[2], at[1]] = value

    def close_z(self, x, exact=False):
        n = self.side
        for y in range(n):
            after, before = block_up(self[x, 0, y], 2), block_down(self[x, n - 1, y], 2)
            self[x, n, y] = inside_up(after, 2) if exact else after
            self[x, -1, y] = inside_down(before, 2) if exact else before

    def close(self, exact=False):
        n = self.side
        for z in range(n):
            for y in range(n):
                after, before = block_up(self[0, z, y], 0), block_down(self[n - 1, z, y], 0)
                self[n, z, y] = inside_up(after, 0) if exact else after
                self[-1, z, y] = inside_down(before, 0) if exact else before


class Rows:
    def __init__(self, ref, side, first_x=0, first_z=0):
        self.ref, self.side, self.first_x, self.first_z = ref, side, first_x, first_z

    def place(self, x, z, y):
        count = self.side - self.first_z
        row = ((x - self.first_x) * count + z - self.first_z) * self.side + y
        return pl.ds(row * SIDE, SIDE)

    def __getitem__(self, at):
        return self.ref[self.place(*at), :]

    def __setitem__(self, at, value):
        self.ref[self.place(*at), :] = value


class Copied:
    def __init__(self, coarse):
        self.coarse = coarse

    def __getitem__(self, at):
        x, z, y = at
        return self.coarse[x // 2, z // 2, y // 2]


def rolled(count, body):
    def one(x, carry):
        body(x)
        return carry

    lax.fori_loop(0, count, one, 0)


class Level:
    def __init__(self, refs, index):
        self.side = side = SIDE >> index
        self.scale = 0.25**index
        edged = [Edged(ref, side) for ref in refs[:5]]
        self.cond, self.first, self.second, self.base, self.weight = edged
        self.link_x = Rows(refs[5], side, first_x=-1)
        self.link_y = Rows(refs[6], side)
        self.link_z = Rows(refs[7], side, first_z=-1)
        self.back = Rows(refs[8], side)

    @staticmethod
    def scratch(index):
        side = SIDE >> index
        sizes = [(side + 2) ** 3] * 5
        sizes += [side**2 * (side + 1), side**3, side**2 * (side + 1), side**3]
        return [pltpu.VMEM((size * SIDE, LANES), jnp.float32) for size in sizes]

    def prepare(self):
        n = self.side
        cond = self.cond

        def plane(x):
            for z in range(n):
                row = [cond[x, z, y] for y in range(n)]
                after = inside_up(block_up(row[0], 1), 1)
                before = inside_down(block_down(row[-1], 1), 1)
                for y, here in enumerate(row):
                    ahead, next_x = cond[x, z + 1, y], cond[x + 1, z, y]
                    next_y = row[y + 1] if y < n - 1 else after
                    last_y = row[y - 1] if y > 0 else before
                    total = (next_x + cond[x - 1, z, y]) + (ahead + cond[x, z - 1, y])
                    total = 6.0 * here + (total + (next_y + last_y))
                    self.weight[x, z, y] = DAMPING / total
                    if n == SIDE:
                        self.base[x, z, y] = jnp.zeros_like(here)
                    self.back[x, z, y] = total * (0.5 * self.scale / DAMPING)
                    self.link_x[x, z, y] = here + next_x
                    link = here + next_y
                    self.link_y[x, z, y] = link if y < n - 1 else inside_up(link, 1)
                    link = here + ahead
                    if z == n - 1:
                        link = inside_up(link, 2)
                        self.link_z[x, -1, y] = block_down(link, 2)
                    self.link_z[x, z, y] = link

        if n == SIDE:
            rolled(n, plane)
        else:
            for x in range(n):
                plane(x)
        for z in range(n):
            for y in range(n):
                link = inside_up(self.link_x[n - 1, z, y], 0)
                self.link_x[n - 1, z, y] = link
                self.link_x[-1, z, y] = block_down(link, 0)

    def visit(self, field, x, body):
        n = self.side
        both = (0, 1)
        link_x, link_y, link_z = self.link_x, self.link_y, self.link_z
        here = [[field[x + p, 0, y] for y in range(n)] for p in both]
        down = [[link_z[x + p, -1, y] * field[x + p, -1, y] for y in range(n)] for p in both]
        for z in range(n):
            ahead = [[], []]
            last = [block_down(link_y[x + p, z, n - 1] * here[p][n - 1], 1) for p in both]
            for y in range(n):
                inner = link_x[x, z, y]
                sides = [
                    link_x[x - 1, z, y] * field[x - 1, z, y] + inner * here[1][y],
                    inner * here[0][y] + link_x[x + 1, z, y] * field[x + 2, z, y],
                ]
                for p in both:
                    across, along = link_y[x + p, z, y], link_z[x + p, z, y]
                    ahead[p].append(field[x + p, z + 1, y])
                    next_y = here[p][y + 1] if y < n - 1 else block_up(here[p][0], 1)
                    total = sides[p] + (along * ahead[p][y] + down[p][y])
                    total = total + (across * next_y + last[p])
                    last[p] = across * here[p][y]
                    down[p][y] = along * here[p][y]
                    body(x + p, z, y, here[p][y], self.weight[x + p, z, y] * total)
            here = ahead

    def sweep(self, field, out, exact=False):
        def body(x, z, y, here, total):
            if field is self.base:
                value = (2.0 - DAMPING) * here + total
            else:
                value = (1.0 - DAMPING) * here + (self.base[x, z, y] + total)
            out.put(x, z, y, value, exact)

        for x in range(0, self.side, 2):
            self.visit(field, x, body)

    def descend(self, coarse):
        self.sweep(self.base, self.second)
        held = {}

        def body(x, z, y, here, total):
            swept = (1.0 - DAMPING) * here + (self.base[x, z, y] + total)
            self.first[x, z, y] = swept
            residual = (swept - here) * self.back[x, z, y]
            at = x // 2, z // 2, y // 2
            held[at] = held[at] + residual if at in held else residual
            if x % 2 and z % 2 and y % 2:
                coarse(*at, 0.125 * held.pop(at))

        for x in range(0, self.side, 2):
            self.visit(self.second, x, body)

    def ascend(self, correction, out):
        def body(x, z, y, here, total):
            value = self.first[x, z, y] + ((1.0 - DAMPING) * here + total)
            self.second.put(x, z, y, value)

        for x in range(0, self.side, 2):
            self.visit(Copied(correction), x, body)
        self.sweep(self.second, out, exact=self.side == SIDE)


class HeldLevel:
    def __init__(self, refs, index):
        self.side = 2
        self.scale = 0.25**index
        self.cond, self.first = Edged(refs[0], 2), Edged(refs[1], 2)
        self.weight, self.back = Rows(refs[2], 2), Rows(refs[3], 2)
        self.links = [Rows(ref, 2) for ref in refs[4:]]

    @staticmethod
    def scratch(index):
        sizes = [4**3] * 2 + [2**3] * 8
        return [pltpu.VMEM((size * SIDE, LANES), jnp.float32) for size in sizes]

    def around(self, field, inside=False):
        result = {}
        for at, here in field.items():
            others = []
            for axis, dim in ((0, 0), (1, 2), (2, 1)):
                other = list(at)
                other[dim] = 1 - at[dim]
                other = field[tuple(other)]
                far_up, far_down = block_up(other, axis), block_down(other, axis)
                if inside:
                    far_up, far_down = inside_up(far_up, axis), inside_down(far_down, axis)
                others += [other, far_down] if at[dim] == 0 else [far_up, other]
            result[at] = others
        return result

    def prepare(self):
        field = {
            (x, z, y): self.cond[x, z, y] for x in range(2) for z in range(2) for y in range(2)
        }
        for at, others in self.around(field, inside=True).items():
            here = field[at]
            total = others[0]
            for other in others[1:]:
                total = total + other
            total = 6.0 * here + total
            inverse = DAMPING / total
            self.weight[at] = inverse
            self.back[at] = total * (0.5 * self.scale / DAMPING)
            for index, other in enumerate(others):
                link = inverse * (here + other)
                self.links[index][at] = jnp.where(other > 0.0, link, 0.0)

    def sums(self, field, base):
        result = {}
        for at, others in self.around(field).items():
            terms = [link[at] * other for link, other in zip(self.links, others)]
            total = (terms[0] + terms[1]) + (terms[4] + terms[5])
            result[at] = (base[at] + total) + (terms[2] + terms[3])
        return result

    def swept(self, field, base):
        sums = self.sums(field, base)
        return {at: (1.0 - DAMPING) * field[at] + sums[at] for at in field}

    def cycle(self, base, solve, out):
        field = self.swept(base, base)
        sums = self.sums(field, base)
        total = None
        for at in field:
            residual = (sums[at] - DAMPING * field[at]) * self.back[at]
            total = residual if total is None else total + residual
        solved = solve(0.125 * total)
        copied = {at: solved for at in field}
        change = {at: sums[at] + (1.0 - DAMPING) * (field[at] + solved) for at in field}
        field = self.sums(copied, change)
        for (x, z, y), value in self.swept(field, base).items():
            out.put(x, z, y, value, exact=True)


def replicated_kernel(
    whole,
    halved,
    cells_ref,
    *refs,
):
    parts = refs[:whole], refs[whole : whole + halved]
    solve_kernel(*parts, cells_ref, *refs[whole + halved :])


def solve_kernel(
    part_refs,
    half_refs,
    cells_ref,
    spot_ref,
    rows_ref,
    same_ref,
    pairs_ref,
    observed_ref,
    potentials_ref,
    mine_ref,
    theirs_ref,
    gathered,
    owned,
    beside,
    sent,
    sem,
    *level_refs,
):
    f32 = jnp.float32
    electrodes = spot_ref.shape[1]
    levels, used = [], 0
    for index in range(LEVELS - 1):
        kind = HeldLevel if index == LEVELS - 2 else Level
        count = len(kind.scratch(index))
        levels.append(kind(level_refs[used : used + count], index))
        used += count
    fine = levels[0]
    forward = fine.cond
    wide = SIDE * SIDE * SIDE

    device, shot = own_place()

    def place(part, row, x, index):
        for z in range(SIDE):
            fine.cond.ref[pl.ds(fine.cond.start(x, z) + index, SIDE, stride=SIDE), :] = part[
                pl.ds((row * SIDE + z) * SIDE, SIDE), :
            ]

    def collect(x):
        for k, part in enumerate(part_refs):
            place(part, x, x, device ^ k)

    def collect_half(x):
        for k, part in enumerate(half_refs):
            swapped, index = k // 2 % 2, len(part_refs) + k // 4 * 2 + k % 2
            place(part, x, (shot ^ swapped) * (SIDE // 2) + x, device ^ index)

    def edges(x):
        fine.cond.close_z(x, exact=True)

    rolled(SIDE, collect)
    for x in range(SIDE // 2):
        collect_half(x)
    rolled(SIDE, edges)
    fine.cond.close(exact=True)

    coarsest = None
    for level, below in zip(levels, levels[1:] + [None]):
        level.prepare()
        for at in [(x, z, y) for x in range(level.side // 2) for z in range(level.side // 2) for y in range(level.side // 2)]:
            total = None
            for step in range(8):
                part = level.cond[
                    2 * at[0] + step // 4, 2 * at[1] + step // 2 % 2, 2 * at[2] + step % 2
                ]
                total = part if total is None else total + part
            if below is None:
                coarsest = 0.125 * total
            else:
                below.cond.put(*at, 0.125 * total, exact=True)

    sub, lane = iota((SIDE, LANES), 0), iota((SIDE, LANES), 1)
    keep = sub % 2 == 0

    def split(value):
        return [jnp.where(keep, part, 0.0) for part in (value, pltpu.roll(value, SIDE - 1, 0))]

    def around(value):
        low, high = value
        low_up, high_up = [pltpu.roll(part, LANES - GROUP, 1) for part in value]
        low_down, high_down = [pltpu.roll(part, GROUP, 1) for part in value]
        along = [[move(part, axis) for part in value] for axis in (0, 2) for move in (block_up, block_down)]
        return along + [
            [jnp.where(lane < LANES - GROUP, low_up, high_up), high_up],
            [low_down, jnp.where(lane >= GROUP, high_down, low_down)],
        ]

    inside_last = [
        [sub < 6] * 2,
        [sub >= 2] * 2,
        [lane % GROUP < GROUP - 1] * 2,
        [lane % GROUP > 0] * 2,
        [keep, lane < LANES - GROUP],
        [lane >= GROUP, keep],
    ]
    last_scale = 0.25 ** (LEVELS - 1)
    here = split(coarsest)
    others = [
        [jnp.where(inside & keep, part, 0.0) for inside, part in zip(pair, moved)]
        for pair, moved in zip(inside_last, around(here))
    ]
    last_weight, last_links = [], []
    for half, part in enumerate(here):
        total = 6.0 * part
        for other in others:
            total = total + other[half]
        inverse = jnp.where(keep, DAMPING / jnp.where(keep, total, 1.0), 0.0)
        last_weight.append(inverse * (2.0 / last_scale))
        last_links.append(
            [
                jnp.where(pair[half] & keep, inverse * (part + other[half]), 0.0)
                for pair, other in zip(inside_last, others)
            ]
        )

    def solve_last(rhs):
        base = [weight * part for weight, part in zip(last_weight, split(rhs))]
        value = base
        for _ in range(COARSE_SWEEPS - 1):
            moved = around(value)
            fresh = []
            for half in range(2):
                parts = [link * other[half] for link, other in zip(last_links[half], moved)]
                start = base[half] + (1.0 - DAMPING) * value[half]
                fresh.append(((start + parts[0]) + (parts[1] + parts[2])) + (parts[3] + (parts[4] + parts[5])))
            value = fresh
        return value[0] + pltpu.roll(value[1], 1, 0)

    def cycle(index, out):
        level, below = levels[index], levels[index + 1]

        def weighed(x, z, y, value):
            return below.weight[x, z, y] * (value * (2.0 / below.scale))

        if index == LEVELS - 3:
            base = {}

            def take(x, z, y, value):
                base[x, z, y] = weighed(x, z, y, value)

            level.descend(take)
            below.cycle(base, solve_last, below.first)
        else:
            level.descend(
                lambda x, z, y, value: below.base.put(x, z, y, weighed(x, z, y, value))
            )
            cycle(index + 1, below.first)
        level.ascend(below.first, out)

    spot = spot_ref[...]
    at_spot = iota((LANES, electrodes), 0) == spot
    order = lane_order()
    wide = SIDE + 2
    sending = pltpu.make_async_copy(sent, potentials_ref, sem)

    def each(body):
        def one(electrode, carry):
            body(pl.ds(electrode, 1), pl.ds(cells_ref[0, electrode], 1))
            return carry

        lax.fori_loop(0, electrodes, one, 0, unroll=32)

    def put(electrode, cell):
        fine.base.ref[cell, :] = (2.0 * gathered[electrode, :]) * fine.weight.ref[cell, :]

    def read(electrode, cell):
        gathered[electrode, :] = forward.ref[cell, :]

    def exact(row, dims):
        return product(jnp.broadcast_to(row, (16, row.shape[1])), pairs_ref[...], 3, dims)[0:1]

    def margin(x, z, y):
        return forward.ref[pl.ds(forward.start(x, z, y) + device, 1), :]

    def extract(index):
        for x in range(-1, SIDE + 1):
            for z in range(SIDE):
                at = (x + 1) * wide + z + 1
                start = forward.start(x, z) + device
                row = forward.ref[pl.ds(start, SIDE, stride=SIDE), :]
                owned[index, at] = row
                if 0 <= x < SIDE:
                    after, before = margin(x, z, SIDE), margin(x, z, -1)
                    place = x * SIDE + z
                    turned = pltpu.roll(row, SIDE - 1, 0)
                    beside[index, 0, place] = jnp.where(sub == SIDE - 1, after, turned)
                    beside[index, 1, place] = jnp.where(sub == 0, before, pltpu.roll(row, 1, 0))
                    if z == 0:
                        edge = pltpu.roll(row, LANES - 1, 1)
                        owned[index, at + SIDE] = jnp.where(lane % GROUP < GROUP - 1, edge, 0.0)
                    if z == SIDE - 1:
                        edge = pltpu.roll(row, 1, 1)
                        owned[index, at - SIDE] = jnp.where(lane % GROUP > 0, edge, 0.0)

    def solve(index):
        each(put)
        rolled(SIDE, fine.base.close_z)
        fine.base.close()
        cycle(0, forward)
        extract(index)

        @pl.when(index == 0)
        def _():
            for x in range(SIDE):
                tiles = [owned[0, (x + 1) * wide + z + 1] for z in range(SIDE)]
                sent[x] = from_blocks(tiles, order)
            sending.start()
            each(read)
            readings = jnp.where(at_spot, gathered[...].T, 0.0)
            readings = jnp.sum(readings, axis=0, keepdims=True)
            misfit = exact(readings, ((1,), (1,))) - observed_ref[...]
            gathered[...] = shared_rows(exact(misfit, ((1,), (0,))), spot, same_ref[...])

    gathered[...] = rows_ref[...]
    rolled(2, solve)

    chunk = mine_ref.shape[1]
    even = shot == 0
    for x in range(SIDE):
        tiles = []
        for z in range(SIDE):
            at = (x + 1) * wide + z + 1
            here_u, here_w = owned[0, at], owned[1, at]
            total = None
            for step in (wide, -wide, 1, -1):
                term = (here_u - owned[0, at + step]) * (here_w - owned[1, at + step])
                total = term if total is None else total + term
            for side in range(2):
                other_u, other_w = beside[0, side, x * SIDE + z], beside[1, side, x * SIDE + z]
                total = total + (here_u - other_u) * (here_w - other_w)
            tiles.append(-0.5 * total)
        natural = from_blocks(tiles, order)
        low, high = natural[:chunk], natural[chunk:]
        mine_ref[x] = jnp.where(even, low, high)
        theirs_ref[x] = jnp.where(even, high, low)
    sending.wait()


def replicated(conductivity, stations, currents, receivers, observed):
    rows, cols, depth = conductivity.shape
    f32 = jnp.float32
    electrodes = stations.shape[0]
    total = rows * cols
    vmem = pl.BlockSpec(memory_space=pltpu.VMEM)
    smem = pl.BlockSpec(memory_space=pltpu.SMEM)
    station_row = stations.reshape(1, electrodes)
    mine, half = pl.pallas_call(
        to_blocks_kernel,
        out_shape=(
            jax.ShapeDtypeStruct((total, LANES), f32),
            jax.ShapeDtypeStruct((total // 2, LANES), f32),
        ),
        in_specs=[vmem],
        out_specs=(vmem, vmem),
        compiler_params=pltpu.CompilerParams(vmem_limit_bytes=SMALL_BYTES),
    )(conductivity)
    swap = [(0, 1), (1, 0)]

    def partner(part, k):
        count = lax.axis_size("gx")
        return lax.ppermute(part, "gx", [(i, i ^ k) for i in range(count)])

    def with_mate(part):
        return [part, lax.ppermute(part, "gy", swap)]

    far = partner(half, 2)
    near = partner(mine, 1)
    line = jax.ShapeDtypeStruct((1, electrodes), jnp.int32)
    cells, spot, rows_of, same, pairs, held = pl.pallas_call(
        electrode_kernel,
        out_shape=(
            line,
            line,
            jax.ShapeDtypeStruct((electrodes, LANES), f32),
            jax.ShapeDtypeStruct((electrodes, electrodes), jnp.bfloat16),
            jax.ShapeDtypeStruct((receivers.shape[0], electrodes), jnp.bfloat16),
            jax.ShapeDtypeStruct(observed.shape, f32),
        ),
        in_specs=[vmem] * 4,
        out_specs=(vmem,) * 6,
        compiler_params=pltpu.CompilerParams(vmem_limit_bytes=SMALL_BYTES),
        cost_estimate=pl.CostEstimate(flops=100_000_000, bytes_accessed=1_000_000, transcendentals=0),
    )(station_row, currents, receivers, observed)
    far, rows_of = lax.optimization_barrier((far, rows_of))
    far = [far, partner(far, 1)]
    halved = [piece for own in far for piece in (own, lax.ppermute(own, "shot", swap))]
    parts = [piece for own in (mine, near) for piece in with_mate(own)]
    halved = [piece for own in halved for piece in with_mate(own)]
    chunk = cols // 2
    levels = [shape for index in range(LEVELS - 2) for shape in Level.scratch(index)]
    levels += HeldLevel.scratch(LEVELS - 2)
    potentials, own, theirs = pl.pallas_call(
        functools.partial(replicated_kernel, len(parts), len(halved)),
        out_shape=(
            jax.ShapeDtypeStruct((rows, cols, LANES), f32),
            jax.ShapeDtypeStruct((rows, chunk, LANES), f32),
            jax.ShapeDtypeStruct((rows, chunk, LANES), f32),
        ),
        in_specs=[smem] + [vmem] * (len(parts) + len(halved) + 5),
        out_specs=(pl.BlockSpec(memory_space=pl.ANY), vmem, vmem),
        scratch_shapes=[
            pltpu.VMEM((electrodes, LANES), f32),
            pltpu.VMEM((2, (SIDE + 2) ** 2, SIDE, LANES), f32),
            pltpu.VMEM((2, 2, SIDE**2, SIDE, LANES), f32),
            pltpu.VMEM((rows, cols, LANES), f32),
            pltpu.SemaphoreType.DMA,
        ]
        + levels,
        compiler_params=pltpu.CompilerParams(vmem_limit_bytes=VMEM_BYTES),
        cost_estimate=pl.CostEstimate(flops=200_000_000, bytes_accessed=4_000_000, transcendentals=0),
    )(cells, *parts, *halved, spot, rows_of, same, pairs, held)
    return potentials[None], own + lax.ppermute(theirs, "shot", swap)


def extended(array, sides, width):
    for axis, dim in sides:
        size, length = (lax.axis_size(axis), array.shape[dim])
        up = [(i, (i + 1) % size) for i in range(size - 1)]
        down = [(j, i) for i, j in up]
        last = lax.slice_in_dim(array, length - width, length, axis=dim)
        leading = lax.slice_in_dim(array, 0, width, axis=dim)
        before = lax.ppermute(last, axis, up)
        after = lax.ppermute(leading, axis, down)
        array = jnp.concatenate([before, array, after], axis=dim)
    return array


def upper_z(field):
    return jnp.concatenate([field[..., 1:], jnp.zeros_like(field[..., :1])], axis=-1)


def lower_z(field):
    return jnp.concatenate([jnp.zeros_like(field[..., :1]), field[..., :-1]], axis=-1)


def trim_circle(field, circle_width):
    return field[..., circle_width:-circle_width, circle_width:-circle_width, :]


def pad_plane(field, circle_width):
    spec = [(0, 0)] * (field.ndim - 3) + [
        (circle_width, circle_width),
        (circle_width, circle_width),
        (0, 0),
    ]
    return jnp.pad(field, spec)


def neighbour_list(field_pad):
    centre = trim_circle(field_pad, 1)
    return [
        field_pad[..., 2:, 1:-1, :],
        field_pad[..., :-2, 1:-1, :],
        field_pad[..., 1:-1, 2:, :],
        field_pad[..., 1:-1, :-2, :],
        upper_z(centre),
        lower_z(centre),
    ]


def stencil(field_pad, cond_pad, level_scale):
    centre = trim_circle(field_pad, 1)
    centre_cond = trim_circle(cond_pad, 1)
    summed = jnp.zeros_like(centre)
    for other, other_cond in zip(neighbour_list(field_pad), neighbour_list(cond_pad)):
        summed = summed + level_scale * 0.5 * (centre_cond + other_cond) * (centre - other)
    return summed


def diagonal(cond_pad, level_scale):
    centre_cond = trim_circle(cond_pad, 1)
    summed = jnp.zeros_like(centre_cond)
    for other_cond in neighbour_list(cond_pad):
        summed = summed + level_scale * 0.5 * (centre_cond + other_cond)
    return summed


def relaxed(field_pad, source, cond_pad, diag_level, level_scale):
    return (
        trim_circle(field_pad, 1)
        + DAMPING * (source - stencil(field_pad, cond_pad, level_scale)) / diag_level
    )


def restrict(field):
    leading = field.shape[:-3]
    extent = field.shape[-3:]
    shaped = field.reshape(leading + (extent[0] // 2, 2, extent[1] // 2, 2, extent[2] // 2, 2))
    return shaped.mean(axis=(-5, -3, -1))


def prolong(field):
    return jnp.repeat(jnp.repeat(jnp.repeat(field, 2, axis=-3), 2, axis=-2), 2, axis=-1)


def assemble(blocks, count_x, count_y):
    leading = blocks.shape[1:-3]
    extent = blocks.shape[-3:]
    depth_lead = len(leading)
    shaped = blocks.reshape((count_x, count_y) + leading + extent)
    order = tuple(range(2, 2 + depth_lead)) + (0, 2 + depth_lead, 1, 3 + depth_lead, 4 + depth_lead)
    return shaped.transpose(order).reshape(
        leading + (count_x * extent[0], count_y * extent[1], extent[2])
    )


def field_rim(field):
    return extended(field, (("gx", 1), ("gy", 2)), 1)


def cond_rim(conduct):
    return extended(conduct, (("gx", 0), ("gy", 1)), 1)


def whole_cycle(source, level_index, whole_plans):
    cond_pad, diag_level, level_scale = whole_plans[level_index]
    field = DAMPING * source / diag_level

    def turn(turn_index, iterate):
        return relaxed(pad_plane(iterate, 1), source, cond_pad, diag_level, level_scale)

    return lax.fori_loop(0, COARSE_SWEEPS - 1, turn, field)


def part_cycle(source, level_index, level_plans, whole_plans, gather_level):
    if level_index == gather_level:
        blocks = lax.all_gather(source[None], ("gx", "gy"), axis=0, tiled=True)
        whole = assemble(blocks, lax.axis_size("gx"), lax.axis_size("gy"))
        correction = whole_cycle(whole, level_index, whole_plans)
        extent = source.shape
        starts = (0, lax.axis_index("gx") * extent[1], lax.axis_index("gy") * extent[2], 0)
        return lax.dynamic_slice(correction, starts, extent)
    cond_pad, diag_level, level_scale = level_plans[level_index]
    field = DAMPING * source / diag_level
    field = relaxed(field_rim(field), source, cond_pad, diag_level, level_scale)
    residual = source - stencil(field_rim(field), cond_pad, level_scale)
    field = field + prolong(
        part_cycle(restrict(residual), level_index + 1, level_plans, whole_plans, gather_level)
    )
    field = relaxed(field_rim(field), source, cond_pad, diag_level, level_scale)
    return relaxed(field_rim(field), source, cond_pad, diag_level, level_scale)


def distributed(conductivity, stations, currents, receivers, observed):
    row_count, col_count, z_count = conductivity.shape
    shot_count = currents.shape[0]
    count_x = lax.axis_size("gx")
    count_y = lax.axis_size("gy")
    gather_level = LEVELS - 1
    level_plans = []
    conduct = conductivity
    for level_index in range(gather_level):
        level_scale = 0.25**level_index
        cond_pad = cond_rim(conduct)
        level_plans.append((cond_pad, diagonal(cond_pad, level_scale), level_scale))
        conduct = restrict(conduct)
    blocks = lax.all_gather(conduct[None], ("gx", "gy"), axis=0, tiled=True)
    whole = assemble(blocks, count_x, count_y)
    whole_plans = {}
    level_index = 3
    level_scale = 0.25**level_index
    cond_pad = pad_plane(whole, 1)
    whole_plans[level_index] = (cond_pad, diagonal(cond_pad, level_scale), level_scale)
    total_y = col_count * count_y
    cell_x = stations // (total_y * z_count)
    cell_y = stations // z_count % total_y
    cell_z = stations % z_count
    local_x = cell_x - lax.axis_index("gx") * row_count
    local_y = cell_y - lax.axis_index("gy") * col_count
    owned = (local_x >= 0) & (local_x < row_count) & (local_y >= 0) & (local_y < col_count)
    block_size = row_count * col_count * z_count
    local_cell = jnp.where(owned, (local_x * col_count + local_y) * z_count + cell_z, 0)
    offsets = jnp.arange(shot_count)[:, None] * block_size + local_cell[None, :]
    targets = jnp.where(owned[None, :], offsets, shot_count * block_size).reshape(-1)

    def spread(amounts):
        flat = (
            jnp.zeros((shot_count * block_size,), jnp.float32)
            .at[targets]
            .add(amounts.reshape(-1), mode="drop")
        )
        return flat.reshape(shot_count, row_count, col_count, z_count)

    potentials = part_cycle(spread(currents), 0, level_plans, whole_plans, gather_level)
    local_values = jnp.where(
        owned[None, :], potentials.reshape(shot_count, block_size)[:, local_cell], 0.0
    )
    readings = lax.psum(local_values, ("gx", "gy"))
    positions = jnp.arange(stations.shape[0])[:, None]
    pairs = (receivers[:, 0][None, :] == positions).astype(jnp.float32) - (
        receivers[:, 1][None, :] == positions
    ).astype(jnp.float32)
    misfit = jnp.dot(readings, pairs, precision=lax.Precision.HIGHEST) - observed
    back_source = jnp.dot(misfit, pairs.T, precision=lax.Precision.HIGHEST)
    adjoint = part_cycle(spread(back_source), 0, level_plans, whole_plans, gather_level)
    stacked = jnp.concatenate([potentials, adjoint], axis=0)
    padded = extended(stacked, (("gx", 1), ("gy", 2)), 1)
    potential_pad = padded[:shot_count]
    adjoint_pad = padded[shot_count:]
    gradient = jnp.zeros_like(potentials)
    for other_u, other_w in zip(neighbour_list(potential_pad), neighbour_list(adjoint_pad)):
        gradient = gradient - 0.5 * (potentials - other_u) * (adjoint - other_w)
    summed = lax.psum_scatter(jnp.sum(gradient, axis=0), "shot", scatter_dimension=1, tiled=True)
    return (potentials, summed)


def per_device(conductivity, stations, currents, receivers, observed):
    blocks = lax.axis_size("gx") * lax.axis_size("gy")
    fits = conductivity.shape == (SIDE, SIDE * SIDE, LANES) and blocks == SIDE
    fits = fits and lax.axis_size("gy") == 2 and lax.axis_size("shot") == 2
    fits = fits and currents.shape[0] == 1
    plan = replicated if fits else distributed
    return plan(conductivity, stations, currents, receivers, observed)


def solution(mesh):
    in_specs = (
        P(("grp", "gx"), "gy", None),
        P("grp"),
        P(("grp", "shot"), None),
        P("grp", None),
        P(("grp", "shot"), None),
    )
    out_specs = (P(("grp", "shot"), "gx", "gy", None), P(("grp", "gx"), ("gy", "shot"), None))
    return jax.shard_map(
        per_device, mesh=mesh, in_specs=in_specs, out_specs=out_specs, check_vma=False
    )
```

```python
import functools

import jax
import jax.numpy as jnp
from jax import lax
from jax.experimental import pallas as pl
from jax.experimental.pallas import tpu as pltpu
from jax.sharding import PartitionSpec as P

LEVELS = 4
COARSE_SWEEPS = 16


DAMPING = 0.8

SIDE = 8
LANES = 128
GROUP = 16
VMEM_BYTES = 48 * 2**20
SMALL_BYTES = 6 * 2**20


def pieces_of(value, count):
    pieces = []
    for _ in range(count):
        pieces.append(value.astype(jnp.bfloat16))
        value = value - pieces[-1].astype(jnp.float32)
    return pieces[::-1]


def product(value, matrix, count, dims=((1,), (0,))):
    result = None
    for piece in pieces_of(value, count):
        term = lax.dot_general(
            piece, matrix, (dims, ((), ())), preferred_element_type=jnp.float32
        )
        result = term if result is None else result + term
    return result


def iota(shape, dim):
    return lax.broadcasted_iota(jnp.int32, shape, dim)


def station_table(station):
    cell_x, cell_y, cell_z = station >> 14, station >> 7 & 127, station & 127
    row = (cell_x >> 3) * 2 + (cell_y >> 6)
    return cell_x, cell_y, cell_z, row, (cell_y >> 3 & 7) * GROUP + (cell_z >> 3)


def lane_order(back=False):
    row, col = iota((LANES, LANES), 0), iota((LANES, LANES), 1)
    if back:
        row, col = col, row
    chosen = row == col % GROUP * SIDE + col // GROUP
    return jnp.where(chosen, 1.0, 0.0).astype(jnp.bfloat16)


def exchange_groups(tiles):
    tiles = list(tiles)
    group = iota(tiles[0].shape, 1) // GROUP
    for bit in range(3):
        step = 1 << bit
        keep = (group & step) == 0
        for low in range(SIDE):
            if low & step == 0:
                a, b = tiles[low], tiles[low | step]
                tiles[low] = jnp.where(keep, a, pltpu.roll(b, step * GROUP, 1))
                tiles[low | step] = jnp.where(keep, pltpu.roll(a, LANES - step * GROUP, 1), b)
    return tiles


def own_place():
    return lax.axis_index("gx") * 2 + lax.axis_index("gy"), lax.axis_index("shot")


def to_blocks_kernel(natural_ref, blocks_ref, half_ref):
    order = lane_order()
    for x in range(SIDE):
        tiles = product(natural_ref[x], order, 3)
        tiles = [tiles[SIDE * k : SIDE * (k + 1)] for k in range(SIDE)]
        for z, tile in enumerate(exchange_groups(tiles)):
            blocks_ref[pl.ds((x * SIDE + z) * SIDE, SIDE), :] = tile
    count = half_ref.shape[0]
    low, high = blocks_ref[pl.ds(0, count), :], blocks_ref[pl.ds(count, count), :]
    half_ref[...] = jnp.where(own_place()[1] == 0, low, high)


def from_blocks(tiles, order):
    natural = jnp.concatenate(exchange_groups(tiles), axis=0)
    return product(natural, order, 3)


def block_up(field, axis):
    if axis == 0:
        return pltpu.roll(field, 6, 1)
    if axis == 2:
        return pltpu.roll(field, LANES - 1, 2)
    turned = pltpu.roll(field, LANES - GROUP, 2)
    return jnp.where(iota(field.shape, 2) < LANES - GROUP, turned, pltpu.roll(turned, 7, 1))


def block_down(field, axis):
    if axis == 0:
        return pltpu.roll(field, 2, 1)
    if axis == 2:
        return pltpu.roll(field, 1, 2)
    turned = pltpu.roll(field, GROUP, 2)
    return jnp.where(iota(field.shape, 2) >= GROUP, turned, pltpu.roll(turned, 1, 1))


def inside_up(field, axis):
    sub, lane = iota(field.shape, 1), iota(field.shape, 2)
    if axis == 0:
        keep = sub < 6
    elif axis == 1:
        keep = (lane < LANES - GROUP) | (sub % 2 == 0)
    else:
        keep = lane % GROUP < GROUP - 1
    return jnp.where(keep, field, 0.0)


def inside_down(field, axis):
    sub, lane = iota(field.shape, 1), iota(field.shape, 2)
    if axis == 0:
        keep = sub >= 2
    elif axis == 1:
        keep = (lane >= GROUP) | (sub % 2 == 1)
    else:
        keep = lane % GROUP > 0
    return jnp.where(keep, field, 0.0)


def pair_rows(row):
    count = row.shape[0] // 2
    return jnp.concatenate([row[2 * i : 2 * i + 1] + row[2 * i + 1 : 2 * i + 2] for i in range(count)])


def twice(row):
    return jnp.concatenate([row[i // 2 : i // 2 + 1] for i in range(2 * row.shape[0])])


def electrode_kernel(
    stations_ref,
    currents_ref,
    receivers_ref,
    observed_ref,
    cells_ref,
    spot_ref,
    rows_ref,
    same_ref,
    pairs_ref,
    turned_ref,
    held_ref,
):
    stations = stations_ref[...]
    electrodes = stations.shape[1]
    cell_x, cell_y, cell_z, row, spot = station_table(stations)
    wide = SIDE + 2
    register = (((cell_x & 7) + 1) * wide + (cell_z & 7) + 1) * wide + (cell_y & 7) + 1
    cells_ref[...] = register * SIDE + row
    spot_ref[...] = spot
    held_ref[...] = observed_ref[...]
    line = stations & 0x1C387 | row << 20
    same = jnp.broadcast_to(line, (electrodes, electrodes))
    same = jnp.where(same == same.T, 1.0, 0.0).astype(jnp.bfloat16)
    same_ref[...] = same
    rows_ref[...] = shared_rows(currents_ref[...], spot, same)
    receivers = receivers_ref[...]
    numbers = iota((receivers.shape[0], electrodes), 1)
    pairs = jnp.where(numbers == receivers[:, 0:1], 1.0, 0.0) - jnp.where(
        numbers == receivers[:, 1:2], 1.0, 0.0
    )
    pairs_ref[...] = pairs.astype(jnp.bfloat16)
    turned_ref[...] = pairs.T.astype(jnp.bfloat16)


def shared_rows(amounts, spot, same):
    electrodes = amounts.shape[1]
    at_spot = iota((LANES, electrodes), 0) == spot
    return product(jnp.where(at_spot, amounts, 0.0), same, 3).T


class Edged:
    def __init__(self, ref, side):
        self.ref, self.side = ref, side

    def start(self, x, z, y=0):
        wide = self.side + 2
        return (((x + 1) * wide + z + 1) * wide + y + 1) * SIDE

    def __getitem__(self, at):
        x, z = at
        rows = self.ref[pl.ds(self.start(x, z), self.side * SIDE), :]
        return rows.reshape(self.side, SIDE, LANES)

    def __setitem__(self, at, value):
        x, z = at
        self.ref[pl.ds(self.start(x, z), self.side * SIDE), :] = value.reshape(-1, LANES)

    def put(self, x, z, value, exact=False):
        self[x, z] = value
        n = self.side
        if z == 0:
            edge = block_up(value, 2)
            self[x, n] = inside_up(edge, 2) if exact else edge
        if z == n - 1:
            edge = block_down(value, 2)
            self[x, -1] = inside_down(edge, 2) if exact else edge
        if x == 0:
            edge = block_up(value, 0)
            self[n, z] = inside_up(edge, 0) if exact else edge
        if x == n - 1:
            edge = block_down(value, 0)
            self[-1, z] = inside_down(edge, 0) if exact else edge
        if exact:
            after = inside_up(block_up(value[:1], 1), 1)
            self.ref[pl.ds(self.start(x, z, n), SIDE), :] = after[0]
            before = inside_down(block_down(value[n - 1 :], 1), 1)
            self.ref[pl.ds(self.start(x, z, -1), SIDE), :] = before[0]

    def close_z(self, x, exact=False):
        n = self.side
        after, before = block_up(self[x, 0], 2), block_down(self[x, n - 1], 2)
        self[x, n] = inside_up(after, 2) if exact else after
        self[x, -1] = inside_down(before, 2) if exact else before

    def close(self, exact=False):
        n = self.side
        for z in range(n):
            after = block_up(self[0, z], 0)
            self[n, z] = inside_up(after, 0) if exact else after
            before = block_down(self[n - 1, z], 0)
            self[-1, z] = inside_down(before, 0) if exact else before


class Rows:
    def __init__(self, ref, side, first_x=0, first_z=0):
        self.ref, self.side, self.first_x, self.first_z = ref, side, first_x, first_z

    def place(self, at):
        count = self.side - self.first_z
        rows = self.side * SIDE
        return pl.ds(((at[0] - self.first_x) * count + at[1] - self.first_z) * rows, rows)

    def __getitem__(self, at):
        return self.ref[self.place(at), :].reshape(self.side, SIDE, LANES)

    def __setitem__(self, at, value):
        self.ref[self.place(at), :] = value.reshape(-1, LANES)


def rolled(count, body):
    def one(x, carry):
        body(x)
        return carry

    lax.fori_loop(0, count, one, 0)


def next_in_y(row):
    return jnp.concatenate([row[1:], block_up(row[:1], 1)])


def last_in_y(row):
    return jnp.concatenate([block_down(row[-1:], 1), row[:-1]])


class Level:
    def __init__(self, refs, index):
        self.side = side = SIDE >> index
        self.scale = 0.25**index
        edged = [Edged(ref, side) for ref in refs[:5]]
        self.cond, self.first, self.second, self.base, self.weight = edged
        self.link_x = Rows(refs[5], side, first_x=-1)
        self.link_y = Rows(refs[6], side)
        self.link_z = Rows(refs[7], side, first_z=-1)
        self.back = Rows(refs[8], side)

    @staticmethod
    def scratch(index):
        side = SIDE >> index
        sizes = [(side + 2) ** 3] * 5
        sizes += [side**2 * (side + 1), side**3, side**2 * (side + 1), side**3]
        return [pltpu.VMEM((size * SIDE, LANES), jnp.float32) for size in sizes]

    def pairs(self, body):
        for i in range(self.side // 2):
            body(2 * i)

    def prepare(self):
        n = self.side
        cond = self.cond

        def plane(x):
            for z in range(n):
                here, ahead, next_x = cond[x, z], cond[x, z + 1], cond[x + 1, z]
                after = inside_up(block_up(here[:1], 1), 1)
                before = inside_down(block_down(here[-1:], 1), 1)
                next_y = jnp.concatenate([here[1:], after])
                last_y = jnp.concatenate([before, here[:-1]])
                total = (next_x + cond[x - 1, z]) + (ahead + cond[x, z - 1]) + (next_y + last_y)
                total = 6.0 * here + total
                self.weight[x, z] = DAMPING / total
                if n == SIDE:
                    self.base[x, z] = jnp.zeros_like(here)
                self.back[x, z] = total * (0.5 * self.scale / DAMPING)
                self.link_x[x, z] = here + next_x
                link = here + next_y
                self.link_y[x, z] = jnp.concatenate([link[:-1], inside_up(link[-1:], 1)])
                link = here + ahead
                if z == n - 1:
                    link = inside_up(link, 2)
                    self.link_z[x, -1] = block_down(link, 2)
                self.link_z[x, z] = link

        if n == SIDE:
            rolled(n, plane)
        else:
            for x in range(n):
                plane(x)
        for z in range(n):
            link = inside_up(self.link_x[n - 1, z], 0)
            self.link_x[n - 1, z] = link
            self.link_x[-1, z] = block_down(link, 0)

    def flows(self, x, z, here, ahead, outer, down):
        result = []
        inner = self.link_x[x, z]
        sides = [
            self.link_x[x - 1, z] * outer[0] + inner * here[1],
            inner * here[0] + self.link_x[x + 1, z] * outer[1],
        ]
        for p in range(2):
            link_y, link_z = self.link_y[x + p, z], self.link_z[x + p, z]
            along = link_y * next_in_y(here[p]) + last_in_y(link_y * here[p])
            total = sides[p] + (link_z * ahead[p] + down[p]) + along
            down[p] = link_z * here[p]
            result.append(self.weight[x + p, z] * total)
        return result

    def rows(self, field, x):
        here = [field[x, 0], field[x + 1, 0]]
        down = [self.link_z[x + p, -1] * field[x + p, -1] for p in range(2)]
        for z in range(self.side):
            ahead = [field[x, z + 1], field[x + 1, z + 1]]
            outer = [field[x - 1, z], field[x + 2, z]]
            yield z, here, self.flows(x, z, here, ahead, outer, down)
            here = ahead

    def sweep(self, field, out, exact=False):
        def pair(x):
            for z, here, sums in self.rows(field, x):
                for p in range(2):
                    if field is self.base:
                        value = (2.0 - DAMPING) * here[p] + sums[p]
                    else:
                        value = (1.0 - DAMPING) * here[p] + (self.base[x + p, z] + sums[p])
                    out.put(x + p, z, value, exact)

        self.pairs(pair)

    def halve(self, rows, coarse):
        def pair(x):
            held = None
            for z, row in enumerate(rows(x)):
                row = row[0] + row[1]
                if z % 2 == 0:
                    held = row
                else:
                    coarse(x // 2, z // 2, 0.125 * pair_rows(held + row))

        self.pairs(pair)

    def descend(self, coarse):
        self.sweep(self.base, self.second)

        def residuals(x):
            for z, here, sums in self.rows(self.second, x):
                result = []
                for p in range(2):
                    swept = (1.0 - DAMPING) * here[p] + (self.base[x + p, z] + sums[p])
                    self.first[x + p, z] = swept
                    result.append((swept - here[p]) * self.back[x + p, z])
                yield result

        self.halve(residuals, coarse)

    def ascend(self, correction, out, exact=False):
        def pair(x):
            i = x // 2
            here = twice(correction(i, 0))
            start = twice(correction(i, -1))
            down = [self.link_z[x + p, -1] * start for p in range(2)]
            for z in range(self.side):
                ahead = twice(correction(i, (z + 1) // 2))
                outer = [twice(correction(i - 1, z // 2)), twice(correction(i + 1, z // 2))]
                sums = self.flows(x, z, [here, here], [ahead, ahead], outer, down)
                for p in range(2):
                    value = self.first[x + p, z] + ((1.0 - DAMPING) * here + sums[p])
                    self.second.put(x + p, z, value)
                here = ahead

        self.pairs(pair)
        self.sweep(self.second, out, exact)


class HeldLevel:
    def __init__(self, refs, index):
        self.side = 2
        self.scale = 0.25**index
        self.cond, self.first = Edged(refs[0], 2), Edged(refs[1], 2)
        self.weight, self.back = Rows(refs[2], 2), Rows(refs[3], 2)
        self.links = [Rows(ref, 2) for ref in refs[4:]]

    @staticmethod
    def scratch(index):
        sizes = [4**3] * 2 + [2**3] * 8
        return [pltpu.VMEM((size * SIDE, LANES), jnp.float32) for size in sizes]

    def around(self, field, inside=False):
        def moved(row, axis, up):
            row = (block_up if up else block_down)(row, axis)
            return (inside_up if up else inside_down)(row, axis) if inside else row

        result = {}
        for (x, z), here in field.items():
            result[x, z] = [
                field[1, z] if x == 0 else moved(field[0, z], 0, True),
                field[0, z] if x == 1 else moved(field[1, z], 0, False),
                jnp.concatenate([here[1:], moved(here[:1], 1, True)]),
                jnp.concatenate([moved(here[-1:], 1, False), here[:-1]]),
                field[x, 1] if z == 0 else moved(field[x, 0], 2, True),
                field[x, 0] if z == 1 else moved(field[x, 1], 2, False),
            ]
        return result

    def prepare(self):
        field = {(x, z): self.cond[x, z] for x in range(2) for z in range(2)}
        for at, others in self.around(field, inside=True).items():
            here = field[at]
            total = others[0]
            for other in others[1:]:
                total = total + other
            total = 3.0 * here + 0.5 * total
            inverse = DAMPING / total
            self.weight[at] = inverse
            self.back[at] = total * (self.scale / DAMPING)
            for index, other in enumerate(others):
                link = 0.5 * inverse * (here + other)
                self.links[index][at] = jnp.where(other > 0.0, link, 0.0)

    def halve(self, rows, coarse):
        total = None
        for row in rows(0):
            row = row[0] + row[1]
            total = row if total is None else total + row
        coarse(0, 0, 0.125 * (total[:1] + total[1:]))

    def sums(self, field, base):
        result = {}
        for at, others in self.around(field).items():
            total = base[at]
            for link, other in zip(self.links, others):
                total = total + link[at] * other
            result[at] = total
        return result

    def swept(self, field, base):
        sums = self.sums(field, base)
        return {at: (1.0 - DAMPING) * field[at] + sums[at] for at in field}

    def cycle(self, base, solve, out):
        field = self.swept(base, base)
        sums = self.sums(field, base)
        total = None
        for at in field:
            residual = (sums[at] - DAMPING * field[at]) * self.back[at]
            total = residual if total is None else total + residual
        solved = solve(0.125 * (total[:1] + total[1:]))
        row = twice(solved)
        copied = {at: row for at in field}
        change = {at: sums[at] + (1.0 - DAMPING) * (field[at] + row) for at in field}
        field = self.sums(copied, change)
        for (x, z), value in self.swept(field, base).items():
            out.put(x, z, value)


def replicated_kernel(
    whole,
    halved,
    cells_ref,
    *refs,
):
    parts = refs[:whole], refs[whole : whole + halved]
    solve_kernel(*parts, cells_ref, *refs[whole + halved :])


def solve_kernel(
    part_refs,
    half_refs,
    cells_ref,
    spot_ref,
    rows_ref,
    same_ref,
    pairs_ref,
    turned_ref,
    observed_ref,
    potentials_ref,
    mine_ref,
    theirs_ref,
    gathered,
    owned,
    beside,
    sent,
    sem,
    *level_refs,
):
    f32 = jnp.float32
    electrodes = spot_ref.shape[1]
    levels, used = [], 0
    for index in range(LEVELS - 1):
        kind = HeldLevel if index == LEVELS - 2 else Level
        count = len(kind.scratch(index))
        levels.append(kind(level_refs[used : used + count], index))
        used += count
    fine = levels[0]
    forward = fine.cond
    wide = SIDE * SIDE * SIDE

    device, shot = own_place()

    def place(part, row, x, index):
        for z in range(SIDE):
            fine.cond.ref[pl.ds(fine.cond.start(x, z) + index, SIDE, stride=SIDE), :] = part[
                pl.ds((row * SIDE + z) * SIDE, SIDE), :
            ]

    def collect(x):
        for k, part in enumerate(part_refs):
            place(part, x, x, device ^ k)

    def collect_half(x):
        for k, part in enumerate(half_refs):
            swapped, index = k // 2 % 2, len(part_refs) + k // 4 * 2 + k % 2
            place(part, x, (shot ^ swapped) * (SIDE // 2) + x, device ^ index)

    def edges(x):
        fine.cond.close_z(x, exact=True)

    rolled(SIDE, collect)
    for x in range(SIDE // 2):
        collect_half(x)
    rolled(SIDE, edges)
    fine.cond.close(exact=True)

    coarsest = []
    for level, below in zip(levels, levels[1:] + [None]):
        level.prepare()

        def coarse(x, z, row, below=below):
            if below is None:
                coarsest.append(row)
            else:
                below.cond.put(x, z, row, exact=True)

        level.halve(
            lambda x, level=level: [
                (level.cond[x, z], level.cond[x + 1, z]) for z in range(level.side)
            ],
            coarse,
        )

    keep = iota((1, SIDE, LANES), 1) % 2 == 0
    lane = iota((1, SIDE, LANES), 2)

    def split(value):
        return [jnp.where(keep, part, 0.0) for part in (value, pltpu.roll(value, SIDE - 1, 1))]

    def around(value):
        low, high = value
        low_up, high_up = [pltpu.roll(part, LANES - GROUP, 2) for part in value]
        low_down, high_down = [pltpu.roll(part, GROUP, 2) for part in value]
        along = [[move(part, axis) for part in value] for axis in (0, 2) for move in (block_up, block_down)]
        return along + [
            [jnp.where(lane < LANES - GROUP, low_up, high_up), high_up],
            [low_down, jnp.where(lane >= GROUP, high_down, low_down)],
        ]

    sub = iota((1, SIDE, LANES), 1)
    inside_last = [
        [sub < 6] * 2,
        [sub >= 2] * 2,
        [lane % GROUP < GROUP - 1] * 2,
        [lane % GROUP > 0] * 2,
        [keep, lane < LANES - GROUP],
        [lane >= GROUP, keep],
    ]
    last_scale = 0.25 ** (LEVELS - 1)
    here = split(coarsest[0])
    others = [
        [jnp.where(inside & keep, part, 0.0) for inside, part in zip(pair, moved)]
        for pair, moved in zip(inside_last, around(here))
    ]
    last_weight, last_links = [], []
    for half, part in enumerate(here):
        total = 3.0 * part
        for other in others:
            total = total + 0.5 * other[half]
        inverse = jnp.where(keep, DAMPING / jnp.where(keep, total, 1.0), 0.0)
        last_weight.append(inverse * (1.0 / last_scale))
        last_links.append(
            [
                jnp.where(pair[half] & keep, 0.5 * inverse * (part + other[half]), 0.0)
                for pair, other in zip(inside_last, others)
            ]
        )

    def solve_last(rhs):
        base = [weight * part for weight, part in zip(last_weight, split(rhs))]
        value = base
        for _ in range(COARSE_SWEEPS - 1):
            moved = around(value)
            fresh = []
            for half in range(2):
                parts = [link * other[half] for link, other in zip(last_links[half], moved)]
                start = base[half] + (1.0 - DAMPING) * value[half]
                fresh.append(((start + parts[0]) + (parts[1] + parts[2])) + (parts[3] + (parts[4] + parts[5])))
            value = fresh
        return value[0] + pltpu.roll(value[1], 1, 1)

    def cycle(index, out, exact=False):
        level = levels[index]
        below = levels[index + 1]
        if index == LEVELS - 3:
            base = {}

            def take(x, z, row):
                base[x, z] = below.weight[x, z] * (row * (1.0 / below.scale))

            level.descend(take)
            below.cycle(base, solve_last, below.first)
        else:
            level.descend(
                lambda x, z, row: below.base.put(
                    x, z, below.weight[x, z] * (row * (2.0 / below.scale))
                )
            )
            cycle(index + 1, below.first)
        level.ascend(lambda x, z: below.first[x, z], out, exact)

    spot = spot_ref[...]
    at_spot = iota((LANES, electrodes), 0) == spot
    order = lane_order(back=True)
    wide = SIDE + 2
    sending = pltpu.make_async_copy(sent, potentials_ref, sem)

    def each(body):
        def one(electrode, carry):
            body(pl.ds(electrode, 1), pl.ds(cells_ref[0, electrode], 1))
            return carry

        lax.fori_loop(0, electrodes, one, 0, unroll=32)

    def put(electrode, cell):
        fine.base.ref[cell, :] = (2.0 * gathered[electrode, :]) * fine.weight.ref[cell, :]

    def read(electrode, cell):
        gathered[electrode, :] = forward.ref[cell, :]

    def exact(row, matrix_ref):
        return product(jnp.broadcast_to(row, (16, row.shape[1])), matrix_ref[...], 3)[0:1]

    sub, lane = iota((SIDE, LANES), 0), iota((SIDE, LANES), 1)

    def margin(x, z, y):
        return forward.ref[pl.ds(forward.start(x, z, y) + device, 1), :]

    def extract(index):
        for x in range(-1, SIDE + 1):
            for z in range(SIDE):
                at = (x + 1) * wide + z + 1
                start = forward.start(x, z) + device
                row = forward.ref[pl.ds(start, SIDE, stride=SIDE), :]
                owned[index, at] = row
                if 0 <= x < SIDE:
                    after, before = margin(x, z, SIDE), margin(x, z, -1)
                    place = x * SIDE + z
                    turned = pltpu.roll(row, SIDE - 1, 0)
                    beside[index, 0, place] = jnp.where(sub == SIDE - 1, after, turned)
                    beside[index, 1, place] = jnp.where(sub == 0, before, pltpu.roll(row, 1, 0))
                    if z == 0:
                        edge = pltpu.roll(row, LANES - 1, 1)
                        owned[index, at + SIDE] = jnp.where(lane % GROUP < GROUP - 1, edge, 0.0)
                    if z == SIDE - 1:
                        edge = pltpu.roll(row, 1, 1)
                        owned[index, at - SIDE] = jnp.where(lane % GROUP > 0, edge, 0.0)

    def solve(index):
        each(put)
        rolled(SIDE, fine.base.close_z)
        fine.base.close()
        cycle(0, forward, exact=True)
        extract(index)

        @pl.when(index == 0)
        def _():
            for x in range(SIDE):
                tiles = [owned[0, (x + 1) * wide + z + 1] for z in range(SIDE)]
                sent[x] = from_blocks(tiles, order)
            sending.start()
            each(read)
            readings = jnp.where(at_spot, gathered[...].T, 0.0)
            readings = jnp.sum(readings, axis=0, keepdims=True)
            misfit = exact(readings, turned_ref) - observed_ref[...]
            gathered[...] = shared_rows(exact(misfit, pairs_ref), spot, same_ref[...])

    gathered[...] = rows_ref[...]
    rolled(2, solve)

    chunk = mine_ref.shape[1]
    even = shot == 0
    for x in range(SIDE):
        tiles = []
        for z in range(SIDE):
            at = (x + 1) * wide + z + 1
            here_u, here_w = owned[0, at], owned[1, at]
            total = None
            for step in (wide, -wide, 1, -1):
                term = (here_u - owned[0, at + step]) * (here_w - owned[1, at + step])
                total = term if total is None else total + term
            for side in range(2):
                other_u, other_w = beside[0, side, x * SIDE + z], beside[1, side, x * SIDE + z]
                total = total + (here_u - other_u) * (here_w - other_w)
            tiles.append(-0.5 * total)
        natural = from_blocks(tiles, order)
        low, high = natural[:chunk], natural[chunk:]
        mine_ref[x] = jnp.where(even, low, high)
        theirs_ref[x] = jnp.where(even, high, low)
    sending.wait()


def replicated(conductivity, stations, currents, receivers, observed):
    rows, cols, depth = conductivity.shape
    f32 = jnp.float32
    electrodes = stations.shape[0]
    total = rows * cols
    vmem = pl.BlockSpec(memory_space=pltpu.VMEM)
    smem = pl.BlockSpec(memory_space=pltpu.SMEM)
    station_row = stations.reshape(1, electrodes)
    mine, half = pl.pallas_call(
        to_blocks_kernel,
        out_shape=(
            jax.ShapeDtypeStruct((total, LANES), f32),
            jax.ShapeDtypeStruct((total // 2, LANES), f32),
        ),
        in_specs=[vmem],
        out_specs=(vmem, vmem),
        compiler_params=pltpu.CompilerParams(vmem_limit_bytes=SMALL_BYTES),
    )(conductivity)
    swap = [(0, 1), (1, 0)]

    def partner(part, k):
        count = lax.axis_size("gx")
        return lax.ppermute(part, "gx", [(i, i ^ k) for i in range(count)])

    def with_mate(part):
        return [part, lax.ppermute(part, "gy", swap)]

    far = partner(half, 2)
    near = partner(mine, 1)
    line = jax.ShapeDtypeStruct((1, electrodes), jnp.int32)
    cells, spot, rows_of, same, pairs, turned, held = pl.pallas_call(
        electrode_kernel,
        out_shape=(
            line,
            line,
            jax.ShapeDtypeStruct((electrodes, LANES), f32),
            jax.ShapeDtypeStruct((electrodes, electrodes), jnp.bfloat16),
            jax.ShapeDtypeStruct((receivers.shape[0], electrodes), jnp.bfloat16),
            jax.ShapeDtypeStruct((electrodes, receivers.shape[0]), jnp.bfloat16),
            jax.ShapeDtypeStruct(observed.shape, f32),
        ),
        in_specs=[vmem] * 4,
        out_specs=(vmem,) * 7,
        compiler_params=pltpu.CompilerParams(vmem_limit_bytes=SMALL_BYTES),
        cost_estimate=pl.CostEstimate(flops=100_000_000, bytes_accessed=1_000_000, transcendentals=0),
    )(station_row, currents, receivers, observed)
    far, rows_of = lax.optimization_barrier((far, rows_of))
    far = [far, lax.ppermute(far, "shot", swap)]
    halved = far + [partner(piece, 1) for piece in far]
    parts = [piece for own in (mine, near) for piece in with_mate(own)]
    halved = [piece for own in halved for piece in with_mate(own)]
    chunk = cols // 2
    levels = [shape for index in range(LEVELS - 2) for shape in Level.scratch(index)]
    levels += HeldLevel.scratch(LEVELS - 2)
    potentials, own, theirs = pl.pallas_call(
        functools.partial(replicated_kernel, len(parts), len(halved)),
        out_shape=(
            jax.ShapeDtypeStruct((rows, cols, LANES), f32),
            jax.ShapeDtypeStruct((rows, chunk, LANES), f32),
            jax.ShapeDtypeStruct((rows, chunk, LANES), f32),
        ),
        in_specs=[smem] + [vmem] * (len(parts) + len(halved) + 6),
        out_specs=(pl.BlockSpec(memory_space=pl.ANY), vmem, vmem),
        scratch_shapes=[
            pltpu.VMEM((electrodes, LANES), f32),
            pltpu.VMEM((2, (SIDE + 2) ** 2, SIDE, LANES), f32),
            pltpu.VMEM((2, 2, SIDE**2, SIDE, LANES), f32),
            pltpu.VMEM((rows, cols, LANES), f32),
            pltpu.SemaphoreType.DMA,
        ]
        + levels,
        compiler_params=pltpu.CompilerParams(vmem_limit_bytes=VMEM_BYTES),
        cost_estimate=pl.CostEstimate(flops=200_000_000, bytes_accessed=4_000_000, transcendentals=0),
    )(cells, *parts, *halved, spot, rows_of, same, pairs, turned, held)
    return potentials[None], own + lax.ppermute(theirs, "shot", swap)


def extended(array, sides, width):
    for axis, dim in sides:
        size, length = (lax.axis_size(axis), array.shape[dim])
        up = [(i, (i + 1) % size) for i in range(size - 1)]
        down = [(j, i) for i, j in up]
        last = lax.slice_in_dim(array, length - width, length, axis=dim)
        leading = lax.slice_in_dim(array, 0, width, axis=dim)
        before = lax.ppermute(last, axis, up)
        after = lax.ppermute(leading, axis, down)
        array = jnp.concatenate([before, array, after], axis=dim)
    return array


def upper_z(field):
    return jnp.concatenate([field[..., 1:], jnp.zeros_like(field[..., :1])], axis=-1)


def lower_z(field):
    return jnp.concatenate([jnp.zeros_like(field[..., :1]), field[..., :-1]], axis=-1)


def trim_circle(field, circle_width):
    return field[..., circle_width:-circle_width, circle_width:-circle_width, :]


def pad_plane(field, circle_width):
    spec = [(0, 0)] * (field.ndim - 3) + [
        (circle_width, circle_width),
        (circle_width, circle_width),
        (0, 0),
    ]
    return jnp.pad(field, spec)


def neighbour_list(field_pad):
    centre = trim_circle(field_pad, 1)
    return [
        field_pad[..., 2:, 1:-1, :],
        field_pad[..., :-2, 1:-1, :],
        field_pad[..., 1:-1, 2:, :],
        field_pad[..., 1:-1, :-2, :],
        upper_z(centre),
        lower_z(centre),
    ]


def stencil(field_pad, cond_pad, level_scale):
    centre = trim_circle(field_pad, 1)
    centre_cond = trim_circle(cond_pad, 1)
    summed = jnp.zeros_like(centre)
    for other, other_cond in zip(neighbour_list(field_pad), neighbour_list(cond_pad)):
        summed = summed + level_scale * 0.5 * (centre_cond + other_cond) * (centre - other)
    return summed


def diagonal(cond_pad, level_scale):
    centre_cond = trim_circle(cond_pad, 1)
    summed = jnp.zeros_like(centre_cond)
    for other_cond in neighbour_list(cond_pad):
        summed = summed + level_scale * 0.5 * (centre_cond + other_cond)
    return summed


def relaxed(field_pad, source, cond_pad, diag_level, level_scale):
    return (
        trim_circle(field_pad, 1)
        + DAMPING * (source - stencil(field_pad, cond_pad, level_scale)) / diag_level
    )


def restrict(field):
    leading = field.shape[:-3]
    extent = field.shape[-3:]
    shaped = field.reshape(leading + (extent[0] // 2, 2, extent[1] // 2, 2, extent[2] // 2, 2))
    return shaped.mean(axis=(-5, -3, -1))


def prolong(field):
    return jnp.repeat(jnp.repeat(jnp.repeat(field, 2, axis=-3), 2, axis=-2), 2, axis=-1)


def assemble(blocks, count_x, count_y):
    leading = blocks.shape[1:-3]
    extent = blocks.shape[-3:]
    depth_lead = len(leading)
    shaped = blocks.reshape((count_x, count_y) + leading + extent)
    order = tuple(range(2, 2 + depth_lead)) + (0, 2 + depth_lead, 1, 3 + depth_lead, 4 + depth_lead)
    return shaped.transpose(order).reshape(
        leading + (count_x * extent[0], count_y * extent[1], extent[2])
    )


def field_rim(field):
    return extended(field, (("gx", 1), ("gy", 2)), 1)


def cond_rim(conduct):
    return extended(conduct, (("gx", 0), ("gy", 1)), 1)


def whole_cycle(source, level_index, whole_plans):
    cond_pad, diag_level, level_scale = whole_plans[level_index]
    field = DAMPING * source / diag_level

    def turn(turn_index, iterate):
        return relaxed(pad_plane(iterate, 1), source, cond_pad, diag_level, level_scale)

    return lax.fori_loop(0, COARSE_SWEEPS - 1, turn, field)


def part_cycle(source, level_index, level_plans, whole_plans, gather_level):
    if level_index == gather_level:
        blocks = lax.all_gather(source[None], ("gx", "gy"), axis=0, tiled=True)
        whole = assemble(blocks, lax.axis_size("gx"), lax.axis_size("gy"))
        correction = whole_cycle(whole, level_index, whole_plans)
        extent = source.shape
        starts = (0, lax.axis_index("gx") * extent[1], lax.axis_index("gy") * extent[2], 0)
        return lax.dynamic_slice(correction, starts, extent)
    cond_pad, diag_level, level_scale = level_plans[level_index]
    field = DAMPING * source / diag_level
    field = relaxed(field_rim(field), source, cond_pad, diag_level, level_scale)
    residual = source - stencil(field_rim(field), cond_pad, level_scale)
    field = field + prolong(
        part_cycle(restrict(residual), level_index + 1, level_plans, whole_plans, gather_level)
    )
    field = relaxed(field_rim(field), source, cond_pad, diag_level, level_scale)
    return relaxed(field_rim(field), source, cond_pad, diag_level, level_scale)


def distributed(conductivity, stations, currents, receivers, observed):
    row_count, col_count, z_count = conductivity.shape
    shot_count = currents.shape[0]
    count_x = lax.axis_size("gx")
    count_y = lax.axis_size("gy")
    gather_level = LEVELS - 1
    level_plans = []
    conduct = conductivity
    for level_index in range(gather_level):
        level_scale = 0.25**level_index
        cond_pad = cond_rim(conduct)
        level_plans.append((cond_pad, diagonal(cond_pad, level_scale), level_scale))
        conduct = restrict(conduct)
    blocks = lax.all_gather(conduct[None], ("gx", "gy"), axis=0, tiled=True)
    whole = assemble(blocks, count_x, count_y)
    whole_plans = {}
    level_index = 3
    level_scale = 0.25**level_index
    cond_pad = pad_plane(whole, 1)
    whole_plans[level_index] = (cond_pad, diagonal(cond_pad, level_scale), level_scale)
    total_y = col_count * count_y
    cell_x = stations // (total_y * z_count)
    cell_y = stations // z_count % total_y
    cell_z = stations % z_count
    local_x = cell_x - lax.axis_index("gx") * row_count
    local_y = cell_y - lax.axis_index("gy") * col_count
    owned = (local_x >= 0) & (local_x < row_count) & (local_y >= 0) & (local_y < col_count)
    block_size = row_count * col_count * z_count
    local_cell = jnp.where(owned, (local_x * col_count + local_y) * z_count + cell_z, 0)
    offsets = jnp.arange(shot_count)[:, None] * block_size + local_cell[None, :]
    targets = jnp.where(owned[None, :], offsets, shot_count * block_size).reshape(-1)

    def spread(amounts):
        flat = (
            jnp.zeros((shot_count * block_size,), jnp.float32)
            .at[targets]
            .add(amounts.reshape(-1), mode="drop")
        )
        return flat.reshape(shot_count, row_count, col_count, z_count)

    potentials = part_cycle(spread(currents), 0, level_plans, whole_plans, gather_level)
    local_values = jnp.where(
        owned[None, :], potentials.reshape(shot_count, block_size)[:, local_cell], 0.0
    )
    readings = lax.psum(local_values, ("gx", "gy"))
    positions = jnp.arange(stations.shape[0])[:, None]
    pairs = (receivers[:, 0][None, :] == positions).astype(jnp.float32) - (
        receivers[:, 1][None, :] == positions
    ).astype(jnp.float32)
    misfit = jnp.dot(readings, pairs, precision=lax.Precision.HIGHEST) - observed
    back_source = jnp.dot(misfit, pairs.T, precision=lax.Precision.HIGHEST)
    adjoint = part_cycle(spread(back_source), 0, level_plans, whole_plans, gather_level)
    stacked = jnp.concatenate([potentials, adjoint], axis=0)
    padded = extended(stacked, (("gx", 1), ("gy", 2)), 1)
    potential_pad = padded[:shot_count]
    adjoint_pad = padded[shot_count:]
    gradient = jnp.zeros_like(potentials)
    for other_u, other_w in zip(neighbour_list(potential_pad), neighbour_list(adjoint_pad)):
        gradient = gradient - 0.5 * (potentials - other_u) * (adjoint - other_w)
    summed = lax.psum_scatter(jnp.sum(gradient, axis=0), "shot", scatter_dimension=1, tiled=True)
    return (potentials, summed)


def per_device(conductivity, stations, currents, receivers, observed):
    blocks = lax.axis_size("gx") * lax.axis_size("gy")
    fits = conductivity.shape == (SIDE, SIDE * SIDE, LANES) and blocks == SIDE
    fits = fits and lax.axis_size("gy") == 2 and lax.axis_size("shot") == 2
    fits = fits and currents.shape[0] == 1
    plan = replicated if fits else distributed
    return plan(conductivity, stations, currents, receivers, observed)


def solution(mesh):
    in_specs = (
        P(("grp", "gx"), "gy", None),
        P("grp"),
        P(("grp", "shot"), None),
        P("grp", None),
        P(("grp", "shot"), None),
    )
    out_specs = (P(("grp", "shot"), "gx", "gy", None), P(("grp", "gx"), ("gy", "shot"), None))
    return jax.shard_map(
        per_device, mesh=mesh, in_specs=in_specs, out_specs=out_specs, check_vma=False
    )
```

```python
import functools

import jax
import jax.numpy as jnp
from jax import lax
from jax.experimental import pallas as pl
from jax.experimental.pallas import tpu as pltpu
from jax.sharding import PartitionSpec as P

LEVELS = 4
COARSE_SWEEPS = 16


DAMPING = 0.8

SIDE = 8
LANES = 128
GROUP = 16
VMEM_BYTES = 48 * 2**20
SMALL_BYTES = 6 * 2**20


def pieces_of(value, count):
    pieces = []
    for _ in range(count):
        pieces.append(value.astype(jnp.bfloat16))
        value = value - pieces[-1].astype(jnp.float32)
    return pieces[::-1]


def product(value, matrix, count, dims=((1,), (0,))):
    result = None
    for piece in pieces_of(value, count):
        term = lax.dot_general(
            piece, matrix, (dims, ((), ())), preferred_element_type=jnp.float32
        )
        result = term if result is None else result + term
    return result


def iota(shape, dim):
    return lax.broadcasted_iota(jnp.int32, shape, dim)


def station_table(station):
    cell_x, cell_y, cell_z = station >> 14, station >> 7 & 127, station & 127
    row = (cell_x >> 3) * 2 + (cell_y >> 6)
    return cell_x, cell_y, cell_z, row, (cell_y >> 3 & 7) * GROUP + (cell_z >> 3)


def lane_order(back=False):
    row, col = iota((LANES, LANES), 0), iota((LANES, LANES), 1)
    if back:
        row, col = col, row
    chosen = row == col % GROUP * SIDE + col // GROUP
    return jnp.where(chosen, 1.0, 0.0).astype(jnp.bfloat16)


def exchange_groups(tiles):
    tiles = list(tiles)
    group = iota(tiles[0].shape, 1) // GROUP
    for bit in range(3):
        step = 1 << bit
        keep = (group & step) == 0
        for low in range(SIDE):
            if low & step == 0:
                a, b = tiles[low], tiles[low | step]
                tiles[low] = jnp.where(keep, a, pltpu.roll(b, step * GROUP, 1))
                tiles[low | step] = jnp.where(keep, pltpu.roll(a, LANES - step * GROUP, 1), b)
    return tiles


def own_place():
    return lax.axis_index("gx") * 2 + lax.axis_index("gy"), lax.axis_index("shot")


def to_blocks_kernel(natural_ref, blocks_ref, half_ref):
    order = lane_order()
    for x in range(SIDE):
        tiles = product(natural_ref[x], order, 3)
        tiles = [tiles[SIDE * k : SIDE * (k + 1)] for k in range(SIDE)]
        for z, tile in enumerate(exchange_groups(tiles)):
            blocks_ref[pl.ds((x * SIDE + z) * SIDE, SIDE), :] = tile
    count = half_ref.shape[0]
    low, high = blocks_ref[pl.ds(0, count), :], blocks_ref[pl.ds(count, count), :]
    half_ref[...] = jnp.where(own_place()[1] == 0, low, high)


def from_blocks(tiles, order):
    natural = jnp.concatenate(exchange_groups(tiles), axis=0)
    return product(natural, order, 3)


def block_up(field, axis):
    if axis == 0:
        return pltpu.roll(field, 6, 1)
    if axis == 2:
        return pltpu.roll(field, LANES - 1, 2)
    turned = pltpu.roll(field, LANES - GROUP, 2)
    return jnp.where(iota(field.shape, 2) < LANES - GROUP, turned, pltpu.roll(turned, 7, 1))


def block_down(field, axis):
    if axis == 0:
        return pltpu.roll(field, 2, 1)
    if axis == 2:
        return pltpu.roll(field, 1, 2)
    turned = pltpu.roll(field, GROUP, 2)
    return jnp.where(iota(field.shape, 2) >= GROUP, turned, pltpu.roll(turned, 1, 1))


def inside_up(field, axis):
    sub, lane = iota(field.shape, 1), iota(field.shape, 2)
    if axis == 0:
        keep = sub < 6
    elif axis == 1:
        keep = (lane < LANES - GROUP) | (sub % 2 == 0)
    else:
        keep = lane % GROUP < GROUP - 1
    return jnp.where(keep, field, 0.0)


def inside_down(field, axis):
    sub, lane = iota(field.shape, 1), iota(field.shape, 2)
    if axis == 0:
        keep = sub >= 2
    elif axis == 1:
        keep = (lane >= GROUP) | (sub % 2 == 1)
    else:
        keep = lane % GROUP > 0
    return jnp.where(keep, field, 0.0)


def pair_rows(row):
    count = row.shape[0] // 2
    return jnp.concatenate([row[2 * i : 2 * i + 1] + row[2 * i + 1 : 2 * i + 2] for i in range(count)])


def twice(row):
    return jnp.concatenate([row[i // 2 : i // 2 + 1] for i in range(2 * row.shape[0])])


def electrode_kernel(
    stations_ref,
    currents_ref,
    receivers_ref,
    observed_ref,
    cells_ref,
    spot_ref,
    rows_ref,
    same_ref,
    pairs_ref,
    turned_ref,
    held_ref,
):
    stations = stations_ref[...]
    electrodes = stations.shape[1]
    cell_x, cell_y, cell_z, row, spot = station_table(stations)
    wide = SIDE + 2
    register = (((cell_x & 7) + 1) * wide + (cell_z & 7) + 1) * wide + (cell_y & 7) + 1
    cells_ref[...] = register * SIDE + row
    spot_ref[...] = spot
    held_ref[...] = observed_ref[...]
    line = stations & 0x1C387 | row << 20
    same = jnp.broadcast_to(line, (electrodes, electrodes))
    same = jnp.where(same == same.T, 1.0, 0.0).astype(jnp.bfloat16)
    same_ref[...] = same
    rows_ref[...] = shared_rows(currents_ref[...], spot, same)
    receivers = receivers_ref[...]
    numbers = iota((receivers.shape[0], electrodes), 1)
    pairs = jnp.where(numbers == receivers[:, 0:1], 1.0, 0.0) - jnp.where(
        numbers == receivers[:, 1:2], 1.0, 0.0
    )
    pairs_ref[...] = pairs.astype(jnp.bfloat16)
    turned_ref[...] = pairs.T.astype(jnp.bfloat16)


def shared_rows(amounts, spot, same):
    electrodes = amounts.shape[1]
    at_spot = iota((LANES, electrodes), 0) == spot
    return product(jnp.where(at_spot, amounts, 0.0), same, 3).T


class Edged:
    def __init__(self, ref, side):
        self.ref, self.side = ref, side

    def start(self, x, z, y=0):
        wide = self.side + 2
        return (((x + 1) * wide + z + 1) * wide + y + 1) * SIDE

    def __getitem__(self, at):
        x, z = at
        rows = self.ref[pl.ds(self.start(x, z), self.side * SIDE), :]
        return rows.reshape(self.side, SIDE, LANES)

    def __setitem__(self, at, value):
        x, z = at
        self.ref[pl.ds(self.start(x, z), self.side * SIDE), :] = value.reshape(-1, LANES)

    def put(self, x, z, value, exact=False):
        self[x, z] = value
        n = self.side
        if z == 0:
            edge = block_up(value, 2)
            self[x, n] = inside_up(edge, 2) if exact else edge
        if z == n - 1:
            edge = block_down(value, 2)
            self[x, -1] = inside_down(edge, 2) if exact else edge
        if x == 0:
            edge = block_up(value, 0)
            self[n, z] = inside_up(edge, 0) if exact else edge
        if x == n - 1:
            edge = block_down(value, 0)
            self[-1, z] = inside_down(edge, 0) if exact else edge
        if exact:
            after = inside_up(block_up(value[:1], 1), 1)
            self.ref[pl.ds(self.start(x, z, n), SIDE), :] = after[0]
            before = inside_down(block_down(value[n - 1 :], 1), 1)
            self.ref[pl.ds(self.start(x, z, -1), SIDE), :] = before[0]

    def close_z(self, x, exact=False):
        n = self.side
        after, before = block_up(self[x, 0], 2), block_down(self[x, n - 1], 2)
        self[x, n] = inside_up(after, 2) if exact else after
        self[x, -1] = inside_down(before, 2) if exact else before

    def close(self, exact=False):
        n = self.side
        for z in range(n):
            after = block_up(self[0, z], 0)
            self[n, z] = inside_up(after, 0) if exact else after
            before = block_down(self[n - 1, z], 0)
            self[-1, z] = inside_down(before, 0) if exact else before


class Rows:
    def __init__(self, ref, side, first_x=0, first_z=0):
        self.ref, self.side, self.first_x, self.first_z = ref, side, first_x, first_z

    def place(self, at):
        count = self.side - self.first_z
        rows = self.side * SIDE
        return pl.ds(((at[0] - self.first_x) * count + at[1] - self.first_z) * rows, rows)

    def __getitem__(self, at):
        return self.ref[self.place(at), :].reshape(self.side, SIDE, LANES)

    def __setitem__(self, at, value):
        self.ref[self.place(at), :] = value.reshape(-1, LANES)


def rolled(count, body, unroll=1):
    def one(x, carry):
        body(x)
        return carry

    lax.fori_loop(0, count, one, 0, unroll=unroll)


def next_in_y(row):
    return jnp.concatenate([row[1:], block_up(row[:1], 1)])


def last_in_y(row):
    return jnp.concatenate([block_down(row[-1:], 1), row[:-1]])


class Level:
    def __init__(self, refs, index):
        self.side = side = SIDE >> index
        self.scale = 0.25**index
        edged = [Edged(ref, side) for ref in refs[:5]]
        self.cond, self.first, self.second, self.base, self.weight = edged
        self.link_x = Rows(refs[5], side, first_x=-1)
        self.link_y = Rows(refs[6], side)
        self.link_z = Rows(refs[7], side, first_z=-1)
        self.back = Rows(refs[8], side)

    @staticmethod
    def scratch(index):
        side = SIDE >> index
        sizes = [(side + 2) ** 3] * 5
        sizes += [side**2 * (side + 1), side**3, side**2 * (side + 1), side**3]
        return [pltpu.VMEM((size * SIDE, LANES), jnp.float32) for size in sizes]

    def pairs(self, body):
        for i in range(self.side // 2):
            body(2 * i)

    def prepare(self):
        n = self.side
        cond = self.cond

        def plane(x):
            for z in range(n):
                here, ahead, next_x = cond[x, z], cond[x, z + 1], cond[x + 1, z]
                after = inside_up(block_up(here[:1], 1), 1)
                before = inside_down(block_down(here[-1:], 1), 1)
                next_y = jnp.concatenate([here[1:], after])
                last_y = jnp.concatenate([before, here[:-1]])
                total = (next_x + cond[x - 1, z]) + (ahead + cond[x, z - 1]) + (next_y + last_y)
                total = 6.0 * here + total
                self.weight[x, z] = DAMPING / total
                if n == SIDE:
                    self.base[x, z] = jnp.zeros_like(here)
                self.back[x, z] = total * (0.5 * self.scale / DAMPING)
                self.link_x[x, z] = here + next_x
                link = here + next_y
                self.link_y[x, z] = jnp.concatenate([link[:-1], inside_up(link[-1:], 1)])
                link = here + ahead
                if z == n - 1:
                    link = inside_up(link, 2)
                    self.link_z[x, -1] = block_down(link, 2)
                self.link_z[x, z] = link

        if n == SIDE:
            rolled(n, plane, unroll=2)
        else:
            for x in range(n):
                plane(x)
        for z in range(n):
            link = inside_up(self.link_x[n - 1, z], 0)
            self.link_x[n - 1, z] = link
            self.link_x[-1, z] = block_down(link, 0)

    def flows(self, x, z, here, ahead, outer, down):
        result = []
        inner = self.link_x[x, z]
        sides = [
            self.link_x[x - 1, z] * outer[0] + inner * here[1],
            inner * here[0] + self.link_x[x + 1, z] * outer[1],
        ]
        for p in range(2):
            link_y, link_z = self.link_y[x + p, z], self.link_z[x + p, z]
            along = link_y * next_in_y(here[p]) + last_in_y(link_y * here[p])
            total = sides[p] + (link_z * ahead[p] + down[p]) + along
            down[p] = link_z * here[p]
            result.append(self.weight[x + p, z] * total)
        return result

    def rows(self, field, x):
        here = [field[x, 0], field[x + 1, 0]]
        down = [self.link_z[x + p, -1] * field[x + p, -1] for p in range(2)]
        for z in range(self.side):
            ahead = [field[x, z + 1], field[x + 1, z + 1]]
            outer = [field[x - 1, z], field[x + 2, z]]
            yield z, here, self.flows(x, z, here, ahead, outer, down)
            here = ahead

    def sweep(self, field, out, exact=False):
        def pair(x):
            for z, here, sums in self.rows(field, x):
                for p in range(2):
                    if field is self.base:
                        value = (2.0 - DAMPING) * here[p] + sums[p]
                    else:
                        value = (1.0 - DAMPING) * here[p] + (self.base[x + p, z] + sums[p])
                    out.put(x + p, z, value, exact)

        self.pairs(pair)

    def halve(self, rows, coarse):
        def pair(x):
            held = None
            for z, row in enumerate(rows(x)):
                row = row[0] + row[1]
                if z % 2 == 0:
                    held = row
                else:
                    coarse(x // 2, z // 2, 0.125 * pair_rows(held + row))

        self.pairs(pair)

    def descend(self, coarse):
        self.sweep(self.base, self.second)

        def residuals(x):
            for z, here, sums in self.rows(self.second, x):
                result = []
                for p in range(2):
                    swept = (1.0 - DAMPING) * here[p] + (self.base[x + p, z] + sums[p])
                    self.first[x + p, z] = swept
                    result.append((swept - here[p]) * self.back[x + p, z])
                yield result

        self.halve(residuals, coarse)

    def ascend(self, correction, out, exact=False):
        def pair(x):
            i = x // 2
            here = twice(correction(i, 0))
            start = twice(correction(i, -1))
            down = [self.link_z[x + p, -1] * start for p in range(2)]
            for z in range(self.side):
                ahead = twice(correction(i, (z + 1) // 2))
                outer = [twice(correction(i - 1, z // 2)), twice(correction(i + 1, z // 2))]
                sums = self.flows(x, z, [here, here], [ahead, ahead], outer, down)
                for p in range(2):
                    value = self.first[x + p, z] + ((1.0 - DAMPING) * here + sums[p])
                    self.second.put(x + p, z, value)
                here = ahead

        self.pairs(pair)
        self.sweep(self.second, out, exact)


class HeldLevel:
    def __init__(self, refs, index):
        self.side = 2
        self.scale = 0.25**index
        self.cond, self.first = Edged(refs[0], 2), Edged(refs[1], 2)
        self.weight, self.back = Rows(refs[2], 2), Rows(refs[3], 2)
        self.links = [Rows(ref, 2) for ref in refs[4:]]

    @staticmethod
    def scratch(index):
        sizes = [4**3] * 2 + [2**3] * 8
        return [pltpu.VMEM((size * SIDE, LANES), jnp.float32) for size in sizes]

    def around(self, field, inside=False):
        def moved(row, axis, up):
            row = (block_up if up else block_down)(row, axis)
            return (inside_up if up else inside_down)(row, axis) if inside else row

        result = {}
        for (x, z), here in field.items():
            result[x, z] = [
                field[1, z] if x == 0 else moved(field[0, z], 0, True),
                field[0, z] if x == 1 else moved(field[1, z], 0, False),
                jnp.concatenate([here[1:], moved(here[:1], 1, True)]),
                jnp.concatenate([moved(here[-1:], 1, False), here[:-1]]),
                field[x, 1] if z == 0 else moved(field[x, 0], 2, True),
                field[x, 0] if z == 1 else moved(field[x, 1], 2, False),
            ]
        return result

    def prepare(self):
        field = {(x, z): self.cond[x, z] for x in range(2) for z in range(2)}
        for at, others in self.around(field, inside=True).items():
            here = field[at]
            total = others[0]
            for other in others[1:]:
                total = total + other
            total = 3.0 * here + 0.5 * total
            inverse = DAMPING / total
            self.weight[at] = inverse
            self.back[at] = total * (self.scale / DAMPING)
            for index, other in enumerate(others):
                link = 0.5 * inverse * (here + other)
                self.links[index][at] = jnp.where(other > 0.0, link, 0.0)

    def halve(self, rows, coarse):
        total = None
        for row in rows(0):
            row = row[0] + row[1]
            total = row if total is None else total + row
        coarse(0, 0, 0.125 * (total[:1] + total[1:]))

    def sums(self, field, base):
        result = {}
        for at, others in self.around(field).items():
            total = base[at]
            for link, other in zip(self.links, others):
                total = total + link[at] * other
            result[at] = total
        return result

    def swept(self, field, base):
        sums = self.sums(field, base)
        return {at: (1.0 - DAMPING) * field[at] + sums[at] for at in field}

    def cycle(self, base, solve, out):
        field = self.swept(base, base)
        sums = self.sums(field, base)
        total = None
        for at in field:
            residual = (sums[at] - DAMPING * field[at]) * self.back[at]
            total = residual if total is None else total + residual
        solved = solve(0.125 * (total[:1] + total[1:]))
        row = twice(solved)
        copied = {at: row for at in field}
        change = {at: sums[at] + (1.0 - DAMPING) * (field[at] + row) for at in field}
        field = self.sums(copied, change)
        for (x, z), value in self.swept(field, base).items():
            out.put(x, z, value)


def replicated_kernel(
    whole,
    halved,
    cells_ref,
    *refs,
):
    parts = refs[:whole], refs[whole : whole + halved]
    solve_kernel(*parts, cells_ref, *refs[whole + halved :])


def solve_kernel(
    part_refs,
    half_refs,
    cells_ref,
    spot_ref,
    rows_ref,
    same_ref,
    pairs_ref,
    turned_ref,
    observed_ref,
    potentials_ref,
    mine_ref,
    theirs_ref,
    gathered,
    owned,
    beside,
    sent,
    sem,
    *level_refs,
):
    f32 = jnp.float32
    electrodes = spot_ref.shape[1]
    levels, used = [], 0
    for index in range(LEVELS - 1):
        kind = HeldLevel if index == LEVELS - 2 else Level
        count = len(kind.scratch(index))
        levels.append(kind(level_refs[used : used + count], index))
        used += count
    fine = levels[0]
    forward = fine.cond
    wide = SIDE * SIDE * SIDE

    device, shot = own_place()

    def place(part, row, x, index):
        for z in range(SIDE):
            fine.cond.ref[pl.ds(fine.cond.start(x, z) + index, SIDE, stride=SIDE), :] = part[
                pl.ds((row * SIDE + z) * SIDE, SIDE), :
            ]

    def collect(x):
        for k, part in enumerate(part_refs):
            place(part, x, x, device ^ k)

    def collect_half(x):
        for k, part in enumerate(half_refs):
            swapped, index = k // 2 % 2, len(part_refs) + k // 4 * 2 + k % 2
            place(part, x, (shot ^ swapped) * (SIDE // 2) + x, device ^ index)

    def edges(x):
        fine.cond.close_z(x, exact=True)

    rolled(SIDE, collect, unroll=4)
    for x in range(SIDE // 2):
        collect_half(x)
    for x in range(SIDE):
        edges(x)
    fine.cond.close(exact=True)

    coarsest = []
    for level, below in zip(levels, levels[1:] + [None]):
        level.prepare()

        def coarse(x, z, row, below=below):
            if below is None:
                coarsest.append(row)
            else:
                below.cond.put(x, z, row, exact=True)

        level.halve(
            lambda x, level=level: [
                (level.cond[x, z], level.cond[x + 1, z]) for z in range(level.side)
            ],
            coarse,
        )

    keep = iota((1, SIDE, LANES), 1) % 2 == 0
    lane = iota((1, SIDE, LANES), 2)

    def split(value):
        return [jnp.where(keep, part, 0.0) for part in (value, pltpu.roll(value, SIDE - 1, 1))]

    def around(value):
        low, high = value
        low_up, high_up = [pltpu.roll(part, LANES - GROUP, 2) for part in value]
        low_down, high_down = [pltpu.roll(part, GROUP, 2) for part in value]
        along = [[move(part, axis) for part in value] for axis in (0, 2) for move in (block_up, block_down)]
        return along + [
            [jnp.where(lane < LANES - GROUP, low_up, high_up), high_up],
            [low_down, jnp.where(lane >= GROUP, high_down, low_down)],
        ]

    sub = iota((1, SIDE, LANES), 1)
    inside_last = [
        [sub < 6] * 2,
        [sub >= 2] * 2,
        [lane % GROUP < GROUP - 1] * 2,
        [lane % GROUP > 0] * 2,
        [keep, lane < LANES - GROUP],
        [lane >= GROUP, keep],
    ]
    last_scale = 0.25 ** (LEVELS - 1)
    here = split(coarsest[0])
    others = [
        [jnp.where(inside & keep, part, 0.0) for inside, part in zip(pair, moved)]
        for pair, moved in zip(inside_last, around(here))
    ]
    last_weight, last_links = [], []
    for half, part in enumerate(here):
        total = 3.0 * part
        for other in others:
            total = total + 0.5 * other[half]
        inverse = jnp.where(keep, DAMPING / jnp.where(keep, total, 1.0), 0.0)
        last_weight.append(inverse * (1.0 / last_scale))
        last_links.append(
            [
                jnp.where(pair[half] & keep, 0.5 * inverse * (part + other[half]), 0.0)
                for pair, other in zip(inside_last, others)
            ]
        )

    def solve_last(rhs):
        base = [weight * part for weight, part in zip(last_weight, split(rhs))]
        value = base
        for _ in range(COARSE_SWEEPS - 1):
            moved = around(value)
            fresh = []
            for half in range(2):
                parts = [link * other[half] for link, other in zip(last_links[half], moved)]
                start = base[half] + (1.0 - DAMPING) * value[half]
                fresh.append(((start + parts[0]) + (parts[1] + parts[2])) + (parts[3] + (parts[4] + parts[5])))
            value = fresh
        return value[0] + pltpu.roll(value[1], 1, 1)

    def cycle(index, out, exact=False):
        level = levels[index]
        below = levels[index + 1]
        if index == LEVELS - 3:
            base = {}

            def take(x, z, row):
                base[x, z] = below.weight[x, z] * (row * (1.0 / below.scale))

            level.descend(take)
            below.cycle(base, solve_last, below.first)
        else:
            level.descend(
                lambda x, z, row: below.base.put(
                    x, z, below.weight[x, z] * (row * (2.0 / below.scale))
                )
            )
            cycle(index + 1, below.first)
        level.ascend(lambda x, z: below.first[x, z], out, exact)

    spot = spot_ref[...]
    at_spot = iota((LANES, electrodes), 0) == spot
    order = lane_order(back=True)
    wide = SIDE + 2
    sending = pltpu.make_async_copy(sent, potentials_ref, sem)

    def each(body):
        def one(electrode, carry):
            body(pl.ds(electrode, 1), pl.ds(cells_ref[0, electrode], 1))
            return carry

        lax.fori_loop(0, electrodes, one, 0, unroll=64)

    def put(electrode, cell):
        fine.base.ref[cell, :] = (2.0 * gathered[electrode, :]) * fine.weight.ref[cell, :]

    def read(electrode, cell):
        gathered[electrode, :] = forward.ref[cell, :]

    def exact(row, matrix_ref):
        return product(jnp.broadcast_to(row, (16, row.shape[1])), matrix_ref[...], 3)[0:1]

    sub, lane = iota((SIDE, LANES), 0), iota((SIDE, LANES), 1)

    def margin(x, z, y):
        return forward.ref[pl.ds(forward.start(x, z, y) + device, 1), :]

    def extract(index):
        for x in range(-1, SIDE + 1):
            for z in range(SIDE):
                at = (x + 1) * wide + z + 1
                start = forward.start(x, z) + device
                row = forward.ref[pl.ds(start, SIDE, stride=SIDE), :]
                owned[index, at] = row
                if 0 <= x < SIDE:
                    after, before = margin(x, z, SIDE), margin(x, z, -1)
                    place = x * SIDE + z
                    turned = pltpu.roll(row, SIDE - 1, 0)
                    beside[index, 0, place] = jnp.where(sub == SIDE - 1, after, turned)
                    beside[index, 1, place] = jnp.where(sub == 0, before, pltpu.roll(row, 1, 0))
                    if z == 0:
                        edge = pltpu.roll(row, LANES - 1, 1)
                        owned[index, at + SIDE] = jnp.where(lane % GROUP < GROUP - 1, edge, 0.0)
                    if z == SIDE - 1:
                        edge = pltpu.roll(row, 1, 1)
                        owned[index, at - SIDE] = jnp.where(lane % GROUP > 0, edge, 0.0)

    def solve(index):
        each(put)
        for x in range(SIDE):
            fine.base.close_z(x)
        fine.base.close()
        cycle(0, forward, exact=True)
        extract(index)

        @pl.when(index == 0)
        def _():
            for x in range(SIDE):
                tiles = [owned[0, (x + 1) * wide + z + 1] for z in range(SIDE)]
                sent[x] = from_blocks(tiles, order)
            sending.start()
            each(read)
            readings = jnp.where(at_spot, gathered[...].T, 0.0)
            readings = jnp.sum(readings, axis=0, keepdims=True)
            misfit = exact(readings, turned_ref) - observed_ref[...]
            gathered[...] = shared_rows(exact(misfit, pairs_ref), spot, same_ref[...])

    gathered[...] = rows_ref[...]
    rolled(2, solve)

    chunk = mine_ref.shape[1]
    even = shot == 0
    for x in range(SIDE):
        tiles = []
        for z in range(SIDE):
            at = (x + 1) * wide + z + 1
            here_u, here_w = owned[0, at], owned[1, at]
            total = None
            for step in (wide, -wide, 1, -1):
                term = (here_u - owned[0, at + step]) * (here_w - owned[1, at + step])
                total = term if total is None else total + term
            for side in range(2):
                other_u, other_w = beside[0, side, x * SIDE + z], beside[1, side, x * SIDE + z]
                total = total + (here_u - other_u) * (here_w - other_w)
            tiles.append(-0.5 * total)
        natural = from_blocks(tiles, order)
        low, high = natural[:chunk], natural[chunk:]
        mine_ref[x] = jnp.where(even, low, high)
        theirs_ref[x] = jnp.where(even, high, low)
    sending.wait()


def replicated(conductivity, stations, currents, receivers, observed):
    rows, cols, depth = conductivity.shape
    f32 = jnp.float32
    electrodes = stations.shape[0]
    total = rows * cols
    vmem = pl.BlockSpec(memory_space=pltpu.VMEM)
    smem = pl.BlockSpec(memory_space=pltpu.SMEM)
    station_row = stations.reshape(1, electrodes)
    mine, half = pl.pallas_call(
        to_blocks_kernel,
        out_shape=(
            jax.ShapeDtypeStruct((total, LANES), f32),
            jax.ShapeDtypeStruct((total // 2, LANES), f32),
        ),
        in_specs=[vmem],
        out_specs=(vmem, vmem),
        compiler_params=pltpu.CompilerParams(vmem_limit_bytes=SMALL_BYTES),
    )(conductivity)
    swap = [(0, 1), (1, 0)]

    def partner(part, k):
        count = lax.axis_size("gx")
        return lax.ppermute(part, "gx", [(i, i ^ k) for i in range(count)])

    def with_mate(part):
        return [part, lax.ppermute(part, "gy", swap)]

    far = partner(half, 2)
    near = partner(mine, 1)
    line = jax.ShapeDtypeStruct((1, electrodes), jnp.int32)
    cells, spot, rows_of, same, pairs, turned, held = pl.pallas_call(
        electrode_kernel,
        out_shape=(
            line,
            line,
            jax.ShapeDtypeStruct((electrodes, LANES), f32),
            jax.ShapeDtypeStruct((electrodes, electrodes), jnp.bfloat16),
            jax.ShapeDtypeStruct((receivers.shape[0], electrodes), jnp.bfloat16),
            jax.ShapeDtypeStruct((electrodes, receivers.shape[0]), jnp.bfloat16),
            jax.ShapeDtypeStruct(observed.shape, f32),
        ),
        in_specs=[vmem] * 4,
        out_specs=(vmem,) * 7,
        compiler_params=pltpu.CompilerParams(vmem_limit_bytes=SMALL_BYTES),
        cost_estimate=pl.CostEstimate(flops=100_000_000, bytes_accessed=1_000_000, transcendentals=0),
    )(station_row, currents, receivers, observed)
    far, rows_of = lax.optimization_barrier((far, rows_of))
    far = [far, lax.ppermute(far, "shot", swap)]
    halved = far + [partner(piece, 1) for piece in far]
    parts = [piece for own in (mine, near) for piece in with_mate(own)]
    halved = [piece for own in halved for piece in with_mate(own)]
    chunk = cols // 2
    levels = [shape for index in range(LEVELS - 2) for shape in Level.scratch(index)]
    levels += HeldLevel.scratch(LEVELS - 2)
    potentials, own, theirs = pl.pallas_call(
        functools.partial(replicated_kernel, len(parts), len(halved)),
        out_shape=(
            jax.ShapeDtypeStruct((rows, cols, LANES), f32),
            jax.ShapeDtypeStruct((rows, chunk, LANES), f32),
            jax.ShapeDtypeStruct((rows, chunk, LANES), f32),
        ),
        in_specs=[smem] + [vmem] * (len(parts) + len(halved) + 6),
        out_specs=(pl.BlockSpec(memory_space=pl.ANY), vmem, vmem),
        scratch_shapes=[
            pltpu.VMEM((electrodes, LANES), f32),
            pltpu.VMEM((2, (SIDE + 2) ** 2, SIDE, LANES), f32),
            pltpu.VMEM((2, 2, SIDE**2, SIDE, LANES), f32),
            pltpu.VMEM((rows, cols, LANES), f32),
            pltpu.SemaphoreType.DMA,
        ]
        + levels,
        compiler_params=pltpu.CompilerParams(vmem_limit_bytes=VMEM_BYTES),
        cost_estimate=pl.CostEstimate(flops=200_000_000, bytes_accessed=4_000_000, transcendentals=0),
    )(cells, *parts, *halved, spot, rows_of, same, pairs, turned, held)
    return potentials[None], own + lax.ppermute(theirs, "shot", swap)


def extended(array, sides, width):
    for axis, dim in sides:
        size, length = (lax.axis_size(axis), array.shape[dim])
        up = [(i, (i + 1) % size) for i in range(size - 1)]
        down = [(j, i) for i, j in up]
        last = lax.slice_in_dim(array, length - width, length, axis=dim)
        leading = lax.slice_in_dim(array, 0, width, axis=dim)
        before = lax.ppermute(last, axis, up)
        after = lax.ppermute(leading, axis, down)
        array = jnp.concatenate([before, array, after], axis=dim)
    return array


def upper_z(field):
    return jnp.concatenate([field[..., 1:], jnp.zeros_like(field[..., :1])], axis=-1)


def lower_z(field):
    return jnp.concatenate([jnp.zeros_like(field[..., :1]), field[..., :-1]], axis=-1)


def trim_circle(field, circle_width):
    return field[..., circle_width:-circle_width, circle_width:-circle_width, :]


def pad_plane(field, circle_width):
    spec = [(0, 0)] * (field.ndim - 3) + [
        (circle_width, circle_width),
        (circle_width, circle_width),
        (0, 0),
    ]
    return jnp.pad(field, spec)


def neighbour_list(field_pad):
    centre = trim_circle(field_pad, 1)
    return [
        field_pad[..., 2:, 1:-1, :],
        field_pad[..., :-2, 1:-1, :],
        field_pad[..., 1:-1, 2:, :],
        field_pad[..., 1:-1, :-2, :],
        upper_z(centre),
        lower_z(centre),
    ]


def stencil(field_pad, cond_pad, level_scale):
    centre = trim_circle(field_pad, 1)
    centre_cond = trim_circle(cond_pad, 1)
    summed = jnp.zeros_like(centre)
    for other, other_cond in zip(neighbour_list(field_pad), neighbour_list(cond_pad)):
        summed = summed + level_scale * 0.5 * (centre_cond + other_cond) * (centre - other)
    return summed


def diagonal(cond_pad, level_scale):
    centre_cond = trim_circle(cond_pad, 1)
    summed = jnp.zeros_like(centre_cond)
    for other_cond in neighbour_list(cond_pad):
        summed = summed + level_scale * 0.5 * (centre_cond + other_cond)
    return summed


def relaxed(field_pad, source, cond_pad, diag_level, level_scale):
    return (
        trim_circle(field_pad, 1)
        + DAMPING * (source - stencil(field_pad, cond_pad, level_scale)) / diag_level
    )


def restrict(field):
    leading = field.shape[:-3]
    extent = field.shape[-3:]
    shaped = field.reshape(leading + (extent[0] // 2, 2, extent[1] // 2, 2, extent[2] // 2, 2))
    return shaped.mean(axis=(-5, -3, -1))


def prolong(field):
    return jnp.repeat(jnp.repeat(jnp.repeat(field, 2, axis=-3), 2, axis=-2), 2, axis=-1)


def assemble(blocks, count_x, count_y):
    leading = blocks.shape[1:-3]
    extent = blocks.shape[-3:]
    depth_lead = len(leading)
    shaped = blocks.reshape((count_x, count_y) + leading + extent)
    order = tuple(range(2, 2 + depth_lead)) + (0, 2 + depth_lead, 1, 3 + depth_lead, 4 + depth_lead)
    return shaped.transpose(order).reshape(
        leading + (count_x * extent[0], count_y * extent[1], extent[2])
    )


def field_rim(field):
    return extended(field, (("gx", 1), ("gy", 2)), 1)


def cond_rim(conduct):
    return extended(conduct, (("gx", 0), ("gy", 1)), 1)


def whole_cycle(source, level_index, whole_plans):
    cond_pad, diag_level, level_scale = whole_plans[level_index]
    field = DAMPING * source / diag_level

    def turn(turn_index, iterate):
        return relaxed(pad_plane(iterate, 1), source, cond_pad, diag_level, level_scale)

    return lax.fori_loop(0, COARSE_SWEEPS - 1, turn, field)


def part_cycle(source, level_index, level_plans, whole_plans, gather_level):
    if level_index == gather_level:
        blocks = lax.all_gather(source[None], ("gx", "gy"), axis=0, tiled=True)
        whole = assemble(blocks, lax.axis_size("gx"), lax.axis_size("gy"))
        correction = whole_cycle(whole, level_index, whole_plans)
        extent = source.shape
        starts = (0, lax.axis_index("gx") * extent[1], lax.axis_index("gy") * extent[2], 0)
        return lax.dynamic_slice(correction, starts, extent)
    cond_pad, diag_level, level_scale = level_plans[level_index]
    field = DAMPING * source / diag_level
    field = relaxed(field_rim(field), source, cond_pad, diag_level, level_scale)
    residual = source - stencil(field_rim(field), cond_pad, level_scale)
    field = field + prolong(
        part_cycle(restrict(residual), level_index + 1, level_plans, whole_plans, gather_level)
    )
    field = relaxed(field_rim(field), source, cond_pad, diag_level, level_scale)
    return relaxed(field_rim(field), source, cond_pad, diag_level, level_scale)


def distributed(conductivity, stations, currents, receivers, observed):
    row_count, col_count, z_count = conductivity.shape
    shot_count = currents.shape[0]
    count_x = lax.axis_size("gx")
    count_y = lax.axis_size("gy")
    gather_level = LEVELS - 1
    level_plans = []
    conduct = conductivity
    for level_index in range(gather_level):
        level_scale = 0.25**level_index
        cond_pad = cond_rim(conduct)
        level_plans.append((cond_pad, diagonal(cond_pad, level_scale), level_scale))
        conduct = restrict(conduct)
    blocks = lax.all_gather(conduct[None], ("gx", "gy"), axis=0, tiled=True)
    whole = assemble(blocks, count_x, count_y)
    whole_plans = {}
    level_index = 3
    level_scale = 0.25**level_index
    cond_pad = pad_plane(whole, 1)
    whole_plans[level_index] = (cond_pad, diagonal(cond_pad, level_scale), level_scale)
    total_y = col_count * count_y
    cell_x = stations // (total_y * z_count)
    cell_y = stations // z_count % total_y
    cell_z = stations % z_count
    local_x = cell_x - lax.axis_index("gx") * row_count
    local_y = cell_y - lax.axis_index("gy") * col_count
    owned = (local_x >= 0) & (local_x < row_count) & (local_y >= 0) & (local_y < col_count)
    block_size = row_count * col_count * z_count
    local_cell = jnp.where(owned, (local_x * col_count + local_y) * z_count + cell_z, 0)
    offsets = jnp.arange(shot_count)[:, None] * block_size + local_cell[None, :]
    targets = jnp.where(owned[None, :], offsets, shot_count * block_size).reshape(-1)

    def spread(amounts):
        flat = (
            jnp.zeros((shot_count * block_size,), jnp.float32)
            .at[targets]
            .add(amounts.reshape(-1), mode="drop")
        )
        return flat.reshape(shot_count, row_count, col_count, z_count)

    potentials = part_cycle(spread(currents), 0, level_plans, whole_plans, gather_level)
    local_values = jnp.where(
        owned[None, :], potentials.reshape(shot_count, block_size)[:, local_cell], 0.0
    )
    readings = lax.psum(local_values, ("gx", "gy"))
    positions = jnp.arange(stations.shape[0])[:, None]
    pairs = (receivers[:, 0][None, :] == positions).astype(jnp.float32) - (
        receivers[:, 1][None, :] == positions
    ).astype(jnp.float32)
    misfit = jnp.dot(readings, pairs, precision=lax.Precision.HIGHEST) - observed
    back_source = jnp.dot(misfit, pairs.T, precision=lax.Precision.HIGHEST)
    adjoint = part_cycle(spread(back_source), 0, level_plans, whole_plans, gather_level)
    stacked = jnp.concatenate([potentials, adjoint], axis=0)
    padded = extended(stacked, (("gx", 1), ("gy", 2)), 1)
    potential_pad = padded[:shot_count]
    adjoint_pad = padded[shot_count:]
    gradient = jnp.zeros_like(potentials)
    for other_u, other_w in zip(neighbour_list(potential_pad), neighbour_list(adjoint_pad)):
        gradient = gradient - 0.5 * (potentials - other_u) * (adjoint - other_w)
    summed = lax.psum_scatter(jnp.sum(gradient, axis=0), "shot", scatter_dimension=1, tiled=True)
    return (potentials, summed)


def per_device(conductivity, stations, currents, receivers, observed):
    blocks = lax.axis_size("gx") * lax.axis_size("gy")
    fits = conductivity.shape == (SIDE, SIDE * SIDE, LANES) and blocks == SIDE
    fits = fits and lax.axis_size("gy") == 2 and lax.axis_size("shot") == 2
    fits = fits and currents.shape[0] == 1
    plan = replicated if fits else distributed
    return plan(conductivity, stations, currents, receivers, observed)


def solution(mesh):
    in_specs = (
        P(("grp", "gx"), "gy", None),
        P("grp"),
        P(("grp", "shot"), None),
        P("grp", None),
        P(("grp", "shot"), None),
    )
    out_specs = (P(("grp", "shot"), "gx", "gy", None), P(("grp", "gx"), ("gy", "shot"), None))
    return jax.shard_map(
        per_device, mesh=mesh, in_specs=in_specs, out_specs=out_specs, check_vma=False
    )
```

```python
import functools

import jax
import jax.numpy as jnp
from jax import lax
from jax.experimental import pallas as pl
from jax.experimental.pallas import tpu as pltpu
from jax.sharding import PartitionSpec as P

LEVELS = 4
COARSE_SWEEPS = 16


DAMPING = 0.8

SIDE = 8
LANES = 128
GROUP = 16
VMEM_BYTES = 48 * 2**20
SMALL_BYTES = 6 * 2**20


def pieces_of(value, count):
    pieces = []
    for _ in range(count):
        pieces.append(value.astype(jnp.bfloat16))
        value = value - pieces[-1].astype(jnp.float32)
    return pieces[::-1]


def product(value, matrix, count, dims=((1,), (0,))):
    result = None
    for piece in pieces_of(value, count):
        term = lax.dot_general(
            piece, matrix, (dims, ((), ())), preferred_element_type=jnp.float32
        )
        result = term if result is None else result + term
    return result


def iota(shape, dim):
    return lax.broadcasted_iota(jnp.int32, shape, dim)


def station_table(station):
    cell_x, cell_y, cell_z = station >> 14, station >> 7 & 127, station & 127
    row = (cell_x >> 3) * 2 + (cell_y >> 6)
    return cell_x, cell_y, cell_z, row, (cell_y >> 3 & 7) * GROUP + (cell_z >> 3)


def lane_order(back=False):
    row, col = iota((LANES, LANES), 0), iota((LANES, LANES), 1)
    if back:
        row, col = col, row
    chosen = row == col % GROUP * SIDE + col // GROUP
    return jnp.where(chosen, 1.0, 0.0).astype(jnp.bfloat16)


def exchange_groups(tiles):
    tiles = list(tiles)
    group = iota(tiles[0].shape, 1) // GROUP
    for bit in range(3):
        step = 1 << bit
        keep = (group & step) == 0
        for low in range(SIDE):
            if low & step == 0:
                a, b = tiles[low], tiles[low | step]
                tiles[low] = jnp.where(keep, a, pltpu.roll(b, step * GROUP, 1))
                tiles[low | step] = jnp.where(keep, pltpu.roll(a, LANES - step * GROUP, 1), b)
    return tiles


def own_place():
    return lax.axis_index("gx") * 2 + lax.axis_index("gy"), lax.axis_index("shot")


def to_blocks_kernel(natural_ref, blocks_ref, half_ref):
    order = lane_order()
    for x in range(SIDE):
        tiles = product(natural_ref[x], order, 3)
        tiles = [tiles[SIDE * k : SIDE * (k + 1)] for k in range(SIDE)]
        for z, tile in enumerate(exchange_groups(tiles)):
            blocks_ref[pl.ds((x * SIDE + z) * SIDE, SIDE), :] = tile
    count = half_ref.shape[0]
    low, high = blocks_ref[pl.ds(0, count), :], blocks_ref[pl.ds(count, count), :]
    half_ref[...] = jnp.where(own_place()[1] == 0, low, high)


def from_blocks(tiles, order):
    natural = jnp.concatenate(exchange_groups(tiles), axis=0)
    return product(natural, order, 3)


def block_up(field, axis):
    if axis == 0:
        return pltpu.roll(field, 6, 1)
    if axis == 2:
        return pltpu.roll(field, LANES - 1, 2)
    turned = pltpu.roll(field, LANES - GROUP, 2)
    return jnp.where(iota(field.shape, 2) < LANES - GROUP, turned, pltpu.roll(turned, 7, 1))


def block_down(field, axis):
    if axis == 0:
        return pltpu.roll(field, 2, 1)
    if axis == 2:
        return pltpu.roll(field, 1, 2)
    turned = pltpu.roll(field, GROUP, 2)
    return jnp.where(iota(field.shape, 2) >= GROUP, turned, pltpu.roll(turned, 1, 1))


def inside_up(field, axis):
    sub, lane = iota(field.shape, 1), iota(field.shape, 2)
    if axis == 0:
        keep = sub < 6
    elif axis == 1:
        keep = (lane < LANES - GROUP) | (sub % 2 == 0)
    else:
        keep = lane % GROUP < GROUP - 1
    return jnp.where(keep, field, 0.0)


def inside_down(field, axis):
    sub, lane = iota(field.shape, 1), iota(field.shape, 2)
    if axis == 0:
        keep = sub >= 2
    elif axis == 1:
        keep = (lane >= GROUP) | (sub % 2 == 1)
    else:
        keep = lane % GROUP > 0
    return jnp.where(keep, field, 0.0)


def pair_rows(row):
    count = row.shape[0] // 2
    return jnp.concatenate([row[2 * i : 2 * i + 1] + row[2 * i + 1 : 2 * i + 2] for i in range(count)])


def twice(row):
    return jnp.concatenate([row[i // 2 : i // 2 + 1] for i in range(2 * row.shape[0])])


def electrode_kernel(
    stations_ref,
    currents_ref,
    receivers_ref,
    observed_ref,
    cells_ref,
    spot_ref,
    rows_ref,
    same_ref,
    pairs_ref,
    turned_ref,
    held_ref,
):
    stations = stations_ref[...]
    electrodes = stations.shape[1]
    cell_x, cell_y, cell_z, row, spot = station_table(stations)
    wide = SIDE + 2
    register = (((cell_x & 7) + 1) * wide + (cell_z & 7) + 1) * wide + (cell_y & 7) + 1
    cells_ref[...] = register * SIDE + row
    spot_ref[...] = spot
    held_ref[...] = observed_ref[...]
    line = stations & 0x1C387 | row << 20
    same = jnp.broadcast_to(line, (electrodes, electrodes))
    same = jnp.where(same == same.T, 1.0, 0.0).astype(jnp.bfloat16)
    same_ref[...] = same
    rows_ref[...] = shared_rows(currents_ref[...], spot, same)
    receivers = receivers_ref[...]
    numbers = iota((receivers.shape[0], electrodes), 1)
    pairs = jnp.where(numbers == receivers[:, 0:1], 1.0, 0.0) - jnp.where(
        numbers == receivers[:, 1:2], 1.0, 0.0
    )
    pairs_ref[...] = pairs.astype(jnp.bfloat16)
    turned_ref[...] = pairs.T.astype(jnp.bfloat16)


def shared_rows(amounts, spot, same):
    electrodes = amounts.shape[1]
    at_spot = iota((LANES, electrodes), 0) == spot
    return product(jnp.where(at_spot, amounts, 0.0), same, 3).T


class Edged:
    def __init__(self, ref, side):
        self.ref, self.side = ref, side

    def start(self, x, z, y=0):
        wide = self.side + 2
        return (((x + 1) * wide + z + 1) * wide + y + 1) * SIDE

    def __getitem__(self, at):
        x, z = at
        rows = self.ref[pl.ds(self.start(x, z), self.side * SIDE), :]
        return rows.reshape(self.side, SIDE, LANES)

    def __setitem__(self, at, value):
        x, z = at
        self.ref[pl.ds(self.start(x, z), self.side * SIDE), :] = value.reshape(-1, LANES)

    def put(self, x, z, value, exact=False):
        self[x, z] = value
        n = self.side
        if z == 0:
            edge = block_up(value, 2)
            self[x, n] = inside_up(edge, 2) if exact else edge
        if z == n - 1:
            edge = block_down(value, 2)
            self[x, -1] = inside_down(edge, 2) if exact else edge
        if x == 0:
            edge = block_up(value, 0)
            self[n, z] = inside_up(edge, 0) if exact else edge
        if x == n - 1:
            edge = block_down(value, 0)
            self[-1, z] = inside_down(edge, 0) if exact else edge
        if exact:
            after = inside_up(block_up(value[:1], 1), 1)
            self.ref[pl.ds(self.start(x, z, n), SIDE), :] = after[0]
            before = inside_down(block_down(value[n - 1 :], 1), 1)
            self.ref[pl.ds(self.start(x, z, -1), SIDE), :] = before[0]

    def close_z(self, x, exact=False):
        n = self.side
        after, before = block_up(self[x, 0], 2), block_down(self[x, n - 1], 2)
        self[x, n] = inside_up(after, 2) if exact else after
        self[x, -1] = inside_down(before, 2) if exact else before

    def close(self, exact=False):
        n = self.side
        for z in range(n):
            after = block_up(self[0, z], 0)
            self[n, z] = inside_up(after, 0) if exact else after
            before = block_down(self[n - 1, z], 0)
            self[-1, z] = inside_down(before, 0) if exact else before


class Rows:
    def __init__(self, ref, side, first_x=0, first_z=0):
        self.ref, self.side, self.first_x, self.first_z = ref, side, first_x, first_z

    def place(self, at):
        count = self.side - self.first_z
        rows = self.side * SIDE
        return pl.ds(((at[0] - self.first_x) * count + at[1] - self.first_z) * rows, rows)

    def __getitem__(self, at):
        return self.ref[self.place(at), :].reshape(self.side, SIDE, LANES)

    def __setitem__(self, at, value):
        self.ref[self.place(at), :] = value.reshape(-1, LANES)


def rolled(count, body, unroll=1):
    def one(x, carry):
        body(x)
        return carry

    lax.fori_loop(0, count, one, 0, unroll=unroll)


def next_in_y(row):
    return jnp.concatenate([row[1:], block_up(row[:1], 1)])


def last_in_y(row):
    return jnp.concatenate([block_down(row[-1:], 1), row[:-1]])


class Level:
    def __init__(self, refs, index):
        self.side = side = SIDE >> index
        self.scale = 0.25**index
        edged = [Edged(ref, side) for ref in refs[:5]]
        self.cond, self.first, self.second, self.base, self.weight = edged
        self.link_x = Rows(refs[5], side, first_x=-1)
        self.link_y = Rows(refs[6], side)
        self.link_z = Rows(refs[7], side, first_z=-1)
        self.back = Rows(refs[8], side)

    @staticmethod
    def scratch(index):
        side = SIDE >> index
        sizes = [(side + 2) ** 3] * 5
        sizes += [side**2 * (side + 1), side**3, side**2 * (side + 1), side**3]
        return [pltpu.VMEM((size * SIDE, LANES), jnp.float32) for size in sizes]

    def pairs(self, body):
        for i in range(self.side // 2):
            body(2 * i)

    def prepare(self):
        n = self.side
        cond = self.cond

        def plane(x):
            for z in range(n):
                here, ahead, next_x = cond[x, z], cond[x, z + 1], cond[x + 1, z]
                after = inside_up(block_up(here[:1], 1), 1)
                before = inside_down(block_down(here[-1:], 1), 1)
                next_y = jnp.concatenate([here[1:], after])
                last_y = jnp.concatenate([before, here[:-1]])
                total = (next_x + cond[x - 1, z]) + (ahead + cond[x, z - 1]) + (next_y + last_y)
                total = 6.0 * here + total
                self.weight[x, z] = DAMPING / total
                if n == SIDE:
                    self.base[x, z] = jnp.zeros_like(here)
                self.back[x, z] = total * (0.5 * self.scale / DAMPING)
                self.link_x[x, z] = here + next_x
                link = here + next_y
                self.link_y[x, z] = jnp.concatenate([link[:-1], inside_up(link[-1:], 1)])
                link = here + ahead
                if z == n - 1:
                    link = inside_up(link, 2)
                    self.link_z[x, -1] = block_down(link, 2)
                self.link_z[x, z] = link

        for x in range(n):
            plane(x)
        for z in range(n):
            link = inside_up(self.link_x[n - 1, z], 0)
            self.link_x[n - 1, z] = link
            self.link_x[-1, z] = block_down(link, 0)

    def flows(self, x, z, here, ahead, outer, down):
        result = []
        inner = self.link_x[x, z]
        sides = [
            self.link_x[x - 1, z] * outer[0] + inner * here[1],
            inner * here[0] + self.link_x[x + 1, z] * outer[1],
        ]
        for p in range(2):
            link_y, link_z = self.link_y[x + p, z], self.link_z[x + p, z]
            along = link_y * next_in_y(here[p]) + last_in_y(link_y * here[p])
            total = sides[p] + (link_z * ahead[p] + down[p]) + along
            down[p] = link_z * here[p]
            result.append(self.weight[x + p, z] * total)
        return result

    def rows(self, field, x):
        here = [field[x, 0], field[x + 1, 0]]
        down = [self.link_z[x + p, -1] * field[x + p, -1] for p in range(2)]
        for z in range(self.side):
            ahead = [field[x, z + 1], field[x + 1, z + 1]]
            outer = [field[x - 1, z], field[x + 2, z]]
            yield z, here, self.flows(x, z, here, ahead, outer, down)
            here = ahead

    def sweep(self, field, out, exact=False):
        def pair(x):
            for z, here, sums in self.rows(field, x):
                for p in range(2):
                    if field is self.base:
                        value = (2.0 - DAMPING) * here[p] + sums[p]
                    else:
                        value = (1.0 - DAMPING) * here[p] + (self.base[x + p, z] + sums[p])
                    out.put(x + p, z, value, exact)

        self.pairs(pair)

    def halve(self, rows, coarse):
        def pair(x):
            held = None
            for z, row in enumerate(rows(x)):
                row = row[0] + row[1]
                if z % 2 == 0:
                    held = row
                else:
                    coarse(x // 2, z // 2, 0.125 * pair_rows(held + row))

        self.pairs(pair)

    def descend(self, coarse):
        self.sweep(self.base, self.second)

        def residuals(x):
            for z, here, sums in self.rows(self.second, x):
                result = []
                for p in range(2):
                    swept = (1.0 - DAMPING) * here[p] + (self.base[x + p, z] + sums[p])
                    self.first[x + p, z] = swept
                    result.append((swept - here[p]) * self.back[x + p, z])
                yield result

        self.halve(residuals, coarse)

    def ascend(self, correction, out, exact=False):
        def pair(x):
            i = x // 2
            here = twice(correction(i, 0))
            start = twice(correction(i, -1))
            down = [self.link_z[x + p, -1] * start for p in range(2)]
            for z in range(self.side):
                ahead = twice(correction(i, (z + 1) // 2))
                outer = [twice(correction(i - 1, z // 2)), twice(correction(i + 1, z // 2))]
                sums = self.flows(x, z, [here, here], [ahead, ahead], outer, down)
                for p in range(2):
                    value = self.first[x + p, z] + ((1.0 - DAMPING) * here + sums[p])
                    self.second.put(x + p, z, value)
                here = ahead

        self.pairs(pair)
        self.sweep(self.second, out, exact)


class HeldLevel:
    def __init__(self, refs, index):
        self.side = 2
        self.scale = 0.25**index
        self.cond, self.first = Edged(refs[0], 2), Edged(refs[1], 2)
        self.weight, self.back = Rows(refs[2], 2), Rows(refs[3], 2)
        self.links = [Rows(ref, 2) for ref in refs[4:]]

    @staticmethod
    def scratch(index):
        sizes = [4**3] * 2 + [2**3] * 8
        return [pltpu.VMEM((size * SIDE, LANES), jnp.float32) for size in sizes]

    def around(self, field, inside=False):
        def moved(row, axis, up):
            row = (block_up if up else block_down)(row, axis)
            return (inside_up if up else inside_down)(row, axis) if inside else row

        result = {}
        for (x, z), here in field.items():
            result[x, z] = [
                field[1, z] if x == 0 else moved(field[0, z], 0, True),
                field[0, z] if x == 1 else moved(field[1, z], 0, False),
                jnp.concatenate([here[1:], moved(here[:1], 1, True)]),
                jnp.concatenate([moved(here[-1:], 1, False), here[:-1]]),
                field[x, 1] if z == 0 else moved(field[x, 0], 2, True),
                field[x, 0] if z == 1 else moved(field[x, 1], 2, False),
            ]
        return result

    def prepare(self):
        field = {(x, z): self.cond[x, z] for x in range(2) for z in range(2)}
        for at, others in self.around(field, inside=True).items():
            here = field[at]
            total = others[0]
            for other in others[1:]:
                total = total + other
            total = 3.0 * here + 0.5 * total
            inverse = DAMPING / total
            self.weight[at] = inverse
            self.back[at] = total * (self.scale / DAMPING)
            for index, other in enumerate(others):
                link = 0.5 * inverse * (here + other)
                self.links[index][at] = jnp.where(other > 0.0, link, 0.0)

    def halve(self, rows, coarse):
        total = None
        for row in rows(0):
            row = row[0] + row[1]
            total = row if total is None else total + row
        coarse(0, 0, 0.125 * (total[:1] + total[1:]))

    def sums(self, field, base):
        result = {}
        for at, others in self.around(field).items():
            total = base[at]
            for link, other in zip(self.links, others):
                total = total + link[at] * other
            result[at] = total
        return result

    def swept(self, field, base):
        sums = self.sums(field, base)
        return {at: (1.0 - DAMPING) * field[at] + sums[at] for at in field}

    def cycle(self, base, solve, out):
        field = self.swept(base, base)
        sums = self.sums(field, base)
        total = None
        for at in field:
            residual = (sums[at] - DAMPING * field[at]) * self.back[at]
            total = residual if total is None else total + residual
        solved = solve(0.125 * (total[:1] + total[1:]))
        row = twice(solved)
        copied = {at: row for at in field}
        change = {at: sums[at] + (1.0 - DAMPING) * (field[at] + row) for at in field}
        field = self.sums(copied, change)
        for (x, z), value in self.swept(field, base).items():
            out.put(x, z, value)


def replicated_kernel(
    whole,
    halved,
    cells_ref,
    *refs,
):
    parts = refs[:whole], refs[whole : whole + halved]
    solve_kernel(*parts, cells_ref, *refs[whole + halved :])


def solve_kernel(
    part_refs,
    half_refs,
    cells_ref,
    spot_ref,
    rows_ref,
    same_ref,
    pairs_ref,
    turned_ref,
    observed_ref,
    potentials_ref,
    mine_ref,
    theirs_ref,
    gathered,
    owned,
    beside,
    sent,
    sem,
    *level_refs,
):
    f32 = jnp.float32
    electrodes = spot_ref.shape[1]
    levels, used = [], 0
    for index in range(LEVELS - 1):
        kind = HeldLevel if index == LEVELS - 2 else Level
        count = len(kind.scratch(index))
        levels.append(kind(level_refs[used : used + count], index))
        used += count
    fine = levels[0]
    forward = fine.cond
    wide = SIDE * SIDE * SIDE

    device, shot = own_place()

    def collect(sources, x):
        held = [
            [part[pl.ds((row * SIDE + z) * SIDE, SIDE), :] for z in range(SIDE)]
            for part, row, _ in sources
        ]
        for rows, (_, _, index) in zip(held, sources):
            for z, row in enumerate(rows):
                start = fine.cond.start(x, z) + (device ^ index)
                fine.cond.ref[pl.ds(start, SIDE, stride=SIDE), :] = row

    for x in range(SIDE):
        collect([(part, x, k) for k, part in enumerate(part_refs)], x)
    for x in range(SIDE // 2):
        for swapped in range(2):
            sources = []
            for k, part in enumerate(half_refs):
                if k // 2 % 2 == swapped:
                    sources.append((part, x, len(part_refs) + k // 4 * 2 + k % 2))
            collect(sources, (shot ^ swapped) * (SIDE // 2) + x)

    def edges(x):
        fine.cond.close_z(x, exact=True)

    for x in range(SIDE):
        edges(x)
    fine.cond.close(exact=True)

    coarsest = []
    for level, below in zip(levels, levels[1:] + [None]):
        level.prepare()

        def coarse(x, z, row, below=below):
            if below is None:
                coarsest.append(row)
            else:
                below.cond.put(x, z, row, exact=True)

        level.halve(
            lambda x, level=level: [
                (level.cond[x, z], level.cond[x + 1, z]) for z in range(level.side)
            ],
            coarse,
        )

    keep = iota((1, SIDE, LANES), 1) % 2 == 0
    lane = iota((1, SIDE, LANES), 2)

    def split(value):
        return [jnp.where(keep, part, 0.0) for part in (value, pltpu.roll(value, SIDE - 1, 1))]

    def around(value):
        low, high = value
        low_up, high_up = [pltpu.roll(part, LANES - GROUP, 2) for part in value]
        low_down, high_down = [pltpu.roll(part, GROUP, 2) for part in value]
        along = [[move(part, axis) for part in value] for axis in (0, 2) for move in (block_up, block_down)]
        return along + [
            [jnp.where(lane < LANES - GROUP, low_up, high_up), high_up],
            [low_down, jnp.where(lane >= GROUP, high_down, low_down)],
        ]

    sub = iota((1, SIDE, LANES), 1)
    inside_last = [
        [sub < 6] * 2,
        [sub >= 2] * 2,
        [lane % GROUP < GROUP - 1] * 2,
        [lane % GROUP > 0] * 2,
        [keep, lane < LANES - GROUP],
        [lane >= GROUP, keep],
    ]
    last_scale = 0.25 ** (LEVELS - 1)
    here = split(coarsest[0])
    others = [
        [jnp.where(inside & keep, part, 0.0) for inside, part in zip(pair, moved)]
        for pair, moved in zip(inside_last, around(here))
    ]
    last_weight, last_links = [], []
    for half, part in enumerate(here):
        total = 3.0 * part
        for other in others:
            total = total + 0.5 * other[half]
        inverse = jnp.where(keep, DAMPING / jnp.where(keep, total, 1.0), 0.0)
        last_weight.append(inverse * (1.0 / last_scale))
        last_links.append(
            [
                jnp.where(pair[half] & keep, 0.5 * inverse * (part + other[half]), 0.0)
                for pair, other in zip(inside_last, others)
            ]
        )

    def solve_last(rhs):
        base = [weight * part for weight, part in zip(last_weight, split(rhs))]
        value = base
        for _ in range(COARSE_SWEEPS - 1):
            moved = around(value)
            fresh = []
            for half in range(2):
                parts = [link * other[half] for link, other in zip(last_links[half], moved)]
                start = base[half] + (1.0 - DAMPING) * value[half]
                fresh.append(((start + parts[0]) + (parts[1] + parts[2])) + (parts[3] + (parts[4] + parts[5])))
            value = fresh
        return value[0] + pltpu.roll(value[1], 1, 1)

    def cycle(index, out, exact=False):
        level = levels[index]
        below = levels[index + 1]
        if index == LEVELS - 3:
            base = {}

            def take(x, z, row):
                base[x, z] = below.weight[x, z] * (row * (1.0 / below.scale))

            level.descend(take)
            below.cycle(base, solve_last, below.first)
        else:
            level.descend(
                lambda x, z, row: below.base.put(
                    x, z, below.weight[x, z] * (row * (2.0 / below.scale))
                )
            )
            cycle(index + 1, below.first)
        level.ascend(lambda x, z: below.first[x, z], out, exact)

    spot = spot_ref[...]
    at_spot = iota((LANES, electrodes), 0) == spot
    order = lane_order(back=True)
    wide = SIDE + 2
    sending = pltpu.make_async_copy(sent, potentials_ref, sem)

    batch = 32

    def each(load, store):
        def one(group, carry):
            first = group * batch
            cells = [pl.ds(cells_ref[0, first + k], 1) for k in range(batch)]
            rows = [load(pl.ds(first + k, 1), cell) for k, cell in enumerate(cells)]
            for k, (cell, row) in enumerate(zip(cells, rows)):
                store(pl.ds(first + k, 1), cell, row)
            return carry

        lax.fori_loop(0, electrodes // batch, one, 0, unroll=2)

    def source_row(electrode, cell):
        return gathered[electrode, :] * fine.weight.ref[cell, :]

    def put(electrode, cell, row):
        fine.base.ref[cell, :] = row

    def read(electrode, cell):
        return forward.ref[cell, :]

    def keep_row(electrode, cell, row):
        gathered[electrode, :] = row

    def exact(row, matrix_ref):
        return product(jnp.broadcast_to(row, (16, row.shape[1])), matrix_ref[...], 3)[0:1]

    sub, lane = iota((SIDE, LANES), 0), iota((SIDE, LANES), 1)

    def margin(x, z, y):
        return forward.ref[pl.ds(forward.start(x, z, y) + device, 1), :]

    def extract(index):
        for x in range(-1, SIDE + 1):
            inner = 0 <= x < SIDE
            starts = [forward.start(x, z) + device for z in range(SIDE)]
            rows = [forward.ref[pl.ds(start, SIDE, stride=SIDE), :] for start in starts]
            if inner:
                after = [margin(x, z, SIDE) for z in range(SIDE)]
                before = [margin(x, z, -1) for z in range(SIDE)]
            for z, row in enumerate(rows):
                at = (x + 1) * wide + z + 1
                owned[index, at] = row
                if not inner:
                    continue
                place = x * SIDE + z
                turned = pltpu.roll(row, SIDE - 1, 0)
                beside[index, 0, place] = jnp.where(sub == SIDE - 1, after[z], turned)
                beside[index, 1, place] = jnp.where(sub == 0, before[z], pltpu.roll(row, 1, 0))
                if z == 0:
                    edge = pltpu.roll(row, LANES - 1, 1)
                    owned[index, at + SIDE] = jnp.where(lane % GROUP < GROUP - 1, edge, 0.0)
                if z == SIDE - 1:
                    edge = pltpu.roll(row, 1, 1)
                    owned[index, at - SIDE] = jnp.where(lane % GROUP > 0, edge, 0.0)

    def solve(index):
        each(source_row, put)
        for x in range(SIDE):
            fine.base.close_z(x)
        fine.base.close()
        cycle(0, forward, exact=True)
        extract(index)

        @pl.when(index == 0)
        def _():
            for x in range(SIDE):
                tiles = [owned[0, (x + 1) * wide + z + 1] for z in range(SIDE)]
                sent[x] = from_blocks(tiles, order)
            sending.start()
            each(read, keep_row)
            readings = jnp.where(at_spot, gathered[...].T, 0.0)
            readings = jnp.sum(readings, axis=0, keepdims=True)
            misfit = exact(readings, turned_ref) - observed_ref[...]
            gathered[...] = 2.0 * shared_rows(exact(misfit, pairs_ref), spot, same_ref[...])

    gathered[...] = 2.0 * rows_ref[...]
    rolled(2, solve)

    chunk = mine_ref.shape[1]
    even = shot == 0
    for x in range(SIDE):
        tiles = []
        for z in range(SIDE):
            at = (x + 1) * wide + z + 1
            here_u, here_w = owned[0, at], owned[1, at]
            total = None
            for step in (wide, -wide, 1, -1):
                term = (here_u - owned[0, at + step]) * (here_w - owned[1, at + step])
                total = term if total is None else total + term
            for side in range(2):
                other_u, other_w = beside[0, side, x * SIDE + z], beside[1, side, x * SIDE + z]
                total = total + (here_u - other_u) * (here_w - other_w)
            tiles.append(-0.5 * total)
        natural = from_blocks(tiles, order)
        low, high = natural[:chunk], natural[chunk:]
        mine_ref[x] = jnp.where(even, low, high)
        theirs_ref[x] = jnp.where(even, high, low)
    sending.wait()


def replicated(conductivity, stations, currents, receivers, observed):
    rows, cols, depth = conductivity.shape
    f32 = jnp.float32
    electrodes = stations.shape[0]
    total = rows * cols
    vmem = pl.BlockSpec(memory_space=pltpu.VMEM)
    smem = pl.BlockSpec(memory_space=pltpu.SMEM)
    station_row = stations.reshape(1, electrodes)
    mine, half = pl.pallas_call(
        to_blocks_kernel,
        out_shape=(
            jax.ShapeDtypeStruct((total, LANES), f32),
            jax.ShapeDtypeStruct((total // 2, LANES), f32),
        ),
        in_specs=[vmem],
        out_specs=(vmem, vmem),
        compiler_params=pltpu.CompilerParams(vmem_limit_bytes=SMALL_BYTES),
    )(conductivity)
    swap = [(0, 1), (1, 0)]

    def partner(part, k):
        count = lax.axis_size("gx")
        return lax.ppermute(part, "gx", [(i, i ^ k) for i in range(count)])

    def with_mate(part):
        return [part, lax.ppermute(part, "gy", swap)]

    far = partner(half, 2)
    near = partner(mine, 1)
    line = jax.ShapeDtypeStruct((1, electrodes), jnp.int32)
    cells, spot, rows_of, same, pairs, turned, held = pl.pallas_call(
        electrode_kernel,
        out_shape=(
            line,
            line,
            jax.ShapeDtypeStruct((electrodes, LANES), f32),
            jax.ShapeDtypeStruct((electrodes, electrodes), jnp.bfloat16),
            jax.ShapeDtypeStruct((receivers.shape[0], electrodes), jnp.bfloat16),
            jax.ShapeDtypeStruct((electrodes, receivers.shape[0]), jnp.bfloat16),
            jax.ShapeDtypeStruct(observed.shape, f32),
        ),
        in_specs=[vmem] * 4,
        out_specs=(vmem,) * 7,
        compiler_params=pltpu.CompilerParams(vmem_limit_bytes=SMALL_BYTES),
        cost_estimate=pl.CostEstimate(flops=100_000_000, bytes_accessed=1_000_000, transcendentals=0),
    )(station_row, currents, receivers, observed)
    far, rows_of = lax.optimization_barrier((far, rows_of))
    far = [far, lax.ppermute(far, "shot", swap)]
    halved = far + [partner(piece, 1) for piece in far]
    parts = [piece for own in (mine, near) for piece in with_mate(own)]
    halved = [piece for own in halved for piece in with_mate(own)]
    chunk = cols // 2
    levels = [shape for index in range(LEVELS - 2) for shape in Level.scratch(index)]
    levels += HeldLevel.scratch(LEVELS - 2)
    potentials, own, theirs = pl.pallas_call(
        functools.partial(replicated_kernel, len(parts), len(halved)),
        out_shape=(
            jax.ShapeDtypeStruct((rows, cols, LANES), f32),
            jax.ShapeDtypeStruct((rows, chunk, LANES), f32),
            jax.ShapeDtypeStruct((rows, chunk, LANES), f32),
        ),
        in_specs=[smem] + [vmem] * (len(parts) + len(halved) + 6),
        out_specs=(pl.BlockSpec(memory_space=pl.ANY), vmem, vmem),
        scratch_shapes=[
            pltpu.VMEM((electrodes, LANES), f32),
            pltpu.VMEM((2, (SIDE + 2) ** 2, SIDE, LANES), f32),
            pltpu.VMEM((2, 2, SIDE**2, SIDE, LANES), f32),
            pltpu.VMEM((rows, cols, LANES), f32),
            pltpu.SemaphoreType.DMA,
        ]
        + levels,
        compiler_params=pltpu.CompilerParams(vmem_limit_bytes=VMEM_BYTES),
        cost_estimate=pl.CostEstimate(flops=200_000_000, bytes_accessed=4_000_000, transcendentals=0),
    )(cells, *parts, *halved, spot, rows_of, same, pairs, turned, held)
    return potentials[None], own + lax.ppermute(theirs, "shot", swap)


def extended(array, sides, width):
    for axis, dim in sides:
        size, length = (lax.axis_size(axis), array.shape[dim])
        up = [(i, (i + 1) % size) for i in range(size - 1)]
        down = [(j, i) for i, j in up]
        last = lax.slice_in_dim(array, length - width, length, axis=dim)
        leading = lax.slice_in_dim(array, 0, width, axis=dim)
        before = lax.ppermute(last, axis, up)
        after = lax.ppermute(leading, axis, down)
        array = jnp.concatenate([before, array, after], axis=dim)
    return array


def upper_z(field):
    return jnp.concatenate([field[..., 1:], jnp.zeros_like(field[..., :1])], axis=-1)


def lower_z(field):
    return jnp.concatenate([jnp.zeros_like(field[..., :1]), field[..., :-1]], axis=-1)


def trim_circle(field, circle_width):
    return field[..., circle_width:-circle_width, circle_width:-circle_width, :]


def pad_plane(field, circle_width):
    spec = [(0, 0)] * (field.ndim - 3) + [
        (circle_width, circle_width),
        (circle_width, circle_width),
        (0, 0),
    ]
    return jnp.pad(field, spec)


def neighbour_list(field_pad):
    centre = trim_circle(field_pad, 1)
    return [
        field_pad[..., 2:, 1:-1, :],
        field_pad[..., :-2, 1:-1, :],
        field_pad[..., 1:-1, 2:, :],
        field_pad[..., 1:-1, :-2, :],
        upper_z(centre),
        lower_z(centre),
    ]


def stencil(field_pad, cond_pad, level_scale):
    centre = trim_circle(field_pad, 1)
    centre_cond = trim_circle(cond_pad, 1)
    summed = jnp.zeros_like(centre)
    for other, other_cond in zip(neighbour_list(field_pad), neighbour_list(cond_pad)):
        summed = summed + level_scale * 0.5 * (centre_cond + other_cond) * (centre - other)
    return summed


def diagonal(cond_pad, level_scale):
    centre_cond = trim_circle(cond_pad, 1)
    summed = jnp.zeros_like(centre_cond)
    for other_cond in neighbour_list(cond_pad):
        summed = summed + level_scale * 0.5 * (centre_cond + other_cond)
    return summed


def relaxed(field_pad, source, cond_pad, diag_level, level_scale):
    return (
        trim_circle(field_pad, 1)
        + DAMPING * (source - stencil(field_pad, cond_pad, level_scale)) / diag_level
    )


def restrict(field):
    leading = field.shape[:-3]
    extent = field.shape[-3:]
    shaped = field.reshape(leading + (extent[0] // 2, 2, extent[1] // 2, 2, extent[2] // 2, 2))
    return shaped.mean(axis=(-5, -3, -1))


def prolong(field):
    return jnp.repeat(jnp.repeat(jnp.repeat(field, 2, axis=-3), 2, axis=-2), 2, axis=-1)


def assemble(blocks, count_x, count_y):
    leading = blocks.shape[1:-3]
    extent = blocks.shape[-3:]
    depth_lead = len(leading)
    shaped = blocks.reshape((count_x, count_y) + leading + extent)
    order = tuple(range(2, 2 + depth_lead)) + (0, 2 + depth_lead, 1, 3 + depth_lead, 4 + depth_lead)
    return shaped.transpose(order).reshape(
        leading + (count_x * extent[0], count_y * extent[1], extent[2])
    )


def field_rim(field):
    return extended(field, (("gx", 1), ("gy", 2)), 1)


def cond_rim(conduct):
    return extended(conduct, (("gx", 0), ("gy", 1)), 1)


def whole_cycle(source, level_index, whole_plans):
    cond_pad, diag_level, level_scale = whole_plans[level_index]
    field = DAMPING * source / diag_level

    def turn(turn_index, iterate):
        return relaxed(pad_plane(iterate, 1), source, cond_pad, diag_level, level_scale)

    return lax.fori_loop(0, COARSE_SWEEPS - 1, turn, field)


def part_cycle(source, level_index, level_plans, whole_plans, gather_level):
    if level_index == gather_level:
        blocks = lax.all_gather(source[None], ("gx", "gy"), axis=0, tiled=True)
        whole = assemble(blocks, lax.axis_size("gx"), lax.axis_size("gy"))
        correction = whole_cycle(whole, level_index, whole_plans)
        extent = source.shape
        starts = (0, lax.axis_index("gx") * extent[1], lax.axis_index("gy") * extent[2], 0)
        return lax.dynamic_slice(correction, starts, extent)
    cond_pad, diag_level, level_scale = level_plans[level_index]
    field = DAMPING * source / diag_level
    field = relaxed(field_rim(field), source, cond_pad, diag_level, level_scale)
    residual = source - stencil(field_rim(field), cond_pad, level_scale)
    field = field + prolong(
        part_cycle(restrict(residual), level_index + 1, level_plans, whole_plans, gather_level)
    )
    field = relaxed(field_rim(field), source, cond_pad, diag_level, level_scale)
    return relaxed(field_rim(field), source, cond_pad, diag_level, level_scale)


def distributed(conductivity, stations, currents, receivers, observed):
    row_count, col_count, z_count = conductivity.shape
    shot_count = currents.shape[0]
    count_x = lax.axis_size("gx")
    count_y = lax.axis_size("gy")
    gather_level = LEVELS - 1
    level_plans = []
    conduct = conductivity
    for level_index in range(gather_level):
        level_scale = 0.25**level_index
        cond_pad = cond_rim(conduct)
        level_plans.append((cond_pad, diagonal(cond_pad, level_scale), level_scale))
        conduct = restrict(conduct)
    blocks = lax.all_gather(conduct[None], ("gx", "gy"), axis=0, tiled=True)
    whole = assemble(blocks, count_x, count_y)
    whole_plans = {}
    level_index = 3
    level_scale = 0.25**level_index
    cond_pad = pad_plane(whole, 1)
    whole_plans[level_index] = (cond_pad, diagonal(cond_pad, level_scale), level_scale)
    total_y = col_count * count_y
    cell_x = stations // (total_y * z_count)
    cell_y = stations // z_count % total_y
    cell_z = stations % z_count
    local_x = cell_x - lax.axis_index("gx") * row_count
    local_y = cell_y - lax.axis_index("gy") * col_count
    owned = (local_x >= 0) & (local_x < row_count) & (local_y >= 0) & (local_y < col_count)
    block_size = row_count * col_count * z_count
    local_cell = jnp.where(owned, (local_x * col_count + local_y) * z_count + cell_z, 0)
    offsets = jnp.arange(shot_count)[:, None] * block_size + local_cell[None, :]
    targets = jnp.where(owned[None, :], offsets, shot_count * block_size).reshape(-1)

    def spread(amounts):
        flat = (
            jnp.zeros((shot_count * block_size,), jnp.float32)
            .at[targets]
            .add(amounts.reshape(-1), mode="drop")
        )
        return flat.reshape(shot_count, row_count, col_count, z_count)

    potentials = part_cycle(spread(currents), 0, level_plans, whole_plans, gather_level)
    local_values = jnp.where(
        owned[None, :], potentials.reshape(shot_count, block_size)[:, local_cell], 0.0
    )
    readings = lax.psum(local_values, ("gx", "gy"))
    positions = jnp.arange(stations.shape[0])[:, None]
    pairs = (receivers[:, 0][None, :] == positions).astype(jnp.float32) - (
        receivers[:, 1][None, :] == positions
    ).astype(jnp.float32)
    misfit = jnp.dot(readings, pairs, precision=lax.Precision.HIGHEST) - observed
    back_source = jnp.dot(misfit, pairs.T, precision=lax.Precision.HIGHEST)
    adjoint = part_cycle(spread(back_source), 0, level_plans, whole_plans, gather_level)
    stacked = jnp.concatenate([potentials, adjoint], axis=0)
    padded = extended(stacked, (("gx", 1), ("gy", 2)), 1)
    potential_pad = padded[:shot_count]
    adjoint_pad = padded[shot_count:]
    gradient = jnp.zeros_like(potentials)
    for other_u, other_w in zip(neighbour_list(potential_pad), neighbour_list(adjoint_pad)):
        gradient = gradient - 0.5 * (potentials - other_u) * (adjoint - other_w)
    summed = lax.psum_scatter(jnp.sum(gradient, axis=0), "shot", scatter_dimension=1, tiled=True)
    return (potentials, summed)


def per_device(conductivity, stations, currents, receivers, observed):
    blocks = lax.axis_size("gx") * lax.axis_size("gy")
    fits = conductivity.shape == (SIDE, SIDE * SIDE, LANES) and blocks == SIDE
    fits = fits and lax.axis_size("gy") == 2 and lax.axis_size("shot") == 2
    fits = fits and currents.shape[0] == 1
    plan = replicated if fits else distributed
    return plan(conductivity, stations, currents, receivers, observed)


def solution(mesh):
    in_specs = (
        P(("grp", "gx"), "gy", None),
        P("grp"),
        P(("grp", "shot"), None),
        P("grp", None),
        P(("grp", "shot"), None),
    )
    out_specs = (P(("grp", "shot"), "gx", "gy", None), P(("grp", "gx"), ("gy", "shot"), None))
    return jax.shard_map(
        per_device, mesh=mesh, in_specs=in_specs, out_specs=out_specs, check_vma=False
    )
```

```python
import functools

import jax
import jax.numpy as jnp
from jax import lax
from jax.experimental import pallas as pl
from jax.experimental.pallas import tpu as pltpu
from jax.sharding import PartitionSpec as P

LEVELS = 4
COARSE_SWEEPS = 16


DAMPING = 0.8

SIDE = 8
LANES = 128
GROUP = 16
VMEM_BYTES = 48 * 2**20
SMALL_BYTES = 6 * 2**20


def pieces_of(value, count):
    pieces = []
    for _ in range(count):
        pieces.append(value.astype(jnp.bfloat16))
        value = value - pieces[-1].astype(jnp.float32)
    return pieces[::-1]


def product(value, matrix, count, dims=((1,), (0,))):
    result = None
    for piece in pieces_of(value, count):
        term = lax.dot_general(
            piece, matrix, (dims, ((), ())), preferred_element_type=jnp.float32
        )
        result = term if result is None else result + term
    return result


def iota(shape, dim):
    return lax.broadcasted_iota(jnp.int32, shape, dim)


def station_table(station):
    cell_x, cell_y, cell_z = station >> 14, station >> 7 & 127, station & 127
    row = (cell_x >> 3) * 2 + (cell_y >> 6)
    return cell_x, cell_y, cell_z, row, (cell_y >> 3 & 7) * GROUP + (cell_z >> 3)


def lane_order(back=False):
    row, col = iota((LANES, LANES), 0), iota((LANES, LANES), 1)
    if back:
        row, col = col, row
    chosen = row == col % GROUP * SIDE + col // GROUP
    return jnp.where(chosen, 1.0, 0.0).astype(jnp.bfloat16)


def exchange_groups(tiles):
    tiles = list(tiles)
    group = iota(tiles[0].shape, 1) // GROUP
    for bit in range(3):
        step = 1 << bit
        keep = (group & step) == 0
        for low in range(SIDE):
            if low & step == 0:
                a, b = tiles[low], tiles[low | step]
                tiles[low] = jnp.where(keep, a, pltpu.roll(b, step * GROUP, 1))
                tiles[low | step] = jnp.where(keep, pltpu.roll(a, LANES - step * GROUP, 1), b)
    return tiles


def own_place():
    return lax.axis_index("gx") * 2 + lax.axis_index("gy"), lax.axis_index("shot")


def to_blocks_kernel(natural_ref, blocks_ref, half_ref):
    order = lane_order()
    for x in range(SIDE):
        tiles = product(natural_ref[x], order, 3)
        tiles = [tiles[SIDE * k : SIDE * (k + 1)] for k in range(SIDE)]
        for z, tile in enumerate(exchange_groups(tiles)):
            blocks_ref[pl.ds((x * SIDE + z) * SIDE, SIDE), :] = tile
    count = half_ref.shape[0]
    low, high = blocks_ref[pl.ds(0, count), :], blocks_ref[pl.ds(count, count), :]
    half_ref[...] = jnp.where(own_place()[1] == 0, low, high)


def from_blocks(tiles, order):
    natural = jnp.concatenate(exchange_groups(tiles), axis=0)
    return product(natural, order, 3)


def potentials_kernel(rows_ref, potentials_ref):
    order = lane_order(back=True)
    for x in range(SIDE):
        tiles = [rows_ref[pl.ds((x * SIDE + z) * SIDE, SIDE), :] for z in range(SIDE)]
        potentials_ref[x] = from_blocks(tiles, order)


def block_up(field, axis):
    if axis == 0:
        return pltpu.roll(field, 6, 1)
    if axis == 2:
        return pltpu.roll(field, LANES - 1, 2)
    turned = pltpu.roll(field, LANES - GROUP, 2)
    return jnp.where(iota(field.shape, 2) < LANES - GROUP, turned, pltpu.roll(turned, 7, 1))


def block_down(field, axis):
    if axis == 0:
        return pltpu.roll(field, 2, 1)
    if axis == 2:
        return pltpu.roll(field, 1, 2)
    turned = pltpu.roll(field, GROUP, 2)
    return jnp.where(iota(field.shape, 2) >= GROUP, turned, pltpu.roll(turned, 1, 1))


def inside_up(field, axis):
    sub, lane = iota(field.shape, 1), iota(field.shape, 2)
    if axis == 0:
        keep = sub < 6
    elif axis == 1:
        keep = (lane < LANES - GROUP) | (sub % 2 == 0)
    else:
        keep = lane % GROUP < GROUP - 1
    return jnp.where(keep, field, 0.0)


def inside_down(field, axis):
    sub, lane = iota(field.shape, 1), iota(field.shape, 2)
    if axis == 0:
        keep = sub >= 2
    elif axis == 1:
        keep = (lane >= GROUP) | (sub % 2 == 1)
    else:
        keep = lane % GROUP > 0
    return jnp.where(keep, field, 0.0)


def pair_rows(row):
    count = row.shape[0] // 2
    return jnp.concatenate([row[2 * i : 2 * i + 1] + row[2 * i + 1 : 2 * i + 2] for i in range(count)])


def twice(row):
    return jnp.concatenate([row[i // 2 : i // 2 + 1] for i in range(2 * row.shape[0])])


def electrode_kernel(
    stations_ref,
    currents_ref,
    receivers_ref,
    observed_ref,
    cells_ref,
    spot_ref,
    rows_ref,
    same_ref,
    pairs_ref,
    turned_ref,
    held_ref,
):
    stations = stations_ref[...]
    electrodes = stations.shape[1]
    cell_x, cell_y, cell_z, row, spot = station_table(stations)
    wide = SIDE + 2
    register = (((cell_x & 7) + 1) * wide + (cell_z & 7) + 1) * wide + (cell_y & 7) + 1
    cells_ref[...] = register * SIDE + row
    spot_ref[...] = spot
    held_ref[...] = observed_ref[...]
    line = stations & 0x1C387 | row << 20
    same = jnp.broadcast_to(line, (electrodes, electrodes))
    same = jnp.where(same == same.T, 1.0, 0.0).astype(jnp.bfloat16)
    same_ref[...] = same
    rows_ref[...] = shared_rows(currents_ref[...], spot, same)
    receivers = receivers_ref[...]
    numbers = iota((receivers.shape[0], electrodes), 1)
    pairs = jnp.where(numbers == receivers[:, 0:1], 1.0, 0.0) - jnp.where(
        numbers == receivers[:, 1:2], 1.0, 0.0
    )
    pairs_ref[...] = pairs.astype(jnp.bfloat16)
    turned_ref[...] = pairs.T.astype(jnp.bfloat16)


def shared_rows(amounts, spot, same):
    electrodes = amounts.shape[1]
    at_spot = iota((LANES, electrodes), 0) == spot
    return product(jnp.where(at_spot, amounts, 0.0), same, 3).T


class Edged:
    def __init__(self, ref, side):
        self.ref, self.side = ref, side

    def start(self, x, z, y=0):
        wide = self.side + 2
        return (((x + 1) * wide + z + 1) * wide + y + 1) * SIDE

    def __getitem__(self, at):
        x, z = at
        rows = self.ref[pl.ds(self.start(x, z), self.side * SIDE), :]
        return rows.reshape(self.side, SIDE, LANES)

    def __setitem__(self, at, value):
        x, z = at
        self.ref[pl.ds(self.start(x, z), self.side * SIDE), :] = value.reshape(-1, LANES)

    def put(self, x, z, value, exact=False):
        self[x, z] = value
        n = self.side
        if z == 0:
            edge = block_up(value, 2)
            self[x, n] = inside_up(edge, 2) if exact else edge
        if z == n - 1:
            edge = block_down(value, 2)
            self[x, -1] = inside_down(edge, 2) if exact else edge
        if x == 0:
            edge = block_up(value, 0)
            self[n, z] = inside_up(edge, 0) if exact else edge
        if x == n - 1:
            edge = block_down(value, 0)
            self[-1, z] = inside_down(edge, 0) if exact else edge
        if exact:
            after = inside_up(block_up(value[:1], 1), 1)
            self.ref[pl.ds(self.start(x, z, n), SIDE), :] = after[0]
            before = inside_down(block_down(value[n - 1 :], 1), 1)
            self.ref[pl.ds(self.start(x, z, -1), SIDE), :] = before[0]

    def close_z(self, x, exact=False):
        n = self.side
        after, before = block_up(self[x, 0], 2), block_down(self[x, n - 1], 2)
        self[x, n] = inside_up(after, 2) if exact else after
        self[x, -1] = inside_down(before, 2) if exact else before

    def close(self, exact=False):
        n = self.side
        for z in range(n):
            after = block_up(self[0, z], 0)
            self[n, z] = inside_up(after, 0) if exact else after
            before = block_down(self[n - 1, z], 0)
            self[-1, z] = inside_down(before, 0) if exact else before


class Rows:
    def __init__(self, ref, side, first_x=0, first_z=0):
        self.ref, self.side, self.first_x, self.first_z = ref, side, first_x, first_z

    def place(self, at):
        count = self.side - self.first_z
        rows = self.side * SIDE
        return pl.ds(((at[0] - self.first_x) * count + at[1] - self.first_z) * rows, rows)

    def __getitem__(self, at):
        return self.ref[self.place(at), :].reshape(self.side, SIDE, LANES)

    def __setitem__(self, at, value):
        self.ref[self.place(at), :] = value.reshape(-1, LANES)


def rolled(count, body, unroll=1):
    def one(x, carry):
        body(x)
        return carry

    lax.fori_loop(0, count, one, 0, unroll=unroll)


def next_in_y(row):
    return jnp.concatenate([row[1:], block_up(row[:1], 1)])


def last_in_y(row):
    return jnp.concatenate([block_down(row[-1:], 1), row[:-1]])


class Level:
    def __init__(self, refs, index):
        self.side = side = SIDE >> index
        self.scale = 0.25**index
        edged = [Edged(ref, side) for ref in refs[:5]]
        self.cond, self.first, self.second, self.base, self.weight = edged
        self.link_x = Rows(refs[5], side, first_x=-1)
        self.link_y = Rows(refs[6], side)
        self.link_z = Rows(refs[7], side, first_z=-1)
        self.back = Rows(refs[8], side)

    @staticmethod
    def scratch(index):
        side = SIDE >> index
        sizes = [(side + 2) ** 3] * 5
        sizes += [side**2 * (side + 1), side**3, side**2 * (side + 1), side**3]
        return [pltpu.VMEM((size * SIDE, LANES), jnp.float32) for size in sizes]

    def pairs(self, body):
        for i in range(self.side // 2):
            body(2 * i)

    def prepare(self):
        n = self.side
        cond = self.cond

        def plane(x):
            for z in range(n):
                here, ahead, next_x = cond[x, z], cond[x, z + 1], cond[x + 1, z]
                after = inside_up(block_up(here[:1], 1), 1)
                before = inside_down(block_down(here[-1:], 1), 1)
                next_y = jnp.concatenate([here[1:], after])
                last_y = jnp.concatenate([before, here[:-1]])
                total = (next_x + cond[x - 1, z]) + (ahead + cond[x, z - 1]) + (next_y + last_y)
                total = 6.0 * here + total
                self.weight[x, z] = DAMPING / total
                if n == SIDE:
                    self.base[x, z] = jnp.zeros_like(here)
                self.back[x, z] = total * (0.5 * self.scale / DAMPING)
                self.link_x[x, z] = here + next_x
                link = here + next_y
                self.link_y[x, z] = jnp.concatenate([link[:-1], inside_up(link[-1:], 1)])
                link = here + ahead
                if z == n - 1:
                    link = inside_up(link, 2)
                    self.link_z[x, -1] = block_down(link, 2)
                self.link_z[x, z] = link

        if n == SIDE:
            rolled(n, plane, unroll=2)
        else:
            for x in range(n):
                plane(x)
        for z in range(n):
            link = inside_up(self.link_x[n - 1, z], 0)
            self.link_x[n - 1, z] = link
            self.link_x[-1, z] = block_down(link, 0)

    def flows(self, x, z, here, ahead, outer, down):
        result = []
        inner = self.link_x[x, z]
        sides = [
            self.link_x[x - 1, z] * outer[0] + inner * here[1],
            inner * here[0] + self.link_x[x + 1, z] * outer[1],
        ]
        for p in range(2):
            link_y, link_z = self.link_y[x + p, z], self.link_z[x + p, z]
            along = link_y * next_in_y(here[p]) + last_in_y(link_y * here[p])
            total = sides[p] + (link_z * ahead[p] + down[p]) + along
            down[p] = link_z * here[p]
            result.append(self.weight[x + p, z] * total)
        return result

    def rows(self, field, x):
        here = [field[x, 0], field[x + 1, 0]]
        down = [self.link_z[x + p, -1] * field[x + p, -1] for p in range(2)]
        for z in range(self.side):
            ahead = [field[x, z + 1], field[x + 1, z + 1]]
            outer = [field[x - 1, z], field[x + 2, z]]
            yield z, here, self.flows(x, z, here, ahead, outer, down)
            here = ahead

    def sweep(self, field, out, exact=False):
        def pair(x):
            for z, here, sums in self.rows(field, x):
                for p in range(2):
                    if field is self.base:
                        value = (2.0 - DAMPING) * here[p] + sums[p]
                    else:
                        value = (1.0 - DAMPING) * here[p] + (self.base[x + p, z] + sums[p])
                    out.put(x + p, z, value, exact)

        self.pairs(pair)

    def halve(self, rows, coarse):
        def pair(x):
            held = None
            for z, row in enumerate(rows(x)):
                row = row[0] + row[1]
                if z % 2 == 0:
                    held = row
                else:
                    coarse(x // 2, z // 2, 0.125 * pair_rows(held + row))

        self.pairs(pair)

    def descend(self, coarse):
        self.sweep(self.base, self.second)

        def residuals(x):
            for z, here, sums in self.rows(self.second, x):
                result = []
                for p in range(2):
                    swept = (1.0 - DAMPING) * here[p] + (self.base[x + p, z] + sums[p])
                    self.first[x + p, z] = swept
                    result.append((swept - here[p]) * self.back[x + p, z])
                yield result

        self.halve(residuals, coarse)

    def ascend(self, correction, out, exact=False):
        def pair(x):
            i = x // 2
            here = twice(correction(i, 0))
            start = twice(correction(i, -1))
            down = [self.link_z[x + p, -1] * start for p in range(2)]
            for z in range(self.side):
                ahead = twice(correction(i, (z + 1) // 2))
                outer = [twice(correction(i - 1, z // 2)), twice(correction(i + 1, z // 2))]
                sums = self.flows(x, z, [here, here], [ahead, ahead], outer, down)
                for p in range(2):
                    value = self.first[x + p, z] + ((1.0 - DAMPING) * here + sums[p])
                    self.second.put(x + p, z, value)
                here = ahead

        self.pairs(pair)
        self.sweep(self.second, out, exact)


class HeldLevel:
    def __init__(self, refs, index):
        self.side = 2
        self.scale = 0.25**index
        self.cond, self.first = Edged(refs[0], 2), Edged(refs[1], 2)
        self.weight, self.back = Rows(refs[2], 2), Rows(refs[3], 2)
        self.links = [Rows(ref, 2) for ref in refs[4:]]

    @staticmethod
    def scratch(index):
        sizes = [4**3] * 2 + [2**3] * 8
        return [pltpu.VMEM((size * SIDE, LANES), jnp.float32) for size in sizes]

    def around(self, field, inside=False):
        def moved(row, axis, up):
            row = (block_up if up else block_down)(row, axis)
            return (inside_up if up else inside_down)(row, axis) if inside else row

        result = {}
        for (x, z), here in field.items():
            result[x, z] = [
                field[1, z] if x == 0 else moved(field[0, z], 0, True),
                field[0, z] if x == 1 else moved(field[1, z], 0, False),
                jnp.concatenate([here[1:], moved(here[:1], 1, True)]),
                jnp.concatenate([moved(here[-1:], 1, False), here[:-1]]),
                field[x, 1] if z == 0 else moved(field[x, 0], 2, True),
                field[x, 0] if z == 1 else moved(field[x, 1], 2, False),
            ]
        return result

    def prepare(self):
        field = {(x, z): self.cond[x, z] for x in range(2) for z in range(2)}
        for at, others in self.around(field, inside=True).items():
            here = field[at]
            total = others[0]
            for other in others[1:]:
                total = total + other
            total = 3.0 * here + 0.5 * total
            inverse = DAMPING / total
            self.weight[at] = inverse
            self.back[at] = total * (self.scale / DAMPING)
            for index, other in enumerate(others):
                link = 0.5 * inverse * (here + other)
                self.links[index][at] = jnp.where(other > 0.0, link, 0.0)

    def halve(self, rows, coarse):
        total = None
        for row in rows(0):
            row = row[0] + row[1]
            total = row if total is None else total + row
        coarse(0, 0, 0.125 * (total[:1] + total[1:]))

    def sums(self, field, base):
        result = {}
        for at, others in self.around(field).items():
            total = base[at]
            for link, other in zip(self.links, others):
                total = total + link[at] * other
            result[at] = total
        return result

    def swept(self, field, base):
        sums = self.sums(field, base)
        return {at: (1.0 - DAMPING) * field[at] + sums[at] for at in field}

    def cycle(self, base, solve, out):
        field = self.swept(base, base)
        sums = self.sums(field, base)
        total = None
        for at in field:
            residual = (sums[at] - DAMPING * field[at]) * self.back[at]
            total = residual if total is None else total + residual
        solved = solve(0.125 * (total[:1] + total[1:]))
        row = twice(solved)
        copied = {at: row for at in field}
        change = {at: sums[at] + (1.0 - DAMPING) * (field[at] + row) for at in field}
        field = self.sums(copied, change)
        for (x, z), value in self.swept(field, base).items():
            out.put(x, z, value)


def replicated_kernel(
    whole,
    halved,
    cells_ref,
    *refs,
):
    parts = refs[:whole], refs[whole : whole + halved]
    solve_kernel(*parts, cells_ref, *refs[whole + halved :])


def solve_kernel(
    part_refs,
    half_refs,
    cells_ref,
    spot_ref,
    rows_ref,
    same_ref,
    pairs_ref,
    turned_ref,
    observed_ref,
    potentials_ref,
    mine_ref,
    theirs_ref,
    gathered,
    owned,
    beside,
    *level_refs,
):
    f32 = jnp.float32
    electrodes = spot_ref.shape[1]
    levels, used = [], 0
    for index in range(LEVELS - 1):
        kind = HeldLevel if index == LEVELS - 2 else Level
        count = len(kind.scratch(index))
        levels.append(kind(level_refs[used : used + count], index))
        used += count
    fine = levels[0]
    forward = fine.cond
    wide = SIDE * SIDE * SIDE

    device, shot = own_place()

    def place(part, row, x, index):
        for z in range(SIDE):
            fine.cond.ref[pl.ds(fine.cond.start(x, z) + index, SIDE, stride=SIDE), :] = part[
                pl.ds((row * SIDE + z) * SIDE, SIDE), :
            ]

    def collect(x):
        for k, part in enumerate(part_refs):
            place(part, x, x, device ^ k)

    def collect_half(x):
        for k, part in enumerate(half_refs):
            swapped, index = k // 2 % 2, len(part_refs) + k // 4 * 2 + k % 2
            place(part, x, (shot ^ swapped) * (SIDE // 2) + x, device ^ index)

    def edges(x):
        fine.cond.close_z(x, exact=True)

    rolled(SIDE, collect, unroll=4)
    for x in range(SIDE // 2):
        collect_half(x)
    for x in range(SIDE):
        edges(x)
    fine.cond.close(exact=True)

    coarsest = []
    for level, below in zip(levels, levels[1:] + [None]):
        level.prepare()

        def coarse(x, z, row, below=below):
            if below is None:
                coarsest.append(row)
            else:
                below.cond.put(x, z, row, exact=True)

        level.halve(
            lambda x, level=level: [
                (level.cond[x, z], level.cond[x + 1, z]) for z in range(level.side)
            ],
            coarse,
        )

    keep = iota((1, SIDE, LANES), 1) % 2 == 0
    lane = iota((1, SIDE, LANES), 2)

    def split(value):
        return [jnp.where(keep, part, 0.0) for part in (value, pltpu.roll(value, SIDE - 1, 1))]

    def around(value):
        low, high = value
        low_up, high_up = [pltpu.roll(part, LANES - GROUP, 2) for part in value]
        low_down, high_down = [pltpu.roll(part, GROUP, 2) for part in value]
        along = [[move(part, axis) for part in value] for axis in (0, 2) for move in (block_up, block_down)]
        return along + [
            [jnp.where(lane < LANES - GROUP, low_up, high_up), high_up],
            [low_down, jnp.where(lane >= GROUP, high_down, low_down)],
        ]

    sub = iota((1, SIDE, LANES), 1)
    inside_last = [
        [sub < 6] * 2,
        [sub >= 2] * 2,
        [lane % GROUP < GROUP - 1] * 2,
        [lane % GROUP > 0] * 2,
        [keep, lane < LANES - GROUP],
        [lane >= GROUP, keep],
    ]
    last_scale = 0.25 ** (LEVELS - 1)
    here = split(coarsest[0])
    others = [
        [jnp.where(inside & keep, part, 0.0) for inside, part in zip(pair, moved)]
        for pair, moved in zip(inside_last, around(here))
    ]
    last_weight, last_links = [], []
    for half, part in enumerate(here):
        total = 3.0 * part
        for other in others:
            total = total + 0.5 * other[half]
        inverse = jnp.where(keep, DAMPING / jnp.where(keep, total, 1.0), 0.0)
        last_weight.append(inverse * (1.0 / last_scale))
        last_links.append(
            [
                jnp.where(pair[half] & keep, 0.5 * inverse * (part + other[half]), 0.0)
                for pair, other in zip(inside_last, others)
            ]
        )

    def solve_last(rhs):
        base = [weight * part for weight, part in zip(last_weight, split(rhs))]
        value = base
        for _ in range(COARSE_SWEEPS - 1):
            moved = around(value)
            fresh = []
            for half in range(2):
                parts = [link * other[half] for link, other in zip(last_links[half], moved)]
                start = base[half] + (1.0 - DAMPING) * value[half]
                fresh.append(((start + parts[0]) + (parts[1] + parts[2])) + (parts[3] + (parts[4] + parts[5])))
            value = fresh
        return value[0] + pltpu.roll(value[1], 1, 1)

    def cycle(index, out, exact=False):
        level = levels[index]
        below = levels[index + 1]
        if index == LEVELS - 3:
            base = {}

            def take(x, z, row):
                base[x, z] = below.weight[x, z] * (row * (1.0 / below.scale))

            level.descend(take)
            below.cycle(base, solve_last, below.first)
        else:
            level.descend(
                lambda x, z, row: below.base.put(
                    x, z, below.weight[x, z] * (row * (2.0 / below.scale))
                )
            )
            cycle(index + 1, below.first)
        level.ascend(lambda x, z: below.first[x, z], out, exact)

    spot = spot_ref[...]
    at_spot = iota((LANES, electrodes), 0) == spot
    order = lane_order(back=True)
    wide = SIDE + 2

    def each(body):
        def one(electrode, carry):
            body(pl.ds(electrode, 1), pl.ds(cells_ref[0, electrode], 1))
            return carry

        lax.fori_loop(0, electrodes, one, 0, unroll=64)

    def put(electrode, cell):
        fine.base.ref[cell, :] = (2.0 * gathered[electrode, :]) * fine.weight.ref[cell, :]

    def read(electrode, cell):
        gathered[electrode, :] = forward.ref[cell, :]

    def exact(row, matrix_ref):
        return product(jnp.broadcast_to(row, (16, row.shape[1])), matrix_ref[...], 3)[0:1]

    sub, lane = iota((SIDE, LANES), 0), iota((SIDE, LANES), 1)

    def margin(x, z, y):
        return forward.ref[pl.ds(forward.start(x, z, y) + device, 1), :]

    def extract(index):
        for x in range(-1, SIDE + 1):
            for z in range(SIDE):
                at = (x + 1) * wide + z + 1
                start = forward.start(x, z) + device
                row = forward.ref[pl.ds(start, SIDE, stride=SIDE), :]
                owned[index, at] = row
                if 0 <= x < SIDE:
                    after, before = margin(x, z, SIDE), margin(x, z, -1)
                    place = x * SIDE + z
                    turned = pltpu.roll(row, SIDE - 1, 0)
                    beside[index, 0, place] = jnp.where(sub == SIDE - 1, after, turned)
                    beside[index, 1, place] = jnp.where(sub == 0, before, pltpu.roll(row, 1, 0))
                    if z == 0:
                        edge = pltpu.roll(row, LANES - 1, 1)
                        owned[index, at + SIDE] = jnp.where(lane % GROUP < GROUP - 1, edge, 0.0)
                    if z == SIDE - 1:
                        edge = pltpu.roll(row, 1, 1)
                        owned[index, at - SIDE] = jnp.where(lane % GROUP > 0, edge, 0.0)

    def solve(index):
        each(put)
        for x in range(SIDE):
            fine.base.close_z(x)
        fine.base.close()
        cycle(0, forward, exact=True)
        extract(index)

        @pl.when(index == 0)
        def _():
            each(read)
            readings = jnp.where(at_spot, gathered[...].T, 0.0)
            readings = jnp.sum(readings, axis=0, keepdims=True)
            misfit = exact(readings, turned_ref) - observed_ref[...]
            gathered[...] = shared_rows(exact(misfit, pairs_ref), spot, same_ref[...])

    gathered[...] = rows_ref[...]
    rolled(2, solve)

    chunk = mine_ref.shape[1]
    even = shot == 0
    for x in range(SIDE):
        tiles = []
        for z in range(SIDE):
            at = (x + 1) * wide + z + 1
            here_u, here_w = owned[0, at], owned[1, at]
            potentials_ref[pl.ds((x * SIDE + z) * SIDE, SIDE), :] = here_u
            total = None
            for step in (wide, -wide, 1, -1):
                term = (here_u - owned[0, at + step]) * (here_w - owned[1, at + step])
                total = term if total is None else total + term
            for side in range(2):
                other_u, other_w = beside[0, side, x * SIDE + z], beside[1, side, x * SIDE + z]
                total = total + (here_u - other_u) * (here_w - other_w)
            tiles.append(-0.5 * total)
        natural = from_blocks(tiles, order)
        low, high = natural[:chunk], natural[chunk:]
        mine_ref[x] = jnp.where(even, low, high)
        theirs_ref[x] = jnp.where(even, high, low)


def replicated(conductivity, stations, currents, receivers, observed):
    rows, cols, depth = conductivity.shape
    f32 = jnp.float32
    electrodes = stations.shape[0]
    total = rows * cols
    vmem = pl.BlockSpec(memory_space=pltpu.VMEM)
    smem = pl.BlockSpec(memory_space=pltpu.SMEM)
    station_row = stations.reshape(1, electrodes)
    mine, half = pl.pallas_call(
        to_blocks_kernel,
        out_shape=(
            jax.ShapeDtypeStruct((total, LANES), f32),
            jax.ShapeDtypeStruct((total // 2, LANES), f32),
        ),
        in_specs=[vmem],
        out_specs=(vmem, vmem),
        compiler_params=pltpu.CompilerParams(vmem_limit_bytes=SMALL_BYTES),
    )(conductivity)
    swap = [(0, 1), (1, 0)]

    def partner(part, k):
        count = lax.axis_size("gx")
        return lax.ppermute(part, "gx", [(i, i ^ k) for i in range(count)])

    def with_mate(part):
        return [part, lax.ppermute(part, "gy", swap)]

    far = partner(half, 2)
    near = partner(mine, 1)
    line = jax.ShapeDtypeStruct((1, electrodes), jnp.int32)
    cells, spot, rows_of, same, pairs, turned, held = pl.pallas_call(
        electrode_kernel,
        out_shape=(
            line,
            line,
            jax.ShapeDtypeStruct((electrodes, LANES), f32),
            jax.ShapeDtypeStruct((electrodes, electrodes), jnp.bfloat16),
            jax.ShapeDtypeStruct((receivers.shape[0], electrodes), jnp.bfloat16),
            jax.ShapeDtypeStruct((electrodes, receivers.shape[0]), jnp.bfloat16),
            jax.ShapeDtypeStruct(observed.shape, f32),
        ),
        in_specs=[vmem] * 4,
        out_specs=(vmem,) * 7,
        compiler_params=pltpu.CompilerParams(vmem_limit_bytes=SMALL_BYTES),
        cost_estimate=pl.CostEstimate(flops=100_000_000, bytes_accessed=1_000_000, transcendentals=0),
    )(station_row, currents, receivers, observed)
    far, rows_of = lax.optimization_barrier((far, rows_of))
    count_x = lax.axis_size("gx")
    diagonal = [(2 * i + j, 2 * (i ^ 1) + 1 - j) for i in range(count_x) for j in range(2)]
    crossed, relayed = lax.ppermute(far, "shot", swap), partner(far, 1)
    slanted = lax.ppermute(far, ("gx", "shot"), diagonal)
    parts = [piece for own in (mine, near) for piece in with_mate(own)]
    halved = [piece for own in (far, crossed, relayed) for piece in with_mate(own)]
    slanted, halved[3] = lax.optimization_barrier((slanted, halved[3]))
    halved += with_mate(slanted)
    chunk = cols // 2
    levels = [shape for index in range(LEVELS - 2) for shape in Level.scratch(index)]
    levels += HeldLevel.scratch(LEVELS - 2)
    potentials, own, theirs = pl.pallas_call(
        functools.partial(replicated_kernel, len(parts), len(halved)),
        out_shape=(
            jax.ShapeDtypeStruct((total, LANES), f32),
            jax.ShapeDtypeStruct((rows, chunk, LANES), f32),
            jax.ShapeDtypeStruct((rows, chunk, LANES), f32),
        ),
        in_specs=[smem] + [vmem] * (len(parts) + len(halved) + 6),
        out_specs=(vmem, vmem, vmem),
        scratch_shapes=[
            pltpu.VMEM((electrodes, LANES), f32),
            pltpu.VMEM((2, (SIDE + 2) ** 2, SIDE, LANES), f32),
            pltpu.VMEM((2, 2, SIDE**2, SIDE, LANES), f32),
        ]
        + levels,
        compiler_params=pltpu.CompilerParams(vmem_limit_bytes=VMEM_BYTES),
        cost_estimate=pl.CostEstimate(flops=200_000_000, bytes_accessed=4_000_000, transcendentals=0),
    )(cells, *parts, *halved, spot, rows_of, same, pairs, turned, held)
    arrived = lax.ppermute(theirs, "shot", swap)
    potentials = pl.pallas_call(
        potentials_kernel,
        out_shape=jax.ShapeDtypeStruct((rows, cols, LANES), f32),
        in_specs=[vmem],
        out_specs=vmem,
        compiler_params=pltpu.CompilerParams(vmem_limit_bytes=SMALL_BYTES),
        cost_estimate=pl.CostEstimate(flops=50_000_000, bytes_accessed=500_000, transcendentals=0),
    )(potentials)
    return potentials[None], own + arrived


def extended(array, sides, width):
    for axis, dim in sides:
        size, length = (lax.axis_size(axis), array.shape[dim])
        up = [(i, (i + 1) % size) for i in range(size - 1)]
        down = [(j, i) for i, j in up]
        last = lax.slice_in_dim(array, length - width, length, axis=dim)
        leading = lax.slice_in_dim(array, 0, width, axis=dim)
        before = lax.ppermute(last, axis, up)
        after = lax.ppermute(leading, axis, down)
        array = jnp.concatenate([before, array, after], axis=dim)
    return array


def upper_z(field):
    return jnp.concatenate([field[..., 1:], jnp.zeros_like(field[..., :1])], axis=-1)


def lower_z(field):
    return jnp.concatenate([jnp.zeros_like(field[..., :1]), field[..., :-1]], axis=-1)


def trim_circle(field, circle_width):
    return field[..., circle_width:-circle_width, circle_width:-circle_width, :]


def pad_plane(field, circle_width):
    spec = [(0, 0)] * (field.ndim - 3) + [
        (circle_width, circle_width),
        (circle_width, circle_width),
        (0, 0),
    ]
    return jnp.pad(field, spec)


def neighbour_list(field_pad):
    centre = trim_circle(field_pad, 1)
    return [
        field_pad[..., 2:, 1:-1, :],
        field_pad[..., :-2, 1:-1, :],
        field_pad[..., 1:-1, 2:, :],
        field_pad[..., 1:-1, :-2, :],
        upper_z(centre),
        lower_z(centre),
    ]


def stencil(field_pad, cond_pad, level_scale):
    centre = trim_circle(field_pad, 1)
    centre_cond = trim_circle(cond_pad, 1)
    summed = jnp.zeros_like(centre)
    for other, other_cond in zip(neighbour_list(field_pad), neighbour_list(cond_pad)):
        summed = summed + level_scale * 0.5 * (centre_cond + other_cond) * (centre - other)
    return summed


def diagonal(cond_pad, level_scale):
    centre_cond = trim_circle(cond_pad, 1)
    summed = jnp.zeros_like(centre_cond)
    for other_cond in neighbour_list(cond_pad):
        summed = summed + level_scale * 0.5 * (centre_cond + other_cond)
    return summed


def relaxed(field_pad, source, cond_pad, diag_level, level_scale):
    return (
        trim_circle(field_pad, 1)
        + DAMPING * (source - stencil(field_pad, cond_pad, level_scale)) / diag_level
    )


def restrict(field):
    leading = field.shape[:-3]
    extent = field.shape[-3:]
    shaped = field.reshape(leading + (extent[0] // 2, 2, extent[1] // 2, 2, extent[2] // 2, 2))
    return shaped.mean(axis=(-5, -3, -1))


def prolong(field):
    return jnp.repeat(jnp.repeat(jnp.repeat(field, 2, axis=-3), 2, axis=-2), 2, axis=-1)


def assemble(blocks, count_x, count_y):
    leading = blocks.shape[1:-3]
    extent = blocks.shape[-3:]
    depth_lead = len(leading)
    shaped = blocks.reshape((count_x, count_y) + leading + extent)
    order = tuple(range(2, 2 + depth_lead)) + (0, 2 + depth_lead, 1, 3 + depth_lead, 4 + depth_lead)
    return shaped.transpose(order).reshape(
        leading + (count_x * extent[0], count_y * extent[1], extent[2])
    )


def field_rim(field):
    return extended(field, (("gx", 1), ("gy", 2)), 1)


def cond_rim(conduct):
    return extended(conduct, (("gx", 0), ("gy", 1)), 1)


def whole_cycle(source, level_index, whole_plans):
    cond_pad, diag_level, level_scale = whole_plans[level_index]
    field = DAMPING * source / diag_level

    def turn(turn_index, iterate):
        return relaxed(pad_plane(iterate, 1), source, cond_pad, diag_level, level_scale)

    return lax.fori_loop(0, COARSE_SWEEPS - 1, turn, field)


def part_cycle(source, level_index, level_plans, whole_plans, gather_level):
    if level_index == gather_level:
        blocks = lax.all_gather(source[None], ("gx", "gy"), axis=0, tiled=True)
        whole = assemble(blocks, lax.axis_size("gx"), lax.axis_size("gy"))
        correction = whole_cycle(whole, level_index, whole_plans)
        extent = source.shape
        starts = (0, lax.axis_index("gx") * extent[1], lax.axis_index("gy") * extent[2], 0)
        return lax.dynamic_slice(correction, starts, extent)
    cond_pad, diag_level, level_scale = level_plans[level_index]
    field = DAMPING * source / diag_level
    field = relaxed(field_rim(field), source, cond_pad, diag_level, level_scale)
    residual = source - stencil(field_rim(field), cond_pad, level_scale)
    field = field + prolong(
        part_cycle(restrict(residual), level_index + 1, level_plans, whole_plans, gather_level)
    )
    field = relaxed(field_rim(field), source, cond_pad, diag_level, level_scale)
    return relaxed(field_rim(field), source, cond_pad, diag_level, level_scale)


def distributed(conductivity, stations, currents, receivers, observed):
    row_count, col_count, z_count = conductivity.shape
    shot_count = currents.shape[0]
    count_x = lax.axis_size("gx")
    count_y = lax.axis_size("gy")
    gather_level = LEVELS - 1
    level_plans = []
    conduct = conductivity
    for level_index in range(gather_level):
        level_scale = 0.25**level_index
        cond_pad = cond_rim(conduct)
        level_plans.append((cond_pad, diagonal(cond_pad, level_scale), level_scale))
        conduct = restrict(conduct)
    blocks = lax.all_gather(conduct[None], ("gx", "gy"), axis=0, tiled=True)
    whole = assemble(blocks, count_x, count_y)
    whole_plans = {}
    level_index = 3
    level_scale = 0.25**level_index
    cond_pad = pad_plane(whole, 1)
    whole_plans[level_index] = (cond_pad, diagonal(cond_pad, level_scale), level_scale)
    total_y = col_count * count_y
    cell_x = stations // (total_y * z_count)
    cell_y = stations // z_count % total_y
    cell_z = stations % z_count
    local_x = cell_x - lax.axis_index("gx") * row_count
    local_y = cell_y - lax.axis_index("gy") * col_count
    owned = (local_x >= 0) & (local_x < row_count) & (local_y >= 0) & (local_y < col_count)
    block_size = row_count * col_count * z_count
    local_cell = jnp.where(owned, (local_x * col_count + local_y) * z_count + cell_z, 0)
    offsets = jnp.arange(shot_count)[:, None] * block_size + local_cell[None, :]
    targets = jnp.where(owned[None, :], offsets, shot_count * block_size).reshape(-1)

    def spread(amounts):
        flat = (
            jnp.zeros((shot_count * block_size,), jnp.float32)
            .at[targets]
            .add(amounts.reshape(-1), mode="drop")
        )
        return flat.reshape(shot_count, row_count, col_count, z_count)

    potentials = part_cycle(spread(currents), 0, level_plans, whole_plans, gather_level)
    local_values = jnp.where(
        owned[None, :], potentials.reshape(shot_count, block_size)[:, local_cell], 0.0
    )
    readings = lax.psum(local_values, ("gx", "gy"))
    positions = jnp.arange(stations.shape[0])[:, None]
    pairs = (receivers[:, 0][None, :] == positions).astype(jnp.float32) - (
        receivers[:, 1][None, :] == positions
    ).astype(jnp.float32)
    misfit = jnp.dot(readings, pairs, precision=lax.Precision.HIGHEST) - observed
    back_source = jnp.dot(misfit, pairs.T, precision=lax.Precision.HIGHEST)
    adjoint = part_cycle(spread(back_source), 0, level_plans, whole_plans, gather_level)
    stacked = jnp.concatenate([potentials, adjoint], axis=0)
    padded = extended(stacked, (("gx", 1), ("gy", 2)), 1)
    potential_pad = padded[:shot_count]
    adjoint_pad = padded[shot_count:]
    gradient = jnp.zeros_like(potentials)
    for other_u, other_w in zip(neighbour_list(potential_pad), neighbour_list(adjoint_pad)):
        gradient = gradient - 0.5 * (potentials - other_u) * (adjoint - other_w)
    summed = lax.psum_scatter(jnp.sum(gradient, axis=0), "shot", scatter_dimension=1, tiled=True)
    return (potentials, summed)


def per_device(conductivity, stations, currents, receivers, observed):
    blocks = lax.axis_size("gx") * lax.axis_size("gy")
    fits = conductivity.shape == (SIDE, SIDE * SIDE, LANES) and blocks == SIDE
    fits = fits and lax.axis_size("gy") == 2 and lax.axis_size("shot") == 2
    fits = fits and currents.shape[0] == 1
    plan = replicated if fits else distributed
    return plan(conductivity, stations, currents, receivers, observed)


def solution(mesh):
    in_specs = (
        P(("grp", "gx"), "gy", None),
        P("grp"),
        P(("grp", "shot"), None),
        P("grp", None),
        P(("grp", "shot"), None),
    )
    out_specs = (P(("grp", "shot"), "gx", "gy", None), P(("grp", "gx"), ("gy", "shot"), None))
    return jax.shard_map(
        per_device, mesh=mesh, in_specs=in_specs, out_specs=out_specs, check_vma=False
    )
```

```python
import functools

import jax
import jax.numpy as jnp
from jax import lax
from jax.experimental import pallas as pl
from jax.experimental.pallas import tpu as pltpu
from jax.sharding import PartitionSpec as P

LEVELS = 4
COARSE_SWEEPS = 16


DAMPING = 0.8

SIDE = 8
LANES = 128
GROUP = 16
VMEM_BYTES = 48 * 2**20
SMALL_BYTES = 6 * 2**20


def pieces_of(value, count):
    pieces = []
    for _ in range(count):
        pieces.append(value.astype(jnp.bfloat16))
        value = value - pieces[-1].astype(jnp.float32)
    return pieces[::-1]


def product(value, matrix, count, dims=((1,), (0,))):
    result = None
    for piece in pieces_of(value, count):
        term = lax.dot_general(
            piece, matrix, (dims, ((), ())), preferred_element_type=jnp.float32
        )
        result = term if result is None else result + term
    return result


def iota(shape, dim):
    return lax.broadcasted_iota(jnp.int32, shape, dim)


def station_table(station):
    cell_x, cell_y, cell_z = station >> 14, station >> 7 & 127, station & 127
    row = (cell_x >> 3) * 2 + (cell_y >> 6)
    return cell_x, cell_y, cell_z, row, (cell_y >> 3 & 7) * GROUP + (cell_z >> 3)


def lane_order(back=False):
    row, col = iota((LANES, LANES), 0), iota((LANES, LANES), 1)
    if back:
        row, col = col, row
    chosen = row == col % GROUP * SIDE + col // GROUP
    return jnp.where(chosen, 1.0, 0.0).astype(jnp.bfloat16)


def exchange_groups(tiles):
    tiles = list(tiles)
    group = iota(tiles[0].shape, 1) // GROUP
    for bit in range(3):
        step = 1 << bit
        keep = (group & step) == 0
        for low in range(SIDE):
            if low & step == 0:
                a, b = tiles[low], tiles[low | step]
                tiles[low] = jnp.where(keep, a, pltpu.roll(b, step * GROUP, 1))
                tiles[low | step] = jnp.where(keep, pltpu.roll(a, LANES - step * GROUP, 1), b)
    return tiles


def own_place():
    return lax.axis_index("gx") * 2 + lax.axis_index("gy"), lax.axis_index("shot")


def to_blocks_kernel(natural_ref, blocks_ref, half_ref):
    order = lane_order()
    for x in range(SIDE):
        tiles = product(natural_ref[x], order, 3)
        tiles = [tiles[SIDE * k : SIDE * (k + 1)] for k in range(SIDE)]
        for z, tile in enumerate(exchange_groups(tiles)):
            blocks_ref[pl.ds((x * SIDE + z) * SIDE, SIDE), :] = tile
    count = half_ref.shape[0]
    low, high = blocks_ref[pl.ds(0, count), :], blocks_ref[pl.ds(count, count), :]
    half_ref[...] = jnp.where(own_place()[1] == 0, low, high)


def from_blocks(tiles, order):
    natural = jnp.concatenate(exchange_groups(tiles), axis=0)
    return product(natural, order, 3)


def potentials_kernel(rows_ref, potentials_ref):
    order = lane_order(back=True)
    for x in range(SIDE):
        tiles = [rows_ref[pl.ds((x * SIDE + z) * SIDE, SIDE), :] for z in range(SIDE)]
        potentials_ref[x] = from_blocks(tiles, order)


def block_up(field, axis):
    if axis == 0:
        return pltpu.roll(field, 6, 1)
    if axis == 2:
        return pltpu.roll(field, LANES - 1, 2)
    turned = pltpu.roll(field, LANES - GROUP, 2)
    return jnp.where(iota(field.shape, 2) < LANES - GROUP, turned, pltpu.roll(turned, 7, 1))


def block_down(field, axis):
    if axis == 0:
        return pltpu.roll(field, 2, 1)
    if axis == 2:
        return pltpu.roll(field, 1, 2)
    turned = pltpu.roll(field, GROUP, 2)
    return jnp.where(iota(field.shape, 2) >= GROUP, turned, pltpu.roll(turned, 1, 1))


def inside_up(field, axis):
    sub, lane = iota(field.shape, 1), iota(field.shape, 2)
    if axis == 0:
        keep = sub < 6
    elif axis == 1:
        keep = (lane < LANES - GROUP) | (sub % 2 == 0)
    else:
        keep = lane % GROUP < GROUP - 1
    return jnp.where(keep, field, 0.0)


def inside_down(field, axis):
    sub, lane = iota(field.shape, 1), iota(field.shape, 2)
    if axis == 0:
        keep = sub >= 2
    elif axis == 1:
        keep = (lane >= GROUP) | (sub % 2 == 1)
    else:
        keep = lane % GROUP > 0
    return jnp.where(keep, field, 0.0)


def pair_rows(row):
    count = row.shape[0] // 2
    return jnp.concatenate([row[2 * i : 2 * i + 1] + row[2 * i + 1 : 2 * i + 2] for i in range(count)])


def twice(row):
    return jnp.concatenate([row[i // 2 : i // 2 + 1] for i in range(2 * row.shape[0])])


def electrode_kernel(
    stations_ref,
    currents_ref,
    receivers_ref,
    observed_ref,
    cells_ref,
    spot_ref,
    rows_ref,
    same_ref,
    pairs_ref,
    turned_ref,
    held_ref,
):
    stations = stations_ref[...]
    electrodes = stations.shape[1]
    cell_x, cell_y, cell_z, row, spot = station_table(stations)
    wide = SIDE + 2
    register = (((cell_x & 7) + 1) * wide + (cell_z & 7) + 1) * wide + (cell_y & 7) + 1
    cells_ref[...] = register * SIDE + row
    spot_ref[...] = spot
    held_ref[...] = observed_ref[...]
    line = stations & 0x1C387 | row << 20
    same = jnp.broadcast_to(line, (electrodes, electrodes))
    same = jnp.where(same == same.T, 1.0, 0.0).astype(jnp.bfloat16)
    same_ref[...] = same
    rows_ref[...] = shared_rows(currents_ref[...], spot, same)
    receivers = receivers_ref[...]
    numbers = iota((receivers.shape[0], electrodes), 1)
    pairs = jnp.where(numbers == receivers[:, 0:1], 1.0, 0.0) - jnp.where(
        numbers == receivers[:, 1:2], 1.0, 0.0
    )
    pairs_ref[...] = pairs.astype(jnp.bfloat16)
    turned_ref[...] = pairs.T.astype(jnp.bfloat16)


def shared_rows(amounts, spot, same):
    electrodes = amounts.shape[1]
    at_spot = iota((LANES, electrodes), 0) == spot
    return product(jnp.where(at_spot, amounts, 0.0), same, 3).T


class Edged:
    def __init__(self, ref, side):
        self.ref, self.side = ref, side

    def start(self, x, z, y=0):
        wide = self.side + 2
        return (((x + 1) * wide + z + 1) * wide + y + 1) * SIDE

    def __getitem__(self, at):
        x, z = at
        rows = self.ref[pl.ds(self.start(x, z), self.side * SIDE), :]
        return rows.reshape(self.side, SIDE, LANES)

    def __setitem__(self, at, value):
        x, z = at
        self.ref[pl.ds(self.start(x, z), self.side * SIDE), :] = value.reshape(-1, LANES)

    def put(self, x, z, value, exact=False):
        self[x, z] = value
        n = self.side
        if z == 0:
            edge = block_up(value, 2)
            self[x, n] = inside_up(edge, 2) if exact else edge
        if z == n - 1:
            edge = block_down(value, 2)
            self[x, -1] = inside_down(edge, 2) if exact else edge
        if x == 0:
            edge = block_up(value, 0)
            self[n, z] = inside_up(edge, 0) if exact else edge
        if x == n - 1:
            edge = block_down(value, 0)
            self[-1, z] = inside_down(edge, 0) if exact else edge
        if exact:
            after = inside_up(block_up(value[:1], 1), 1)
            self.ref[pl.ds(self.start(x, z, n), SIDE), :] = after[0]
            before = inside_down(block_down(value[n - 1 :], 1), 1)
            self.ref[pl.ds(self.start(x, z, -1), SIDE), :] = before[0]

    def close_z(self, x, exact=False):
        n = self.side
        after, before = block_up(self[x, 0], 2), block_down(self[x, n - 1], 2)
        self[x, n] = inside_up(after, 2) if exact else after
        self[x, -1] = inside_down(before, 2) if exact else before

    def close(self, exact=False):
        n = self.side
        for z in range(n):
            after = block_up(self[0, z], 0)
            self[n, z] = inside_up(after, 0) if exact else after
            before = block_down(self[n - 1, z], 0)
            self[-1, z] = inside_down(before, 0) if exact else before


class Rows:
    def __init__(self, ref, side, first_x=0, first_z=0):
        self.ref, self.side, self.first_x, self.first_z = ref, side, first_x, first_z

    def place(self, at):
        count = self.side - self.first_z
        rows = self.side * SIDE
        return pl.ds(((at[0] - self.first_x) * count + at[1] - self.first_z) * rows, rows)

    def __getitem__(self, at):
        return self.ref[self.place(at), :].reshape(self.side, SIDE, LANES)

    def __setitem__(self, at, value):
        self.ref[self.place(at), :] = value.reshape(-1, LANES)


def rolled(count, body, unroll=1):
    def one(x, carry):
        body(x)
        return carry

    lax.fori_loop(0, count, one, 0, unroll=unroll)


def next_in_y(row):
    return jnp.concatenate([row[1:], block_up(row[:1], 1)])


def last_in_y(row):
    return jnp.concatenate([block_down(row[-1:], 1), row[:-1]])


class Level:
    def __init__(self, refs, index):
        self.side = side = SIDE >> index
        self.scale = 0.25**index
        edged = [Edged(ref, side) for ref in refs[:5]]
        self.cond, self.first, self.second, self.base, self.weight = edged
        self.link_x = Rows(refs[5], side, first_x=-1)
        self.link_y = Rows(refs[6], side)
        self.link_z = Rows(refs[7], side, first_z=-1)
        self.back = Rows(refs[8], side)

    @staticmethod
    def scratch(index):
        side = SIDE >> index
        sizes = [(side + 2) ** 3] * 5
        sizes += [side**2 * (side + 1), side**3, side**2 * (side + 1), side**3]
        return [pltpu.VMEM((size * SIDE, LANES), jnp.float32) for size in sizes]

    def pairs(self, body):
        for i in range(self.side // 2):
            body(2 * i)

    def prepare(self):
        n = self.side
        cond = self.cond

        def plane(x):
            for z in range(n):
                here, ahead, next_x = cond[x, z], cond[x, z + 1], cond[x + 1, z]
                after = inside_up(block_up(here[:1], 1), 1)
                before = inside_down(block_down(here[-1:], 1), 1)
                next_y = jnp.concatenate([here[1:], after])
                last_y = jnp.concatenate([before, here[:-1]])
                total = (next_x + cond[x - 1, z]) + (ahead + cond[x, z - 1]) + (next_y + last_y)
                total = 6.0 * here + total
                self.weight[x, z] = DAMPING / total
                if n == SIDE:
                    self.base[x, z] = jnp.zeros_like(here)
                self.back[x, z] = total * (0.5 * self.scale / DAMPING)
                self.link_x[x, z] = here + next_x
                link = here + next_y
                self.link_y[x, z] = jnp.concatenate([link[:-1], inside_up(link[-1:], 1)])
                link = here + ahead
                if z == n - 1:
                    link = inside_up(link, 2)
                    self.link_z[x, -1] = block_down(link, 2)
                self.link_z[x, z] = link

        if n == SIDE:
            rolled(n, plane, unroll=2)
        else:
            for x in range(n):
                plane(x)
        for z in range(n):
            link = inside_up(self.link_x[n - 1, z], 0)
            self.link_x[n - 1, z] = link
            self.link_x[-1, z] = block_down(link, 0)

    def flows(self, x, z, here, ahead, outer, down):
        result = []
        inner = self.link_x[x, z]
        sides = [
            self.link_x[x - 1, z] * outer[0] + inner * here[1],
            inner * here[0] + self.link_x[x + 1, z] * outer[1],
        ]
        for p in range(2):
            link_y, link_z = self.link_y[x + p, z], self.link_z[x + p, z]
            along = link_y * next_in_y(here[p]) + last_in_y(link_y * here[p])
            total = sides[p] + (link_z * ahead[p] + down[p]) + along
            down[p] = link_z * here[p]
            result.append(self.weight[x + p, z] * total)
        return result

    def rows(self, field, x):
        here = [field[x, 0], field[x + 1, 0]]
        down = [self.link_z[x + p, -1] * field[x + p, -1] for p in range(2)]
        for z in range(self.side):
            ahead = [field[x, z + 1], field[x + 1, z + 1]]
            outer = [field[x - 1, z], field[x + 2, z]]
            yield z, here, self.flows(x, z, here, ahead, outer, down)
            here = ahead

    def sweep(self, field, out, exact=False):
        def pair(x):
            for z, here, sums in self.rows(field, x):
                for p in range(2):
                    if field is self.base:
                        value = (2.0 - DAMPING) * here[p] + sums[p]
                    else:
                        value = (1.0 - DAMPING) * here[p] + (self.base[x + p, z] + sums[p])
                    out.put(x + p, z, value, exact)

        self.pairs(pair)

    def halve(self, rows, coarse):
        def pair(x):
            held = None
            for z, row in enumerate(rows(x)):
                row = row[0] + row[1]
                if z % 2 == 0:
                    held = row
                else:
                    coarse(x // 2, z // 2, 0.125 * pair_rows(held + row))

        self.pairs(pair)

    def descend(self, coarse):
        self.sweep(self.base, self.second)

        def residuals(x):
            for z, here, sums in self.rows(self.second, x):
                result = []
                for p in range(2):
                    swept = (1.0 - DAMPING) * here[p] + (self.base[x + p, z] + sums[p])
                    self.first[x + p, z] = swept
                    result.append((swept - here[p]) * self.back[x + p, z])
                yield result

        self.halve(residuals, coarse)

    def ascend(self, correction, out, exact=False):
        def pair(x):
            i = x // 2
            here = twice(correction(i, 0))
            start = twice(correction(i, -1))
            down = [self.link_z[x + p, -1] * start for p in range(2)]
            for z in range(self.side):
                ahead = twice(correction(i, (z + 1) // 2))
                outer = [twice(correction(i - 1, z // 2)), twice(correction(i + 1, z // 2))]
                sums = self.flows(x, z, [here, here], [ahead, ahead], outer, down)
                for p in range(2):
                    value = self.first[x + p, z] + ((1.0 - DAMPING) * here + sums[p])
                    self.second.put(x + p, z, value)
                here = ahead

        self.pairs(pair)
        self.sweep(self.second, out, exact)


class HeldLevel:
    def __init__(self, refs, index):
        self.side = 2
        self.scale = 0.25**index
        self.cond, self.first = Edged(refs[0], 2), Edged(refs[1], 2)
        self.weight, self.back = Rows(refs[2], 2), Rows(refs[3], 2)
        self.links = [Rows(ref, 2) for ref in refs[4:]]

    @staticmethod
    def scratch(index):
        sizes = [4**3] * 2 + [2**3] * 8
        return [pltpu.VMEM((size * SIDE, LANES), jnp.float32) for size in sizes]

    def around(self, field, inside=False):
        def moved(row, axis, up):
            row = (block_up if up else block_down)(row, axis)
            return (inside_up if up else inside_down)(row, axis) if inside else row

        result = {}
        for (x, z), here in field.items():
            result[x, z] = [
                field[1, z] if x == 0 else moved(field[0, z], 0, True),
                field[0, z] if x == 1 else moved(field[1, z], 0, False),
                jnp.concatenate([here[1:], moved(here[:1], 1, True)]),
                jnp.concatenate([moved(here[-1:], 1, False), here[:-1]]),
                field[x, 1] if z == 0 else moved(field[x, 0], 2, True),
                field[x, 0] if z == 1 else moved(field[x, 1], 2, False),
            ]
        return result

    def prepare(self):
        field = {(x, z): self.cond[x, z] for x in range(2) for z in range(2)}
        for at, others in self.around(field, inside=True).items():
            here = field[at]
            total = others[0]
            for other in others[1:]:
                total = total + other
            total = 3.0 * here + 0.5 * total
            inverse = DAMPING / total
            self.weight[at] = inverse
            self.back[at] = total * (self.scale / DAMPING)
            for index, other in enumerate(others):
                link = 0.5 * inverse * (here + other)
                self.links[index][at] = jnp.where(other > 0.0, link, 0.0)

    def halve(self, rows, coarse):
        total = None
        for row in rows(0):
            row = row[0] + row[1]
            total = row if total is None else total + row
        coarse(0, 0, 0.125 * (total[:1] + total[1:]))

    def sums(self, field, base):
        result = {}
        for at, others in self.around(field).items():
            total = base[at]
            for link, other in zip(self.links, others):
                total = total + link[at] * other
            result[at] = total
        return result

    def swept(self, field, base):
        sums = self.sums(field, base)
        return {at: (1.0 - DAMPING) * field[at] + sums[at] for at in field}

    def cycle(self, base, solve, out):
        field = self.swept(base, base)
        sums = self.sums(field, base)
        total = None
        for at in field:
            residual = (sums[at] - DAMPING * field[at]) * self.back[at]
            total = residual if total is None else total + residual
        solved = solve(0.125 * (total[:1] + total[1:]))
        row = twice(solved)
        copied = {at: row for at in field}
        change = {at: sums[at] + (1.0 - DAMPING) * (field[at] + row) for at in field}
        field = self.sums(copied, change)
        for (x, z), value in self.swept(field, base).items():
            out.put(x, z, value)


def replicated_kernel(
    whole,
    halved,
    cells_ref,
    *refs,
):
    parts = refs[:whole], refs[whole : whole + halved]
    solve_kernel(*parts, cells_ref, *refs[whole + halved :])


def solve_kernel(
    part_refs,
    half_refs,
    cells_ref,
    spot_ref,
    rows_ref,
    same_ref,
    pairs_ref,
    turned_ref,
    observed_ref,
    potentials_ref,
    mine_ref,
    theirs_ref,
    gathered,
    owned,
    beside,
    *level_refs,
):
    f32 = jnp.float32
    electrodes = spot_ref.shape[1]
    levels, used = [], 0
    for index in range(LEVELS - 1):
        kind = HeldLevel if index == LEVELS - 2 else Level
        count = len(kind.scratch(index))
        levels.append(kind(level_refs[used : used + count], index))
        used += count
    fine = levels[0]
    forward = fine.cond
    wide = SIDE * SIDE * SIDE

    device, shot = own_place()

    def place(part, row, x, index):
        for z in range(SIDE):
            fine.cond.ref[pl.ds(fine.cond.start(x, z) + index, SIDE, stride=SIDE), :] = part[
                pl.ds((row * SIDE + z) * SIDE, SIDE), :
            ]

    def collect(x):
        for k, part in enumerate(part_refs):
            place(part, x, x, device ^ k)

    def collect_half(x):
        for k, part in enumerate(half_refs):
            swapped, index = k // 2 % 2, len(part_refs) + k // 4 * 2 + k % 2
            place(part, x, (shot ^ swapped) * (SIDE // 2) + x, device ^ index)

    def edges(x):
        fine.cond.close_z(x, exact=True)

    rolled(SIDE, collect, unroll=4)
    for x in range(SIDE // 2):
        collect_half(x)
    for x in range(SIDE):
        edges(x)
    fine.cond.close(exact=True)

    coarsest = []
    for level, below in zip(levels, levels[1:] + [None]):
        level.prepare()

        def coarse(x, z, row, below=below):
            if below is None:
                coarsest.append(row)
            else:
                below.cond.put(x, z, row, exact=True)

        level.halve(
            lambda x, level=level: [
                (level.cond[x, z], level.cond[x + 1, z]) for z in range(level.side)
            ],
            coarse,
        )

    keep = iota((1, SIDE, LANES), 1) % 2 == 0
    lane = iota((1, SIDE, LANES), 2)

    def split(value):
        return [jnp.where(keep, part, 0.0) for part in (value, pltpu.roll(value, SIDE - 1, 1))]

    def around(value):
        low, high = value
        low_up, high_up = [pltpu.roll(part, LANES - GROUP, 2) for part in value]
        low_down, high_down = [pltpu.roll(part, GROUP, 2) for part in value]
        along = [[move(part, axis) for part in value] for axis in (0, 2) for move in (block_up, block_down)]
        return along + [
            [jnp.where(lane < LANES - GROUP, low_up, high_up), high_up],
            [low_down, jnp.where(lane >= GROUP, high_down, low_down)],
        ]

    sub = iota((1, SIDE, LANES), 1)
    inside_last = [
        [sub < 6] * 2,
        [sub >= 2] * 2,
        [lane % GROUP < GROUP - 1] * 2,
        [lane % GROUP > 0] * 2,
        [keep, lane < LANES - GROUP],
        [lane >= GROUP, keep],
    ]
    last_scale = 0.25 ** (LEVELS - 1)
    here = split(coarsest[0])
    others = [
        [jnp.where(inside & keep, part, 0.0) for inside, part in zip(pair, moved)]
        for pair, moved in zip(inside_last, around(here))
    ]
    last_weight, last_links = [], []
    for half, part in enumerate(here):
        total = 3.0 * part
        for other in others:
            total = total + 0.5 * other[half]
        inverse = jnp.where(keep, DAMPING / jnp.where(keep, total, 1.0), 0.0)
        last_weight.append(inverse * (1.0 / last_scale))
        last_links.append(
            [
                jnp.where(pair[half] & keep, 0.5 * inverse * (part + other[half]), 0.0)
                for pair, other in zip(inside_last, others)
            ]
        )

    def solve_last(rhs):
        base = [weight * part for weight, part in zip(last_weight, split(rhs))]
        value = base
        for _ in range(COARSE_SWEEPS - 1):
            moved = around(value)
            fresh = []
            for half in range(2):
                parts = [link * other[half] for link, other in zip(last_links[half], moved)]
                start = base[half] + (1.0 - DAMPING) * value[half]
                fresh.append(((start + parts[0]) + (parts[1] + parts[2])) + (parts[3] + (parts[4] + parts[5])))
            value = fresh
        return value[0] + pltpu.roll(value[1], 1, 1)

    def cycle(index, out, exact=False):
        level = levels[index]
        below = levels[index + 1]
        if index == LEVELS - 3:
            base = {}

            def take(x, z, row):
                base[x, z] = below.weight[x, z] * (row * (1.0 / below.scale))

            level.descend(take)
            below.cycle(base, solve_last, below.first)
        else:
            level.descend(
                lambda x, z, row: below.base.put(
                    x, z, below.weight[x, z] * (row * (2.0 / below.scale))
                )
            )
            cycle(index + 1, below.first)
        level.ascend(lambda x, z: below.first[x, z], out, exact)

    spot = spot_ref[...]
    at_spot = iota((LANES, electrodes), 0) == spot
    order = lane_order(back=True)
    wide = SIDE + 2

    def each(body):
        def one(electrode, carry):
            body(pl.ds(electrode, 1), pl.ds(cells_ref[0, electrode], 1))
            return carry

        lax.fori_loop(0, electrodes, one, 0, unroll=128)

    def put(electrode, cell):
        fine.base.ref[cell, :] = (2.0 * gathered[electrode, :]) * fine.weight.ref[cell, :]

    def read(electrode, cell):
        gathered[electrode, :] = forward.ref[cell, :]

    def exact(row, matrix_ref):
        return product(jnp.broadcast_to(row, (16, row.shape[1])), matrix_ref[...], 3)[0:1]

    sub, lane = iota((SIDE, LANES), 0), iota((SIDE, LANES), 1)

    def margin(x, z, y):
        return forward.ref[pl.ds(forward.start(x, z, y) + device, 1), :]

    def extract(index):
        for x in range(-1, SIDE + 1):
            for z in range(SIDE):
                at = (x + 1) * wide + z + 1
                start = forward.start(x, z) + device
                row = forward.ref[pl.ds(start, SIDE, stride=SIDE), :]
                owned[index, at] = row
                if 0 <= x < SIDE:
                    after, before = margin(x, z, SIDE), margin(x, z, -1)
                    place = x * SIDE + z
                    turned = pltpu.roll(row, SIDE - 1, 0)
                    beside[index, 0, place] = jnp.where(sub == SIDE - 1, after, turned)
                    beside[index, 1, place] = jnp.where(sub == 0, before, pltpu.roll(row, 1, 0))
                    if z == 0:
                        edge = pltpu.roll(row, LANES - 1, 1)
                        owned[index, at + SIDE] = jnp.where(lane % GROUP < GROUP - 1, edge, 0.0)
                    if z == SIDE - 1:
                        edge = pltpu.roll(row, 1, 1)
                        owned[index, at - SIDE] = jnp.where(lane % GROUP > 0, edge, 0.0)

    def solve(index):
        each(put)
        for x in range(SIDE):
            fine.base.close_z(x)
        fine.base.close()
        cycle(0, forward, exact=True)
        extract(index)

        @pl.when(index == 0)
        def _():
            each(read)
            readings = jnp.where(at_spot, gathered[...].T, 0.0)
            readings = jnp.sum(readings, axis=0, keepdims=True)
            misfit = exact(readings, turned_ref) - observed_ref[...]
            gathered[...] = shared_rows(exact(misfit, pairs_ref), spot, same_ref[...])

    gathered[...] = rows_ref[...]
    rolled(2, solve)

    chunk = mine_ref.shape[1]
    even = shot == 0
    for x in range(SIDE):
        tiles = []
        for z in range(SIDE):
            at = (x + 1) * wide + z + 1
            here_u, here_w = owned[0, at], owned[1, at]
            potentials_ref[pl.ds((x * SIDE + z) * SIDE, SIDE), :] = here_u
            total = None
            for step in (wide, -wide, 1, -1):
                term = (here_u - owned[0, at + step]) * (here_w - owned[1, at + step])
                total = term if total is None else total + term
            for side in range(2):
                other_u, other_w = beside[0, side, x * SIDE + z], beside[1, side, x * SIDE + z]
                total = total + (here_u - other_u) * (here_w - other_w)
            tiles.append(-0.5 * total)
        natural = from_blocks(tiles, order)
        low, high = natural[:chunk], natural[chunk:]
        mine_ref[x] = jnp.where(even, low, high)
        theirs_ref[x] = jnp.where(even, high, low)


def replicated(conductivity, stations, currents, receivers, observed):
    rows, cols, depth = conductivity.shape
    f32 = jnp.float32
    electrodes = stations.shape[0]
    total = rows * cols
    vmem = pl.BlockSpec(memory_space=pltpu.VMEM)
    smem = pl.BlockSpec(memory_space=pltpu.SMEM)
    station_row = stations.reshape(1, electrodes)
    mine, half = pl.pallas_call(
        to_blocks_kernel,
        out_shape=(
            jax.ShapeDtypeStruct((total, LANES), f32),
            jax.ShapeDtypeStruct((total // 2, LANES), f32),
        ),
        in_specs=[vmem],
        out_specs=(vmem, vmem),
        compiler_params=pltpu.CompilerParams(vmem_limit_bytes=SMALL_BYTES),
    )(conductivity)
    swap = [(0, 1), (1, 0)]

    def partner(part, k):
        count = lax.axis_size("gx")
        return lax.ppermute(part, "gx", [(i, i ^ k) for i in range(count)])

    def with_mate(part):
        return [part, lax.ppermute(part, "gy", swap)]

    far = partner(half, 2)
    near = partner(mine, 1)
    line = jax.ShapeDtypeStruct((1, electrodes), jnp.int32)
    cells, spot, rows_of, same, pairs, turned, held = pl.pallas_call(
        electrode_kernel,
        out_shape=(
            line,
            line,
            jax.ShapeDtypeStruct((electrodes, LANES), f32),
            jax.ShapeDtypeStruct((electrodes, electrodes), jnp.bfloat16),
            jax.ShapeDtypeStruct((receivers.shape[0], electrodes), jnp.bfloat16),
            jax.ShapeDtypeStruct((electrodes, receivers.shape[0]), jnp.bfloat16),
            jax.ShapeDtypeStruct(observed.shape, f32),
        ),
        in_specs=[vmem] * 4,
        out_specs=(vmem,) * 7,
        compiler_params=pltpu.CompilerParams(vmem_limit_bytes=SMALL_BYTES),
        cost_estimate=pl.CostEstimate(flops=100_000_000, bytes_accessed=1_000_000, transcendentals=0),
    )(station_row, currents, receivers, observed)
    far, rows_of = lax.optimization_barrier((far, rows_of))
    count_x = lax.axis_size("gx")
    diagonal = [(2 * i + j, 2 * (i ^ 1) + 1 - j) for i in range(count_x) for j in range(2)]
    crossed, relayed = lax.ppermute(far, "shot", swap), partner(far, 1)
    slanted = with_mate(lax.ppermute(far, ("gx", "shot"), diagonal))
    parts = [piece for own in (mine, near) for piece in with_mate(own)]
    halved = [piece for own in (far, crossed) for piece in with_mate(own)]
    relayed, slanted[1] = lax.optimization_barrier((relayed, slanted[1]))
    halved += with_mate(relayed) + slanted
    chunk = cols // 2
    levels = [shape for index in range(LEVELS - 2) for shape in Level.scratch(index)]
    levels += HeldLevel.scratch(LEVELS - 2)
    potentials, own, theirs = pl.pallas_call(
        functools.partial(replicated_kernel, len(parts), len(halved)),
        out_shape=(
            jax.ShapeDtypeStruct((total, LANES), f32),
            jax.ShapeDtypeStruct((rows, chunk, LANES), f32),
            jax.ShapeDtypeStruct((rows, chunk, LANES), f32),
        ),
        in_specs=[smem] + [vmem] * (len(parts) + len(halved) + 6),
        out_specs=(vmem, vmem, vmem),
        scratch_shapes=[
            pltpu.VMEM((electrodes, LANES), f32),
            pltpu.VMEM((2, (SIDE + 2) ** 2, SIDE, LANES), f32),
            pltpu.VMEM((2, 2, SIDE**2, SIDE, LANES), f32),
        ]
        + levels,
        compiler_params=pltpu.CompilerParams(vmem_limit_bytes=VMEM_BYTES),
        cost_estimate=pl.CostEstimate(flops=200_000_000, bytes_accessed=4_000_000, transcendentals=0),
    )(cells, *parts, *halved, spot, rows_of, same, pairs, turned, held)
    arrived = lax.ppermute(theirs, "shot", swap)
    potentials = pl.pallas_call(
        potentials_kernel,
        out_shape=jax.ShapeDtypeStruct((rows, cols, LANES), f32),
        in_specs=[vmem],
        out_specs=vmem,
        compiler_params=pltpu.CompilerParams(vmem_limit_bytes=SMALL_BYTES),
        cost_estimate=pl.CostEstimate(flops=50_000_000, bytes_accessed=500_000, transcendentals=0),
    )(potentials)
    return potentials[None], own + arrived


def extended(array, sides, width):
    for axis, dim in sides:
        size, length = (lax.axis_size(axis), array.shape[dim])
        up = [(i, (i + 1) % size) for i in range(size - 1)]
        down = [(j, i) for i, j in up]
        last = lax.slice_in_dim(array, length - width, length, axis=dim)
        leading = lax.slice_in_dim(array, 0, width, axis=dim)
        before = lax.ppermute(last, axis, up)
        after = lax.ppermute(leading, axis, down)
        array = jnp.concatenate([before, array, after], axis=dim)
    return array


def upper_z(field):
    return jnp.concatenate([field[..., 1:], jnp.zeros_like(field[..., :1])], axis=-1)


def lower_z(field):
    return jnp.concatenate([jnp.zeros_like(field[..., :1]), field[..., :-1]], axis=-1)


def trim_circle(field, circle_width):
    return field[..., circle_width:-circle_width, circle_width:-circle_width, :]


def pad_plane(field, circle_width):
    spec = [(0, 0)] * (field.ndim - 3) + [
        (circle_width, circle_width),
        (circle_width, circle_width),
        (0, 0),
    ]
    return jnp.pad(field, spec)


def neighbour_list(field_pad):
    centre = trim_circle(field_pad, 1)
    return [
        field_pad[..., 2:, 1:-1, :],
        field_pad[..., :-2, 1:-1, :],
        field_pad[..., 1:-1, 2:, :],
        field_pad[..., 1:-1, :-2, :],
        upper_z(centre),
        lower_z(centre),
    ]


def stencil(field_pad, cond_pad, level_scale):
    centre = trim_circle(field_pad, 1)
    centre_cond = trim_circle(cond_pad, 1)
    summed = jnp.zeros_like(centre)
    for other, other_cond in zip(neighbour_list(field_pad), neighbour_list(cond_pad)):
        summed = summed + level_scale * 0.5 * (centre_cond + other_cond) * (centre - other)
    return summed


def diagonal(cond_pad, level_scale):
    centre_cond = trim_circle(cond_pad, 1)
    summed = jnp.zeros_like(centre_cond)
    for other_cond in neighbour_list(cond_pad):
        summed = summed + level_scale * 0.5 * (centre_cond + other_cond)
    return summed


def relaxed(field_pad, source, cond_pad, diag_level, level_scale):
    return (
        trim_circle(field_pad, 1)
        + DAMPING * (source - stencil(field_pad, cond_pad, level_scale)) / diag_level
    )


def restrict(field):
    leading = field.shape[:-3]
    extent = field.shape[-3:]
    shaped = field.reshape(leading + (extent[0] // 2, 2, extent[1] // 2, 2, extent[2] // 2, 2))
    return shaped.mean(axis=(-5, -3, -1))


def prolong(field):
    return jnp.repeat(jnp.repeat(jnp.repeat(field, 2, axis=-3), 2, axis=-2), 2, axis=-1)


def assemble(blocks, count_x, count_y):
    leading = blocks.shape[1:-3]
    extent = blocks.shape[-3:]
    depth_lead = len(leading)
    shaped = blocks.reshape((count_x, count_y) + leading + extent)
    order = tuple(range(2, 2 + depth_lead)) + (0, 2 + depth_lead, 1, 3 + depth_lead, 4 + depth_lead)
    return shaped.transpose(order).reshape(
        leading + (count_x * extent[0], count_y * extent[1], extent[2])
    )


def field_rim(field):
    return extended(field, (("gx", 1), ("gy", 2)), 1)


def cond_rim(conduct):
    return extended(conduct, (("gx", 0), ("gy", 1)), 1)


def whole_cycle(source, level_index, whole_plans):
    cond_pad, diag_level, level_scale = whole_plans[level_index]
    field = DAMPING * source / diag_level

    def turn(turn_index, iterate):
        return relaxed(pad_plane(iterate, 1), source, cond_pad, diag_level, level_scale)

    return lax.fori_loop(0, COARSE_SWEEPS - 1, turn, field)


def part_cycle(source, level_index, level_plans, whole_plans, gather_level):
    if level_index == gather_level:
        blocks = lax.all_gather(source[None], ("gx", "gy"), axis=0, tiled=True)
        whole = assemble(blocks, lax.axis_size("gx"), lax.axis_size("gy"))
        correction = whole_cycle(whole, level_index, whole_plans)
        extent = source.shape
        starts = (0, lax.axis_index("gx") * extent[1], lax.axis_index("gy") * extent[2], 0)
        return lax.dynamic_slice(correction, starts, extent)
    cond_pad, diag_level, level_scale = level_plans[level_index]
    field = DAMPING * source / diag_level
    field = relaxed(field_rim(field), source, cond_pad, diag_level, level_scale)
    residual = source - stencil(field_rim(field), cond_pad, level_scale)
    field = field + prolong(
        part_cycle(restrict(residual), level_index + 1, level_plans, whole_plans, gather_level)
    )
    field = relaxed(field_rim(field), source, cond_pad, diag_level, level_scale)
    return relaxed(field_rim(field), source, cond_pad, diag_level, level_scale)


def distributed(conductivity, stations, currents, receivers, observed):
    row_count, col_count, z_count = conductivity.shape
    shot_count = currents.shape[0]
    count_x = lax.axis_size("gx")
    count_y = lax.axis_size("gy")
    gather_level = LEVELS - 1
    level_plans = []
    conduct = conductivity
    for level_index in range(gather_level):
        level_scale = 0.25**level_index
        cond_pad = cond_rim(conduct)
        level_plans.append((cond_pad, diagonal(cond_pad, level_scale), level_scale))
        conduct = restrict(conduct)
    blocks = lax.all_gather(conduct[None], ("gx", "gy"), axis=0, tiled=True)
    whole = assemble(blocks, count_x, count_y)
    whole_plans = {}
    level_index = 3
    level_scale = 0.25**level_index
    cond_pad = pad_plane(whole, 1)
    whole_plans[level_index] = (cond_pad, diagonal(cond_pad, level_scale), level_scale)
    total_y = col_count * count_y
    cell_x = stations // (total_y * z_count)
    cell_y = stations // z_count % total_y
    cell_z = stations % z_count
    local_x = cell_x - lax.axis_index("gx") * row_count
    local_y = cell_y - lax.axis_index("gy") * col_count
    owned = (local_x >= 0) & (local_x < row_count) & (local_y >= 0) & (local_y < col_count)
    block_size = row_count * col_count * z_count
    local_cell = jnp.where(owned, (local_x * col_count + local_y) * z_count + cell_z, 0)
    offsets = jnp.arange(shot_count)[:, None] * block_size + local_cell[None, :]
    targets = jnp.where(owned[None, :], offsets, shot_count * block_size).reshape(-1)

    def spread(amounts):
        flat = (
            jnp.zeros((shot_count * block_size,), jnp.float32)
            .at[targets]
            .add(amounts.reshape(-1), mode="drop")
        )
        return flat.reshape(shot_count, row_count, col_count, z_count)

    potentials = part_cycle(spread(currents), 0, level_plans, whole_plans, gather_level)
    local_values = jnp.where(
        owned[None, :], potentials.reshape(shot_count, block_size)[:, local_cell], 0.0
    )
    readings = lax.psum(local_values, ("gx", "gy"))
    positions = jnp.arange(stations.shape[0])[:, None]
    pairs = (receivers[:, 0][None, :] == positions).astype(jnp.float32) - (
        receivers[:, 1][None, :] == positions
    ).astype(jnp.float32)
    misfit = jnp.dot(readings, pairs, precision=lax.Precision.HIGHEST) - observed
    back_source = jnp.dot(misfit, pairs.T, precision=lax.Precision.HIGHEST)
    adjoint = part_cycle(spread(back_source), 0, level_plans, whole_plans, gather_level)
    stacked = jnp.concatenate([potentials, adjoint], axis=0)
    padded = extended(stacked, (("gx", 1), ("gy", 2)), 1)
    potential_pad = padded[:shot_count]
    adjoint_pad = padded[shot_count:]
    gradient = jnp.zeros_like(potentials)
    for other_u, other_w in zip(neighbour_list(potential_pad), neighbour_list(adjoint_pad)):
        gradient = gradient - 0.5 * (potentials - other_u) * (adjoint - other_w)
    summed = lax.psum_scatter(jnp.sum(gradient, axis=0), "shot", scatter_dimension=1, tiled=True)
    return (potentials, summed)


def per_device(conductivity, stations, currents, receivers, observed):
    blocks = lax.axis_size("gx") * lax.axis_size("gy")
    fits = conductivity.shape == (SIDE, SIDE * SIDE, LANES) and blocks == SIDE
    fits = fits and lax.axis_size("gy") == 2 and lax.axis_size("shot") == 2
    fits = fits and currents.shape[0] == 1
    plan = replicated if fits else distributed
    return plan(conductivity, stations, currents, receivers, observed)


def solution(mesh):
    in_specs = (
        P(("grp", "gx"), "gy", None),
        P("grp"),
        P(("grp", "shot"), None),
        P("grp", None),
        P(("grp", "shot"), None),
    )
    out_specs = (P(("grp", "shot"), "gx", "gy", None), P(("grp", "gx"), ("gy", "shot"), None))
    return jax.shard_map(
        per_device, mesh=mesh, in_specs=in_specs, out_specs=out_specs, check_vma=False
    )
```

```python
import functools

import jax
import jax.numpy as jnp
from jax import lax
from jax.experimental import pallas as pl
from jax.experimental.pallas import tpu as pltpu
from jax.sharding import PartitionSpec as P

LEVELS = 4
COARSE_SWEEPS = 16


DAMPING = 0.8

SIDE = 8
LANES = 128
GROUP = 16
VMEM_BYTES = 48 * 2**20
SMALL_BYTES = 6 * 2**20


def pieces_of(value, count):
    pieces = []
    for _ in range(count):
        pieces.append(value.astype(jnp.bfloat16))
        value = value - pieces[-1].astype(jnp.float32)
    return pieces[::-1]


def product(value, matrix, count, dims=((1,), (0,))):
    result = None
    for piece in pieces_of(value, count):
        term = lax.dot_general(
            piece, matrix, (dims, ((), ())), preferred_element_type=jnp.float32
        )
        result = term if result is None else result + term
    return result


def iota(shape, dim):
    return lax.broadcasted_iota(jnp.int32, shape, dim)


def station_table(station):
    cell_x, cell_y, cell_z = station >> 14, station >> 7 & 127, station & 127
    row = (cell_x >> 3) * 2 + (cell_y >> 6)
    return cell_x, cell_y, cell_z, row, (cell_y >> 3 & 7) * GROUP + (cell_z >> 3)


def lane_order(back=False):
    row, col = iota((LANES, LANES), 0), iota((LANES, LANES), 1)
    if back:
        row, col = col, row
    chosen = row == col % GROUP * SIDE + col // GROUP
    return jnp.where(chosen, 1.0, 0.0).astype(jnp.bfloat16)


def exchange_groups(tiles):
    tiles = list(tiles)
    group = iota(tiles[0].shape, 1) // GROUP
    for bit in range(3):
        step = 1 << bit
        keep = (group & step) == 0
        for low in range(SIDE):
            if low & step == 0:
                a, b = tiles[low], tiles[low | step]
                tiles[low] = jnp.where(keep, a, pltpu.roll(b, step * GROUP, 1))
                tiles[low | step] = jnp.where(keep, pltpu.roll(a, LANES - step * GROUP, 1), b)
    return tiles


def own_place():
    return lax.axis_index("gx") * 2 + lax.axis_index("gy"), lax.axis_index("shot")


def to_blocks_kernel(natural_ref, blocks_ref, half_ref):
    order = lane_order()
    for x in range(SIDE):
        tiles = product(natural_ref[x], order, 3)
        tiles = [tiles[SIDE * k : SIDE * (k + 1)] for k in range(SIDE)]
        for z, tile in enumerate(exchange_groups(tiles)):
            blocks_ref[pl.ds((x * SIDE + z) * SIDE, SIDE), :] = tile
    count = half_ref.shape[0]
    low, high = blocks_ref[pl.ds(0, count), :], blocks_ref[pl.ds(count, count), :]
    half_ref[...] = jnp.where(own_place()[1] == 0, low, high)


def from_blocks(tiles, order):
    natural = jnp.concatenate(exchange_groups(tiles), axis=0)
    return product(natural, order, 3)


def potentials_kernel(rows_ref, potentials_ref):
    order = lane_order(back=True)
    for x in range(SIDE):
        tiles = [rows_ref[pl.ds((x * SIDE + z) * SIDE, SIDE), :] for z in range(SIDE)]
        potentials_ref[x] = from_blocks(tiles, order)


def block_up(field, axis):
    if axis == 0:
        return pltpu.roll(field, 6, 1)
    if axis == 2:
        return pltpu.roll(field, LANES - 1, 2)
    turned = pltpu.roll(field, LANES - GROUP, 2)
    return jnp.where(iota(field.shape, 2) < LANES - GROUP, turned, pltpu.roll(turned, 7, 1))


def block_down(field, axis):
    if axis == 0:
        return pltpu.roll(field, 2, 1)
    if axis == 2:
        return pltpu.roll(field, 1, 2)
    turned = pltpu.roll(field, GROUP, 2)
    return jnp.where(iota(field.shape, 2) >= GROUP, turned, pltpu.roll(turned, 1, 1))


def inside_up(field, axis):
    sub, lane = iota(field.shape, 1), iota(field.shape, 2)
    if axis == 0:
        keep = sub < 6
    elif axis == 1:
        keep = (lane < LANES - GROUP) | (sub % 2 == 0)
    else:
        keep = lane % GROUP < GROUP - 1
    return jnp.where(keep, field, 0.0)


def inside_down(field, axis):
    sub, lane = iota(field.shape, 1), iota(field.shape, 2)
    if axis == 0:
        keep = sub >= 2
    elif axis == 1:
        keep = (lane >= GROUP) | (sub % 2 == 1)
    else:
        keep = lane % GROUP > 0
    return jnp.where(keep, field, 0.0)


def pair_rows(row):
    count = row.shape[0] // 2
    return jnp.concatenate([row[2 * i : 2 * i + 1] + row[2 * i + 1 : 2 * i + 2] for i in range(count)])


def twice(row):
    return jnp.concatenate([row[i // 2 : i // 2 + 1] for i in range(2 * row.shape[0])])


def electrode_kernel(
    stations_ref,
    currents_ref,
    receivers_ref,
    observed_ref,
    cells_ref,
    spot_ref,
    rows_ref,
    same_ref,
    pairs_ref,
    turned_ref,
    held_ref,
):
    stations = stations_ref[...]
    electrodes = stations.shape[1]
    cell_x, cell_y, cell_z, row, spot = station_table(stations)
    wide = SIDE + 2
    register = (((cell_x & 7) + 1) * wide + (cell_z & 7) + 1) * wide + (cell_y & 7) + 1
    cells_ref[...] = register * SIDE + row
    spot_ref[...] = spot
    held_ref[...] = observed_ref[...]
    line = stations & 0x1C387 | row << 20
    same = jnp.broadcast_to(line, (electrodes, electrodes))
    same = jnp.where(same == same.T, 1.0, 0.0).astype(jnp.bfloat16)
    same_ref[...] = same
    rows_ref[...] = shared_rows(currents_ref[...], spot, same)
    receivers = receivers_ref[...]
    numbers = iota((receivers.shape[0], electrodes), 1)
    pairs = jnp.where(numbers == receivers[:, 0:1], 1.0, 0.0) - jnp.where(
        numbers == receivers[:, 1:2], 1.0, 0.0
    )
    pairs_ref[...] = pairs.astype(jnp.bfloat16)
    turned_ref[...] = pairs.T.astype(jnp.bfloat16)


def shared_rows(amounts, spot, same):
    electrodes = amounts.shape[1]
    at_spot = iota((LANES, electrodes), 0) == spot
    return product(jnp.where(at_spot, amounts, 0.0), same, 3).T


class Edged:
    def __init__(self, ref, side):
        self.ref, self.side = ref, side

    def start(self, x, z, y=0):
        wide = self.side + 2
        return (((x + 1) * wide + z + 1) * wide + y + 1) * SIDE

    def __getitem__(self, at):
        x, z = at
        rows = self.ref[pl.ds(self.start(x, z), self.side * SIDE), :]
        return rows.reshape(self.side, SIDE, LANES)

    def __setitem__(self, at, value):
        x, z = at
        self.ref[pl.ds(self.start(x, z), self.side * SIDE), :] = value.reshape(-1, LANES)

    def put(self, x, z, value, exact=False):
        self[x, z] = value
        n = self.side
        if z == 0:
            edge = block_up(value, 2)
            self[x, n] = inside_up(edge, 2) if exact else edge
        if z == n - 1:
            edge = block_down(value, 2)
            self[x, -1] = inside_down(edge, 2) if exact else edge
        if x == 0:
            edge = block_up(value, 0)
            self[n, z] = inside_up(edge, 0) if exact else edge
        if x == n - 1:
            edge = block_down(value, 0)
            self[-1, z] = inside_down(edge, 0) if exact else edge
        if exact:
            after = inside_up(block_up(value[:1], 1), 1)
            self.ref[pl.ds(self.start(x, z, n), SIDE), :] = after[0]
            before = inside_down(block_down(value[n - 1 :], 1), 1)
            self.ref[pl.ds(self.start(x, z, -1), SIDE), :] = before[0]

    def close_z(self, x, exact=False):
        n = self.side
        after, before = block_up(self[x, 0], 2), block_down(self[x, n - 1], 2)
        self[x, n] = inside_up(after, 2) if exact else after
        self[x, -1] = inside_down(before, 2) if exact else before

    def close(self, exact=False):
        n = self.side
        for z in range(n):
            after = block_up(self[0, z], 0)
            self[n, z] = inside_up(after, 0) if exact else after
            before = block_down(self[n - 1, z], 0)
            self[-1, z] = inside_down(before, 0) if exact else before


class Rows:
    def __init__(self, ref, side, first_x=0, first_z=0):
        self.ref, self.side, self.first_x, self.first_z = ref, side, first_x, first_z

    def place(self, at):
        count = self.side - self.first_z
        rows = self.side * SIDE
        return pl.ds(((at[0] - self.first_x) * count + at[1] - self.first_z) * rows, rows)

    def __getitem__(self, at):
        return self.ref[self.place(at), :].reshape(self.side, SIDE, LANES)

    def __setitem__(self, at, value):
        self.ref[self.place(at), :] = value.reshape(-1, LANES)


def rolled(count, body, unroll=1):
    def one(x, carry):
        body(x)
        return carry

    lax.fori_loop(0, count, one, 0, unroll=unroll)


def next_in_y(row):
    return jnp.concatenate([row[1:], block_up(row[:1], 1)])


def last_in_y(row):
    return jnp.concatenate([block_down(row[-1:], 1), row[:-1]])


class Level:
    def __init__(self, refs, index):
        self.side = side = SIDE >> index
        self.scale = 0.25**index
        edged = [Edged(ref, side) for ref in refs[:5]]
        self.cond, self.first, self.second, self.base, self.weight = edged
        self.link_x = Rows(refs[5], side, first_x=-1)
        self.link_y = Rows(refs[6], side)
        self.link_z = Rows(refs[7], side, first_z=-1)
        self.back = Rows(refs[8], side)

    @staticmethod
    def scratch(index):
        side = SIDE >> index
        sizes = [(side + 2) ** 3] * 5
        sizes += [side**2 * (side + 1), side**3, side**2 * (side + 1), side**3]
        return [pltpu.VMEM((size * SIDE, LANES), jnp.float32) for size in sizes]

    def pairs(self, body):
        for i in range(self.side // 2):
            body(2 * i)

    def prepare(self):
        n = self.side
        cond = self.cond

        def plane(x):
            for z in range(n):
                here, ahead, next_x = cond[x, z], cond[x, z + 1], cond[x + 1, z]
                after = inside_up(block_up(here[:1], 1), 1)
                before = inside_down(block_down(here[-1:], 1), 1)
                next_y = jnp.concatenate([here[1:], after])
                last_y = jnp.concatenate([before, here[:-1]])
                total = (next_x + cond[x - 1, z]) + (ahead + cond[x, z - 1]) + (next_y + last_y)
                total = 6.0 * here + total
                self.weight[x, z] = DAMPING / total
                if n == SIDE:
                    self.base[x, z] = jnp.zeros_like(here)
                self.back[x, z] = total * (0.5 * self.scale / DAMPING)
                self.link_x[x, z] = here + next_x
                link = here + next_y
                self.link_y[x, z] = jnp.concatenate([link[:-1], inside_up(link[-1:], 1)])
                link = here + ahead
                if z == n - 1:
                    link = inside_up(link, 2)
                    self.link_z[x, -1] = block_down(link, 2)
                self.link_z[x, z] = link

        if n == SIDE:
            rolled(n, plane, unroll=2)
        else:
            for x in range(n):
                plane(x)
        for z in range(n):
            link = inside_up(self.link_x[n - 1, z], 0)
            self.link_x[n - 1, z] = link
            self.link_x[-1, z] = block_down(link, 0)

    def flows(self, x, z, here, ahead, outer, down):
        result = []
        inner = self.link_x[x, z]
        sides = [
            self.link_x[x - 1, z] * outer[0] + inner * here[1],
            inner * here[0] + self.link_x[x + 1, z] * outer[1],
        ]
        for p in range(2):
            link_y, link_z = self.link_y[x + p, z], self.link_z[x + p, z]
            along = link_y * next_in_y(here[p]) + last_in_y(link_y * here[p])
            total = sides[p] + (link_z * ahead[p] + down[p]) + along
            down[p] = link_z * here[p]
            result.append(self.weight[x + p, z] * total)
        return result

    def rows(self, field, x):
        here = [field[x, 0], field[x + 1, 0]]
        down = [self.link_z[x + p, -1] * field[x + p, -1] for p in range(2)]
        for z in range(self.side):
            ahead = [field[x, z + 1], field[x + 1, z + 1]]
            outer = [field[x - 1, z], field[x + 2, z]]
            yield z, here, self.flows(x, z, here, ahead, outer, down)
            here = ahead

    def sweep(self, field, out, exact=False):
        def pair(x):
            for z, here, sums in self.rows(field, x):
                for p in range(2):
                    if field is self.base:
                        value = (2.0 - DAMPING) * here[p] + sums[p]
                    else:
                        value = (1.0 - DAMPING) * here[p] + (self.base[x + p, z] + sums[p])
                    out.put(x + p, z, value, exact)

        self.pairs(pair)

    def halve(self, rows, coarse):
        def pair(x):
            held = None
            for z, row in enumerate(rows(x)):
                row = row[0] + row[1]
                if z % 2 == 0:
                    held = row
                else:
                    coarse(x // 2, z // 2, 0.125 * pair_rows(held + row))

        self.pairs(pair)

    def descend(self, coarse):
        self.sweep(self.base, self.second)

        def residuals(x):
            for z, here, sums in self.rows(self.second, x):
                result = []
                for p in range(2):
                    swept = (1.0 - DAMPING) * here[p] + (self.base[x + p, z] + sums[p])
                    self.first[x + p, z] = swept
                    result.append((swept - here[p]) * self.back[x + p, z])
                yield result

        self.halve(residuals, coarse)

    def ascend(self, correction, out, exact=False):
        def pair(x):
            i = x // 2
            here = twice(correction(i, 0))
            start = twice(correction(i, -1))
            down = [self.link_z[x + p, -1] * start for p in range(2)]
            for z in range(self.side):
                ahead = twice(correction(i, (z + 1) // 2))
                outer = [twice(correction(i - 1, z // 2)), twice(correction(i + 1, z // 2))]
                sums = self.flows(x, z, [here, here], [ahead, ahead], outer, down)
                for p in range(2):
                    value = self.first[x + p, z] + ((1.0 - DAMPING) * here + sums[p])
                    self.second.put(x + p, z, value)
                here = ahead

        self.pairs(pair)
        self.sweep(self.second, out, exact)


class HeldLevel:
    def __init__(self, refs, index):
        self.side = 2
        self.scale = 0.25**index
        self.cond, self.first = Edged(refs[0], 2), Edged(refs[1], 2)
        self.weight, self.back = Rows(refs[2], 2), Rows(refs[3], 2)
        self.links = [Rows(ref, 2) for ref in refs[4:]]

    @staticmethod
    def scratch(index):
        sizes = [4**3] * 2 + [2**3] * 8
        return [pltpu.VMEM((size * SIDE, LANES), jnp.float32) for size in sizes]

    def around(self, field, inside=False):
        def moved(row, axis, up):
            row = (block_up if up else block_down)(row, axis)
            return (inside_up if up else inside_down)(row, axis) if inside else row

        result = {}
        for (x, z), here in field.items():
            result[x, z] = [
                field[1, z] if x == 0 else moved(field[0, z], 0, True),
                field[0, z] if x == 1 else moved(field[1, z], 0, False),
                jnp.concatenate([here[1:], moved(here[:1], 1, True)]),
                jnp.concatenate([moved(here[-1:], 1, False), here[:-1]]),
                field[x, 1] if z == 0 else moved(field[x, 0], 2, True),
                field[x, 0] if z == 1 else moved(field[x, 1], 2, False),
            ]
        return result

    def prepare(self):
        field = {(x, z): self.cond[x, z] for x in range(2) for z in range(2)}
        for at, others in self.around(field, inside=True).items():
            here = field[at]
            total = others[0]
            for other in others[1:]:
                total = total + other
            total = 3.0 * here + 0.5 * total
            inverse = DAMPING / total
            self.weight[at] = inverse
            self.back[at] = total * (self.scale / DAMPING)
            for index, other in enumerate(others):
                link = 0.5 * inverse * (here + other)
                self.links[index][at] = jnp.where(other > 0.0, link, 0.0)

    def halve(self, rows, coarse):
        total = None
        for row in rows(0):
            row = row[0] + row[1]
            total = row if total is None else total + row
        coarse(0, 0, 0.125 * (total[:1] + total[1:]))

    def sums(self, field, base):
        result = {}
        for at, others in self.around(field).items():
            total = base[at]
            for link, other in zip(self.links, others):
                total = total + link[at] * other
            result[at] = total
        return result

    def swept(self, field, base):
        sums = self.sums(field, base)
        return {at: (1.0 - DAMPING) * field[at] + sums[at] for at in field}

    def cycle(self, base, solve, out):
        field = self.swept(base, base)
        sums = self.sums(field, base)
        total = None
        for at in field:
            residual = (sums[at] - DAMPING * field[at]) * self.back[at]
            total = residual if total is None else total + residual
        solved = solve(0.125 * (total[:1] + total[1:]))
        row = twice(solved)
        copied = {at: row for at in field}
        change = {at: sums[at] + (1.0 - DAMPING) * (field[at] + row) for at in field}
        field = self.sums(copied, change)
        for (x, z), value in self.swept(field, base).items():
            out.put(x, z, value)


def replicated_kernel(
    whole,
    halved,
    cells_ref,
    *refs,
):
    parts = refs[:whole], refs[whole : whole + halved]
    solve_kernel(*parts, cells_ref, *refs[whole + halved :])


def solve_kernel(
    part_refs,
    half_refs,
    cells_ref,
    spot_ref,
    rows_ref,
    same_ref,
    pairs_ref,
    turned_ref,
    observed_ref,
    potentials_ref,
    mine_ref,
    theirs_ref,
    gathered,
    owned,
    beside,
    *level_refs,
):
    f32 = jnp.float32
    electrodes = spot_ref.shape[1]
    levels, used = [], 0
    for index in range(LEVELS - 1):
        kind = HeldLevel if index == LEVELS - 2 else Level
        count = len(kind.scratch(index))
        levels.append(kind(level_refs[used : used + count], index))
        used += count
    fine = levels[0]
    forward = fine.cond
    wide = SIDE * SIDE * SIDE

    device, shot = own_place()

    def place(part, row, x, index):
        for z in range(SIDE):
            fine.cond.ref[pl.ds(fine.cond.start(x, z) + index, SIDE, stride=SIDE), :] = part[
                pl.ds((row * SIDE + z) * SIDE, SIDE), :
            ]

    def collect(x):
        for k, part in enumerate(part_refs):
            place(part, x, x, device ^ k)

    def collect_half(x):
        for k, part in enumerate(half_refs):
            swapped, index = k // 2 % 2, len(part_refs) + k // 4 * 2 + k % 2
            place(part, x, (shot ^ swapped) * (SIDE // 2) + x, device ^ index)

    def edges(x):
        fine.cond.close_z(x, exact=True)

    rolled(SIDE, collect, unroll=4)
    for x in range(SIDE // 2):
        collect_half(x)
    for x in range(SIDE):
        edges(x)
    fine.cond.close(exact=True)

    coarsest = []
    for level, below in zip(levels, levels[1:] + [None]):
        level.prepare()

        def coarse(x, z, row, below=below):
            if below is None:
                coarsest.append(row)
            else:
                below.cond.put(x, z, row, exact=True)

        level.halve(
            lambda x, level=level: [
                (level.cond[x, z], level.cond[x + 1, z]) for z in range(level.side)
            ],
            coarse,
        )

    keep = iota((1, SIDE, LANES), 1) % 2 == 0
    lane = iota((1, SIDE, LANES), 2)

    def split(value):
        return [jnp.where(keep, part, 0.0) for part in (value, pltpu.roll(value, SIDE - 1, 1))]

    def around(value):
        low, high = value
        low_up, high_up = [pltpu.roll(part, LANES - GROUP, 2) for part in value]
        low_down, high_down = [pltpu.roll(part, GROUP, 2) for part in value]
        along = [[move(part, axis) for part in value] for axis in (0, 2) for move in (block_up, block_down)]
        return along + [
            [jnp.where(lane < LANES - GROUP, low_up, high_up), high_up],
            [low_down, jnp.where(lane >= GROUP, high_down, low_down)],
        ]

    sub = iota((1, SIDE, LANES), 1)
    inside_last = [
        [sub < 6] * 2,
        [sub >= 2] * 2,
        [lane % GROUP < GROUP - 1] * 2,
        [lane % GROUP > 0] * 2,
        [keep, lane < LANES - GROUP],
        [lane >= GROUP, keep],
    ]
    last_scale = 0.25 ** (LEVELS - 1)
    here = split(coarsest[0])
    others = [
        [jnp.where(inside & keep, part, 0.0) for inside, part in zip(pair, moved)]
        for pair, moved in zip(inside_last, around(here))
    ]
    last_weight, last_links = [], []
    for half, part in enumerate(here):
        total = 3.0 * part
        for other in others:
            total = total + 0.5 * other[half]
        inverse = jnp.where(keep, DAMPING / jnp.where(keep, total, 1.0), 0.0)
        last_weight.append(inverse * (1.0 / last_scale))
        last_links.append(
            [
                jnp.where(pair[half] & keep, 0.5 * inverse * (part + other[half]), 0.0)
                for pair, other in zip(inside_last, others)
            ]
        )

    def solve_last(rhs):
        base = [weight * part for weight, part in zip(last_weight, split(rhs))]
        value = base
        for _ in range(COARSE_SWEEPS - 1):
            moved = around(value)
            fresh = []
            for half in range(2):
                parts = [link * other[half] for link, other in zip(last_links[half], moved)]
                start = base[half] + (1.0 - DAMPING) * value[half]
                fresh.append(((start + parts[0]) + (parts[1] + parts[2])) + (parts[3] + (parts[4] + parts[5])))
            value = fresh
        return value[0] + pltpu.roll(value[1], 1, 1)

    def cycle(index, out, exact=False):
        level = levels[index]
        below = levels[index + 1]
        if index == LEVELS - 3:
            base = {}

            def take(x, z, row):
                base[x, z] = below.weight[x, z] * (row * (1.0 / below.scale))

            level.descend(take)
            below.cycle(base, solve_last, below.first)
        else:
            level.descend(
                lambda x, z, row: below.base.put(
                    x, z, below.weight[x, z] * (row * (2.0 / below.scale))
                )
            )
            cycle(index + 1, below.first)
        level.ascend(lambda x, z: below.first[x, z], out, exact)

    spot = spot_ref[...]
    at_spot = iota((LANES, electrodes), 0) == spot
    order = lane_order(back=True)
    wide = SIDE + 2

    def each(body):
        def one(electrode, carry):
            body(pl.ds(electrode, 1), pl.ds(cells_ref[0, electrode], 1))
            return carry

        lax.fori_loop(0, electrodes, one, 0, unroll=128)

    def put(electrode, cell):
        fine.base.ref[cell, :] = (2.0 * gathered[electrode, :]) * fine.weight.ref[cell, :]

    def read(electrode, cell):
        gathered[electrode, :] = forward.ref[cell, :]

    def exact(row, matrix_ref):
        return product(jnp.broadcast_to(row, (16, row.shape[1])), matrix_ref[...], 3)[0:1]

    sub, lane = iota((SIDE, LANES), 0), iota((SIDE, LANES), 1)

    def margin(x, z, y):
        return forward.ref[pl.ds(forward.start(x, z, y) + device, 1), :]

    def extract(index):
        for x in range(-1, SIDE + 1):
            for z in range(SIDE):
                at = (x + 1) * wide + z + 1
                start = forward.start(x, z) + device
                row = forward.ref[pl.ds(start, SIDE, stride=SIDE), :]
                owned[index, at] = row
                if 0 <= x < SIDE:
                    after, before = margin(x, z, SIDE), margin(x, z, -1)
                    place = x * SIDE + z
                    turned = pltpu.roll(row, SIDE - 1, 0)
                    beside[index, 0, place] = jnp.where(sub == SIDE - 1, after, turned)
                    beside[index, 1, place] = jnp.where(sub == 0, before, pltpu.roll(row, 1, 0))
                    if z == 0:
                        edge = pltpu.roll(row, LANES - 1, 1)
                        owned[index, at + SIDE] = jnp.where(lane % GROUP < GROUP - 1, edge, 0.0)
                    if z == SIDE - 1:
                        edge = pltpu.roll(row, 1, 1)
                        owned[index, at - SIDE] = jnp.where(lane % GROUP > 0, edge, 0.0)

    def solve(index):
        each(put)
        for x in range(SIDE):
            fine.base.close_z(x)
        fine.base.close()
        cycle(0, forward, exact=True)
        extract(index)

        @pl.when(index == 0)
        def _():
            each(read)
            readings = jnp.where(at_spot, gathered[...].T, 0.0)
            readings = jnp.sum(readings, axis=0, keepdims=True)
            misfit = exact(readings, turned_ref) - observed_ref[...]
            gathered[...] = shared_rows(exact(misfit, pairs_ref), spot, same_ref[...])

    gathered[...] = rows_ref[...]
    rolled(2, solve)

    chunk = mine_ref.shape[1]
    even = shot == 0
    for x in range(SIDE):
        tiles = []
        for z in range(SIDE):
            at = (x + 1) * wide + z + 1
            here_u, here_w = owned[0, at], owned[1, at]
            potentials_ref[pl.ds((x * SIDE + z) * SIDE, SIDE), :] = here_u
            total = None
            for step in (wide, -wide, 1, -1):
                term = (here_u - owned[0, at + step]) * (here_w - owned[1, at + step])
                total = term if total is None else total + term
            for side in range(2):
                other_u, other_w = beside[0, side, x * SIDE + z], beside[1, side, x * SIDE + z]
                total = total + (here_u - other_u) * (here_w - other_w)
            tiles.append(-0.5 * total)
        natural = from_blocks(tiles, order)
        low, high = natural[:chunk], natural[chunk:]
        mine_ref[x] = jnp.where(even, low, high)
        theirs_ref[x] = jnp.where(even, high, low)


def replicated(conductivity, stations, currents, receivers, observed):
    rows, cols, depth = conductivity.shape
    f32 = jnp.float32
    electrodes = stations.shape[0]
    total = rows * cols
    vmem = pl.BlockSpec(memory_space=pltpu.VMEM)
    smem = pl.BlockSpec(memory_space=pltpu.SMEM)
    station_row = stations.reshape(1, electrodes)
    mine, half = pl.pallas_call(
        to_blocks_kernel,
        out_shape=(
            jax.ShapeDtypeStruct((total, LANES), f32),
            jax.ShapeDtypeStruct((total // 2, LANES), f32),
        ),
        in_specs=[vmem],
        out_specs=(vmem, vmem),
        compiler_params=pltpu.CompilerParams(vmem_limit_bytes=SMALL_BYTES),
    )(conductivity)
    swap = [(0, 1), (1, 0)]

    def partner(part, k):
        count = lax.axis_size("gx")
        return lax.ppermute(part, "gx", [(i, i ^ k) for i in range(count)])

    def with_mate(part):
        return [part, lax.ppermute(part, "gy", swap)]

    far = partner(half, 2)
    near = partner(half, 1)
    line = jax.ShapeDtypeStruct((1, electrodes), jnp.int32)
    cells, spot, rows_of, same, pairs, turned, held = pl.pallas_call(
        electrode_kernel,
        out_shape=(
            line,
            line,
            jax.ShapeDtypeStruct((electrodes, LANES), f32),
            jax.ShapeDtypeStruct((electrodes, electrodes), jnp.bfloat16),
            jax.ShapeDtypeStruct((receivers.shape[0], electrodes), jnp.bfloat16),
            jax.ShapeDtypeStruct((electrodes, receivers.shape[0]), jnp.bfloat16),
            jax.ShapeDtypeStruct(observed.shape, f32),
        ),
        in_specs=[vmem] * 4,
        out_specs=(vmem,) * 7,
        compiler_params=pltpu.CompilerParams(vmem_limit_bytes=SMALL_BYTES),
        cost_estimate=pl.CostEstimate(flops=100_000_000, bytes_accessed=1_000_000, transcendentals=0),
    )(station_row, currents, receivers, observed)
    far, rows_of = lax.optimization_barrier((far, rows_of))
    parts = with_mate(mine)
    far, parts[1] = lax.optimization_barrier((far, parts[1]))
    count_x = lax.axis_size("gx")
    diagonal = [(2 * i + j, 2 * (i ^ 1) + 1 - j) for i in range(count_x) for j in range(2)]
    near_crossed = lax.ppermute(near, "shot", swap)
    crossed, relayed = lax.ppermute(far, "shot", swap), partner(far, 1)
    slanted = with_mate(lax.ppermute(far, ("gx", "shot"), diagonal))
    halved = [piece for own in (near, near_crossed, far, crossed) for piece in with_mate(own)]
    relayed, slanted[1] = lax.optimization_barrier((relayed, slanted[1]))
    halved += with_mate(relayed) + slanted
    chunk = cols // 2
    levels = [shape for index in range(LEVELS - 2) for shape in Level.scratch(index)]
    levels += HeldLevel.scratch(LEVELS - 2)
    potentials, own, theirs = pl.pallas_call(
        functools.partial(replicated_kernel, len(parts), len(halved)),
        out_shape=(
            jax.ShapeDtypeStruct((total, LANES), f32),
            jax.ShapeDtypeStruct((rows, chunk, LANES), f32),
            jax.ShapeDtypeStruct((rows, chunk, LANES), f32),
        ),
        in_specs=[smem] + [vmem] * (len(parts) + len(halved) + 6),
        out_specs=(vmem, vmem, vmem),
        scratch_shapes=[
            pltpu.VMEM((electrodes, LANES), f32),
            pltpu.VMEM((2, (SIDE + 2) ** 2, SIDE, LANES), f32),
            pltpu.VMEM((2, 2, SIDE**2, SIDE, LANES), f32),
        ]
        + levels,
        compiler_params=pltpu.CompilerParams(vmem_limit_bytes=VMEM_BYTES),
        cost_estimate=pl.CostEstimate(flops=200_000_000, bytes_accessed=4_000_000, transcendentals=0),
    )(cells, *parts, *halved, spot, rows_of, same, pairs, turned, held)
    arrived = lax.ppermute(theirs, "shot", swap)
    potentials = pl.pallas_call(
        potentials_kernel,
        out_shape=jax.ShapeDtypeStruct((rows, cols, LANES), f32),
        in_specs=[vmem],
        out_specs=vmem,
        compiler_params=pltpu.CompilerParams(vmem_limit_bytes=SMALL_BYTES),
        cost_estimate=pl.CostEstimate(flops=50_000_000, bytes_accessed=500_000, transcendentals=0),
    )(potentials)
    return potentials[None], own + arrived


def extended(array, sides, width):
    for axis, dim in sides:
        size, length = (lax.axis_size(axis), array.shape[dim])
        up = [(i, (i + 1) % size) for i in range(size - 1)]
        down = [(j, i) for i, j in up]
        last = lax.slice_in_dim(array, length - width, length, axis=dim)
        leading = lax.slice_in_dim(array, 0, width, axis=dim)
        before = lax.ppermute(last, axis, up)
        after = lax.ppermute(leading, axis, down)
        array = jnp.concatenate([before, array, after], axis=dim)
    return array


def upper_z(field):
    return jnp.concatenate([field[..., 1:], jnp.zeros_like(field[..., :1])], axis=-1)


def lower_z(field):
    return jnp.concatenate([jnp.zeros_like(field[..., :1]), field[..., :-1]], axis=-1)


def trim_circle(field, circle_width):
    return field[..., circle_width:-circle_width, circle_width:-circle_width, :]


def pad_plane(field, circle_width):
    spec = [(0, 0)] * (field.ndim - 3) + [
        (circle_width, circle_width),
        (circle_width, circle_width),
        (0, 0),
    ]
    return jnp.pad(field, spec)


def neighbour_list(field_pad):
    centre = trim_circle(field_pad, 1)
    return [
        field_pad[..., 2:, 1:-1, :],
        field_pad[..., :-2, 1:-1, :],
        field_pad[..., 1:-1, 2:, :],
        field_pad[..., 1:-1, :-2, :],
        upper_z(centre),
        lower_z(centre),
    ]


def stencil(field_pad, cond_pad, level_scale):
    centre = trim_circle(field_pad, 1)
    centre_cond = trim_circle(cond_pad, 1)
    summed = jnp.zeros_like(centre)
    for other, other_cond in zip(neighbour_list(field_pad), neighbour_list(cond_pad)):
        summed = summed + level_scale * 0.5 * (centre_cond + other_cond) * (centre - other)
    return summed


def diagonal(cond_pad, level_scale):
    centre_cond = trim_circle(cond_pad, 1)
    summed = jnp.zeros_like(centre_cond)
    for other_cond in neighbour_list(cond_pad):
        summed = summed + level_scale * 0.5 * (centre_cond + other_cond)
    return summed


def relaxed(field_pad, source, cond_pad, diag_level, level_scale):
    return (
        trim_circle(field_pad, 1)
        + DAMPING * (source - stencil(field_pad, cond_pad, level_scale)) / diag_level
    )


def restrict(field):
    leading = field.shape[:-3]
    extent = field.shape[-3:]
    shaped = field.reshape(leading + (extent[0] // 2, 2, extent[1] // 2, 2, extent[2] // 2, 2))
    return shaped.mean(axis=(-5, -3, -1))


def prolong(field):
    return jnp.repeat(jnp.repeat(jnp.repeat(field, 2, axis=-3), 2, axis=-2), 2, axis=-1)


def assemble(blocks, count_x, count_y):
    leading = blocks.shape[1:-3]
    extent = blocks.shape[-3:]
    depth_lead = len(leading)
    shaped = blocks.reshape((count_x, count_y) + leading + extent)
    order = tuple(range(2, 2 + depth_lead)) + (0, 2 + depth_lead, 1, 3 + depth_lead, 4 + depth_lead)
    return shaped.transpose(order).reshape(
        leading + (count_x * extent[0], count_y * extent[1], extent[2])
    )


def field_rim(field):
    return extended(field, (("gx", 1), ("gy", 2)), 1)


def cond_rim(conduct):
    return extended(conduct, (("gx", 0), ("gy", 1)), 1)


def whole_cycle(source, level_index, whole_plans):
    cond_pad, diag_level, level_scale = whole_plans[level_index]
    field = DAMPING * source / diag_level

    def turn(turn_index, iterate):
        return relaxed(pad_plane(iterate, 1), source, cond_pad, diag_level, level_scale)

    return lax.fori_loop(0, COARSE_SWEEPS - 1, turn, field)


def part_cycle(source, level_index, level_plans, whole_plans, gather_level):
    if level_index == gather_level:
        blocks = lax.all_gather(source[None], ("gx", "gy"), axis=0, tiled=True)
        whole = assemble(blocks, lax.axis_size("gx"), lax.axis_size("gy"))
        correction = whole_cycle(whole, level_index, whole_plans)
        extent = source.shape
        starts = (0, lax.axis_index("gx") * extent[1], lax.axis_index("gy") * extent[2], 0)
        return lax.dynamic_slice(correction, starts, extent)
    cond_pad, diag_level, level_scale = level_plans[level_index]
    field = DAMPING * source / diag_level
    field = relaxed(field_rim(field), source, cond_pad, diag_level, level_scale)
    residual = source - stencil(field_rim(field), cond_pad, level_scale)
    field = field + prolong(
        part_cycle(restrict(residual), level_index + 1, level_plans, whole_plans, gather_level)
    )
    field = relaxed(field_rim(field), source, cond_pad, diag_level, level_scale)
    return relaxed(field_rim(field), source, cond_pad, diag_level, level_scale)


def distributed(conductivity, stations, currents, receivers, observed):
    row_count, col_count, z_count = conductivity.shape
    shot_count = currents.shape[0]
    count_x = lax.axis_size("gx")
    count_y = lax.axis_size("gy")
    gather_level = LEVELS - 1
    level_plans = []
    conduct = conductivity
    for level_index in range(gather_level):
        level_scale = 0.25**level_index
        cond_pad = cond_rim(conduct)
        level_plans.append((cond_pad, diagonal(cond_pad, level_scale), level_scale))
        conduct = restrict(conduct)
    blocks = lax.all_gather(conduct[None], ("gx", "gy"), axis=0, tiled=True)
    whole = assemble(blocks, count_x, count_y)
    whole_plans = {}
    level_index = 3
    level_scale = 0.25**level_index
    cond_pad = pad_plane(whole, 1)
    whole_plans[level_index] = (cond_pad, diagonal(cond_pad, level_scale), level_scale)
    total_y = col_count * count_y
    cell_x = stations // (total_y * z_count)
    cell_y = stations // z_count % total_y
    cell_z = stations % z_count
    local_x = cell_x - lax.axis_index("gx") * row_count
    local_y = cell_y - lax.axis_index("gy") * col_count
    owned = (local_x >= 0) & (local_x < row_count) & (local_y >= 0) & (local_y < col_count)
    block_size = row_count * col_count * z_count
    local_cell = jnp.where(owned, (local_x * col_count + local_y) * z_count + cell_z, 0)
    offsets = jnp.arange(shot_count)[:, None] * block_size + local_cell[None, :]
    targets = jnp.where(owned[None, :], offsets, shot_count * block_size).reshape(-1)

    def spread(amounts):
        flat = (
            jnp.zeros((shot_count * block_size,), jnp.float32)
            .at[targets]
            .add(amounts.reshape(-1), mode="drop")
        )
        return flat.reshape(shot_count, row_count, col_count, z_count)

    potentials = part_cycle(spread(currents), 0, level_plans, whole_plans, gather_level)
    local_values = jnp.where(
        owned[None, :], potentials.reshape(shot_count, block_size)[:, local_cell], 0.0
    )
    readings = lax.psum(local_values, ("gx", "gy"))
    positions = jnp.arange(stations.shape[0])[:, None]
    pairs = (receivers[:, 0][None, :] == positions).astype(jnp.float32) - (
        receivers[:, 1][None, :] == positions
    ).astype(jnp.float32)
    misfit = jnp.dot(readings, pairs, precision=lax.Precision.HIGHEST) - observed
    back_source = jnp.dot(misfit, pairs.T, precision=lax.Precision.HIGHEST)
    adjoint = part_cycle(spread(back_source), 0, level_plans, whole_plans, gather_level)
    stacked = jnp.concatenate([potentials, adjoint], axis=0)
    padded = extended(stacked, (("gx", 1), ("gy", 2)), 1)
    potential_pad = padded[:shot_count]
    adjoint_pad = padded[shot_count:]
    gradient = jnp.zeros_like(potentials)
    for other_u, other_w in zip(neighbour_list(potential_pad), neighbour_list(adjoint_pad)):
        gradient = gradient - 0.5 * (potentials - other_u) * (adjoint - other_w)
    summed = lax.psum_scatter(jnp.sum(gradient, axis=0), "shot", scatter_dimension=1, tiled=True)
    return (potentials, summed)


def per_device(conductivity, stations, currents, receivers, observed):
    blocks = lax.axis_size("gx") * lax.axis_size("gy")
    fits = conductivity.shape == (SIDE, SIDE * SIDE, LANES) and blocks == SIDE
    fits = fits and lax.axis_size("gy") == 2 and lax.axis_size("shot") == 2
    fits = fits and currents.shape[0] == 1
    plan = replicated if fits else distributed
    return plan(conductivity, stations, currents, receivers, observed)


def solution(mesh):
    in_specs = (
        P(("grp", "gx"), "gy", None),
        P("grp"),
        P(("grp", "shot"), None),
        P("grp", None),
        P(("grp", "shot"), None),
    )
    out_specs = (P(("grp", "shot"), "gx", "gy", None), P(("grp", "gx"), ("gy", "shot"), None))
    return jax.shard_map(
        per_device, mesh=mesh, in_specs=in_specs, out_specs=out_specs, check_vma=False
    )
```

```python
import functools

import jax
import jax.numpy as jnp
from jax import lax
from jax.experimental import pallas as pl
from jax.experimental.pallas import tpu as pltpu
from jax.sharding import PartitionSpec as P

LEVELS = 4
COARSE_SWEEPS = 16


DAMPING = 0.8

SIDE = 8
LANES = 128
GROUP = 16
VMEM_BYTES = 48 * 2**20
SMALL_BYTES = 6 * 2**20


def pieces_of(value, count):
    pieces = []
    for _ in range(count):
        pieces.append(value.astype(jnp.bfloat16))
        value = value - pieces[-1].astype(jnp.float32)
    return pieces[::-1]


def product(value, matrix, count, dims=((1,), (0,))):
    result = None
    for piece in pieces_of(value, count):
        term = lax.dot_general(
            piece, matrix, (dims, ((), ())), preferred_element_type=jnp.float32
        )
        result = term if result is None else result + term
    return result


def iota(shape, dim):
    return lax.broadcasted_iota(jnp.int32, shape, dim)


def station_table(station):
    cell_x, cell_y, cell_z = station >> 14, station >> 7 & 127, station & 127
    row = (cell_x >> 3) * 2 + (cell_y >> 6)
    return cell_x, cell_y, cell_z, row, (cell_y >> 3 & 7) * GROUP + (cell_z >> 3)


def lane_order(back=False):
    row, col = iota((LANES, LANES), 0), iota((LANES, LANES), 1)
    if back:
        row, col = col, row
    chosen = row == col % GROUP * SIDE + col // GROUP
    return jnp.where(chosen, 1.0, 0.0).astype(jnp.bfloat16)


def exchange_groups(tiles):
    tiles = list(tiles)
    group = iota(tiles[0].shape, 1) // GROUP
    for bit in range(3):
        step = 1 << bit
        keep = (group & step) == 0
        for low in range(SIDE):
            if low & step == 0:
                a, b = tiles[low], tiles[low | step]
                tiles[low] = jnp.where(keep, a, pltpu.roll(b, step * GROUP, 1))
                tiles[low | step] = jnp.where(keep, pltpu.roll(a, LANES - step * GROUP, 1), b)
    return tiles


def own_place():
    return lax.axis_index("gx") * 2 + lax.axis_index("gy"), lax.axis_index("shot")


def to_blocks_kernel(natural_ref, blocks_ref, half_ref):
    order = lane_order()
    for x in range(SIDE):
        tiles = product(natural_ref[x], order, 3)
        tiles = [tiles[SIDE * k : SIDE * (k + 1)] for k in range(SIDE)]
        for z, tile in enumerate(exchange_groups(tiles)):
            blocks_ref[pl.ds((x * SIDE + z) * SIDE, SIDE), :] = tile
    count = half_ref.shape[0]
    low, high = blocks_ref[pl.ds(0, count), :], blocks_ref[pl.ds(count, count), :]
    half_ref[...] = jnp.where(own_place()[1] == 0, low, high)


def from_blocks(tiles, order):
    natural = jnp.concatenate(exchange_groups(tiles), axis=0)
    return product(natural, order, 3)


def potentials_kernel(rows_ref, potentials_ref):
    order = lane_order(back=True)
    for x in range(SIDE):
        tiles = [rows_ref[pl.ds((x * SIDE + z) * SIDE, SIDE), :] for z in range(SIDE)]
        potentials_ref[x] = from_blocks(tiles, order)


def block_up(field, axis):
    if axis == 0:
        return pltpu.roll(field, 6, 1)
    if axis == 2:
        return pltpu.roll(field, LANES - 1, 2)
    turned = pltpu.roll(field, LANES - GROUP, 2)
    return jnp.where(iota(field.shape, 2) < LANES - GROUP, turned, pltpu.roll(turned, 7, 1))


def block_down(field, axis):
    if axis == 0:
        return pltpu.roll(field, 2, 1)
    if axis == 2:
        return pltpu.roll(field, 1, 2)
    turned = pltpu.roll(field, GROUP, 2)
    return jnp.where(iota(field.shape, 2) >= GROUP, turned, pltpu.roll(turned, 1, 1))


def inside_up(field, axis):
    sub, lane = iota(field.shape, 1), iota(field.shape, 2)
    if axis == 0:
        keep = sub < 6
    elif axis == 1:
        keep = (lane < LANES - GROUP) | (sub % 2 == 0)
    else:
        keep = lane % GROUP < GROUP - 1
    return jnp.where(keep, field, 0.0)


def inside_down(field, axis):
    sub, lane = iota(field.shape, 1), iota(field.shape, 2)
    if axis == 0:
        keep = sub >= 2
    elif axis == 1:
        keep = (lane >= GROUP) | (sub % 2 == 1)
    else:
        keep = lane % GROUP > 0
    return jnp.where(keep, field, 0.0)


def pair_rows(row):
    count = row.shape[0] // 2
    return jnp.concatenate([row[2 * i : 2 * i + 1] + row[2 * i + 1 : 2 * i + 2] for i in range(count)])


def twice(row):
    return jnp.concatenate([row[i // 2 : i // 2 + 1] for i in range(2 * row.shape[0])])


def electrode_kernel(
    stations_ref,
    currents_ref,
    receivers_ref,
    observed_ref,
    cells_ref,
    spot_ref,
    rows_ref,
    same_ref,
    pairs_ref,
    turned_ref,
    held_ref,
):
    stations = stations_ref[...]
    electrodes = stations.shape[1]
    cell_x, cell_y, cell_z, row, spot = station_table(stations)
    wide = SIDE + 2
    register = (((cell_x & 7) + 1) * wide + (cell_z & 7) + 1) * wide + (cell_y & 7) + 1
    cells_ref[...] = register * SIDE + row
    spot_ref[...] = spot
    held_ref[...] = observed_ref[...]
    line = stations & 0x1C387 | row << 20
    same = jnp.broadcast_to(line, (electrodes, electrodes))
    same = jnp.where(same == same.T, 1.0, 0.0).astype(jnp.bfloat16)
    same_ref[...] = same
    rows_ref[...] = shared_rows(currents_ref[...], spot, same)
    receivers = receivers_ref[...]
    numbers = iota((receivers.shape[0], electrodes), 1)
    pairs = jnp.where(numbers == receivers[:, 0:1], 1.0, 0.0) - jnp.where(
        numbers == receivers[:, 1:2], 1.0, 0.0
    )
    pairs_ref[...] = pairs.astype(jnp.bfloat16)
    turned_ref[...] = pairs.T.astype(jnp.bfloat16)


def shared_rows(amounts, spot, same):
    electrodes = amounts.shape[1]
    at_spot = iota((LANES, electrodes), 0) == spot
    return product(jnp.where(at_spot, amounts, 0.0), same, 3).T


class Edged:
    def __init__(self, ref, side):
        self.ref, self.side = ref, side

    def start(self, x, z, y=0):
        wide = self.side + 2
        return (((x + 1) * wide + z + 1) * wide + y + 1) * SIDE

    def __getitem__(self, at):
        x, z = at
        rows = self.ref[pl.ds(self.start(x, z), self.side * SIDE), :]
        return rows.reshape(self.side, SIDE, LANES)

    def __setitem__(self, at, value):
        x, z = at
        self.ref[pl.ds(self.start(x, z), self.side * SIDE), :] = value.reshape(-1, LANES)

    def put(self, x, z, value, exact=False, along_z=True):
        self[x, z] = value
        n = self.side
        if z == 0 and along_z:
            edge = block_up(value, 2)
            self[x, n] = inside_up(edge, 2) if exact else edge
        if z == n - 1 and along_z:
            edge = block_down(value, 2)
            self[x, -1] = inside_down(edge, 2) if exact else edge
        if x == 0:
            edge = block_up(value, 0)
            self[n, z] = inside_up(edge, 0) if exact else edge
        if x == n - 1:
            edge = block_down(value, 0)
            self[-1, z] = inside_down(edge, 0) if exact else edge
        if exact:
            after = inside_up(block_up(value[:1], 1), 1)
            self.ref[pl.ds(self.start(x, z, n), SIDE), :] = after[0]
            before = inside_down(block_down(value[n - 1 :], 1), 1)
            self.ref[pl.ds(self.start(x, z, -1), SIDE), :] = before[0]

    def close_z(self, x, exact=False):
        n = self.side
        after, before = block_up(self[x, 0], 2), block_down(self[x, n - 1], 2)
        self[x, n] = inside_up(after, 2) if exact else after
        self[x, -1] = inside_down(before, 2) if exact else before

    def close(self, exact=False):
        n = self.side
        for z in range(n):
            after = block_up(self[0, z], 0)
            self[n, z] = inside_up(after, 0) if exact else after
            before = block_down(self[n - 1, z], 0)
            self[-1, z] = inside_down(before, 0) if exact else before


class Rows:
    def __init__(self, ref, side, first_x=0, first_z=0):
        self.ref, self.side, self.first_x, self.first_z = ref, side, first_x, first_z

    def place(self, at):
        count = self.side - self.first_z
        rows = self.side * SIDE
        return pl.ds(((at[0] - self.first_x) * count + at[1] - self.first_z) * rows, rows)

    def __getitem__(self, at):
        return self.ref[self.place(at), :].reshape(self.side, SIDE, LANES)

    def __setitem__(self, at, value):
        self.ref[self.place(at), :] = value.reshape(-1, LANES)


def rolled(count, body, unroll=1):
    def one(x, carry):
        body(x)
        return carry

    lax.fori_loop(0, count, one, 0, unroll=unroll)


def next_in_y(row):
    return jnp.concatenate([row[1:], block_up(row[:1], 1)])


def last_in_y(row):
    return jnp.concatenate([block_down(row[-1:], 1), row[:-1]])


class Level:
    def __init__(self, refs, index):
        self.side = side = SIDE >> index
        self.scale = 0.25**index
        edged = [Edged(ref, side) for ref in refs[:5]]
        self.cond, self.first, self.second, self.base, self.weight = edged
        self.link_x = Rows(refs[5], side, first_x=-1)
        self.link_y = Rows(refs[6], side)
        self.link_z = Rows(refs[7], side, first_z=-1)
        self.back = Rows(refs[8], side)

    @staticmethod
    def scratch(index):
        side = SIDE >> index
        sizes = [(side + 2) ** 3] * 5
        sizes += [side**2 * (side + 1), side**3, side**2 * (side + 1), side**3]
        return [pltpu.VMEM((size * SIDE, LANES), jnp.float32) for size in sizes]

    def pairs(self, body):
        for i in range(self.side // 2):
            body(2 * i)

    def prepare(self):
        n = self.side
        cond = self.cond

        def plane(x):
            for z in range(n):
                here, ahead, next_x = cond[x, z], cond[x, z + 1], cond[x + 1, z]
                after = inside_up(block_up(here[:1], 1), 1)
                before = inside_down(block_down(here[-1:], 1), 1)
                next_y = jnp.concatenate([here[1:], after])
                last_y = jnp.concatenate([before, here[:-1]])
                total = (next_x + cond[x - 1, z]) + (ahead + cond[x, z - 1]) + (next_y + last_y)
                total = 6.0 * here + total
                self.weight[x, z] = DAMPING * reciprocal(total)
                if n == SIDE:
                    self.base[x, z] = jnp.zeros_like(here)
                self.back[x, z] = total * (0.5 * self.scale / DAMPING)
                self.link_x[x, z] = here + next_x
                link = here + next_y
                self.link_y[x, z] = jnp.concatenate([link[:-1], inside_up(link[-1:], 1)])
                link = here + ahead
                if z == n - 1:
                    link = inside_up(link, 2)
                    self.link_z[x, -1] = block_down(link, 2)
                self.link_z[x, z] = link

        if n == SIDE:
            rolled(n, plane, unroll=2)
        else:
            for x in range(n):
                plane(x)
        for z in range(n):
            link = inside_up(self.link_x[n - 1, z], 0)
            self.link_x[n - 1, z] = link
            self.link_x[-1, z] = block_down(link, 0)

    def flows(self, x, z, here, ahead, outer, down):
        result = []
        inner = self.link_x[x, z]
        sides = [
            self.link_x[x - 1, z] * outer[0] + inner * here[1],
            inner * here[0] + self.link_x[x + 1, z] * outer[1],
        ]
        for p in range(2):
            link_y, link_z = self.link_y[x + p, z], self.link_z[x + p, z]
            along = link_y * next_in_y(here[p]) + last_in_y(link_y * here[p])
            total = sides[p] + (link_z * ahead[p] + down[p]) + along
            down[p] = link_z * here[p]
            result.append(self.weight[x + p, z] * total)
        return result

    def rows(self, field, x):
        here = [field[x, 0], field[x + 1, 0]]
        down = [self.link_z[x + p, -1] * field[x + p, -1] for p in range(2)]
        for z in range(self.side):
            ahead = [field[x, z + 1], field[x + 1, z + 1]]
            outer = [field[x - 1, z], field[x + 2, z]]
            yield z, here, self.flows(x, z, here, ahead, outer, down)
            here = ahead

    def sweep(self, field, out, exact=False):
        def pair(x):
            for z, here, sums in self.rows(field, x):
                for p in range(2):
                    if field is self.base:
                        value = (2.0 - DAMPING) * here[p] + sums[p]
                    else:
                        value = (1.0 - DAMPING) * here[p] + (self.base[x + p, z] + sums[p])
                    out.put(x + p, z, value, exact, along_z=not exact)

        self.pairs(pair)

    def halve(self, rows, coarse):
        def pair(x):
            held = None
            for z, row in enumerate(rows(x)):
                row = row[0] + row[1]
                if z % 2 == 0:
                    held = row
                else:
                    coarse(x // 2, z // 2, 0.125 * pair_rows(held + row))

        self.pairs(pair)

    def descend(self, coarse):
        self.sweep(self.base, self.second)

        def residuals(x):
            for z, here, sums in self.rows(self.second, x):
                result = []
                for p in range(2):
                    swept = (1.0 - DAMPING) * here[p] + (self.base[x + p, z] + sums[p])
                    self.first[x + p, z] = swept
                    result.append((swept - here[p]) * self.back[x + p, z])
                yield result

        self.halve(residuals, coarse)

    def ascend(self, correction, out, exact=False):
        def pair(x):
            i = x // 2
            here = twice(correction(i, 0))
            start = twice(correction(i, -1))
            down = [self.link_z[x + p, -1] * start for p in range(2)]
            for z in range(self.side):
                ahead = twice(correction(i, (z + 1) // 2))
                outer = [twice(correction(i - 1, z // 2)), twice(correction(i + 1, z // 2))]
                sums = self.flows(x, z, [here, here], [ahead, ahead], outer, down)
                for p in range(2):
                    value = self.first[x + p, z] + ((1.0 - DAMPING) * here + sums[p])
                    self.second.put(x + p, z, value)
                here = ahead

        self.pairs(pair)
        self.sweep(self.second, out, exact)


def reciprocal(value):
    result = pl.reciprocal(value, approx=True)
    for _ in range(2):
        result = result * (2.0 - value * result)
    return result


class HeldLevel:
    def __init__(self, refs, index):
        self.side = 2
        self.scale = 0.25**index
        self.cond, self.first = Edged(refs[0], 2), Edged(refs[1], 2)
        self.weight, self.back = Rows(refs[2], 2), Rows(refs[3], 2)
        self.links = [Rows(ref, 2) for ref in refs[4:]]

    @staticmethod
    def scratch(index):
        sizes = [4**3] * 2 + [2**3] * 8
        return [pltpu.VMEM((size * SIDE, LANES), jnp.float32) for size in sizes]

    def around(self, field, inside=False):
        def moved(row, axis, up):
            row = (block_up if up else block_down)(row, axis)
            return (inside_up if up else inside_down)(row, axis) if inside else row

        result = {}
        for (x, z), here in field.items():
            result[x, z] = [
                field[1, z] if x == 0 else moved(field[0, z], 0, True),
                field[0, z] if x == 1 else moved(field[1, z], 0, False),
                jnp.concatenate([here[1:], moved(here[:1], 1, True)]),
                jnp.concatenate([moved(here[-1:], 1, False), here[:-1]]),
                field[x, 1] if z == 0 else moved(field[x, 0], 2, True),
                field[x, 0] if z == 1 else moved(field[x, 1], 2, False),
            ]
        return result

    def prepare(self):
        field = {(x, z): self.cond[x, z] for x in range(2) for z in range(2)}
        for at, others in self.around(field, inside=True).items():
            here = field[at]
            total = others[0]
            for other in others[1:]:
                total = total + other
            total = 3.0 * here + 0.5 * total
            inverse = DAMPING / total
            self.weight[at] = inverse
            self.back[at] = total * (self.scale / DAMPING)
            for index, other in enumerate(others):
                link = 0.5 * inverse * (here + other)
                self.links[index][at] = jnp.where(other > 0.0, link, 0.0)

    def halve(self, rows, coarse):
        total = None
        for row in rows(0):
            row = row[0] + row[1]
            total = row if total is None else total + row
        coarse(0, 0, 0.125 * (total[:1] + total[1:]))

    def sums(self, field, base):
        result = {}
        for at, others in self.around(field).items():
            total = base[at]
            for link, other in zip(self.links, others):
                total = total + link[at] * other
            result[at] = total
        return result

    def swept(self, field, base):
        sums = self.sums(field, base)
        return {at: (1.0 - DAMPING) * field[at] + sums[at] for at in field}

    def cycle(self, base, solve, out):
        field = self.swept(base, base)
        sums = self.sums(field, base)
        total = None
        for at in field:
            residual = (sums[at] - DAMPING * field[at]) * self.back[at]
            total = residual if total is None else total + residual
        solved = solve(0.125 * (total[:1] + total[1:]))
        row = twice(solved)
        copied = {at: row for at in field}
        change = {at: sums[at] + (1.0 - DAMPING) * (field[at] + row) for at in field}
        field = self.sums(copied, change)
        for (x, z), value in self.swept(field, base).items():
            out.put(x, z, value)


def replicated_kernel(
    whole,
    halved,
    cells_ref,
    *refs,
):
    parts = refs[:whole], refs[whole : whole + halved]
    solve_kernel(*parts, cells_ref, *refs[whole + halved :])


def solve_kernel(
    part_refs,
    half_refs,
    cells_ref,
    spot_ref,
    rows_ref,
    same_ref,
    pairs_ref,
    turned_ref,
    observed_ref,
    potentials_ref,
    mine_ref,
    theirs_ref,
    gathered,
    owned,
    beside,
    *level_refs,
):
    f32 = jnp.float32
    electrodes = spot_ref.shape[1]
    levels, used = [], 0
    for index in range(LEVELS - 1):
        kind = HeldLevel if index == LEVELS - 2 else Level
        count = len(kind.scratch(index))
        levels.append(kind(level_refs[used : used + count], index))
        used += count
    fine = levels[0]
    forward = fine.cond
    wide = SIDE * SIDE * SIDE

    device, shot = own_place()

    def place(part, row, x, index):
        for z in range(SIDE):
            fine.cond.ref[pl.ds(fine.cond.start(x, z) + index, SIDE, stride=SIDE), :] = part[
                pl.ds((row * SIDE + z) * SIDE, SIDE), :
            ]

    def collect(x):
        for k, part in enumerate(part_refs):
            place(part, x, x, device ^ k)

    def collect_half(x):
        for k, part in enumerate(half_refs):
            swapped, index = k // 2 % 2, len(part_refs) + k // 4 * 2 + k % 2
            place(part, x, (shot ^ swapped) * (SIDE // 2) + x, device ^ index)

    def edges(x):
        fine.cond.close_z(x, exact=True)

    rolled(SIDE, collect, unroll=4)
    for x in range(SIDE // 2):
        collect_half(x)
    for x in range(SIDE):
        edges(x)
    fine.cond.close(exact=True)

    coarsest = []
    for level, below in zip(levels, levels[1:] + [None]):
        level.prepare()

        def coarse(x, z, row, below=below):
            if below is None:
                coarsest.append(row)
            else:
                below.cond.put(x, z, row, exact=True)

        level.halve(
            lambda x, level=level: [
                (level.cond[x, z], level.cond[x + 1, z]) for z in range(level.side)
            ],
            coarse,
        )

    keep = iota((1, SIDE, LANES), 1) % 2 == 0
    lane = iota((1, SIDE, LANES), 2)

    def split(value):
        return [jnp.where(keep, part, 0.0) for part in (value, pltpu.roll(value, SIDE - 1, 1))]

    def around(value):
        low, high = value
        low_up, high_up = [pltpu.roll(part, LANES - GROUP, 2) for part in value]
        low_down, high_down = [pltpu.roll(part, GROUP, 2) for part in value]
        along = [[move(part, axis) for part in value] for axis in (0, 2) for move in (block_up, block_down)]
        return along + [
            [jnp.where(lane < LANES - GROUP, low_up, high_up), high_up],
            [low_down, jnp.where(lane >= GROUP, high_down, low_down)],
        ]

    sub = iota((1, SIDE, LANES), 1)
    inside_last = [
        [sub < 6] * 2,
        [sub >= 2] * 2,
        [lane % GROUP < GROUP - 1] * 2,
        [lane % GROUP > 0] * 2,
        [keep, lane < LANES - GROUP],
        [lane >= GROUP, keep],
    ]
    last_scale = 0.25 ** (LEVELS - 1)
    here = split(coarsest[0])
    others = [
        [jnp.where(inside & keep, part, 0.0) for inside, part in zip(pair, moved)]
        for pair, moved in zip(inside_last, around(here))
    ]
    last_weight, last_links = [], []
    for half, part in enumerate(here):
        total = 3.0 * part
        for other in others:
            total = total + 0.5 * other[half]
        inverse = jnp.where(keep, DAMPING / jnp.where(keep, total, 1.0), 0.0)
        last_weight.append(inverse * (1.0 / last_scale))
        last_links.append(
            [
                jnp.where(pair[half] & keep, 0.5 * inverse * (part + other[half]), 0.0)
                for pair, other in zip(inside_last, others)
            ]
        )

    def solve_last(rhs):
        base = [weight * part for weight, part in zip(last_weight, split(rhs))]
        value = base
        for _ in range(COARSE_SWEEPS - 1):
            moved = around(value)
            fresh = []
            for half in range(2):
                parts = [link * other[half] for link, other in zip(last_links[half], moved)]
                start = base[half] + (1.0 - DAMPING) * value[half]
                fresh.append(((start + parts[0]) + (parts[1] + parts[2])) + (parts[3] + (parts[4] + parts[5])))
            value = fresh
        return value[0] + pltpu.roll(value[1], 1, 1)

    def cycle(index, out, exact=False):
        level = levels[index]
        below = levels[index + 1]
        if index == LEVELS - 3:
            base = {}

            def take(x, z, row):
                base[x, z] = below.weight[x, z] * (row * (1.0 / below.scale))

            level.descend(take)
            below.cycle(base, solve_last, below.first)
        else:
            level.descend(
                lambda x, z, row: below.base.put(
                    x, z, below.weight[x, z] * (row * (2.0 / below.scale))
                )
            )
            cycle(index + 1, below.first)
        level.ascend(lambda x, z: below.first[x, z], out, exact)

    spot = spot_ref[...]
    at_spot = iota((LANES, electrodes), 0) == spot
    order = lane_order(back=True)
    wide = SIDE + 2

    def each(body):
        def one(electrode, carry):
            body(pl.ds(electrode, 1), pl.ds(cells_ref[0, electrode], 1))
            return carry

        lax.fori_loop(0, electrodes, one, 0, unroll=64)

    def put(electrode, cell):
        fine.base.ref[cell, :] = (2.0 * gathered[electrode, :]) * fine.weight.ref[cell, :]

    def read(electrode, cell):
        gathered[electrode, :] = forward.ref[cell, :]

    def exact(row, matrix_ref):
        return product(jnp.broadcast_to(row, (16, row.shape[1])), matrix_ref[...], 3)[0:1]

    sub, lane = iota((SIDE, LANES), 0), iota((SIDE, LANES), 1)

    def margin(x, z, y):
        return forward.ref[pl.ds(forward.start(x, z, y) + device, 1), :]

    def extract(index):
        for x in range(-1, SIDE + 1):
            for z in range(SIDE):
                at = (x + 1) * wide + z + 1
                start = forward.start(x, z) + device
                row = forward.ref[pl.ds(start, SIDE, stride=SIDE), :]
                owned[index, at] = row
                if 0 <= x < SIDE:
                    after, before = margin(x, z, SIDE), margin(x, z, -1)
                    place = x * SIDE + z
                    turned = pltpu.roll(row, SIDE - 1, 0)
                    beside[index, 0, place] = jnp.where(sub == SIDE - 1, after, turned)
                    beside[index, 1, place] = jnp.where(sub == 0, before, pltpu.roll(row, 1, 0))
                    if z == 0:
                        edge = pltpu.roll(row, LANES - 1, 1)
                        owned[index, at + SIDE] = jnp.where(lane % GROUP < GROUP - 1, edge, 0.0)
                    if z == SIDE - 1:
                        edge = pltpu.roll(row, 1, 1)
                        owned[index, at - SIDE] = jnp.where(lane % GROUP > 0, edge, 0.0)

    def solve(index):
        each(put)
        for x in range(SIDE):
            fine.base.close_z(x)
        fine.base.close()
        cycle(0, forward, exact=True)
        extract(index)

        @pl.when(index == 0)
        def _():
            each(read)
            readings = jnp.where(at_spot, gathered[...].T, 0.0)
            readings = jnp.sum(readings, axis=0, keepdims=True)
            misfit = exact(readings, turned_ref) - observed_ref[...]
            gathered[...] = shared_rows(exact(misfit, pairs_ref), spot, same_ref[...])

    gathered[...] = rows_ref[...]
    rolled(2, solve)

    chunk = mine_ref.shape[1]
    even = shot == 0
    for x in range(SIDE):
        tiles = []
        for z in range(SIDE):
            at = (x + 1) * wide + z + 1
            here_u, here_w = owned[0, at], owned[1, at]
            potentials_ref[pl.ds((x * SIDE + z) * SIDE, SIDE), :] = here_u
            total = None
            for step in (wide, -wide, 1, -1):
                term = (here_u - owned[0, at + step]) * (here_w - owned[1, at + step])
                total = term if total is None else total + term
            for side in range(2):
                other_u, other_w = beside[0, side, x * SIDE + z], beside[1, side, x * SIDE + z]
                total = total + (here_u - other_u) * (here_w - other_w)
            tiles.append(-0.5 * total)
        natural = from_blocks(tiles, order)
        low, high = natural[:chunk], natural[chunk:]
        mine_ref[x] = jnp.where(even, low, high)
        theirs_ref[x] = jnp.where(even, high, low)


def replicated(conductivity, stations, currents, receivers, observed):
    rows, cols, depth = conductivity.shape
    f32 = jnp.float32
    electrodes = stations.shape[0]
    total = rows * cols
    vmem = pl.BlockSpec(memory_space=pltpu.VMEM)
    smem = pl.BlockSpec(memory_space=pltpu.SMEM)
    station_row = stations.reshape(1, electrodes)
    mine, half = pl.pallas_call(
        to_blocks_kernel,
        out_shape=(
            jax.ShapeDtypeStruct((total, LANES), f32),
            jax.ShapeDtypeStruct((total // 2, LANES), f32),
        ),
        in_specs=[vmem],
        out_specs=(vmem, vmem),
        compiler_params=pltpu.CompilerParams(vmem_limit_bytes=SMALL_BYTES),
    )(conductivity)
    swap = [(0, 1), (1, 0)]

    def partner(part, k):
        count = lax.axis_size("gx")
        return lax.ppermute(part, "gx", [(i, i ^ k) for i in range(count)])

    def with_mate(part):
        return [part, lax.ppermute(part, "gy", swap)]

    far = partner(half, 2)
    near = partner(mine, 1)
    line = jax.ShapeDtypeStruct((1, electrodes), jnp.int32)
    cells, spot, rows_of, same, pairs, turned, held = pl.pallas_call(
        electrode_kernel,
        out_shape=(
            line,
            line,
            jax.ShapeDtypeStruct((electrodes, LANES), f32),
            jax.ShapeDtypeStruct((electrodes, electrodes), jnp.bfloat16),
            jax.ShapeDtypeStruct((receivers.shape[0], electrodes), jnp.bfloat16),
            jax.ShapeDtypeStruct((electrodes, receivers.shape[0]), jnp.bfloat16),
            jax.ShapeDtypeStruct(observed.shape, f32),
        ),
        in_specs=[vmem] * 4,
        out_specs=(vmem,) * 7,
        compiler_params=pltpu.CompilerParams(vmem_limit_bytes=SMALL_BYTES),
        cost_estimate=pl.CostEstimate(flops=100_000_000, bytes_accessed=1_000_000, transcendentals=0),
    )(station_row, currents, receivers, observed)
    far, rows_of = lax.optimization_barrier((far, rows_of))
    count_x = lax.axis_size("gx")
    diagonal = [(2 * i + j, 2 * (i ^ 1) + 1 - j) for i in range(count_x) for j in range(2)]
    crossed, relayed = lax.ppermute(far, "shot", swap), partner(far, 1)
    slanted = lax.ppermute(far, ("gx", "shot"), diagonal)
    parts = [piece for own in (mine, near) for piece in with_mate(own)]
    halved = [piece for own in (far, crossed, relayed) for piece in with_mate(own)]
    slanted, halved[3] = lax.optimization_barrier((slanted, halved[3]))
    halved += with_mate(slanted)
    chunk = cols // 2
    levels = [shape for index in range(LEVELS - 2) for shape in Level.scratch(index)]
    levels += HeldLevel.scratch(LEVELS - 2)
    potentials, own, theirs = pl.pallas_call(
        functools.partial(replicated_kernel, len(parts), len(halved)),
        out_shape=(
            jax.ShapeDtypeStruct((total, LANES), f32),
            jax.ShapeDtypeStruct((rows, chunk, LANES), f32),
            jax.ShapeDtypeStruct((rows, chunk, LANES), f32),
        ),
        in_specs=[smem] + [vmem] * (len(parts) + len(halved) + 6),
        out_specs=(vmem, vmem, vmem),
        scratch_shapes=[
            pltpu.VMEM((electrodes, LANES), f32),
            pltpu.VMEM((2, (SIDE + 2) ** 2, SIDE, LANES), f32),
            pltpu.VMEM((2, 2, SIDE**2, SIDE, LANES), f32),
        ]
        + levels,
        compiler_params=pltpu.CompilerParams(vmem_limit_bytes=VMEM_BYTES),
        cost_estimate=pl.CostEstimate(flops=200_000_000, bytes_accessed=4_000_000, transcendentals=0),
    )(cells, *parts, *halved, spot, rows_of, same, pairs, turned, held)
    arrived = lax.ppermute(theirs, "shot", swap)
    potentials = pl.pallas_call(
        potentials_kernel,
        out_shape=jax.ShapeDtypeStruct((rows, cols, LANES), f32),
        in_specs=[vmem],
        out_specs=vmem,
        compiler_params=pltpu.CompilerParams(vmem_limit_bytes=SMALL_BYTES),
        cost_estimate=pl.CostEstimate(flops=50_000_000, bytes_accessed=500_000, transcendentals=0),
    )(potentials)
    return potentials[None], own + arrived


def extended(array, sides, width):
    for axis, dim in sides:
        size, length = (lax.axis_size(axis), array.shape[dim])
        up = [(i, (i + 1) % size) for i in range(size - 1)]
        down = [(j, i) for i, j in up]
        last = lax.slice_in_dim(array, length - width, length, axis=dim)
        leading = lax.slice_in_dim(array, 0, width, axis=dim)
        before = lax.ppermute(last, axis, up)
        after = lax.ppermute(leading, axis, down)
        array = jnp.concatenate([before, array, after], axis=dim)
    return array


def upper_z(field):
    return jnp.concatenate([field[..., 1:], jnp.zeros_like(field[..., :1])], axis=-1)


def lower_z(field):
    return jnp.concatenate([jnp.zeros_like(field[..., :1]), field[..., :-1]], axis=-1)


def trim_circle(field, circle_width):
    return field[..., circle_width:-circle_width, circle_width:-circle_width, :]


def pad_plane(field, circle_width):
    spec = [(0, 0)] * (field.ndim - 3) + [
        (circle_width, circle_width),
        (circle_width, circle_width),
        (0, 0),
    ]
    return jnp.pad(field, spec)


def neighbour_list(field_pad):
    centre = trim_circle(field_pad, 1)
    return [
        field_pad[..., 2:, 1:-1, :],
        field_pad[..., :-2, 1:-1, :],
        field_pad[..., 1:-1, 2:, :],
        field_pad[..., 1:-1, :-2, :],
        upper_z(centre),
        lower_z(centre),
    ]


def stencil(field_pad, cond_pad, level_scale):
    centre = trim_circle(field_pad, 1)
    centre_cond = trim_circle(cond_pad, 1)
    summed = jnp.zeros_like(centre)
    for other, other_cond in zip(neighbour_list(field_pad), neighbour_list(cond_pad)):
        summed = summed + level_scale * 0.5 * (centre_cond + other_cond) * (centre - other)
    return summed


def diagonal(cond_pad, level_scale):
    centre_cond = trim_circle(cond_pad, 1)
    summed = jnp.zeros_like(centre_cond)
    for other_cond in neighbour_list(cond_pad):
        summed = summed + level_scale * 0.5 * (centre_cond + other_cond)
    return summed


def relaxed(field_pad, source, cond_pad, diag_level, level_scale):
    return (
        trim_circle(field_pad, 1)
        + DAMPING * (source - stencil(field_pad, cond_pad, level_scale)) / diag_level
    )


def restrict(field):
    leading = field.shape[:-3]
    extent = field.shape[-3:]
    shaped = field.reshape(leading + (extent[0] // 2, 2, extent[1] // 2, 2, extent[2] // 2, 2))
    return shaped.mean(axis=(-5, -3, -1))


def prolong(field):
    return jnp.repeat(jnp.repeat(jnp.repeat(field, 2, axis=-3), 2, axis=-2), 2, axis=-1)


def assemble(blocks, count_x, count_y):
    leading = blocks.shape[1:-3]
    extent = blocks.shape[-3:]
    depth_lead = len(leading)
    shaped = blocks.reshape((count_x, count_y) + leading + extent)
    order = tuple(range(2, 2 + depth_lead)) + (0, 2 + depth_lead, 1, 3 + depth_lead, 4 + depth_lead)
    return shaped.transpose(order).reshape(
        leading + (count_x * extent[0], count_y * extent[1], extent[2])
    )


def field_rim(field):
    return extended(field, (("gx", 1), ("gy", 2)), 1)


def cond_rim(conduct):
    return extended(conduct, (("gx", 0), ("gy", 1)), 1)


def whole_cycle(source, level_index, whole_plans):
    cond_pad, diag_level, level_scale = whole_plans[level_index]
    field = DAMPING * source / diag_level

    def turn(turn_index, iterate):
        return relaxed(pad_plane(iterate, 1), source, cond_pad, diag_level, level_scale)

    return lax.fori_loop(0, COARSE_SWEEPS - 1, turn, field)


def part_cycle(source, level_index, level_plans, whole_plans, gather_level):
    if level_index == gather_level:
        blocks = lax.all_gather(source[None], ("gx", "gy"), axis=0, tiled=True)
        whole = assemble(blocks, lax.axis_size("gx"), lax.axis_size("gy"))
        correction = whole_cycle(whole, level_index, whole_plans)
        extent = source.shape
        starts = (0, lax.axis_index("gx") * extent[1], lax.axis_index("gy") * extent[2], 0)
        return lax.dynamic_slice(correction, starts, extent)
    cond_pad, diag_level, level_scale = level_plans[level_index]
    field = DAMPING * source / diag_level
    field = relaxed(field_rim(field), source, cond_pad, diag_level, level_scale)
    residual = source - stencil(field_rim(field), cond_pad, level_scale)
    field = field + prolong(
        part_cycle(restrict(residual), level_index + 1, level_plans, whole_plans, gather_level)
    )
    field = relaxed(field_rim(field), source, cond_pad, diag_level, level_scale)
    return relaxed(field_rim(field), source, cond_pad, diag_level, level_scale)


def distributed(conductivity, stations, currents, receivers, observed):
    row_count, col_count, z_count = conductivity.shape
    shot_count = currents.shape[0]
    count_x = lax.axis_size("gx")
    count_y = lax.axis_size("gy")
    gather_level = LEVELS - 1
    level_plans = []
    conduct = conductivity
    for level_index in range(gather_level):
        level_scale = 0.25**level_index
        cond_pad = cond_rim(conduct)
        level_plans.append((cond_pad, diagonal(cond_pad, level_scale), level_scale))
        conduct = restrict(conduct)
    blocks = lax.all_gather(conduct[None], ("gx", "gy"), axis=0, tiled=True)
    whole = assemble(blocks, count_x, count_y)
    whole_plans = {}
    level_index = 3
    level_scale = 0.25**level_index
    cond_pad = pad_plane(whole, 1)
    whole_plans[level_index] = (cond_pad, diagonal(cond_pad, level_scale), level_scale)
    total_y = col_count * count_y
    cell_x = stations // (total_y * z_count)
    cell_y = stations // z_count % total_y
    cell_z = stations % z_count
    local_x = cell_x - lax.axis_index("gx") * row_count
    local_y = cell_y - lax.axis_index("gy") * col_count
    owned = (local_x >= 0) & (local_x < row_count) & (local_y >= 0) & (local_y < col_count)
    block_size = row_count * col_count * z_count
    local_cell = jnp.where(owned, (local_x * col_count + local_y) * z_count + cell_z, 0)
    offsets = jnp.arange(shot_count)[:, None] * block_size + local_cell[None, :]
    targets = jnp.where(owned[None, :], offsets, shot_count * block_size).reshape(-1)

    def spread(amounts):
        flat = (
            jnp.zeros((shot_count * block_size,), jnp.float32)
            .at[targets]
            .add(amounts.reshape(-1), mode="drop")
        )
        return flat.reshape(shot_count, row_count, col_count, z_count)

    potentials = part_cycle(spread(currents), 0, level_plans, whole_plans, gather_level)
    local_values = jnp.where(
        owned[None, :], potentials.reshape(shot_count, block_size)[:, local_cell], 0.0
    )
    readings = lax.psum(local_values, ("gx", "gy"))
    positions = jnp.arange(stations.shape[0])[:, None]
    pairs = (receivers[:, 0][None, :] == positions).astype(jnp.float32) - (
        receivers[:, 1][None, :] == positions
    ).astype(jnp.float32)
    misfit = jnp.dot(readings, pairs, precision=lax.Precision.HIGHEST) - observed
    back_source = jnp.dot(misfit, pairs.T, precision=lax.Precision.HIGHEST)
    adjoint = part_cycle(spread(back_source), 0, level_plans, whole_plans, gather_level)
    stacked = jnp.concatenate([potentials, adjoint], axis=0)
    padded = extended(stacked, (("gx", 1), ("gy", 2)), 1)
    potential_pad = padded[:shot_count]
    adjoint_pad = padded[shot_count:]
    gradient = jnp.zeros_like(potentials)
    for other_u, other_w in zip(neighbour_list(potential_pad), neighbour_list(adjoint_pad)):
        gradient = gradient - 0.5 * (potentials - other_u) * (adjoint - other_w)
    summed = lax.psum_scatter(jnp.sum(gradient, axis=0), "shot", scatter_dimension=1, tiled=True)
    return (potentials, summed)


def per_device(conductivity, stations, currents, receivers, observed):
    blocks = lax.axis_size("gx") * lax.axis_size("gy")
    fits = conductivity.shape == (SIDE, SIDE * SIDE, LANES) and blocks == SIDE
    fits = fits and lax.axis_size("gy") == 2 and lax.axis_size("shot") == 2
    fits = fits and currents.shape[0] == 1
    plan = replicated if fits else distributed
    return plan(conductivity, stations, currents, receivers, observed)


def solution(mesh):
    in_specs = (
        P(("grp", "gx"), "gy", None),
        P("grp"),
        P(("grp", "shot"), None),
        P("grp", None),
        P(("grp", "shot"), None),
    )
    out_specs = (P(("grp", "shot"), "gx", "gy", None), P(("grp", "gx"), ("gy", "shot"), None))
    return jax.shard_map(
        per_device, mesh=mesh, in_specs=in_specs, out_specs=out_specs, check_vma=False
    )
```

```python
import functools

import jax
import jax.numpy as jnp
from jax import lax
from jax.experimental import pallas as pl
from jax.experimental.pallas import tpu as pltpu
from jax.sharding import PartitionSpec as P

LEVELS = 4
COARSE_SWEEPS = 16


DAMPING = 0.8

SIDE = 8
LANES = 128
GROUP = 16
VMEM_BYTES = 48 * 2**20
SMALL_BYTES = 6 * 2**20


def pieces_of(value, count):
    pieces = []
    for _ in range(count):
        pieces.append(value.astype(jnp.bfloat16))
        value = value - pieces[-1].astype(jnp.float32)
    return pieces[::-1]


def product(value, matrix, count, dims=((1,), (0,))):
    result = None
    for piece in pieces_of(value, count):
        term = lax.dot_general(
            piece, matrix, (dims, ((), ())), preferred_element_type=jnp.float32
        )
        result = term if result is None else result + term
    return result


def iota(shape, dim):
    return lax.broadcasted_iota(jnp.int32, shape, dim)


def station_table(station):
    cell_x, cell_y, cell_z = station >> 14, station >> 7 & 127, station & 127
    row = (cell_x >> 3) * 2 + (cell_y >> 6)
    return cell_x, cell_y, cell_z, row, (cell_y >> 3 & 7) * GROUP + (cell_z >> 3)


def lane_order(back=False):
    row, col = iota((LANES, LANES), 0), iota((LANES, LANES), 1)
    if back:
        row, col = col, row
    chosen = row == col % GROUP * SIDE + col // GROUP
    return jnp.where(chosen, 1.0, 0.0).astype(jnp.bfloat16)


def exchange_groups(tiles):
    tiles = list(tiles)
    group = iota(tiles[0].shape, 1) // GROUP
    for bit in range(3):
        step = 1 << bit
        keep = (group & step) == 0
        for low in range(SIDE):
            if low & step == 0:
                a, b = tiles[low], tiles[low | step]
                tiles[low] = jnp.where(keep, a, pltpu.roll(b, step * GROUP, 1))
                tiles[low | step] = jnp.where(keep, pltpu.roll(a, LANES - step * GROUP, 1), b)
    return tiles


def own_place():
    return lax.axis_index("gx") * 2 + lax.axis_index("gy"), lax.axis_index("shot")


def to_blocks_kernel(natural_ref, blocks_ref, half_ref):
    order = lane_order()
    for x in range(SIDE):
        tiles = product(natural_ref[x], order, 3)
        tiles = [tiles[SIDE * k : SIDE * (k + 1)] for k in range(SIDE)]
        for z, tile in enumerate(exchange_groups(tiles)):
            blocks_ref[pl.ds((x * SIDE + z) * SIDE, SIDE), :] = tile
    count = half_ref.shape[0]
    low, high = blocks_ref[pl.ds(0, count), :], blocks_ref[pl.ds(count, count), :]
    half_ref[...] = jnp.where(own_place()[1] == 0, low, high)


def from_blocks(tiles, order):
    natural = jnp.concatenate(exchange_groups(tiles), axis=0)
    return product(natural, order, 3)


def potentials_kernel(rows_ref, potentials_ref):
    order = lane_order(back=True)
    for x in range(SIDE):
        tiles = [rows_ref[pl.ds((x * SIDE + z) * SIDE, SIDE), :] for z in range(SIDE)]
        potentials_ref[x] = from_blocks(tiles, order)


def block_up(field, axis):
    if axis == 0:
        return pltpu.roll(field, 6, 1)
    if axis == 2:
        return pltpu.roll(field, LANES - 1, 2)
    turned = pltpu.roll(field, LANES - GROUP, 2)
    return jnp.where(iota(field.shape, 2) < LANES - GROUP, turned, pltpu.roll(turned, 7, 1))


def block_down(field, axis):
    if axis == 0:
        return pltpu.roll(field, 2, 1)
    if axis == 2:
        return pltpu.roll(field, 1, 2)
    turned = pltpu.roll(field, GROUP, 2)
    return jnp.where(iota(field.shape, 2) >= GROUP, turned, pltpu.roll(turned, 1, 1))


def inside_up(field, axis):
    sub, lane = iota(field.shape, 1), iota(field.shape, 2)
    if axis == 0:
        keep = sub < 6
    elif axis == 1:
        keep = (lane < LANES - GROUP) | (sub % 2 == 0)
    else:
        keep = lane % GROUP < GROUP - 1
    return jnp.where(keep, field, 0.0)


def inside_down(field, axis):
    sub, lane = iota(field.shape, 1), iota(field.shape, 2)
    if axis == 0:
        keep = sub >= 2
    elif axis == 1:
        keep = (lane >= GROUP) | (sub % 2 == 1)
    else:
        keep = lane % GROUP > 0
    return jnp.where(keep, field, 0.0)


def pair_rows(row):
    count = row.shape[0] // 2
    return jnp.concatenate([row[2 * i : 2 * i + 1] + row[2 * i + 1 : 2 * i + 2] for i in range(count)])


def twice(row):
    return jnp.concatenate([row[i // 2 : i // 2 + 1] for i in range(2 * row.shape[0])])


def electrode_kernel(
    stations_ref,
    currents_ref,
    receivers_ref,
    observed_ref,
    cells_ref,
    spot_ref,
    rows_ref,
    same_ref,
    pairs_ref,
    turned_ref,
    held_ref,
):
    stations = stations_ref[...]
    electrodes = stations.shape[1]
    cell_x, cell_y, cell_z, row, spot = station_table(stations)
    wide = SIDE + 2
    register = (((cell_x & 7) + 1) * wide + (cell_z & 7) + 1) * wide + (cell_y & 7) + 1
    cells_ref[...] = register * SIDE + row
    spot_ref[...] = spot
    held_ref[...] = observed_ref[...]
    line = stations & 0x1C387 | row << 20
    same = jnp.broadcast_to(line, (electrodes, electrodes))
    same = jnp.where(same == same.T, 1.0, 0.0).astype(jnp.bfloat16)
    same_ref[...] = same
    rows_ref[...] = shared_rows(currents_ref[...], spot, same)
    receivers = receivers_ref[...]
    numbers = iota((receivers.shape[0], electrodes), 1)
    pairs = jnp.where(numbers == receivers[:, 0:1], 1.0, 0.0) - jnp.where(
        numbers == receivers[:, 1:2], 1.0, 0.0
    )
    pairs_ref[...] = pairs.astype(jnp.bfloat16)
    turned_ref[...] = pairs.T.astype(jnp.bfloat16)


def shared_rows(amounts, spot, same):
    electrodes = amounts.shape[1]
    at_spot = iota((LANES, electrodes), 0) == spot
    return product(jnp.where(at_spot, amounts, 0.0), same, 3).T


class Edged:
    def __init__(self, ref, side):
        self.ref, self.side = ref, side

    def start(self, x, z, y=0):
        wide = self.side + 2
        return (((x + 1) * wide + z + 1) * wide + y + 1) * SIDE

    def __getitem__(self, at):
        x, z = at
        rows = self.ref[pl.ds(self.start(x, z), self.side * SIDE), :]
        return rows.reshape(self.side, SIDE, LANES)

    def __setitem__(self, at, value):
        x, z = at
        self.ref[pl.ds(self.start(x, z), self.side * SIDE), :] = value.reshape(-1, LANES)

    def put(self, x, z, value, exact=False, along_z=True):
        self[x, z] = value
        n = self.side
        if z == 0 and along_z:
            edge = block_up(value, 2)
            self[x, n] = inside_up(edge, 2) if exact else edge
        if z == n - 1 and along_z:
            edge = block_down(value, 2)
            self[x, -1] = inside_down(edge, 2) if exact else edge
        if x == 0:
            edge = block_up(value, 0)
            self[n, z] = inside_up(edge, 0) if exact else edge
        if x == n - 1:
            edge = block_down(value, 0)
            self[-1, z] = inside_down(edge, 0) if exact else edge
        if exact:
            after = inside_up(block_up(value[:1], 1), 1)
            self.ref[pl.ds(self.start(x, z, n), SIDE), :] = after[0]
            before = inside_down(block_down(value[n - 1 :], 1), 1)
            self.ref[pl.ds(self.start(x, z, -1), SIDE), :] = before[0]

    def close_z(self, x, exact=False):
        n = self.side
        after, before = block_up(self[x, 0], 2), block_down(self[x, n - 1], 2)
        self[x, n] = inside_up(after, 2) if exact else after
        self[x, -1] = inside_down(before, 2) if exact else before

    def close(self, exact=False):
        n = self.side
        for z in range(n):
            after = block_up(self[0, z], 0)
            self[n, z] = inside_up(after, 0) if exact else after
            before = block_down(self[n - 1, z], 0)
            self[-1, z] = inside_down(before, 0) if exact else before


class Rows:
    def __init__(self, ref, side, first_x=0, first_z=0):
        self.ref, self.side, self.first_x, self.first_z = ref, side, first_x, first_z

    def place(self, at):
        count = self.side - self.first_z
        rows = self.side * SIDE
        return pl.ds(((at[0] - self.first_x) * count + at[1] - self.first_z) * rows, rows)

    def __getitem__(self, at):
        return self.ref[self.place(at), :].reshape(self.side, SIDE, LANES)

    def __setitem__(self, at, value):
        self.ref[self.place(at), :] = value.reshape(-1, LANES)


def rolled(count, body, unroll=1):
    def one(x, carry):
        body(x)
        return carry

    lax.fori_loop(0, count, one, 0, unroll=unroll)


def next_in_y(row):
    return jnp.concatenate([row[1:], block_up(row[:1], 1)])


def last_in_y(row):
    return jnp.concatenate([block_down(row[-1:], 1), row[:-1]])


class Level:
    def __init__(self, refs, index):
        self.side = side = SIDE >> index
        self.scale = 0.25**index
        edged = [Edged(ref, side) for ref in refs[:5]]
        self.cond, self.first, self.second, self.base, self.weight = edged
        self.link_x = Rows(refs[5], side, first_x=-1)
        self.link_y = Rows(refs[6], side)
        self.link_z = Rows(refs[7], side, first_z=-1)
        self.back = Rows(refs[8], side)

    @staticmethod
    def scratch(index):
        side = SIDE >> index
        sizes = [(side + 2) ** 3] * 5
        sizes += [side**2 * (side + 1), side**3, side**2 * (side + 1), side**3]
        return [pltpu.VMEM((size * SIDE, LANES), jnp.float32) for size in sizes]

    def pairs(self, body):
        for i in range(self.side // 2):
            body(2 * i)

    def prepare(self):
        n = self.side
        cond = self.cond

        def plane(x):
            for z in range(n):
                here, ahead, next_x = cond[x, z], cond[x, z + 1], cond[x + 1, z]
                after = inside_up(block_up(here[:1], 1), 1)
                before = inside_down(block_down(here[-1:], 1), 1)
                next_y = jnp.concatenate([here[1:], after])
                last_y = jnp.concatenate([before, here[:-1]])
                total = (next_x + cond[x - 1, z]) + (ahead + cond[x, z - 1]) + (next_y + last_y)
                total = 6.0 * here + total
                self.weight[x, z] = DAMPING * reciprocal(total)
                if n == SIDE:
                    self.base[x, z] = jnp.zeros_like(here)
                self.back[x, z] = total * (0.5 * self.scale / DAMPING)
                self.link_x[x, z] = here + next_x
                link = here + next_y
                self.link_y[x, z] = jnp.concatenate([link[:-1], inside_up(link[-1:], 1)])
                link = here + ahead
                if z == n - 1:
                    link = inside_up(link, 2)
                    self.link_z[x, -1] = block_down(link, 2)
                self.link_z[x, z] = link

        if n == SIDE:
            rolled(n, plane, unroll=2)
        else:
            for x in range(n):
                plane(x)
        for z in range(n):
            link = inside_up(self.link_x[n - 1, z], 0)
            self.link_x[n - 1, z] = link
            self.link_x[-1, z] = block_down(link, 0)

    def flows(self, x, z, here, ahead, outer, down):
        result = []
        inner = self.link_x[x, z]
        sides = [
            self.link_x[x - 1, z] * outer[0] + inner * here[1],
            inner * here[0] + self.link_x[x + 1, z] * outer[1],
        ]
        for p in range(2):
            link_y, link_z = self.link_y[x + p, z], self.link_z[x + p, z]
            along = link_y * next_in_y(here[p]) + last_in_y(link_y * here[p])
            total = sides[p] + (link_z * ahead[p] + down[p]) + along
            down[p] = link_z * here[p]
            result.append(self.weight[x + p, z] * total)
        return result

    def rows(self, field, x):
        here = [field[x, 0], field[x + 1, 0]]
        down = [self.link_z[x + p, -1] * field[x + p, -1] for p in range(2)]
        for z in range(self.side):
            ahead = [field[x, z + 1], field[x + 1, z + 1]]
            outer = [field[x - 1, z], field[x + 2, z]]
            yield z, here, self.flows(x, z, here, ahead, outer, down)
            here = ahead

    def sweep(self, field, out, exact=False):
        def pair(x):
            for z, here, sums in self.rows(field, x):
                for p in range(2):
                    if field is self.base:
                        value = (2.0 - DAMPING) * here[p] + sums[p]
                    else:
                        value = (1.0 - DAMPING) * here[p] + (self.base[x + p, z] + sums[p])
                    out.put(x + p, z, value, exact, along_z=not exact)

        self.pairs(pair)

    def halve(self, rows, coarse):
        def pair(x):
            held = None
            for z, row in enumerate(rows(x)):
                row = row[0] + row[1]
                if z % 2 == 0:
                    held = row
                else:
                    coarse(x // 2, z // 2, 0.125 * pair_rows(held + row))

        self.pairs(pair)

    def descend(self, coarse):
        self.sweep(self.base, self.second)

        def residuals(x):
            for z, here, sums in self.rows(self.second, x):
                result = []
                for p in range(2):
                    swept = (1.0 - DAMPING) * here[p] + (self.base[x + p, z] + sums[p])
                    self.first[x + p, z] = swept
                    result.append((swept - here[p]) * self.back[x + p, z])
                yield result

        self.halve(residuals, coarse)

    def ascend(self, correction, out, exact=False):
        def pair(x):
            i = x // 2
            here = twice(correction(i, 0))
            start = twice(correction(i, -1))
            down = [self.link_z[x + p, -1] * start for p in range(2)]
            for z in range(self.side):
                ahead = twice(correction(i, (z + 1) // 2))
                outer = [twice(correction(i - 1, z // 2)), twice(correction(i + 1, z // 2))]
                sums = self.flows(x, z, [here, here], [ahead, ahead], outer, down)
                for p in range(2):
                    value = self.first[x + p, z] + ((1.0 - DAMPING) * here + sums[p])
                    self.second.put(x + p, z, value)
                here = ahead

        self.pairs(pair)
        self.sweep(self.second, out, exact)


def reciprocal(value):
    result = pl.reciprocal(value, approx=True)
    for _ in range(2):
        result = result * (2.0 - value * result)
    return result


class HeldLevel:
    def __init__(self, refs, index):
        self.side = 2
        self.scale = 0.25**index
        self.cond, self.first = Edged(refs[0], 2), Edged(refs[1], 2)
        self.weight, self.back = Rows(refs[2], 2), Rows(refs[3], 2)
        self.links = [Rows(ref, 2) for ref in refs[4:]]

    @staticmethod
    def scratch(index):
        sizes = [4**3] * 2 + [2**3] * 8
        return [pltpu.VMEM((size * SIDE, LANES), jnp.float32) for size in sizes]

    def around(self, field, inside=False):
        def moved(row, axis, up):
            row = (block_up if up else block_down)(row, axis)
            return (inside_up if up else inside_down)(row, axis) if inside else row

        result = {}
        for (x, z), here in field.items():
            result[x, z] = [
                field[1, z] if x == 0 else moved(field[0, z], 0, True),
                field[0, z] if x == 1 else moved(field[1, z], 0, False),
                jnp.concatenate([here[1:], moved(here[:1], 1, True)]),
                jnp.concatenate([moved(here[-1:], 1, False), here[:-1]]),
                field[x, 1] if z == 0 else moved(field[x, 0], 2, True),
                field[x, 0] if z == 1 else moved(field[x, 1], 2, False),
            ]
        return result

    def prepare(self):
        field = {(x, z): self.cond[x, z] for x in range(2) for z in range(2)}
        for at, others in self.around(field, inside=True).items():
            here = field[at]
            total = others[0]
            for other in others[1:]:
                total = total + other
            total = 3.0 * here + 0.5 * total
            inverse = DAMPING / total
            self.weight[at] = inverse
            self.back[at] = total * (self.scale / DAMPING)
            for index, other in enumerate(others):
                link = 0.5 * inverse * (here + other)
                self.links[index][at] = jnp.where(other > 0.0, link, 0.0)

    def halve(self, rows, coarse):
        total = None
        for row in rows(0):
            row = row[0] + row[1]
            total = row if total is None else total + row
        coarse(0, 0, 0.125 * (total[:1] + total[1:]))

    def sums(self, field, base):
        result = {}
        for at, others in self.around(field).items():
            total = base[at]
            for link, other in zip(self.links, others):
                total = total + link[at] * other
            result[at] = total
        return result

    def swept(self, field, base):
        sums = self.sums(field, base)
        return {at: (1.0 - DAMPING) * field[at] + sums[at] for at in field}

    def cycle(self, base, solve, out):
        field = self.swept(base, base)
        sums = self.sums(field, base)
        total = None
        for at in field:
            residual = (sums[at] - DAMPING * field[at]) * self.back[at]
            total = residual if total is None else total + residual
        solved = solve(0.125 * (total[:1] + total[1:]))
        row = twice(solved)
        copied = {at: row for at in field}
        change = {at: sums[at] + (1.0 - DAMPING) * (field[at] + row) for at in field}
        field = self.sums(copied, change)
        for (x, z), value in self.swept(field, base).items():
            out.put(x, z, value)


def replicated_kernel(
    whole,
    halved,
    cells_ref,
    *refs,
):
    parts = refs[:whole], refs[whole : whole + halved]
    solve_kernel(*parts, cells_ref, *refs[whole + halved :])


def solve_kernel(
    part_refs,
    half_refs,
    cells_ref,
    spot_ref,
    rows_ref,
    same_ref,
    pairs_ref,
    turned_ref,
    observed_ref,
    potentials_ref,
    mine_ref,
    theirs_ref,
    gathered,
    owned,
    beside,
    *level_refs,
):
    f32 = jnp.float32
    electrodes = spot_ref.shape[1]
    levels, used = [], 0
    for index in range(LEVELS - 1):
        kind = HeldLevel if index == LEVELS - 2 else Level
        count = len(kind.scratch(index))
        levels.append(kind(level_refs[used : used + count], index))
        used += count
    fine = levels[0]
    forward = fine.cond
    wide = SIDE * SIDE * SIDE

    device, shot = own_place()

    def place(part, row, x, index):
        for z in range(SIDE):
            fine.cond.ref[pl.ds(fine.cond.start(x, z) + index, SIDE, stride=SIDE), :] = part[
                pl.ds((row * SIDE + z) * SIDE, SIDE), :
            ]

    def collect(x):
        for k, part in enumerate(part_refs):
            place(part, x, x, device ^ k)

    def collect_half(x):
        for k, part in enumerate(half_refs):
            swapped, index = k // 2 % 2, len(part_refs) + k // 4 * 2 + k % 2
            place(part, x, (shot ^ swapped) * (SIDE // 2) + x, device ^ index)

    def edges(x):
        fine.cond.close_z(x, exact=True)

    rolled(SIDE, collect, unroll=4)
    for x in range(SIDE // 2):
        collect_half(x)
    for x in range(SIDE):
        edges(x)
    fine.cond.close(exact=True)

    coarsest = []
    for level, below in zip(levels, levels[1:] + [None]):
        level.prepare()

        def coarse(x, z, row, below=below):
            if below is None:
                coarsest.append(row)
            else:
                below.cond.put(x, z, row, exact=True)

        level.halve(
            lambda x, level=level: [
                (level.cond[x, z], level.cond[x + 1, z]) for z in range(level.side)
            ],
            coarse,
        )

    here = coarsest[0]
    moves = [(axis, up) for axis in range(3) for up in (True, False)]

    def moved(value, axis, up):
        return block_up(value, axis) if up else block_down(value, axis)

    def inside(value, axis, up):
        return inside_up(value, axis) if up else inside_down(value, axis)

    others = [inside(moved(here, axis, up), axis, up) for axis, up in moves]
    total = 6.0 * here
    for other in others:
        total = total + other
    inverse = DAMPING / total
    last_weight = inverse * (2.0 / 0.25 ** (LEVELS - 1))
    last_links = [
        inside(inverse * (here + other), axis, up) for other, (axis, up) in zip(others, moves)
    ]

    def solve_last(rhs):
        base = last_weight * rhs
        value = base
        for _ in range(COARSE_SWEEPS - 1):
            parts = [
                link * moved(value, axis, up) for link, (axis, up) in zip(last_links, moves)
            ]
            start = base + (1.0 - DAMPING) * value
            value = ((start + parts[0]) + (parts[1] + parts[4])) + parts[5]
            value = value + (parts[2] + parts[3])
        return value

    def cycle(index, out, exact=False):
        level = levels[index]
        below = levels[index + 1]
        if index == LEVELS - 3:
            base = {}

            def take(x, z, row):
                base[x, z] = below.weight[x, z] * (row * (1.0 / below.scale))

            level.descend(take)
            below.cycle(base, solve_last, below.first)
        else:
            level.descend(
                lambda x, z, row: below.base.put(
                    x, z, below.weight[x, z] * (row * (2.0 / below.scale))
                )
            )
            cycle(index + 1, below.first)
        level.ascend(lambda x, z: below.first[x, z], out, exact)

    spot = spot_ref[...]
    at_spot = iota((LANES, electrodes), 0) == spot
    order = lane_order(back=True)
    wide = SIDE + 2

    def each(body):
        def one(electrode, carry):
            body(pl.ds(electrode, 1), pl.ds(cells_ref[0, electrode], 1))
            return carry

        lax.fori_loop(0, electrodes, one, 0, unroll=64)

    def put(electrode, cell):
        fine.base.ref[cell, :] = (2.0 * gathered[electrode, :]) * fine.weight.ref[cell, :]

    def read(electrode, cell):
        gathered[electrode, :] = forward.ref[cell, :]

    def exact(row, matrix_ref):
        return product(jnp.broadcast_to(row, (16, row.shape[1])), matrix_ref[...], 3)[0:1]

    sub, lane = iota((SIDE, LANES), 0), iota((SIDE, LANES), 1)

    def margin(x, z, y):
        return forward.ref[pl.ds(forward.start(x, z, y) + device, 1), :]

    def extract(index):
        for x in range(-1, SIDE + 1):
            for z in range(SIDE):
                at = (x + 1) * wide + z + 1
                start = forward.start(x, z) + device
                row = forward.ref[pl.ds(start, SIDE, stride=SIDE), :]
                owned[index, at] = row
                if 0 <= x < SIDE:
                    after, before = margin(x, z, SIDE), margin(x, z, -1)
                    place = x * SIDE + z
                    turned = pltpu.roll(row, SIDE - 1, 0)
                    beside[index, 0, place] = jnp.where(sub == SIDE - 1, after, turned)
                    beside[index, 1, place] = jnp.where(sub == 0, before, pltpu.roll(row, 1, 0))
                    if z == 0:
                        edge = pltpu.roll(row, LANES - 1, 1)
                        owned[index, at + SIDE] = jnp.where(lane % GROUP < GROUP - 1, edge, 0.0)
                    if z == SIDE - 1:
                        edge = pltpu.roll(row, 1, 1)
                        owned[index, at - SIDE] = jnp.where(lane % GROUP > 0, edge, 0.0)

    def solve(index):
        each(put)
        for x in range(SIDE):
            fine.base.close_z(x)
        fine.base.close()
        cycle(0, forward, exact=True)
        extract(index)

        @pl.when(index == 0)
        def _():
            each(read)
            readings = jnp.where(at_spot, gathered[...].T, 0.0)
            readings = jnp.sum(readings, axis=0, keepdims=True)
            misfit = exact(readings, turned_ref) - observed_ref[...]
            gathered[...] = shared_rows(exact(misfit, pairs_ref), spot, same_ref[...])

    gathered[...] = rows_ref[...]
    rolled(2, solve)

    chunk = mine_ref.shape[1]
    even = shot == 0
    for x in range(SIDE):
        tiles = []
        for z in range(SIDE):
            at = (x + 1) * wide + z + 1
            here_u, here_w = owned[0, at], owned[1, at]
            potentials_ref[pl.ds((x * SIDE + z) * SIDE, SIDE), :] = here_u
            total = None
            for step in (wide, -wide, 1, -1):
                term = (here_u - owned[0, at + step]) * (here_w - owned[1, at + step])
                total = term if total is None else total + term
            for side in range(2):
                other_u, other_w = beside[0, side, x * SIDE + z], beside[1, side, x * SIDE + z]
                total = total + (here_u - other_u) * (here_w - other_w)
            tiles.append(-0.5 * total)
        natural = from_blocks(tiles, order)
        low, high = natural[:chunk], natural[chunk:]
        mine_ref[x] = jnp.where(even, low, high)
        theirs_ref[x] = jnp.where(even, high, low)


def replicated(conductivity, stations, currents, receivers, observed):
    rows, cols, depth = conductivity.shape
    f32 = jnp.float32
    electrodes = stations.shape[0]
    total = rows * cols
    vmem = pl.BlockSpec(memory_space=pltpu.VMEM)
    smem = pl.BlockSpec(memory_space=pltpu.SMEM)
    station_row = stations.reshape(1, electrodes)
    mine, half = pl.pallas_call(
        to_blocks_kernel,
        out_shape=(
            jax.ShapeDtypeStruct((total, LANES), f32),
            jax.ShapeDtypeStruct((total // 2, LANES), f32),
        ),
        in_specs=[vmem],
        out_specs=(vmem, vmem),
        compiler_params=pltpu.CompilerParams(vmem_limit_bytes=SMALL_BYTES),
    )(conductivity)
    swap = [(0, 1), (1, 0)]

    def partner(part, k):
        count = lax.axis_size("gx")
        return lax.ppermute(part, "gx", [(i, i ^ k) for i in range(count)])

    def with_mate(part):
        return [part, lax.ppermute(part, "gy", swap)]

    far = partner(half, 2)
    near = partner(mine, 1)
    line = jax.ShapeDtypeStruct((1, electrodes), jnp.int32)
    cells, spot, rows_of, same, pairs, turned, held = pl.pallas_call(
        electrode_kernel,
        out_shape=(
            line,
            line,
            jax.ShapeDtypeStruct((electrodes, LANES), f32),
            jax.ShapeDtypeStruct((electrodes, electrodes), jnp.bfloat16),
            jax.ShapeDtypeStruct((receivers.shape[0], electrodes), jnp.bfloat16),
            jax.ShapeDtypeStruct((electrodes, receivers.shape[0]), jnp.bfloat16),
            jax.ShapeDtypeStruct(observed.shape, f32),
        ),
        in_specs=[vmem] * 4,
        out_specs=(vmem,) * 7,
        compiler_params=pltpu.CompilerParams(vmem_limit_bytes=SMALL_BYTES),
        cost_estimate=pl.CostEstimate(flops=100_000_000, bytes_accessed=1_000_000, transcendentals=0),
    )(station_row, currents, receivers, observed)
    far, rows_of = lax.optimization_barrier((far, rows_of))
    count_x = lax.axis_size("gx")
    diagonal = [(2 * i + j, 2 * (i ^ 1) + 1 - j) for i in range(count_x) for j in range(2)]
    crossed, relayed = lax.ppermute(far, "shot", swap), partner(far, 1)
    slanted = lax.ppermute(far, ("gx", "shot"), diagonal)
    parts = [piece for own in (mine, near) for piece in with_mate(own)]
    halved = [piece for own in (far, crossed, relayed) for piece in with_mate(own)]
    slanted, halved[3] = lax.optimization_barrier((slanted, halved[3]))
    halved += with_mate(slanted)
    chunk = cols // 2
    levels = [shape for index in range(LEVELS - 2) for shape in Level.scratch(index)]
    levels += HeldLevel.scratch(LEVELS - 2)
    potentials, own, theirs = pl.pallas_call(
        functools.partial(replicated_kernel, len(parts), len(halved)),
        out_shape=(
            jax.ShapeDtypeStruct((total, LANES), f32),
            jax.ShapeDtypeStruct((rows, chunk, LANES), f32),
            jax.ShapeDtypeStruct((rows, chunk, LANES), f32),
        ),
        in_specs=[smem] + [vmem] * (len(parts) + len(halved) + 6),
        out_specs=(vmem, vmem, vmem),
        scratch_shapes=[
            pltpu.VMEM((electrodes, LANES), f32),
            pltpu.VMEM((2, (SIDE + 2) ** 2, SIDE, LANES), f32),
            pltpu.VMEM((2, 2, SIDE**2, SIDE, LANES), f32),
        ]
        + levels,
        compiler_params=pltpu.CompilerParams(vmem_limit_bytes=VMEM_BYTES),
        cost_estimate=pl.CostEstimate(flops=200_000_000, bytes_accessed=4_000_000, transcendentals=0),
    )(cells, *parts, *halved, spot, rows_of, same, pairs, turned, held)
    arrived = lax.ppermute(theirs, "shot", swap)
    potentials = pl.pallas_call(
        potentials_kernel,
        out_shape=jax.ShapeDtypeStruct((rows, cols, LANES), f32),
        in_specs=[vmem],
        out_specs=vmem,
        compiler_params=pltpu.CompilerParams(vmem_limit_bytes=SMALL_BYTES),
        cost_estimate=pl.CostEstimate(flops=50_000_000, bytes_accessed=500_000, transcendentals=0),
    )(potentials)
    return potentials[None], own + arrived


def extended(array, sides, width):
    for axis, dim in sides:
        size, length = (lax.axis_size(axis), array.shape[dim])
        up = [(i, (i + 1) % size) for i in range(size - 1)]
        down = [(j, i) for i, j in up]
        last = lax.slice_in_dim(array, length - width, length, axis=dim)
        leading = lax.slice_in_dim(array, 0, width, axis=dim)
        before = lax.ppermute(last, axis, up)
        after = lax.ppermute(leading, axis, down)
        array = jnp.concatenate([before, array, after], axis=dim)
    return array


def upper_z(field):
    return jnp.concatenate([field[..., 1:], jnp.zeros_like(field[..., :1])], axis=-1)


def lower_z(field):
    return jnp.concatenate([jnp.zeros_like(field[..., :1]), field[..., :-1]], axis=-1)


def trim_circle(field, circle_width):
    return field[..., circle_width:-circle_width, circle_width:-circle_width, :]


def pad_plane(field, circle_width):
    spec = [(0, 0)] * (field.ndim - 3) + [
        (circle_width, circle_width),
        (circle_width, circle_width),
        (0, 0),
    ]
    return jnp.pad(field, spec)


def neighbour_list(field_pad):
    centre = trim_circle(field_pad, 1)
    return [
        field_pad[..., 2:, 1:-1, :],
        field_pad[..., :-2, 1:-1, :],
        field_pad[..., 1:-1, 2:, :],
        field_pad[..., 1:-1, :-2, :],
        upper_z(centre),
        lower_z(centre),
    ]


def stencil(field_pad, cond_pad, level_scale):
    centre = trim_circle(field_pad, 1)
    centre_cond = trim_circle(cond_pad, 1)
    summed = jnp.zeros_like(centre)
    for other, other_cond in zip(neighbour_list(field_pad), neighbour_list(cond_pad)):
        summed = summed + level_scale * 0.5 * (centre_cond + other_cond) * (centre - other)
    return summed


def diagonal(cond_pad, level_scale):
    centre_cond = trim_circle(cond_pad, 1)
    summed = jnp.zeros_like(centre_cond)
    for other_cond in neighbour_list(cond_pad):
        summed = summed + level_scale * 0.5 * (centre_cond + other_cond)
    return summed


def relaxed(field_pad, source, cond_pad, diag_level, level_scale):
    return (
        trim_circle(field_pad, 1)
        + DAMPING * (source - stencil(field_pad, cond_pad, level_scale)) / diag_level
    )


def restrict(field):
    leading = field.shape[:-3]
    extent = field.shape[-3:]
    shaped = field.reshape(leading + (extent[0] // 2, 2, extent[1] // 2, 2, extent[2] // 2, 2))
    return shaped.mean(axis=(-5, -3, -1))


def prolong(field):
    return jnp.repeat(jnp.repeat(jnp.repeat(field, 2, axis=-3), 2, axis=-2), 2, axis=-1)


def assemble(blocks, count_x, count_y):
    leading = blocks.shape[1:-3]
    extent = blocks.shape[-3:]
    depth_lead = len(leading)
    shaped = blocks.reshape((count_x, count_y) + leading + extent)
    order = tuple(range(2, 2 + depth_lead)) + (0, 2 + depth_lead, 1, 3 + depth_lead, 4 + depth_lead)
    return shaped.transpose(order).reshape(
        leading + (count_x * extent[0], count_y * extent[1], extent[2])
    )


def field_rim(field):
    return extended(field, (("gx", 1), ("gy", 2)), 1)


def cond_rim(conduct):
    return extended(conduct, (("gx", 0), ("gy", 1)), 1)


def whole_cycle(source, level_index, whole_plans):
    cond_pad, diag_level, level_scale = whole_plans[level_index]
    field = DAMPING * source / diag_level

    def turn(turn_index, iterate):
        return relaxed(pad_plane(iterate, 1), source, cond_pad, diag_level, level_scale)

    return lax.fori_loop(0, COARSE_SWEEPS - 1, turn, field)


def part_cycle(source, level_index, level_plans, whole_plans, gather_level):
    if level_index == gather_level:
        blocks = lax.all_gather(source[None], ("gx", "gy"), axis=0, tiled=True)
        whole = assemble(blocks, lax.axis_size("gx"), lax.axis_size("gy"))
        correction = whole_cycle(whole, level_index, whole_plans)
        extent = source.shape
        starts = (0, lax.axis_index("gx") * extent[1], lax.axis_index("gy") * extent[2], 0)
        return lax.dynamic_slice(correction, starts, extent)
    cond_pad, diag_level, level_scale = level_plans[level_index]
    field = DAMPING * source / diag_level
    field = relaxed(field_rim(field), source, cond_pad, diag_level, level_scale)
    residual = source - stencil(field_rim(field), cond_pad, level_scale)
    field = field + prolong(
        part_cycle(restrict(residual), level_index + 1, level_plans, whole_plans, gather_level)
    )
    field = relaxed(field_rim(field), source, cond_pad, diag_level, level_scale)
    return relaxed(field_rim(field), source, cond_pad, diag_level, level_scale)


def distributed(conductivity, stations, currents, receivers, observed):
    row_count, col_count, z_count = conductivity.shape
    shot_count = currents.shape[0]
    count_x = lax.axis_size("gx")
    count_y = lax.axis_size("gy")
    gather_level = LEVELS - 1
    level_plans = []
    conduct = conductivity
    for level_index in range(gather_level):
        level_scale = 0.25**level_index
        cond_pad = cond_rim(conduct)
        level_plans.append((cond_pad, diagonal(cond_pad, level_scale), level_scale))
        conduct = restrict(conduct)
    blocks = lax.all_gather(conduct[None], ("gx", "gy"), axis=0, tiled=True)
    whole = assemble(blocks, count_x, count_y)
    whole_plans = {}
    level_index = 3
    level_scale = 0.25**level_index
    cond_pad = pad_plane(whole, 1)
    whole_plans[level_index] = (cond_pad, diagonal(cond_pad, level_scale), level_scale)
    total_y = col_count * count_y
    cell_x = stations // (total_y * z_count)
    cell_y = stations // z_count % total_y
    cell_z = stations % z_count
    local_x = cell_x - lax.axis_index("gx") * row_count
    local_y = cell_y - lax.axis_index("gy") * col_count
    owned = (local_x >= 0) & (local_x < row_count) & (local_y >= 0) & (local_y < col_count)
    block_size = row_count * col_count * z_count
    local_cell = jnp.where(owned, (local_x * col_count + local_y) * z_count + cell_z, 0)
    offsets = jnp.arange(shot_count)[:, None] * block_size + local_cell[None, :]
    targets = jnp.where(owned[None, :], offsets, shot_count * block_size).reshape(-1)

    def spread(amounts):
        flat = (
            jnp.zeros((shot_count * block_size,), jnp.float32)
            .at[targets]
            .add(amounts.reshape(-1), mode="drop")
        )
        return flat.reshape(shot_count, row_count, col_count, z_count)

    potentials = part_cycle(spread(currents), 0, level_plans, whole_plans, gather_level)
    local_values = jnp.where(
        owned[None, :], potentials.reshape(shot_count, block_size)[:, local_cell], 0.0
    )
    readings = lax.psum(local_values, ("gx", "gy"))
    positions = jnp.arange(stations.shape[0])[:, None]
    pairs = (receivers[:, 0][None, :] == positions).astype(jnp.float32) - (
        receivers[:, 1][None, :] == positions
    ).astype(jnp.float32)
    misfit = jnp.dot(readings, pairs, precision=lax.Precision.HIGHEST) - observed
    back_source = jnp.dot(misfit, pairs.T, precision=lax.Precision.HIGHEST)
    adjoint = part_cycle(spread(back_source), 0, level_plans, whole_plans, gather_level)
    stacked = jnp.concatenate([potentials, adjoint], axis=0)
    padded = extended(stacked, (("gx", 1), ("gy", 2)), 1)
    potential_pad = padded[:shot_count]
    adjoint_pad = padded[shot_count:]
    gradient = jnp.zeros_like(potentials)
    for other_u, other_w in zip(neighbour_list(potential_pad), neighbour_list(adjoint_pad)):
        gradient = gradient - 0.5 * (potentials - other_u) * (adjoint - other_w)
    summed = lax.psum_scatter(jnp.sum(gradient, axis=0), "shot", scatter_dimension=1, tiled=True)
    return (potentials, summed)


def per_device(conductivity, stations, currents, receivers, observed):
    blocks = lax.axis_size("gx") * lax.axis_size("gy")
    fits = conductivity.shape == (SIDE, SIDE * SIDE, LANES) and blocks == SIDE
    fits = fits and lax.axis_size("gy") == 2 and lax.axis_size("shot") == 2
    fits = fits and currents.shape[0] == 1
    plan = replicated if fits else distributed
    return plan(conductivity, stations, currents, receivers, observed)


def solution(mesh):
    in_specs = (
        P(("grp", "gx"), "gy", None),
        P("grp"),
        P(("grp", "shot"), None),
        P("grp", None),
        P(("grp", "shot"), None),
    )
    out_specs = (P(("grp", "shot"), "gx", "gy", None), P(("grp", "gx"), ("gy", "shot"), None))
    return jax.shard_map(
        per_device, mesh=mesh, in_specs=in_specs, out_specs=out_specs, check_vma=False
    )
```
